128 devices in a mesh: dp: 32 (over y, x_lo, z), tensor: 4 (over x_hi, core).
Axes of the slice: x: 4 (x_hi: 2, x_lo: 2; x = x_hi * 2 + x_lo), y: 4, z: 4, core: 2. Of those that a mesh axis runs over, the one named last changes fastest.
Arguments:
- inputs: bfloat16 [16384, 2048], P(('dp', 'tensor')), may hold values from -6 to 6
- segments: int32 [16384], P('dp'), may hold values from 0 to 2, as said below
- att_routes: int32 [16384, 2], P('dp'), may hold values from 0 to 2, all different within a row; in each aligned block of 512 rows (0 to 511, 512 to 1023, ...) at most 384 rows name the same one
- mlp_routes: int32 [16384, 2], P('dp'), may hold values from 0 to 3, all different within a row; in each aligned block of 512 rows (0 to 511, 512 to 1023, ...) at most 320 rows name the same one
- key_value: bfloat16 [2048, 2, 2048], P('dp', None, 'tensor'), may hold values from -0.125 to 0.125
- query_proj: bfloat16 [3, 2048, 2048], P(None, 'dp', 'tensor'), may hold values from -0.125 to 0.125
- output_proj: bfloat16 [3, 2048, 2048], P(None, 'tensor', 'dp'), may hold values from -1 to 1
- router_att: bfloat16 [2048, 3], P('dp'), may hold values from -0.09375 to 0.09375
- gain_att: bfloat16 [2048], P('dp'), may hold values from 0.5 to 1.5
- gate_up: bfloat16 [4, 2048, 2, 5632], P(None, 'dp', None, 'tensor'), may hold values from -0.125 to 0.125
- down_proj: bfloat16 [4, 5632, 2048], P(None, 'tensor', 'dp'), may hold values from -0.15625 to 0.15625
- router_mlp: bfloat16 [2048, 4], P('dp'), may hold values from -0.09375 to 0.09375
- gain_mlp: bfloat16 [2048], P('dp'), may hold values from 0.5 to 1.5
- out_grad: bfloat16 [16384, 2048], P(('dp', 'tensor')), may hold values from -6 to 6
Outputs:
- output: bfloat16 [16384, 2048], P(('dp', 'tensor'))
- grad_inputs: float32 [16384, 2048], P(('dp', 'tensor'))
- grad_key_value: float32 [2048, 2, 2048], P('dp', None, 'tensor')
- grad_query_proj: float32 [3, 2048, 2048], P(None, 'dp', 'tensor')
- grad_output_proj: float32 [3, 2048, 2048], P(None, 'tensor', 'dp')
- grad_router_att: float32 [2048, 3], P('dp')
- grad_gain_att: float32 [2048], P('dp')
- grad_gate_up: float32 [4, 2048, 2, 5632], P(None, 'dp', None, 'tensor')
- grad_down_proj: float32 [4, 5632, 2048], P(None, 'tensor', 'dp')
- grad_router_mlp: float32 [2048, 4], P('dp')
- grad_gain_mlp: float32 [2048], P('dp')
The draws below stay inside these ranges and needn't reach their ends.
Inputs may be any that keep to these rules, and one draw needn't show every extreme that they name: `segments`: in each group of 512 consecutive tokens the first 256 have segment 0 (the prompt), then come a run of 1 and a run of 2 (two continuations), together 2 * 128 tokens. `att_routes`: each token names two different experts; within each group of 512 consecutive tokens no expert is named by more than 384 tokens, and in some group one is named by exactly 384. `mlp_routes`: each token names two different experts; within each group of 512 consecutive tokens no expert is named by more than 320 tokens, and in some group one is named by exactly 320.
All inputs are finite; a program needn't handle non-finite values.
Results may differ from the reference program's by a relative error of at most 0.03.
Values may be sent and summed in bfloat16 or wider, within the bound.
A program may use at most 320 MiB of HBM per device.

```python
import math
import jax
import jax.numpy as jnp
import numpy as np
from jax import lax

D = 2048
HEADS = 16
HD = 128
FF = 5632
ATT_EXPERTS = 3
EXPERTS = 4
TOP = 2
PROMPT = 256
CONT = 128
GROUP = 512
CAP = 320
ATT_CAP = 384
TOKENS = 16384
N_DP = 32


def draw_segments(key, part):
    key = jax.random.fold_in(key, 7)
    groups = TOKENS // GROUP
    first = jax.random.randint(key, (groups, 1), CONT // 2, CONT + CONT // 2 + 1)
    seq_index = jnp.arange(GROUP, dtype=jnp.int32)[None, :]
    labels = jnp.where(seq_index < PROMPT, 0, jnp.where(seq_index < PROMPT + first, 1, 2))
    return labels.reshape(-1).astype(jnp.int32)


def level_of(own_key, dims, shards, smallest, high):
    gain = 1.0
    for dim, shards_of in shards:
        steps = jax.random.uniform(jax.random.fold_in(jax.random.fold_in(own_key, 6), dim), (shards_of,), jnp.float32, smallest / len(shards), high / len(shards))
        gain = gain * jnp.repeat(jnp.exp(steps), dims[dim] // shards_of).reshape((-1,) + (1,) * (len(dims) - 1 - dim))
    return gain


def shared_out(rng, own, number, rows, count, top, most, slope):
    ranking = jax.random.permutation(rng, count)
    crowded, ordinary = portions_of(count, rows * top, most, slope, True), portions_of(count, rows * top, most, slope, False)
    places = jnp.arange(count)

    def named(tallies, offset_by):
        used = int((tallies > 0).sum())
        fixed = max(1, used // 4)
        passed = fixed + (places - fixed + offset_by * (used - fixed)) % max(1, count - fixed)
        return jnp.zeros((count,), jnp.int32).at[ranking[jnp.where(places < fixed, places, passed)]].set(jnp.asarray(tallies, jnp.int32))

    tallies = jnp.where(number % 4 == 0, named(crowded, number // 4), named(ordinary, number - number // 4 - 1))
    mixed = jax.random.permutation(jax.random.fold_in(own, 3), count)
    giver, receiver = mixed[0:count // 2 * 2:2], mixed[1:count // 2 * 2:2]
    room = jnp.minimum(tallies[giver] - 1, most - tallies[receiver]) // 2
    room = jnp.where((giver == ranking[0]) | (receiver == ranking[0]) | (tallies[receiver] == 0), 0, jnp.maximum(room, 0))
    passed = jax.random.randint(jax.random.fold_in(own, 4), (count // 2,), 0, 1 << 20) % (room + 1)
    tallies = tallies.at[giver].add(-passed).at[receiver].add(passed)
    members = jnp.searchsorted(jnp.cumsum(tallies), jnp.arange(rows * top), side="right").astype(jnp.int32)
    listing = members.reshape(top, rows).T
    listing = listing[jax.random.permutation(jax.random.fold_in(own, 1), rows)]
    offset_by = jax.random.randint(jax.random.fold_in(own, 2), (rows, 1), 0, top)
    return jnp.take_along_axis(listing, (jnp.arange(top)[None, :] + offset_by) % top, axis=1)


def portions_of(count, total, reach, slope, full):
    portions = [(1 << 20) // math.isqrt(standing ** slope) + 1 for standing in range(1, count + 1)]
    largest = reach if full else min(reach, max(-(-total // count), total * portions[0] // sum(portions)))
    least = 1 if total - largest >= count - 1 else 0
    holding, surplus = [largest] + [least] * (count - 1), total - largest - least * (count - 1)
    while surplus > 0:
        movable = [i for i in range(1, count) if holding[i] < largest] or [i for i in range(1, count) if holding[i] < reach]
        pool, left = sum([portions[i] for i in movable]), surplus
        for i in movable:
            addition = min(reach - holding[i], max(1, left * portions[i] // pool), surplus)
            holding[i] = holding[i] + addition
            surplus = surplus - addition
    return np.array(holding)


def gaussian(rng, dims, scale, reach, split=(), held_as=jnp.bfloat16):
    drawn = scale * jax.random.normal(rng, dims, jnp.float32)
    if split:
        drawn = drawn * level_of(rng, dims, split, -0.22, 0.18)
    return jnp.clip(drawn, -reach, reach).astype(held_as)


def setup_inputs(seed: int = 0) -> dict:
    streams_of = jax.random.split(jax.random.key(seed), 15)
    inputs = gaussian(streams_of[0], (TOKENS, D), 1.0, 6.0, ((0, 128),))
    segments = draw_segments(jax.random.fold_in(streams_of[14], 71), 0)
    att_routes_keys = jax.random.split(jax.random.fold_in(streams_of[2], 1), TOKENS // GROUP)
    att_routes_turns = jax.random.permutation(jax.random.fold_in(streams_of[2], 3), TOKENS // GROUP)
    att_routes = jax.vmap(lambda own, number: shared_out(jax.random.fold_in(streams_of[2], 2), own, number, GROUP, ATT_EXPERTS, TOP, ATT_CAP, 1))(att_routes_keys, att_routes_turns).reshape((TOKENS, TOP))
    mlp_routes_keys = jax.random.split(jax.random.fold_in(streams_of[3], 1), TOKENS // GROUP)
    mlp_routes_turns = jax.random.permutation(jax.random.fold_in(streams_of[3], 3), TOKENS // GROUP)
    mlp_routes = jax.vmap(lambda own, number: shared_out(jax.random.fold_in(streams_of[3], 2), own, number, GROUP, EXPERTS, TOP, CAP, 1))(mlp_routes_keys, mlp_routes_turns).reshape((TOKENS, TOP))
    key_value = gaussian(streams_of[4], (D, 2, HEADS * HD), D ** -0.5, 0.125, ((0, 32), (2, 4)))
    query_proj = gaussian(streams_of[5], (ATT_EXPERTS, D, HEADS * HD), D ** -0.5, 0.125, ((1, 32), (2, 4)))
    output_proj = gaussian(streams_of[6], (ATT_EXPERTS, HEADS * HD, D), (HEADS * HD // 64) ** -0.5, 1.0, ((1, 4), (2, 32)))
    router_att = gaussian(streams_of[7], (D, ATT_EXPERTS), (2 * D) ** -0.5, 0.09375, ((0, 32),))
    gain_att = jnp.clip(1.0 + 0.1 * jax.random.normal(streams_of[8], (D,), jnp.float32), 0.5, 1.5).astype(jnp.bfloat16)
    gate_up = gaussian(streams_of[9], (EXPERTS, D, 2, FF), D ** -0.5, 0.125, ((1, 32), (3, 4)))
    down_proj = gaussian(streams_of[10], (EXPERTS, FF, D), (FF // 4) ** -0.5, 0.15625, ((1, 4), (2, 32)))
    router_mlp = gaussian(streams_of[11], (D, EXPERTS), (2 * D) ** -0.5, 0.09375, ((0, 32),))
    gain_mlp = jnp.clip(1.0 + 0.1 * jax.random.normal(streams_of[12], (D,), jnp.float32), 0.5, 1.5).astype(jnp.bfloat16)
    out_grad = gaussian(streams_of[13], (TOKENS, D), 1.0, 6.0, ((0, 128),))
    return dict(inputs=inputs, segments=segments, att_routes=att_routes, mlp_routes=mlp_routes, key_value=key_value, query_proj=query_proj, output_proj=output_proj, router_att=router_att, gain_att=gain_att, gate_up=gate_up, down_proj=down_proj, router_mlp=router_mlp, gain_mlp=gain_mlp, out_grad=out_grad)


EPSILON = 1e-06
NEGATIVE = -1e+30
ROPE_BASE = 10000.0
HIGHEST = lax.Precision.HIGHEST

@jax.custom_vjp
def low(v):
    return lax.optimization_barrier(v.astype(jnp.bfloat16)).astype(jnp.float32)

@jax.custom_vjp
def low_back(v):
    return v

def low_keep(v):
    return (low(v), None)

def low_pass(kept, grad):
    return (grad,)

def back_keep(v):
    return (v, None)

def back_low(kept, grad):
    return (low(grad),)
low.defvjp(low_keep, low_pass)
low_back.defvjp(back_keep, back_low)

def rotate(vectors, places, direction):
    half_size = vectors.shape[-1] // 2
    rungs = jnp.arange(half_size, dtype=jnp.float32)
    frequency = ROPE_BASE ** (-2.0 * rungs / vectors.shape[-1])
    angles = places.astype(jnp.float32)[:, None] * frequency[None, :]
    cosine = jnp.cos(angles)[:, None, :]
    sine_part = direction * jnp.sin(angles)[:, None, :]
    lower_half = vectors[..., :half_size]
    upper_half = vectors[..., half_size:]
    return jnp.concatenate([lower_half * cosine - upper_half * sine_part, upper_half * cosine + lower_half * sine_part], -1)

def positions(segments):
    seq_index = jnp.arange(segments.shape[0], dtype=jnp.int32)
    before = lax.optimization_barrier(jnp.sum((segments[None, :] < segments[:, None]).astype(jnp.int32), 1))
    prompt_len = jnp.sum((segments == 0).astype(jnp.int32))
    return jnp.where(segments == 0, seq_index, prompt_len + seq_index - before)

def visible(segments, picked_ids):
    seq_index = jnp.arange(segments.shape[0], dtype=jnp.int32)
    own_segment = segments[picked_ids]
    earlier = seq_index[None, :] <= picked_ids[:, None]
    shared = (segments[None, :] == 0) | (segments[None, :] == own_segment[:, None])
    return earlier & shared

def route_gates(logits, routes, expert_count):
    chosen = jnp.take_along_axis(logits, routes, 1)
    largest = lax.optimization_barrier(jnp.max(chosen, -1, keepdims=True))
    expsum = jnp.exp(chosen - largest)
    weights = expsum / lax.optimization_barrier(jnp.sum(expsum, -1, keepdims=True))
    onehot = (routes[:, :, None] == jnp.arange(expert_count, dtype=jnp.int32)[None, None, :]).astype(jnp.float32)
    return (weights, onehot, lax.optimization_barrier(jnp.sum(weights[:, :, None] * onehot, 1)))

def slot_ids(routes, expert, capacity):
    matches = lax.optimization_barrier(jnp.sum((routes == expert).astype(jnp.int32), 1))
    return jnp.argsort(1 - matches, stable=True)[:capacity].astype(jnp.int32)

def normalize(activations):
    inverse = lax.rsqrt(lax.optimization_barrier(jnp.mean(activations * activations, -1, keepdims=True)) + EPSILON)
    return (activations * inverse, inverse)

def group_forward(params, inputs, segments, att_routes, mlp_routes):
    key_value, query_proj, output_proj, router_att, gain_att, gate_up, down_proj, router_mlp, gain_mlp = params
    group, width = inputs.shape
    inner_width = query_proj.shape[2]
    heads_local = inner_width // HD
    scale_q = 1.0 / math.sqrt(HD)
    places = positions(segments)
    unit_one = low(normalize(inputs)[0] * gain_att)
    kv_raw = jnp.dot(unit_one, key_value.reshape(width, 2 * inner_width), precision=HIGHEST)
    key_rot = low(rotate(low_back(kv_raw[:, :inner_width]).reshape(group, heads_local, HD), places, 1.0))
    val_rows = low(low_back(kv_raw[:, inner_width:])).reshape(group, heads_local, HD)
    logit_att = low_back(jnp.dot(unit_one, router_att, precision=HIGHEST))
    gate_att = route_gates(logit_att, att_routes, ATT_EXPERTS)[2]
    attention = jnp.zeros((group, width), jnp.float32)
    for expert in range(ATT_EXPERTS):
        picked_ids = slot_ids(att_routes, expert, ATT_CAP)
        picked = unit_one[picked_ids]
        query_raw = low_back(jnp.dot(picked, query_proj[expert], precision=HIGHEST))
        queries = low(rotate(query_raw.reshape(ATT_CAP, heads_local, HD), places[picked_ids], 1.0) * scale_q)
        raw_scores = low_back(jnp.einsum('chd,khd->hck', queries, key_rot, precision=HIGHEST))
        masked = jnp.where(visible(segments, picked_ids)[None], raw_scores, NEGATIVE)
        largest = lax.optimization_barrier(jnp.max(masked, -1, keepdims=True))
        expsum = jnp.exp(masked - largest)
        attn_prob = expsum / lax.optimization_barrier(jnp.sum(expsum, -1, keepdims=True))
        mixed_out = jnp.einsum('hck,khd->chd', low(attn_prob), val_rows, precision=HIGHEST)
        mixed_out = low(low_back(mixed_out.reshape(ATT_CAP, inner_width)))
        branch = low_back(jnp.dot(mixed_out, output_proj[expert], precision=HIGHEST))
        attention = attention.at[picked_ids].add(branch * gate_att[picked_ids, expert][:, None])
    middle = inputs + low_back(attention)
    unit_two = low(normalize(middle)[0] * gain_mlp)
    logit_mlp = low_back(jnp.dot(unit_two, router_mlp, precision=HIGHEST))
    gate_mlp = route_gates(logit_mlp, mlp_routes, EXPERTS)[2]
    hidden_width = down_proj.shape[1]
    feed = jnp.zeros((group, width), jnp.float32)
    for expert in range(EXPERTS):
        picked_ids = slot_ids(mlp_routes, expert, CAP)
        picked = unit_two[picked_ids]
        joined = jnp.dot(picked, gate_up[expert].reshape(width, 2 * hidden_width), precision=HIGHEST)
        gate_pre = low_back(joined[:, :hidden_width])
        linear = low_back(joined[:, hidden_width:])
        hidden = low(jax.nn.silu(gate_pre) * linear)
        branch = low_back(jnp.dot(hidden, down_proj[expert], precision=HIGHEST))
        feed = feed.at[picked_ids].add(branch * gate_mlp[picked_ids, expert][:, None])
    return middle + feed

def reference(inputs, segments, att_routes, mlp_routes, key_value, query_proj, output_proj, router_att, gain_att, gate_up, down_proj, router_mlp, gain_mlp, out_grad):
    floats = tuple((item.astype(jnp.float32) for item in (inputs, key_value, query_proj, output_proj, router_att, gain_att, gate_up, down_proj, router_mlp, gain_mlp)))

    def forward(inputs_f, *params):

        def one_group(pieces):
            return group_forward(params, pieces[0], pieces[1], pieces[2], pieces[3])
        stacked = (inputs_f.reshape(N_DP, GROUP, D), segments.reshape(N_DP, GROUP), att_routes.reshape(N_DP, GROUP, TOP), mlp_routes.reshape(N_DP, GROUP, TOP))
        result = lax.map(jax.checkpoint(one_group), stacked)
        return result.reshape(TOKENS, D)
    result, pullback = jax.vjp(forward, *floats)
    grads = pullback(out_grad.astype(jnp.float32))
    return (result.astype(jnp.bfloat16), grads[0], grads[1], grads[2], grads[3], grads[4], grads[5], grads[6], grads[7], grads[8], grads[9])
```

```python
import functools
import math

import jax
import jax.numpy as jnp
from jax import lax
from jax.experimental import pallas as pl
from jax.experimental.pallas import tpu as pltpu
from jax.sharding import Mesh, PartitionSpec as P

HD = 128
CAP = 320
EPSILON = 1e-06
NEGATIVE = -1e30
ROPE_BASE = 10000.0
MESH_ID = pl.DeviceIdType.MESH
DP = ("y", "xl", "z")
TP = ("xh", "core")
ALL = DP + TP
F32 = jnp.float32
BF16 = jnp.bfloat16


def mod4(place):
    return lax.rem(place + 4, 4)


def neighbour(axis, step):
    size = 2 if axis == "xl" else 4
    return {axis: lax.rem(lax.axis_index(axis) + step + size, size)}


def gather_body(x_ref, out_ref, loc, xs, xr, s1, r1m, r1p, f1s, f1r, s2, r2m, r2p, f2s, f2r):
    y, xl, z = lax.axis_index("y"), lax.axis_index("xl"), lax.axis_index("z")
    half = x_ref.shape[0] // 2
    quarter = half // 2
    barrier = pltpu.get_barrier_semaphore()
    for axis, step in (("xl", 1), ("y", 1), ("y", -1), ("z", 1), ("z", -1)):
        pl.semaphore_signal(
            barrier, inc=1, device_id=neighbour(axis, step), device_id_type=MESH_ID
        )
    pl.semaphore_wait(barrier, 5)
    rings = (("z", "y"), ("y", "z"))
    place = {"y": y, "z": z}
    other = 1 - xl
    both = pl.ds(0, 2)
    sends = []

    def slot(h, first, second, j, start, count):
        yy, zz = (second, first) if h == 0 else (first, second)
        return out_ref.at[yy, j, zz, pl.ds(start, count)]

    def send(src, dst, send_sem, recv_sem, device):
        copy = pltpu.make_async_remote_copy(
            src_ref=src,
            dst_ref=dst,
            send_sem=send_sem,
            recv_sem=recv_sem,
            device_id=device,
            device_id_type=MESH_ID,
        )
        copy.start()
        sends.append(copy)

    def arrived(ref, sem):
        pltpu.make_async_copy(ref, ref, sem).wait()

    own = pltpu.make_async_copy(x_ref, out_ref.at[y, xl, z], loc)
    own.start()
    for h in (0, 1):
        first, second = place[rings[h][0]], place[rings[h][1]]
        src = x_ref.at[pl.ds(h * half, half)]
        dst = slot(h, first, second, xl, h * half, half)
        send(src, dst, xs.at[h], xr.at[h], neighbour("xl", 1))
        send(src, dst, s1.at[h, 0, 0], r1m.at[h, 0], neighbour(rings[h][0], 1))
        send(src, dst, s1.at[h, 0, 1], r1p.at[h, 0], neighbour(rings[h][0], -1))
    own.wait()

    def send_second(h, k, first):
        block = slot(h, first, place[rings[h][1]], both, h * half, half)
        send(block, block, s2.at[h, k, 0], r2m.at[h, k], neighbour(rings[h][1], 1))
        send(block, block, s2.at[h, k, 1], r2p.at[h, k], neighbour(rings[h][1], -1))

    for h in (0, 1):
        first, second = place[rings[h][0]], place[rings[h][1]]
        block = slot(h, first, second, other, h * half, half)
        arrived(block, xr.at[h])
        send(block, block, s1.at[h, 1, 0], r1m.at[h, 1], neighbour(rings[h][0], 1))
        send(block, block, s1.at[h, 1, 1], r1p.at[h, 1], neighbour(rings[h][0], -1))
        send_second(h, 0, first)
    for j, jx in ((0, xl), (1, other)):
        for h in (0, 1):
            first, second = place[rings[h][0]], place[rings[h][1]]
            arrived(slot(h, mod4(first - 1), second, jx, h * half, half), r1m.at[h, j])
            block = slot(h, mod4(first - 1), second, jx, h * half, quarter)
            send(block, block, f1s.at[h, j, 0], f1r.at[h, j, 0], neighbour(rings[h][0], 1))
            arrived(slot(h, mod4(first + 1), second, jx, h * half, half), r1p.at[h, j])
            block = slot(h, mod4(first + 1), second, jx, h * half + quarter, quarter)
            send(block, block, f1s.at[h, j, 1], f1r.at[h, j, 1], neighbour(rings[h][0], -1))
    for k, step in ((1, -1), (2, 1)):
        for h in (0, 1):
            send_second(h, k, mod4(place[rings[h][0]] + step))
    for h in (0, 1):
        first, second = place[rings[h][0]], place[rings[h][1]]
        for j, jx in ((0, xl), (1, other)):
            for p in (0, 1):
                block = slot(h, mod4(first + 2), second, jx, h * half + p * quarter, quarter)
                arrived(block, f1r.at[h, j, p])
        send_second(h, 3, mod4(first + 2))
    steps = ((0, 0), (1, -1), (2, 1), (3, 2))
    for k, step in steps:
        for h in (0, 1):
            first, second = mod4(place[rings[h][0]] + step), place[rings[h][1]]
            arrived(slot(h, first, mod4(second - 1), both, h * half, half), r2m.at[h, k])
            block = slot(h, first, mod4(second - 1), both, h * half, quarter)
            send(block, block, f2s.at[h, k, 0], f2r.at[h, k, 0], neighbour(rings[h][1], 1))
            arrived(slot(h, first, mod4(second + 1), both, h * half, half), r2p.at[h, k])
            block = slot(h, first, mod4(second + 1), both, h * half + quarter, quarter)
            send(block, block, f2s.at[h, k, 1], f2r.at[h, k, 1], neighbour(rings[h][1], -1))
    for k, step in steps:
        for h in (0, 1):
            first, second = mod4(place[rings[h][0]] + step), place[rings[h][1]]
            for p in (0, 1):
                block = slot(h, first, mod4(second + 2), both, h * half + p * quarter, quarter)
                arrived(block, f2r.at[h, k, p])
    for copy in sends:
        copy.wait_send()


def gather_dp(shard, collective_id):
    rows, cols = shard.shape
    dma = pltpu.SemaphoreType.DMA
    whole = pl.pallas_call(
        gather_body,
        out_shape=jax.ShapeDtypeStruct((4, 2, 4, rows, cols), shard.dtype),
        in_specs=[pl.BlockSpec(memory_space=pl.ANY)],
        out_specs=pl.BlockSpec(memory_space=pl.ANY),
        scratch_shapes=[
            dma,
            dma((2,)),
            dma((2,)),
            dma((2, 2, 2)),
            dma((2, 2)),
            dma((2, 2)),
            dma((2, 2, 2)),
            dma((2, 2, 2)),
            dma((2, 4, 2)),
            dma((2, 4)),
            dma((2, 4)),
            dma((2, 4, 2)),
            dma((2, 4, 2)),
        ],
        compiler_params=pltpu.CompilerParams(collective_id=collective_id, has_side_effects=True),
        name="gather_weights",
    )(shard)
    return whole.reshape(32 * rows, cols)


def dot(a, b, dims):
    return lax.dot_general(a, b, (dims, ((), ())), preferred_element_type=F32)


def attention_body(
    k_ref, v_ref, q0, q1, q2, cos_ref, sin_ref, col_ref, row_ref, gate_ref,
    key_out, val_out, que_out, mix_out, gmix_out, prob_out,
):
    h = pl.program_id(0)
    cosine, sine = cos_ref[...], sin_ref[...]
    scale = 1.0 / math.sqrt(HD)

    def rotated(v):
        return v * cosine + pltpu.roll(v, HD // 2, 1) * sine

    key = rotated(k_ref[...]).astype(BF16)
    val = v_ref[...].astype(BF16)
    key_out[...] = key
    val_out[...] = val
    tokens = key.shape[0]
    seg_col, seg_row = col_ref[...], row_ref[...]
    at_row = lax.broadcasted_iota(jnp.int32, (tokens, tokens), 0)
    at_col = lax.broadcasted_iota(jnp.int32, (tokens, tokens), 1)
    allowed = (at_col <= at_row) & ((seg_row == 0) | (seg_row == seg_col))
    for e, q_ref in enumerate((q0, q1, q2)):
        query = (rotated(q_ref[...]) * scale).astype(BF16)
        scores = jnp.where(allowed, dot(query, key, ((1,), (1,))), NEGATIVE)
        largest = jnp.max(scores, 1, keepdims=True)
        expsum = jnp.exp(scores - largest)
        prob = (expsum * (1.0 / jnp.sum(expsum, 1, keepdims=True))).astype(BF16)
        prob_out[0, e] = prob
        mixed = dot(prob, val, ((1,), (0,))).astype(BF16)
        at = pl.ds(pl.multiple_of(e * 4 * HD + h * HD, HD), HD)
        que_out[:, at] = query
        mix_out[:, at] = mixed
        gmix_out[:, at] = (mixed.astype(F32) * gate_ref[:, e : e + 1]).astype(BF16)


def attention_forward(joined, cosine, sine, segments, gates):
    tokens = joined.shape[0]
    heads = 4

    def column(start):
        return pl.BlockSpec((tokens, HD), lambda h: (0, start // HD + h))

    def whole(shape):
        return pl.BlockSpec(shape, lambda h: (0,) * len(shape))

    wide = jax.ShapeDtypeStruct((tokens, 12 * HD), BF16)
    narrow = jax.ShapeDtypeStruct((tokens, 4 * HD), BF16)
    return pl.pallas_call(
        attention_body,
        grid=(heads,),
        in_specs=[column(s) for s in (0, 512, 1024, 1536, 2048)]
        + [whole((tokens, HD))] * 2
        + [whole((tokens, 1)), whole((1, tokens)), whole(gates.shape)],
        out_specs=[column(0), column(0)]
        + [whole(wide.shape)] * 3
        + [pl.BlockSpec((1, 3, tokens, tokens), lambda h: (h, 0, 0, 0))],
        out_shape=[narrow, narrow, wide, wide, wide]
        + [jax.ShapeDtypeStruct((heads, 3, tokens, tokens), BF16)],
        compiler_params=pltpu.CompilerParams(vmem_limit_bytes=48 * 1024 * 1024),
        name="attention_forward",
    )(joined, joined, joined, joined, joined, cosine, sine, segments[:, None], segments[None], gates)


def attention_back_body(
    key_ref, val_ref, q0, q1, q2, m0, m1, m2, h0, h1, h2, prob_ref, cos_ref, sin_ref, gate_ref,
    grad_out, dgate_out,
):
    h = pl.program_id(0)
    cosine, sine = cos_ref[...], sin_ref[...]
    scale = 1.0 / math.sqrt(HD)

    def rotated_back(v):
        return v * cosine - pltpu.roll(v, HD // 2, 1) * sine

    key, val = key_ref[...], val_ref[...]
    tokens = key.shape[0]
    dkey = jnp.zeros((tokens, HD), F32)
    dval = jnp.zeros((tokens, HD), F32)
    lane = lax.broadcasted_iota(jnp.int32, (tokens, HD), 1)
    dgates = jnp.zeros((tokens, HD), F32)
    for e, (q_ref, m_ref, h_ref) in enumerate(((q0, m0, h0), (q1, m1, h1), (q2, m2, h2))):
        query, mixed, raw = q_ref[...], m_ref[...].astype(F32), h_ref[...]
        inner = jnp.sum(mixed * raw, 1, keepdims=True)
        dgates = dgates + jnp.where(lane == e, inner, 0.0)
        gate = gate_ref[:, e : e + 1]
        dmixed = (raw * gate).astype(BF16)
        prob = prob_ref[0, e]
        dval = dval + dot(prob, dmixed, ((0,), (0,)))
        dprob = dot(dmixed, val, ((1,), (1,)))
        delta = jnp.sum(dmixed.astype(F32) * mixed, 1, keepdims=True)
        dscores = (prob.astype(F32) * (dprob - delta)).astype(BF16)
        dquery = dot(dscores, key, ((1,), (0,)))
        dkey = dkey + dot(dscores, query, ((0,), (0,)))
        at = pl.ds(pl.multiple_of(1024 + e * 4 * HD + h * HD, HD), HD)
        grad_out[:, at] = rotated_back(dquery * scale).astype(BF16)
    grad_out[:, pl.ds(pl.multiple_of(h * HD, HD), HD)] = rotated_back(dkey).astype(BF16)
    grad_out[:, pl.ds(pl.multiple_of(512 + h * HD, HD), HD)] = dval.astype(BF16)

    @pl.when(h == 0)
    def _():
        dgate_out[...] = dgates

    @pl.when(h > 0)
    def _():
        dgate_out[...] += dgates


def attention_back(key, val, que, mix, raw, prob, cosine, sine, gates):
    tokens = key.shape[0]
    heads = 4

    def column(start):
        return pl.BlockSpec((tokens, HD), lambda h: (0, start // HD + h))

    def whole(shape):
        return pl.BlockSpec(shape, lambda h: (0,) * len(shape))

    thirds = [column(s) for s in (0, 512, 1024)]
    return pl.pallas_call(
        attention_back_body,
        grid=(heads,),
        in_specs=[column(0), column(0)]
        + thirds * 3
        + [pl.BlockSpec((1, 3, tokens, tokens), lambda h: (h, 0, 0, 0))]
        + [whole((tokens, HD))] * 2
        + [whole(gates.shape)],
        out_specs=[whole((tokens, 2560)), whole((tokens, HD))],
        out_shape=[
            jax.ShapeDtypeStruct((tokens, 2560), BF16),
            jax.ShapeDtypeStruct((tokens, HD), F32),
        ],
        compiler_params=pltpu.CompilerParams(vmem_limit_bytes=48 * 1024 * 1024),
        name="attention_back",
    )(key, val, que, que, que, mix, mix, mix, raw, raw, raw, prob, cosine, sine, gates)


def positions(segments):
    index = jnp.arange(segments.shape[0], dtype=jnp.int32)
    prompt = jnp.sum((segments == 0).astype(jnp.int32))
    first = jnp.sum((segments == 1).astype(jnp.int32))
    before = jnp.where(segments == 0, 0, jnp.where(segments == 1, prompt, prompt + first))
    return jnp.where(segments == 0, index, prompt + index - before)


def route_gates(logits, routes, count):
    onehot = (routes[:, :, None] == jnp.arange(count, dtype=jnp.int32)).astype(F32)
    chosen = jnp.sum(onehot * logits[:, None, :], -1)
    expsum = jnp.exp(chosen - jnp.max(chosen, -1, keepdims=True))
    weights = expsum / jnp.sum(expsum, -1, keepdims=True)
    return weights, onehot, jnp.sum(weights[:, :, None] * onehot, 1)


def router_back(dgate, weights, onehot):
    dchosen = jnp.sum(dgate[:, None, :] * onehot, -1)
    dselect = weights * (dchosen - jnp.sum(weights * dchosen, -1, keepdims=True))
    return jnp.sum(dselect[:, :, None] * onehot, 1).astype(BF16)


def normalize(activations):
    inverse = lax.rsqrt(jnp.mean(activations * activations, -1, keepdims=True) + EPSILON)
    return activations * inverse, inverse


def norm_back(dunit, normed, inverse, gain):
    dscaled = dunit * gain
    return inverse * (dscaled - normed * jnp.mean(dscaled * normed, -1, keepdims=True))


def swiglu_back(dhidden, gate_pre, linear):
    sigmoid_pre = jax.nn.sigmoid(gate_pre)
    dgate_pre = dhidden * linear * sigmoid_pre * (1.0 + gate_pre * (1.0 - sigmoid_pre))
    dlinear = dhidden * gate_pre * sigmoid_pre
    return jnp.concatenate([dgate_pre, dlinear], 1).astype(BF16)


def sum_over_tensor(partial):
    rows, width = partial.shape
    pieces = lax.all_to_all(partial.reshape(4, rows // 4, width), TP, 0, 0, tiled=True)
    return jnp.sum(pieces.astype(F32), 0)


def pad_to(array, width):
    return jnp.pad(array, ((0, 0), (0, width - array.shape[1])))


def on_device(
    inputs,
    segments,
    att_routes,
    mlp_routes,
    key_value,
    query_proj,
    output_proj,
    router_att,
    gain_att,
    gate_up,
    down_proj,
    router_mlp,
    gain_mlp,
    out_grad,
):
    width = inputs.shape[1]
    inner = query_proj.shape[2]
    hidden_local = down_proj.shape[1]
    att_count = query_proj.shape[0]
    mlp_count = gate_up.shape[0]
    share = gate_up.shape[1]
    qkv_cols = (2 + att_count) * inner
    small_at = qkv_cols
    out_at = qkv_cols + 128
    small = jnp.concatenate([router_att, router_mlp, gain_att[:, None], gain_mlp[:, None]], 1)
    own_att = jnp.concatenate(
        [
            key_value.reshape(share, 2 * inner),
            jnp.swapaxes(query_proj, 0, 1).reshape(share, att_count * inner),
            pad_to(small, 128),
            jnp.transpose(output_proj, (2, 0, 1)).reshape(share, att_count * inner),
        ],
        1,
    )
    own_mlp = jnp.concatenate(
        [
            gate_up.reshape(mlp_count, share, 2 * hidden_local),
            jnp.swapaxes(down_proj, 1, 2),
        ],
        2,
    )
    x_all = lax.all_gather(inputs, TP, axis=0, tiled=True)
    grad_all = lax.all_gather(out_grad, TP, axis=0, tiled=True)
    weights = gather_dp(own_att, 0)
    owned = lax.all_to_all(jnp.repeat(own_mlp, 8, axis=0), DP, split_axis=0, concat_axis=1, tiled=True)[0]

    tokens = x_all.shape[0]
    match = jnp.sum((mlp_routes[:, :, None] == jnp.arange(mlp_count, dtype=jnp.int32)).astype(BF16), 1)
    index = jnp.arange(tokens, dtype=jnp.int32)
    lower = (index[None, :] < index[:, None]).astype(BF16)
    rank = dot(lower, match, ((1,), (0,)))
    slot = jnp.where(match > 0, rank.astype(jnp.int32), -1)
    pick = (slot.T[:, None, :] == jnp.arange(CAP, dtype=jnp.int32)[None, :, None]).astype(BF16)
    pick_rows = pick.reshape(mlp_count * CAP, tokens)
    grad_rows = dot(pick_rows, grad_all, ((1,), (0,))).astype(BF16)
    grad_in = lax.all_to_all(grad_rows.reshape(mlp_count, CAP, width), "y", 0, 0, tiled=True)
    grad_in = grad_in.reshape(mlp_count * CAP, width)

    small_all = weights[:, small_at : small_at + 128].astype(F32)
    gain_one, gain_two = small_all[:, 7], small_all[:, 8]
    places = positions(segments).astype(F32)
    frequency = ROPE_BASE ** (-2.0 * jnp.arange(HD // 2, dtype=F32) / HD)
    angles = places[:, None] * frequency[None, :]
    cosine = jnp.concatenate([jnp.cos(angles)] * 2, 1)
    sine = jnp.concatenate([-jnp.sin(angles), jnp.sin(angles)], 1)
    normed_one, inverse_one = normalize(x_all.astype(F32))
    unit_one = (normed_one * gain_one).astype(BF16)
    joined_att = dot(unit_one, weights[:, :out_at], ((1,), (0,)))
    weights_att, onehot_att, gate_att = route_gates(
        joined_att[:, small_at : small_at + att_count], att_routes, att_count
    )
    key_rot, val_rows, queries, mixed, gmixed, prob = attention_forward(
        joined_att, cosine, sine, segments, gate_att
    )
    out_weights = weights[:, out_at:]
    attention = dot(gmixed, out_weights, ((1,), (1,))).astype(BF16)
    middle = inputs.astype(F32) + sum_over_tensor(attention)
    normed_two, inverse_two = normalize(middle)
    own_two = (normed_two * gain_two).astype(BF16)
    unit_two = lax.all_gather(own_two, TP, axis=0, tiled=True)

    router_two = weights[:, small_at + att_count : small_at + att_count + mlp_count]
    logit_mlp = dot(unit_two, router_two, ((1,), (0,)))
    weights_mlp, onehot_mlp, gate_mlp = route_gates(logit_mlp, mlp_routes, mlp_count)
    gate_high = gate_mlp.astype(BF16)
    gate_low = (gate_mlp - gate_high.astype(F32)).astype(BF16)
    extended = jnp.concatenate([unit_two, pad_to(jnp.concatenate([gate_high, gate_low], 1), 128)], 1)
    rows_out = dot(pick_rows, extended, ((1,), (0,))).astype(BF16)
    rows_ext = lax.all_to_all(rows_out.reshape(mlp_count, CAP, width + 128), "y", 0, 0, tiled=True)
    rows_ext = rows_ext.reshape(mlp_count * CAP, width + 128)
    rows_in = rows_ext[:, :width]
    gates_ext = rows_ext[:, width : width + 2 * mlp_count].astype(F32)
    mine = (jnp.arange(2 * mlp_count) % mlp_count == lax.axis_index("y")).astype(F32)
    gates_in = jnp.sum(gates_ext * mine, 1, keepdims=True)
    dbranch_in = (grad_in.astype(F32) * gates_in).astype(BF16)
    up_whole = owned[:, : 2 * hidden_local]
    down_whole = owned[:, 2 * hidden_local :]
    joined = dot(rows_in, up_whole, ((1,), (0,)))
    gate_pre = joined[:, :hidden_local]
    linear = joined[:, hidden_local:]
    hidden = (jax.nn.silu(gate_pre) * linear).astype(BF16)
    branch_part = dot(hidden, down_whole, ((1,), (1,))).astype(BF16)
    dhidden = dot(dbranch_in, down_whole, ((1,), (0,)))
    djoined = swiglu_back(dhidden, gate_pre, linear)
    dunit_part = dot(djoined, up_whole, ((1,), (1,))).astype(BF16)
    branch_back = lax.all_to_all(
        branch_part.reshape(mlp_count, CAP, width), "y", 0, 0, tiled=True
    ).reshape(mlp_count * CAP, width)
    dunit_back = lax.all_to_all(
        dunit_part.reshape(mlp_count, CAP, width), "y", 0, 0, tiled=True
    ).reshape(mlp_count * CAP, width)
    grad_up_whole = dot(rows_in, djoined, ((0,), (0,))).astype(BF16)
    grad_down_whole = dot(dbranch_in, hidden, ((0,), (0,))).astype(BF16)
    grad_pieces = lax.all_to_all(
        jnp.concatenate([grad_up_whole, grad_down_whole], 1), DP, 0, 0, tiled=True
    )

    gate_slots = jnp.sum(pick.astype(F32) * gate_mlp.T[:, None, :], -1).reshape(mlp_count * CAP, 1)
    branch_f32 = branch_back.astype(F32)
    feed = dot(pick_rows, (branch_f32 * gate_slots).astype(BF16), ((0,), (0,))).astype(BF16)
    dgate_slots = jnp.sum(grad_rows.astype(F32) * branch_f32, -1).reshape(mlp_count, CAP, 1)
    dgate_two = jnp.sum(pick.astype(F32) * dgate_slots, 1).T
    dlogit_mlp = router_back(dgate_two, weights_mlp, onehot_mlp)
    dunit_two = dot(pick_rows, dunit_back, ((0,), (0,))) + dot(dlogit_mlp, router_two, ((1,), (1,)))
    dunit_own = sum_over_tensor(dunit_two.astype(BF16))
    grad_rmlp = dot(unit_two, dlogit_mlp, ((0,), (0,)))
    grad_gain_two = jnp.sum(dunit_own * normed_two, 0)
    dmiddle = out_grad.astype(F32) + norm_back(dunit_own, normed_two, inverse_two, gain_two)
    dattention = lax.all_gather(dmiddle.astype(BF16), TP, axis=0, tiled=True)

    raw = dot(dattention, out_weights, ((1,), (0,)))
    grad_qkv, dgate_one = attention_back(
        key_rot, val_rows, queries, mixed, raw, prob, cosine, sine, gate_att
    )
    dlogit_att = router_back(dgate_one[:, :att_count], weights_att, onehot_att)
    grad_joined = jnp.concatenate([grad_qkv, pad_to(dlogit_att, 128)], 1)
    dunit_one = dot(grad_joined, weights[:, :out_at], ((1,), (1,)))
    grad_gain_one = jnp.sum(dunit_one * normed_one, 0)
    grad_small = jnp.concatenate(
        [
            dot(unit_one, dlogit_att, ((0,), (0,))),
            grad_rmlp,
            grad_gain_one[:, None],
            grad_gain_two[:, None],
        ],
        1,
    )
    grad_att = jnp.concatenate(
        [
            dot(unit_one, grad_qkv, ((0,), (0,))).astype(BF16),
            pad_to(grad_small, 128).astype(BF16),
            dot(dattention, gmixed, ((0,), (0,))).astype(BF16),
        ],
        1,
    )
    att_pieces = lax.all_to_all(grad_att.reshape(32, share, grad_att.shape[1]), DP, 0, 0, tiled=True)
    dunit_first = sum_over_tensor(dunit_one.astype(BF16))
    my_start = (lax.axis_index("xh") * 2 + lax.axis_index("core")) * inputs.shape[0]
    own_rows = lambda array: lax.dynamic_slice_in_dim(array, my_start, inputs.shape[0], 0)
    grad_input = dmiddle + norm_back(
        dunit_first, own_rows(normed_one), own_rows(inverse_one), gain_one
    )

    summed_mlp = jnp.sum(grad_pieces.reshape(mlp_count, 8, share, 3 * hidden_local).astype(F32), 1)
    grads_up = summed_mlp[:, :, : 2 * hidden_local].reshape(mlp_count, share, 2, hidden_local)
    grads_down = jnp.swapaxes(summed_mlp[:, :, 2 * hidden_local :], 1, 2)
    summed_att = jnp.sum(att_pieces.astype(F32), 0)
    grad_kv = summed_att[:, : 2 * inner].reshape(share, 2, inner)
    grad_query = jnp.swapaxes(
        summed_att[:, 2 * inner : qkv_cols].reshape(share, att_count, inner), 0, 1
    )
    grad_output = jnp.transpose(
        summed_att[:, out_at:].reshape(share, att_count, inner), (1, 2, 0)
    )
    small_sum = lax.psum(summed_att[:, small_at:out_at], TP)

    feed_rows = sum_over_tensor(feed)
    output = (middle + feed_rows).astype(BF16)
    return (
        output,
        grad_input,
        grad_kv,
        grad_query,
        grad_output,
        small_sum[:, :3],
        small_sum[:, 7],
        grads_up,
        grads_down,
        small_sum[:, 3:7],
        small_sum[:, 8],
    )


def solution(mesh):
    fine = Mesh(mesh.devices.reshape(4, 2, 4, 2, 2), ALL)
    return jax.shard_map(
        on_device,
        mesh=fine,
        in_specs=(
            P(ALL, None),
            P(DP),
            P(DP, None),
            P(DP, None),
            P(DP, None, TP),
            P(None, DP, TP),
            P(None, TP, DP),
            P(DP, None),
            P(DP),
            P(None, DP, None, TP),
            P(None, TP, DP),
            P(DP, None),
            P(DP),
            P(ALL, None),
        ),
        out_specs=(
            P(ALL, None),
            P(ALL, None),
            P(DP, None, TP),
            P(None, DP, TP),
            P(None, TP, DP),
            P(DP, None),
            P(DP),
            P(None, DP, None, TP),
            P(None, TP, DP),
            P(DP, None),
            P(DP),
        ),
        check_vma=False,
    )
```

```python
import functools
import math

import jax
import jax.numpy as jnp
from jax import lax
from jax.experimental import pallas as pl
from jax.experimental.pallas import tpu as pltpu
from jax.sharding import Mesh, PartitionSpec as P

HD = 128
CAP = 320
EPSILON = 1e-06
NEGATIVE = -1e30
ROPE_BASE = 10000.0
MESH_ID = pl.DeviceIdType.MESH
MIB = 1024 * 1024
DP = ("y", "xl", "z")
TP = ("xh", "core")
ALL = DP + TP
F32 = jnp.float32
BF16 = jnp.bfloat16


def mod4(place):
    return lax.rem(place + 4, 4)


def neighbour(axis, step):
    size = 4 if axis in ("y", "z") else 2
    return {axis: lax.rem(lax.axis_index(axis) + step + size, size)}


def greet(*devices):
    barrier = pltpu.get_barrier_semaphore()
    for device in devices:
        pl.semaphore_signal(barrier, inc=1, device_id=device, device_id_type=MESH_ID)
    pl.semaphore_wait(barrier, len(devices))


def arrived(ref, sem):
    pltpu.make_async_copy(ref, ref, sem).wait()


class Sends:
    def __init__(self):
        self.copies = []

    def __call__(self, src, dst, send_sem, recv_sem, device):
        copy = pltpu.make_async_remote_copy(
            src_ref=src,
            dst_ref=dst,
            send_sem=send_sem,
            recv_sem=recv_sem,
            device_id=device,
            device_id_type=MESH_ID,
        )
        copy.start()
        self.copies.append(copy)

    def finish(self):
        for copy in self.copies:
            copy.wait_send()


def gather_body(
    x_ref, experts_ref, out_ref, expert_ref,
    loc, xs, xr, s1, r1m, r1p, f1s, f1r, s2, r2m, r2p, f2s, f2r, es, er,
):
    y, xl, z = lax.axis_index("y"), lax.axis_index("xl"), lax.axis_index("z")
    half = x_ref.shape[0] // 2
    quarter = half // 2
    greet(
        neighbour("xl", 1),
        *(neighbour("y", step) for step in (1, 2, 3)),
        *(neighbour("z", step) for step in (1, -1)),
    )
    rings = (("z", "y"), ("y", "z"))
    place = {"y": y, "z": z}
    other = 1 - xl
    both = pl.ds(0, 2)
    sends = Sends()
    send = sends

    def slot(h, first, second, j, start, count):
        yy, zz = (second, first) if h == 0 else (first, second)
        return out_ref.at[j, zz, yy, pl.ds(start, count)]

    own = pltpu.make_async_copy(x_ref, out_ref.at[xl, z, y], loc.at[0])
    own.start()
    expert = pltpu.make_async_copy(experts_ref.at[y], expert_ref.at[y], loc.at[1])
    expert.start()
    for h in (0, 1):
        first, second = place[rings[h][0]], place[rings[h][1]]
        src = x_ref.at[pl.ds(h * half, half)]
        dst = slot(h, first, second, xl, h * half, half)
        send(src, dst, xs.at[h], xr.at[h], neighbour("xl", 1))
        send(src, dst, s1.at[h, 0, 0], r1m.at[h, 0], neighbour(rings[h][0], 1))
        send(src, dst, s1.at[h, 0, 1], r1p.at[h, 0], neighbour(rings[h][0], -1))
    own.wait()

    def send_second(h, k, first):
        block = slot(h, first, place[rings[h][1]], both, h * half, half)
        send(block, block, s2.at[h, k, 0], r2m.at[h, k], neighbour(rings[h][1], 1))
        send(block, block, s2.at[h, k, 1], r2p.at[h, k], neighbour(rings[h][1], -1))

    for h in (0, 1):
        first, second = place[rings[h][0]], place[rings[h][1]]
        block = slot(h, first, second, other, h * half, half)
        arrived(block, xr.at[h])
        send(block, block, s1.at[h, 1, 0], r1m.at[h, 1], neighbour(rings[h][0], 1))
        send(block, block, s1.at[h, 1, 1], r1p.at[h, 1], neighbour(rings[h][0], -1))
        send_second(h, 0, first)
    for j, jx in ((0, xl), (1, other)):
        for h in (0, 1):
            first, second = place[rings[h][0]], place[rings[h][1]]
            arrived(slot(h, mod4(first - 1), second, jx, h * half, half), r1m.at[h, j])
            block = slot(h, mod4(first - 1), second, jx, h * half, quarter)
            send(block, block, f1s.at[h, j, 0], f1r.at[h, j, 0], neighbour(rings[h][0], 1))
            arrived(slot(h, mod4(first + 1), second, jx, h * half, half), r1p.at[h, j])
            block = slot(h, mod4(first + 1), second, jx, h * half + quarter, quarter)
            send(block, block, f1s.at[h, j, 1], f1r.at[h, j, 1], neighbour(rings[h][0], -1))
    for k, step in ((1, -1), (2, 1)):
        for h in (0, 1):
            send_second(h, k, mod4(place[rings[h][0]] + step))
    for h in (0, 1):
        first, second = place[rings[h][0]], place[rings[h][1]]
        for j, jx in ((0, xl), (1, other)):
            for p in (0, 1):
                block = slot(h, mod4(first + 2), second, jx, h * half + p * quarter, quarter)
                arrived(block, f1r.at[h, j, p])
        send_second(h, 3, mod4(first + 2))
    for step in (1, 3, 2):
        send(
            experts_ref.at[mod4(y + step)],
            expert_ref.at[y],
            es.at[step - 1],
            er.at[step - 1],
            neighbour("y", step),
        )
    steps = ((0, 0), (1, -1), (2, 1), (3, 2))
    for k, step in steps:
        for h in (0, 1):
            first, second = mod4(place[rings[h][0]] + step), place[rings[h][1]]
            arrived(slot(h, first, mod4(second - 1), both, h * half, half), r2m.at[h, k])
            block = slot(h, first, mod4(second - 1), both, h * half, quarter)
            send(block, block, f2s.at[h, k, 0], f2r.at[h, k, 0], neighbour(rings[h][1], 1))
            arrived(slot(h, first, mod4(second + 1), both, h * half, half), r2p.at[h, k])
            block = slot(h, first, mod4(second + 1), both, h * half + quarter, quarter)
            send(block, block, f2s.at[h, k, 1], f2r.at[h, k, 1], neighbour(rings[h][1], -1))
    for k, step in steps:
        for h in (0, 1):
            first, second = mod4(place[rings[h][0]] + step), place[rings[h][1]]
            for p in (0, 1):
                block = slot(h, first, mod4(second + 2), both, h * half + p * quarter, quarter)
                arrived(block, f2r.at[h, k, p])
    for step in (1, 3, 2):
        arrived(expert_ref.at[mod4(y - step)], er.at[step - 1])
    expert.wait()
    sends.finish()


def gather_dp(shard, experts):
    rows, cols = shard.shape
    dma = pltpu.SemaphoreType.DMA
    whole, expert = pl.pallas_call(
        gather_body,
        out_shape=[
            jax.ShapeDtypeStruct((2, 4, 4, rows, cols), shard.dtype),
            jax.ShapeDtypeStruct(experts.shape, experts.dtype),
        ],
        in_specs=[pl.BlockSpec(memory_space=pl.ANY)] * 2,
        out_specs=[pl.BlockSpec(memory_space=pl.ANY)] * 2,
        scratch_shapes=[
            dma((2,)),
            dma((2,)),
            dma((2,)),
            dma((2, 2, 2)),
            dma((2, 2)),
            dma((2, 2)),
            dma((2, 2, 2)),
            dma((2, 2, 2)),
            dma((2, 4, 2)),
            dma((2, 4)),
            dma((2, 4)),
            dma((2, 4, 2)),
            dma((2, 4, 2)),
            dma((3,)),
            dma((3,)),
        ],
        compiler_params=pltpu.CompilerParams(collective_id=0, has_side_effects=True),
        name="gather_weights",
    )(shard, experts)
    return whole.reshape(32 * rows, cols), expert


def reduce_body(scatter_count, part_refs, core_buf, sum_buf, far_buf, core_s, core_r, far_s, far_r, sends):
    xh, core = lax.axis_index("xh"), lax.axis_index("core")
    rows = part_refs[0].shape[1]
    step = rows // scatter_count
    far, here = 1 - xh, xh
    for n, chunk in enumerate(range(0, rows, step)):
        at = pl.ds(chunk, step)
        for i, part in enumerate(part_refs):
            sends(
                part.at[far * 2 + 1 - core, at],
                core_buf.at[i, 0, at],
                core_s.at[i, n, 0],
                core_r.at[i, n, 0],
                neighbour("core", 1),
            )
    for n, chunk in enumerate(range(0, rows, step)):
        at = pl.ds(chunk, step)
        for i, part in enumerate(part_refs):
            sends(
                part.at[here * 2 + 1 - core, at],
                core_buf.at[i, 1, at],
                core_s.at[i, n, 1],
                core_r.at[i, n, 1],
                neighbour("core", 1),
            )
    for n, chunk in enumerate(range(0, rows, step)):
        at = pl.ds(chunk, step)
        for i, part in enumerate(part_refs):
            arrived(core_buf.at[i, 0, at], core_r.at[i, n, 0])
            mine = part[far * 2 + core, chunk : chunk + step, :].astype(F32)
            sum_buf[i, chunk : chunk + step, :] = (
                mine + core_buf[i, 0, chunk : chunk + step, :].astype(F32)
            ).astype(BF16)
            sends(
                sum_buf.at[i, at],
                far_buf.at[i, at],
                far_s.at[i, n],
                far_r.at[i, n],
                neighbour("xh", 1),
            )

    def total(i, n):
        chunk = n * step
        at = pl.ds(chunk, step)
        arrived(core_buf.at[i, 1, at], core_r.at[i, n, 1])
        near = part_refs[i][here * 2 + core, chunk : chunk + step, :].astype(F32)
        near = near + core_buf[i, 1, chunk : chunk + step, :].astype(F32)
        arrived(far_buf.at[i, at], far_r.at[i, n])
        return near + far_buf[i, chunk : chunk + step, :].astype(F32)

    return total


CHUNKS = 4


def reduce_scratch(count, rows, width):
    dma = pltpu.SemaphoreType.DMA
    return [
        pltpu.VMEM((count, 2, rows, width), BF16),
        pltpu.VMEM((count, rows, width), BF16),
        pltpu.VMEM((count, rows, width), BF16),
        dma((count, CHUNKS, 2)),
        dma((count, CHUNKS, 2)),
        dma((count, CHUNKS)),
        dma((count, CHUNKS)),
    ]


def spread_chunk(out_ref, n, step, sems, sends):
    xh, core = lax.axis_index("xh"), lax.axis_index("core")
    at = pl.ds(n * step, step)
    mine = out_ref.at[xh * 2 + core, at]
    far_s, far_r, core_s, core_r = sems
    sends(mine, mine, far_s.at[n], far_r.at[n], neighbour("xh", 1))
    sends(mine, mine, core_s.at[n, 0], core_r.at[n, 0], neighbour("core", 1))


def spread_finish(out_ref, step, sems, sends):
    xh, core = lax.axis_index("xh"), lax.axis_index("core")
    far_s, far_r, core_s, core_r = sems
    for n in range(CHUNKS):
        at = pl.ds(n * step, step)
        theirs = out_ref.at[(1 - xh) * 2 + core, at]
        arrived(theirs, far_r.at[n])
        sends(theirs, theirs, core_s.at[n, 1], core_r.at[n, 1], neighbour("core", 1))
    for n in range(CHUNKS):
        at = pl.ds(n * step, step)
        arrived(out_ref.at[xh * 2 + 1 - core, at], core_r.at[n, 0])
        arrived(out_ref.at[(1 - xh) * 2 + 1 - core, at], core_r.at[n, 1])


def spread_scratch():
    dma = pltpu.SemaphoreType.DMA
    return [dma((CHUNKS,)), dma((CHUNKS,)), dma((CHUNKS, 2)), dma((CHUNKS, 2))]


def middle_body(part_ref, x_ref, gain_ref, middle_ref, unit_ref, *scratch):
    sends = Sends()
    greet(neighbour("core", 1), neighbour("xh", 1))
    total = reduce_body(CHUNKS, [part_ref], *scratch[:7], sends)
    me = lax.axis_index("xh") * 2 + lax.axis_index("core")
    step = x_ref.shape[0] // CHUNKS
    for n in range(CHUNKS):
        rows = slice(n * step, (n + 1) * step)
        middle = x_ref[rows, :].astype(F32) + total(0, n)
        middle_ref[rows, :] = middle
        inverse = lax.rsqrt(jnp.mean(middle * middle, 1, keepdims=True) + EPSILON)
        unit_ref[me, rows, :] = (middle * inverse * gain_ref[...]).astype(BF16)
        spread_chunk(unit_ref, n, step, scratch[7:], sends)
    spread_finish(unit_ref, step, scratch[7:], sends)
    sends.finish()


def vmem(count):
    return [pl.BlockSpec(memory_space=pltpu.VMEM)] * count


def middle_and_unit(part, x, gain):
    rows, width = x.shape
    middle, unit = pl.pallas_call(
        middle_body,
        out_shape=[
            jax.ShapeDtypeStruct((rows, width), F32),
            jax.ShapeDtypeStruct((4, rows, width), BF16),
        ],
        in_specs=vmem(3),
        out_specs=vmem(2),
        scratch_shapes=reduce_scratch(1, rows, width) + spread_scratch(),
        compiler_params=pltpu.CompilerParams(
            collective_id=1, has_side_effects=True, vmem_limit_bytes=32 * MIB
        ),
        name="middle_and_unit",
    )(part.reshape(4, rows, width), x, gain[None])
    return middle, unit.reshape(4 * rows, width)


def back_body(part_ref, middle_ref, grad_ref, gain_ref, dmiddle_ref, dgain_ref, spread_ref, *scratch):
    sends = Sends()
    greet(neighbour("core", 1), neighbour("xh", 1))
    total = reduce_body(CHUNKS, [part_ref], *scratch[:7], sends)
    me = lax.axis_index("xh") * 2 + lax.axis_index("core")
    step = middle_ref.shape[0] // CHUNKS
    for n in range(CHUNKS):
        rows = slice(n * step, (n + 1) * step)
        middle = middle_ref[rows, :]
        inverse = lax.rsqrt(jnp.mean(middle * middle, 1, keepdims=True) + EPSILON)
        normed = middle * inverse
        dunit = total(0, n)
        product = dunit * normed
        dgain = jnp.sum(product, 0, keepdims=True)
        if n == 0:
            dgain_ref[...] = dgain
        else:
            dgain_ref[...] += dgain
        mean = jnp.mean(product * gain_ref[...], 1, keepdims=True)
        dmiddle = grad_ref[rows, :].astype(F32) + inverse * (dunit * gain_ref[...] - normed * mean)
        dmiddle_ref[rows, :] = dmiddle
        spread_ref[me, rows, :] = dmiddle.astype(BF16)
        spread_chunk(spread_ref, n, step, scratch[7:], sends)
    spread_finish(spread_ref, step, scratch[7:], sends)
    sends.finish()


def middle_back(part, middle, grad, gain):
    rows, width = middle.shape
    dmiddle, dgain, spread = pl.pallas_call(
        back_body,
        out_shape=[
            jax.ShapeDtypeStruct((rows, width), F32),
            jax.ShapeDtypeStruct((1, width), F32),
            jax.ShapeDtypeStruct((4, rows, width), BF16),
        ],
        in_specs=vmem(4),
        out_specs=vmem(3),
        scratch_shapes=reduce_scratch(1, rows, width) + spread_scratch(),
        compiler_params=pltpu.CompilerParams(
            collective_id=2, has_side_effects=True, vmem_limit_bytes=32 * MIB
        ),
        name="middle_back",
    )(part.reshape(4, rows, width), middle, grad, gain[None])
    return dmiddle, dgain[0], spread.reshape(4 * rows, width)


def last_body(
    part_ref, feed_ref, x_ref, middle_ref, dmiddle_ref, gain_ref, small_ref,
    output_ref, dinput_ref, small_out, *scratch,
):
    sends = Sends()
    xh, core = lax.axis_index("xh"), lax.axis_index("core")
    peers = ({"xh": xh, "core": 1 - core}, {"xh": 1 - xh, "core": core}, {"xh": 1 - xh, "core": 1 - core})
    greet(*peers)
    small_buf, small_s, small_r = scratch[7:]
    for n, peer in enumerate(peers):
        sends(small_ref, small_buf.at[n], small_s.at[n], small_r.at[n], peer)
    total = reduce_body(CHUNKS, [part_ref, feed_ref], *scratch[:7], sends)
    step = x_ref.shape[0] // CHUNKS
    for n in range(CHUNKS):
        rows = slice(n * step, (n + 1) * step)
        x = x_ref[rows, :].astype(F32)
        inverse = lax.rsqrt(jnp.mean(x * x, 1, keepdims=True) + EPSILON)
        normed = x * inverse
        dscaled = total(0, n) * gain_ref[...]
        mean = jnp.mean(dscaled * normed, 1, keepdims=True)
        dinput_ref[rows, :] = dmiddle_ref[rows, :] + inverse * (dscaled - normed * mean)
        output_ref[rows, :] = (middle_ref[rows, :] + total(1, n)).astype(BF16)
    for n in range(3):
        arrived(small_buf.at[n], small_r.at[n])
    small_out[...] = (small_ref[...] + small_buf[1]) + (small_buf[0] + small_buf[2])
    sends.finish()


def last_sums(part, feed, x, middle, dmiddle, gain, small):
    rows, width = x.shape
    dma = pltpu.SemaphoreType.DMA
    return pl.pallas_call(
        last_body,
        out_shape=[
            jax.ShapeDtypeStruct((rows, width), BF16),
            jax.ShapeDtypeStruct((rows, width), F32),
            jax.ShapeDtypeStruct(small.shape, F32),
        ],
        in_specs=vmem(7),
        out_specs=vmem(3),
        scratch_shapes=reduce_scratch(2, rows, width)
        + [pltpu.VMEM((3, *small.shape), F32), dma((3,)), dma((3,))],
        compiler_params=pltpu.CompilerParams(
            collective_id=3, has_side_effects=True, vmem_limit_bytes=40 * MIB
        ),
        name="last_sums",
    )(part.reshape(4, rows, width), feed.reshape(4, rows, width), x, middle, dmiddle, gain[None], small)


def rows_body(rows_ref, out_ref, loc, far_s, far_r, core_s, core_r):
    y, core = lax.axis_index("y"), lax.axis_index("core")
    half = rows_ref.shape[1] // 2
    sends = Sends()
    greet(neighbour("core", 1), *(neighbour("y", step) for step in (1, 2, 3)))
    at = pl.ds(pl.multiple_of(core * half, half), half)
    own = pltpu.make_async_copy(rows_ref.at[y], out_ref.at[y], loc)
    own.start()
    for step in (2, 1, 3):
        target = mod4(y + step)
        sends(
            rows_ref.at[target, at],
            out_ref.at[y, at],
            far_s.at[step - 1],
            far_r.at[step - 1],
            neighbour("y", step),
        )
    for step in (1, 3, 2):
        source = mod4(y - step)
        block = out_ref.at[source, at]
        arrived(block, far_r.at[step - 1])
        sends(block, block, core_s.at[step - 1], core_r.at[step - 1], neighbour("core", 1))
    own.wait()
    other = pl.ds(pl.multiple_of((1 - core) * half, half), half)
    for step in (1, 3, 2):
        arrived(out_ref.at[mod4(y - step), other], core_r.at[step - 1])
    sends.finish()


def rows_to_experts(rows):
    dma = pltpu.SemaphoreType.DMA
    return pl.pallas_call(
        rows_body,
        out_shape=jax.ShapeDtypeStruct(rows.shape, rows.dtype),
        in_specs=[pl.BlockSpec(memory_space=pl.ANY)],
        out_specs=pl.BlockSpec(memory_space=pl.ANY),
        scratch_shapes=[dma, dma((3,)), dma((3,)), dma((3,)), dma((3,))],
        compiler_params=pltpu.CompilerParams(collective_id=4, has_side_effects=True),
        name="rows_to_experts",
    )(rows)


STEPS = (2, 1, -1, 0)


def scatter_body(
    qkv_ref, small_ref, o_ref, out_ref, g_ref, loc, t_buf, r_buf, tb_buf, rb_buf, c_buf,
    t_s, t_r, r_s, r_r, tb_s, tb_r, rb_s, rb_r, c_s, c_r,
):
    xl = lax.axis_index("xl")
    place = {"y": lax.axis_index("y"), "z": lax.axis_index("z")}
    half = g_ref.shape[3] // 2
    quarter = half // 2
    rings = (("z", "y"), ("y", "z"))
    sends = Sends()
    column = 0
    parts = []
    for n, ref in enumerate((qkv_ref, small_ref, o_ref)):
        cols = ref.shape[-1]
        parts.append(pltpu.make_async_copy(ref, g_ref.at[..., pl.ds(column, cols)], loc.at[n]))
        parts[-1].start()
        column += cols
    greet(neighbour("xl", 1), *(neighbour(axis, step) for axis in ("y", "z") for step in (1, -1)))
    both = slice(0, 2)
    for part in parts:
        part.wait()

    def grad_ref(h, first, second, start):
        zz, yy = (first, second) if h == 0 else (second, first)
        return g_ref.at[both, zz, yy, pl.ds(h * half + start, quarter)]

    def grad(h, first, second, j, start, count):
        zz, yy = (first, second) if h == 0 else (second, first)
        return g_ref[j, zz, yy, h * half + start : h * half + start + count, :].astype(F32)

    def firsts(h, k):
        return mod4(place[rings[h][0]] + STEPS[k])

    for k in range(4):
        for h in (0, 1):
            second = place[rings[h][1]]
            for d, way in ((0, 1), (1, -1)):
                sends(
                    grad_ref(h, firsts(h, k), mod4(second + 2), d * quarter),
                    t_buf.at[h, d, k],
                    t_s.at[h, d, k],
                    t_r.at[h, d, k],
                    neighbour(rings[h][1], way),
                )
    for k in range(4):
        for h in (0, 1):
            second = place[rings[h][1]]
            for d, way in ((0, 1), (1, -1)):
                sends(
                    grad_ref(h, firsts(h, k), mod4(second + way), (1 - d) * quarter),
                    r_buf.at[h, d, k, both, pl.ds((1 - d) * quarter, quarter)],
                    r_s.at[h, d, k, 0],
                    r_r.at[h, d, k, 0],
                    neighbour(rings[h][1], way),
                )
    for k in range(4):
        for h in (0, 1):
            second = place[rings[h][1]]
            for d, way in ((0, 1), (1, -1)):
                arrived(t_buf.at[h, d, k], t_r.at[h, d, k])
                for j in (0, 1):
                    t_buf[h, d, k, j] = (
                        t_buf[h, d, k, j].astype(F32)
                        + grad(h, firsts(h, k), mod4(second + way), j, d * quarter, quarter)
                    ).astype(BF16)
                sends(
                    t_buf.at[h, d, k],
                    r_buf.at[h, d, k, both, pl.ds(d * quarter, quarter)],
                    r_s.at[h, d, k, 1],
                    r_r.at[h, d, k, 1],
                    neighbour(rings[h][1], way),
                )
    for k in range(4):
        for h in (0, 1):
            second = place[rings[h][1]]
            for d in (0, 1):
                arrived(r_buf.at[h, d, k, both, pl.ds((1 - d) * quarter, quarter)], r_r.at[h, d, k, 0])
                arrived(r_buf.at[h, d, k, both, pl.ds(d * quarter, quarter)], r_r.at[h, d, k, 1])
            for j in (0, 1):
                r_buf[h, 0, k, j] = (
                    r_buf[h, 0, k, j].astype(F32)
                    + r_buf[h, 1, k, j].astype(F32)
                    + grad(h, firsts(h, k), second, j, 0, half)
                ).astype(BF16)
            for d, way in ((0, 1), (1, -1)):
                device = neighbour(rings[h][0], way)
                if k == 0:
                    sends(
                        r_buf.at[h, 0, 0, both, pl.ds(d * quarter, quarter)],
                        tb_buf.at[h, d],
                        tb_s.at[h, d],
                        tb_r.at[h, d],
                        device,
                    )
                if k == 1 + d:
                    sends(
                        r_buf.at[h, 0, k, both, pl.ds((1 - d) * quarter, quarter)],
                        rb_buf.at[h, d, both, pl.ds((1 - d) * quarter, quarter)],
                        rb_s.at[h, d, 0],
                        rb_r.at[h, d, 0],
                        device,
                    )
                    arrived(tb_buf.at[h, d], tb_r.at[h, d])
                    for j in (0, 1):
                        tb_buf[h, d, j] = (
                            tb_buf[h, d, j].astype(F32)
                            + r_buf[h, 0, k, j, d * quarter : (d + 1) * quarter, :].astype(F32)
                        ).astype(BF16)
                    sends(
                        tb_buf.at[h, d],
                        rb_buf.at[h, d, both, pl.ds(d * quarter, quarter)],
                        rb_s.at[h, d, 1],
                        rb_r.at[h, d, 1],
                        device,
                    )
    for h in (0, 1):
        for d in (0, 1):
            arrived(rb_buf.at[h, d, both, pl.ds((1 - d) * quarter, quarter)], rb_r.at[h, d, 0])
            arrived(rb_buf.at[h, d, both, pl.ds(d * quarter, quarter)], rb_r.at[h, d, 1])
        for j in (0, 1):
            rb_buf[h, 0, j] = (
                rb_buf[h, 0, j].astype(F32)
                + rb_buf[h, 1, j].astype(F32)
                + r_buf[h, 0, 3, j].astype(F32)
            ).astype(BF16)
        sends(rb_buf.at[h, 0, 1 - xl], c_buf.at[h], c_s.at[h], c_r.at[h], neighbour("xl", 1))
    for h in (0, 1):
        arrived(c_buf.at[h], c_r.at[h])
        out_ref[h * half : (h + 1) * half, :] = rb_buf[h, 0, xl].astype(F32) + c_buf[h].astype(F32)
    sends.finish()


def scatter_dp(*grads):
    rows, cols = grads[0].shape[0], sum(grad.shape[1] for grad in grads)
    share = rows // 32
    half, quarter = share // 2, share // 4
    dma = pltpu.SemaphoreType.DMA
    return pl.pallas_call(
        scatter_body,
        out_shape=jax.ShapeDtypeStruct((share, cols), F32),
        in_specs=[pl.BlockSpec(memory_space=pl.ANY)] * 3,
        out_specs=pl.BlockSpec(memory_space=pltpu.VMEM),
        scratch_shapes=[
            pltpu.VMEM((2, 4, 4, share, cols), BF16),
            dma((3,)),
            pltpu.VMEM((2, 2, 4, 2, quarter, cols), BF16),
            pltpu.VMEM((2, 2, 4, 2, half, cols), BF16),
            pltpu.VMEM((2, 2, 2, quarter, cols), BF16),
            pltpu.VMEM((2, 2, 2, half, cols), BF16),
            pltpu.VMEM((2, half, cols), BF16),
            dma((2, 2, 4)),
            dma((2, 2, 4)),
            dma((2, 2, 4, 2)),
            dma((2, 2, 4, 2)),
            dma((2, 2)),
            dma((2, 2)),
            dma((2, 2, 2)),
            dma((2, 2, 2)),
            dma((2,)),
            dma((2,)),
        ],
        compiler_params=pltpu.CompilerParams(
            collective_id=5, has_side_effects=True, vmem_limit_bytes=56 * MIB
        ),
        name="scatter_grads",
    )(*(grad.reshape(2, 4, 4, share, grad.shape[1]) for grad in grads))


def dot(a, b, dims):
    return lax.dot_general(a, b, (dims, ((), ())), preferred_element_type=F32)


def attention_body(
    k_ref, v_ref, q0, q1, q2, cos_ref, sin_ref, col_ref, row_ref, gate_ref,
    key_out, val_out, que_out, mix_out, gmix_out, prob_out,
):
    h = pl.program_id(0)
    cosine, sine = cos_ref[...], sin_ref[...]
    scale = 1.0 / math.sqrt(HD)

    def rotated(v):
        return v * cosine + pltpu.roll(v, HD // 2, 1) * sine

    key = rotated(k_ref[...]).astype(BF16)
    val = v_ref[...].astype(BF16)
    key_out[...] = key
    val_out[...] = val
    tokens = key.shape[0]
    seg_col, seg_row = col_ref[...], row_ref[...]
    at_row = lax.broadcasted_iota(jnp.int32, (tokens, tokens), 0)
    at_col = lax.broadcasted_iota(jnp.int32, (tokens, tokens), 1)
    allowed = (at_col <= at_row) & ((seg_row == 0) | (seg_row == seg_col))
    for e, q_ref in enumerate((q0, q1, q2)):
        query = (rotated(q_ref[...]) * scale).astype(BF16)
        scores = jnp.where(allowed, dot(query, key, ((1,), (1,))), NEGATIVE)
        largest = jnp.max(scores, 1, keepdims=True)
        expsum = jnp.exp(scores - largest)
        prob = (expsum * (1.0 / jnp.sum(expsum, 1, keepdims=True))).astype(BF16)
        prob_out[0, e] = prob
        mixed = dot(prob, val, ((1,), (0,))).astype(BF16)
        at = pl.ds(pl.multiple_of(e * 4 * HD + h * HD, HD), HD)
        que_out[:, at] = query
        mix_out[:, at] = mixed
        gmix_out[:, at] = (mixed.astype(F32) * gate_ref[:, e : e + 1]).astype(BF16)


def attention_forward(joined, cosine, sine, segments, gates):
    tokens = joined.shape[0]
    heads = 4

    def column(start):
        return pl.BlockSpec((tokens, HD), lambda h: (0, start // HD + h))

    def whole(shape):
        return pl.BlockSpec(shape, lambda h: (0,) * len(shape))

    wide = jax.ShapeDtypeStruct((tokens, 12 * HD), BF16)
    narrow = jax.ShapeDtypeStruct((tokens, 4 * HD), BF16)
    return pl.pallas_call(
        attention_body,
        grid=(heads,),
        in_specs=[column(s) for s in (0, 512, 1024, 1536, 2048)]
        + [whole((tokens, HD))] * 2
        + [whole((tokens, 1)), whole((1, tokens)), whole(gates.shape)],
        out_specs=[column(0), column(0)]
        + [whole(wide.shape)] * 3
        + [pl.BlockSpec((1, 3, tokens, tokens), lambda h: (h, 0, 0, 0))],
        out_shape=[narrow, narrow, wide, wide, wide]
        + [jax.ShapeDtypeStruct((heads, 3, tokens, tokens), BF16)],
        compiler_params=pltpu.CompilerParams(vmem_limit_bytes=48 * MIB),
        name="attention_forward",
    )(joined, joined, joined, joined, joined, cosine, sine, segments[:, None], segments[None], gates)


def attention_back_body(
    key_ref, val_ref, q0, q1, q2, m0, m1, m2, h0, h1, h2, prob_ref, cos_ref, sin_ref, gate_ref,
    grad_out, dgate_out,
):
    h = pl.program_id(0)
    cosine, sine = cos_ref[...], sin_ref[...]
    scale = 1.0 / math.sqrt(HD)

    def rotated_back(v):
        return v * cosine - pltpu.roll(v, HD // 2, 1) * sine

    key, val = key_ref[...], val_ref[...]
    tokens = key.shape[0]
    dkey = jnp.zeros((tokens, HD), F32)
    dval = jnp.zeros((tokens, HD), F32)
    lane = lax.broadcasted_iota(jnp.int32, (tokens, HD), 1)
    dgates = jnp.zeros((tokens, HD), F32)
    for e, (q_ref, m_ref, h_ref) in enumerate(((q0, m0, h0), (q1, m1, h1), (q2, m2, h2))):
        query, mixed, raw = q_ref[...], m_ref[...].astype(F32), h_ref[...]
        inner = jnp.sum(mixed * raw, 1, keepdims=True)
        dgates = dgates + jnp.where(lane == e, inner, 0.0)
        gate = gate_ref[:, e : e + 1]
        dmixed = (raw * gate).astype(BF16)
        prob = prob_ref[0, e]
        dval = dval + dot(prob, dmixed, ((0,), (0,)))
        dprob = dot(dmixed, val, ((1,), (1,)))
        delta = jnp.sum(dmixed.astype(F32) * mixed, 1, keepdims=True)
        dscores = (prob.astype(F32) * (dprob - delta)).astype(BF16)
        dquery = dot(dscores, key, ((1,), (0,)))
        dkey = dkey + dot(dscores, query, ((0,), (0,)))
        at = pl.ds(pl.multiple_of(1024 + e * 4 * HD + h * HD, HD), HD)
        grad_out[:, at] = rotated_back(dquery * scale).astype(BF16)
    grad_out[:, pl.ds(pl.multiple_of(h * HD, HD), HD)] = rotated_back(dkey).astype(BF16)
    grad_out[:, pl.ds(pl.multiple_of(512 + h * HD, HD), HD)] = dval.astype(BF16)

    @pl.when(h == 0)
    def _():
        dgate_out[...] = dgates

    @pl.when(h > 0)
    def _():
        dgate_out[...] += dgates


def attention_back(key, val, que, mix, raw, prob, cosine, sine, gates):
    tokens = key.shape[0]
    heads = 4

    def column(start):
        return pl.BlockSpec((tokens, HD), lambda h: (0, start // HD + h))

    def whole(shape):
        return pl.BlockSpec(shape, lambda h: (0,) * len(shape))

    thirds = [column(s) for s in (0, 512, 1024)]
    return pl.pallas_call(
        attention_back_body,
        grid=(heads,),
        in_specs=[column(0), column(0)]
        + thirds * 3
        + [pl.BlockSpec((1, 3, tokens, tokens), lambda h: (h, 0, 0, 0))]
        + [whole((tokens, HD))] * 2
        + [whole(gates.shape)],
        out_specs=[whole((tokens, 2560)), whole((tokens, HD))],
        out_shape=[
            jax.ShapeDtypeStruct((tokens, 2560), BF16),
            jax.ShapeDtypeStruct((tokens, HD), F32),
        ],
        compiler_params=pltpu.CompilerParams(vmem_limit_bytes=48 * MIB),
        name="attention_back",
    )(key, val, que, que, que, mix, mix, mix, raw, raw, raw, prob, cosine, sine, gates)


def positions(segments):
    index = jnp.arange(segments.shape[0], dtype=jnp.int32)
    prompt = jnp.sum((segments == 0).astype(jnp.int32))
    first = jnp.sum((segments == 1).astype(jnp.int32))
    before = jnp.where(segments == 0, 0, jnp.where(segments == 1, prompt, prompt + first))
    return jnp.where(segments == 0, index, prompt + index - before)


def route_gates(logits, routes, count):
    onehot = (routes[:, :, None] == jnp.arange(count, dtype=jnp.int32)).astype(F32)
    chosen = jnp.sum(onehot * logits[:, None, :], -1)
    expsum = jnp.exp(chosen - jnp.max(chosen, -1, keepdims=True))
    weights = expsum / jnp.sum(expsum, -1, keepdims=True)
    return weights, onehot, jnp.sum(weights[:, :, None] * onehot, 1)


def router_back(dgate, weights, onehot):
    dchosen = jnp.sum(dgate[:, None, :] * onehot, -1)
    dselect = weights * (dchosen - jnp.sum(weights * dchosen, -1, keepdims=True))
    return jnp.sum(dselect[:, :, None] * onehot, 1).astype(BF16)


def normalize(activations):
    inverse = lax.rsqrt(jnp.mean(activations * activations, -1, keepdims=True) + EPSILON)
    return activations * inverse, inverse


def swiglu_back(dhidden, gate_pre, linear):
    sigmoid_pre = jax.nn.sigmoid(gate_pre)
    dgate_pre = dhidden * linear * sigmoid_pre * (1.0 + gate_pre * (1.0 - sigmoid_pre))
    dlinear = dhidden * gate_pre * sigmoid_pre
    return jnp.concatenate([dgate_pre, dlinear], 1).astype(BF16)


def reorder(rows):
    count, width = rows.shape
    return jnp.swapaxes(rows.reshape(count, 4, 8, width // 32), 1, 2).reshape(count, width)


def order_back(rows):
    count, width = rows.shape
    return jnp.swapaxes(rows.reshape(count, 8, 4, width // 32), 1, 2).reshape(count, width)


def pad_to(array, width):
    return jnp.pad(array, ((0, 0), (0, width - array.shape[1])))


def on_device(
    inputs,
    segments,
    att_routes,
    mlp_routes,
    key_value,
    query_proj,
    output_proj,
    router_att,
    gain_att,
    gate_up,
    down_proj,
    router_mlp,
    gain_mlp,
    out_grad,
):
    width = inputs.shape[1]
    inner = query_proj.shape[2]
    hidden_local = down_proj.shape[1]
    att_count = query_proj.shape[0]
    mlp_count = gate_up.shape[0]
    share = gate_up.shape[1]
    qkv_cols = (2 + att_count) * inner
    small_at = qkv_cols
    out_at = qkv_cols + 128
    small = jnp.concatenate([router_att, router_mlp, gain_att[:, None], gain_mlp[:, None]], 1)
    own_att = jnp.concatenate(
        [
            key_value.reshape(share, 2 * inner),
            jnp.swapaxes(query_proj, 0, 1).reshape(share, att_count * inner),
            pad_to(small, 128),
            jnp.transpose(output_proj, (2, 0, 1)).reshape(share, att_count * inner),
        ],
        1,
    )
    own_mlp = jnp.concatenate(
        [
            gate_up.reshape(mlp_count, share, 2 * hidden_local),
            jnp.swapaxes(down_proj, 1, 2),
        ],
        2,
    )
    inputs = reorder(inputs)
    out_grad = reorder(out_grad)
    x_all = lax.all_gather(inputs, TP, axis=0, tiled=True)
    grad_all = lax.all_gather(out_grad, TP, axis=0, tiled=True)
    weights, own_expert = gather_dp(own_att, own_mlp)
    own_expert = own_expert.reshape(mlp_count * share, 3 * hidden_local)
    up_whole = lax.all_gather(own_expert[:, : 2 * hidden_local], ("xl", "z"), axis=0, tiled=True)
    down_whole = lax.all_gather(own_expert[:, 2 * hidden_local :], ("xl", "z"), axis=0, tiled=True)

    tokens = x_all.shape[0]
    match = jnp.sum((mlp_routes[:, :, None] == jnp.arange(mlp_count, dtype=jnp.int32)).astype(BF16), 1)
    index = jnp.arange(tokens, dtype=jnp.int32)
    lower = (index[None, :] < index[:, None]).astype(BF16)
    rank = dot(lower, match, ((1,), (0,)))
    slot = jnp.where(match > 0, rank.astype(jnp.int32), -1)
    pick = (slot.T[:, None, :] == jnp.arange(CAP, dtype=jnp.int32)[None, :, None]).astype(BF16)
    pick_rows = pick.reshape(mlp_count * CAP, tokens)
    grad_rows = dot(pick_rows, grad_all, ((1,), (0,))).astype(BF16)
    grad_in = lax.all_to_all(grad_rows.reshape(mlp_count, CAP, width), "y", 0, 0, tiled=True)
    grad_in = grad_in.reshape(mlp_count * CAP, width)

    small_all = weights[:, small_at : small_at + 128].astype(F32)
    gain_one, gain_two = small_all[:, 7], small_all[:, 8]
    places = positions(segments).astype(F32)
    frequency = ROPE_BASE ** (-2.0 * jnp.arange(HD // 2, dtype=F32) / HD)
    angles = places[:, None] * frequency[None, :]
    cosine = jnp.concatenate([jnp.cos(angles)] * 2, 1)
    sine = jnp.concatenate([-jnp.sin(angles), jnp.sin(angles)], 1)
    normed_one, inverse_one = normalize(x_all.astype(F32))
    unit_one = (normed_one * gain_one).astype(BF16)
    joined_att = dot(unit_one, weights[:, :out_at], ((1,), (0,)))
    weights_att, onehot_att, gate_att = route_gates(
        joined_att[:, small_at : small_at + att_count], att_routes, att_count
    )
    key_rot, val_rows, queries, mixed, gmixed, prob = attention_forward(
        joined_att, cosine, sine, segments, gate_att
    )
    out_weights = weights[:, out_at:]
    attention = dot(gmixed, out_weights, ((1,), (1,))).astype(BF16)
    middle, unit_two = middle_and_unit(attention, inputs, gain_two)

    router_two = weights[:, small_at + att_count : small_at + att_count + mlp_count]
    logit_mlp = dot(unit_two, router_two, ((1,), (0,)))
    weights_mlp, onehot_mlp, gate_mlp = route_gates(logit_mlp, mlp_routes, mlp_count)
    gate_high = gate_mlp.astype(BF16)
    gate_low = (gate_mlp - gate_high.astype(F32)).astype(BF16)
    extended = jnp.concatenate([unit_two, pad_to(jnp.concatenate([gate_high, gate_low], 1), 128)], 1)
    rows_out = dot(pick_rows, extended, ((1,), (0,))).astype(BF16)
    rows_ext = rows_to_experts(rows_out.reshape(mlp_count, CAP, width + 128))
    rows_ext = rows_ext.reshape(mlp_count * CAP, width + 128)
    rows_in = rows_ext[:, :width]
    gates_ext = rows_ext[:, width : width + 2 * mlp_count].astype(F32)
    mine = (jnp.arange(2 * mlp_count) % mlp_count == lax.axis_index("y")).astype(F32)
    gates_in = jnp.sum(gates_ext * mine, 1, keepdims=True)
    joined = dot(rows_in, up_whole, ((1,), (0,)))
    gate_pre = joined[:, :hidden_local]
    linear = joined[:, hidden_local:]
    hidden_f32 = jax.nn.silu(gate_pre) * linear
    hidden = hidden_f32.astype(BF16)
    dhidden = dot(grad_in, down_whole, ((1,), (0,)))
    dgate_in = jnp.sum(hidden_f32 * dhidden, 1, keepdims=True)
    djoined = swiglu_back(dhidden * gates_in, gate_pre, linear)
    grad_down_whole = dot(
        grad_in, (hidden_f32 * gates_in).astype(BF16), ((0,), (0,))
    ).astype(BF16)
    djoined, grad_down_whole = lax.optimization_barrier((djoined, grad_down_whole))
    grad_down_sum = lax.psum_scatter(grad_down_whole, ("xl", "z"), scatter_dimension=0, tiled=True)
    dunit_part = dot(djoined, up_whole, ((1,), (1,))).astype(BF16)
    dgate_high = dgate_in.astype(BF16)
    dgate_low = (dgate_in - dgate_high.astype(F32)).astype(BF16)
    dunit_ext = jnp.concatenate(
        [dunit_part, pad_to(jnp.concatenate([dgate_high, dgate_low], 1), 128)], 1
    )
    dunit_back = lax.all_to_all(dunit_ext.reshape(mlp_count, CAP, width + 128), "y", 0, 0, tiled=True)
    djoined, dunit_ext = lax.optimization_barrier((djoined, dunit_ext))
    grad_up_whole = dot(rows_in, djoined, ((0,), (0,))).astype(BF16)
    hidden, grad_up_whole = lax.optimization_barrier((hidden, grad_up_whole))
    grad_up_sum = lax.psum_scatter(grad_up_whole, ("xl", "z"), scatter_dimension=0, tiled=True)
    branch_part = dot(hidden, down_whole, ((1,), (1,))).astype(BF16)
    dunit_back, branch_part = lax.optimization_barrier((dunit_back, branch_part))
    branch_back = lax.all_to_all(
        branch_part.reshape(mlp_count, CAP, width), "y", 0, 0, tiled=True
    ).reshape(mlp_count * CAP, width)
    dunit_back = dunit_back.reshape(mlp_count * CAP, width + 128)
    dgate_slots = (
        dunit_back[:, width : width + 1].astype(F32) + dunit_back[:, width + 1 : width + 2].astype(F32)
    ).reshape(mlp_count, CAP, 1)
    dgate_two = jnp.sum(pick.astype(F32) * dgate_slots, 1).T
    dlogit_mlp = router_back(dgate_two, weights_mlp, onehot_mlp)
    dunit_two = dot(pick_rows, dunit_back[:, :width], ((0,), (0,))) + dot(
        dlogit_mlp, router_two, ((1,), (1,))
    )
    grad_rmlp = dot(unit_two, dlogit_mlp, ((0,), (0,)))
    dmiddle, grad_gain_two, dattention = middle_back(
        dunit_two.astype(BF16), middle, out_grad, gain_two
    )

    raw = dot(dattention, out_weights, ((1,), (0,)))
    grad_qkv, dgate_one = attention_back(
        key_rot, val_rows, queries, mixed, raw, prob, cosine, sine, gate_att
    )
    dlogit_att = router_back(dgate_one[:, :att_count], weights_att, onehot_att)
    grad_joined = jnp.concatenate([grad_qkv, pad_to(dlogit_att, 128)], 1)
    dunit_one = dot(grad_joined, weights[:, :out_at], ((1,), (1,)))
    grad_gain_one = jnp.sum(dunit_one * normed_one, 0)
    grad_small = jnp.concatenate(
        [
            dot(unit_one, dlogit_att, ((0,), (0,))),
            grad_rmlp,
            grad_gain_one[:, None],
            grad_gain_two[:, None],
        ],
        1,
    )
    gate_slots = jnp.sum(pick.astype(F32) * gate_mlp.T[:, None, :], -1).reshape(mlp_count * CAP, 1)
    feed = dot(pick_rows, (branch_back.astype(F32) * gate_slots).astype(BF16), ((0,), (0,)))
    summed_att = scatter_dp(
        dot(unit_one, grad_qkv, ((0,), (0,))).astype(BF16),
        pad_to(grad_small, 128).astype(BF16),
        dot(dattention, gmixed, ((0,), (0,))).astype(BF16),
    )
    grad_up_sum, grad_down_sum, summed_att = lax.optimization_barrier(
        (grad_up_sum, grad_down_sum, summed_att)
    )
    grad_kv = summed_att[:, : 2 * inner].reshape(share, 2, inner)
    grad_query = jnp.swapaxes(
        summed_att[:, 2 * inner : qkv_cols].reshape(share, att_count, inner), 0, 1
    )
    grad_output = jnp.transpose(
        summed_att[:, out_at:].reshape(share, att_count, inner), (1, 2, 0)
    )
    output, grad_input, small_sum = last_sums(
        dunit_one.astype(BF16),
        feed.astype(BF16),
        inputs,
        middle,
        dmiddle,
        gain_one,
        summed_att[:, small_at:out_at],
    )
    output = order_back(output)
    grad_input = order_back(grad_input)

    summed_mlp = lax.all_to_all(
        jnp.concatenate([grad_up_sum, grad_down_sum], 1).reshape(mlp_count, share, 3 * hidden_local),
        "y",
        0,
        0,
        tiled=True,
    ).astype(F32)
    grads_up = summed_mlp[:, :, : 2 * hidden_local].reshape(mlp_count, share, 2, hidden_local)
    grads_down = jnp.swapaxes(summed_mlp[:, :, 2 * hidden_local :], 1, 2)
    return (
        output,
        grad_input,
        grad_kv,
        grad_query,
        grad_output,
        small_sum[:, :3],
        small_sum[:, 7],
        grads_up,
        grads_down,
        small_sum[:, 3:7],
        small_sum[:, 8],
    )


def solution(mesh):
    fine = Mesh(mesh.devices.reshape(4, 2, 4, 2, 2), ALL)
    return jax.shard_map(
        on_device,
        mesh=fine,
        in_specs=(
            P(ALL, None),
            P(DP),
            P(DP, None),
            P(DP, None),
            P(DP, None, TP),
            P(None, DP, TP),
            P(None, TP, DP),
            P(DP, None),
            P(DP),
            P(None, DP, None, TP),
            P(None, TP, DP),
            P(DP, None),
            P(DP),
            P(ALL, None),
        ),
        out_specs=(
            P(ALL, None),
            P(ALL, None),
            P(DP, None, TP),
            P(None, DP, TP),
            P(None, TP, DP),
            P(DP, None),
            P(DP),
            P(None, DP, None, TP),
            P(None, TP, DP),
            P(DP, None),
            P(DP),
        ),
        check_vma=False,
    )
```

```python
import functools
import math

import jax
import jax.numpy as jnp
from jax import lax
from jax.experimental import pallas as pl
from jax.experimental.pallas import tpu as pltpu
from jax.sharding import Mesh, PartitionSpec as P

HD = 128
HEADS = 2
CAP = 320
EPSILON = 1e-06
NEGATIVE = -1e30
ROPE_BASE = 10000.0
MESH_ID = pl.DeviceIdType.MESH
MIB = 1024 * 1024
DP = ("y", "xl", "z")
TP = ("xh", "core")
ALL = DP + TP
F32 = jnp.float32
BF16 = jnp.bfloat16


def mod4(place):
    return lax.rem(place + 4, 4)


def neighbour(axis, step):
    size = 4 if axis in ("y", "z") else 2
    return {axis: lax.rem(lax.axis_index(axis) + step + size, size)}


def chip_along(step):
    at = lax.rem(lax.axis_index("xh") * 2 + lax.axis_index("xl") + step + 4, 4)
    return {"xh": lax.div(at, 2), "xl": lax.rem(at, 2)}


def greet(*devices):
    barrier = pltpu.get_barrier_semaphore()
    for device in devices:
        pl.semaphore_signal(barrier, inc=1, device_id=device, device_id_type=MESH_ID)
    pl.semaphore_wait(barrier, len(devices))


def arrived(ref, sem):
    pltpu.make_async_copy(ref, ref, sem).wait()


class Sends:
    def __init__(self):
        self.copies = []

    def __call__(self, src, dst, send_sem, recv_sem, device):
        copy = pltpu.make_async_remote_copy(
            src_ref=src,
            dst_ref=dst,
            send_sem=send_sem,
            recv_sem=recv_sem,
            device_id=device,
            device_id_type=MESH_ID,
        )
        copy.start()
        self.copies.append(copy)

    def finish(self):
        for copy in self.copies:
            copy.wait_send()


def gather_body(
    x_ref, ups_ref, downs_ref, out_ref, up_ref, down_ref,
    loc, xs, xr, s1, r1m, r1p, f1s, f1r, s2, r2m, r2p, f2s, f2r, es, er, ex, ey,
):
    y, xl, z = lax.axis_index("y"), lax.axis_index("xl"), lax.axis_index("z")
    half = x_ref.shape[1] // 2
    quarter = half // 2
    greet(
        neighbour("xl", 1),
        *(neighbour("y", step) for step in (1, 2, 3)),
        *(neighbour("z", step) for step in (1, -1)),
    )
    rings = (("z", "y"), ("y", "z"))
    place = {"y": y, "z": z}
    other = 1 - xl
    both = pl.ds(0, 2)
    sends = Sends()
    send = sends

    def slot(h, first, second, j, start, count):
        yy, zz = (second, first) if h == 0 else (first, second)
        return out_ref.at[zz, j, yy, pl.ds(start, count)]

    own = pltpu.make_async_copy(x_ref.at[xl], out_ref.at[z, xl, y], loc.at[0])
    own.start()
    experts = ((ups_ref, up_ref), (downs_ref, down_ref))
    kept = []
    for n, (shards, expert) in enumerate(experts):
        kept.append(pltpu.make_async_copy(shards.at[y], expert.at[xl, y], loc.at[1 + n]))
        kept[-1].start()
        send(shards.at[y], expert.at[xl, y], ex.at[n, 0], ey.at[n, 0], neighbour("xl", 1))
        for step in (1, 3, 2):
            send(
                shards.at[mod4(y + step)],
                expert.at[xl, y],
                es.at[n, step - 1],
                er.at[n, step - 1],
                neighbour("y", step),
            )
    for h in (0, 1):
        first, second = place[rings[h][0]], place[rings[h][1]]
        src = x_ref.at[xl, pl.ds(h * half, half)]
        dst = slot(h, first, second, xl, h * half, half)
        send(x_ref.at[other, pl.ds(h * half, half)], dst, xs.at[h], xr.at[h], neighbour("xl", 1))
        send(src, dst, s1.at[h, 0, 0], r1m.at[h, 0], neighbour(rings[h][0], 1))
        send(src, dst, s1.at[h, 0, 1], r1p.at[h, 0], neighbour(rings[h][0], -1))
    own.wait()

    def send_second(h, k, first):
        block = slot(h, first, place[rings[h][1]], both, h * half, half)
        send(block, block, s2.at[h, k, 0], r2m.at[h, k], neighbour(rings[h][1], 1))
        send(block, block, s2.at[h, k, 1], r2p.at[h, k], neighbour(rings[h][1], -1))

    for h in (0, 1):
        first, second = place[rings[h][0]], place[rings[h][1]]
        block = slot(h, first, second, other, h * half, half)
        arrived(block, xr.at[h])
        send(block, block, s1.at[h, 1, 0], r1m.at[h, 1], neighbour(rings[h][0], 1))
        send(block, block, s1.at[h, 1, 1], r1p.at[h, 1], neighbour(rings[h][0], -1))
        send_second(h, 0, first)
    for j, jx in ((0, xl), (1, other)):
        for h in (0, 1):
            first, second = place[rings[h][0]], place[rings[h][1]]
            arrived(slot(h, mod4(first - 1), second, jx, h * half, half), r1m.at[h, j])
            block = slot(h, mod4(first - 1), second, jx, h * half, quarter)
            send(block, block, f1s.at[h, j, 0], f1r.at[h, j, 0], neighbour(rings[h][0], 1))
            arrived(slot(h, mod4(first + 1), second, jx, h * half, half), r1p.at[h, j])
            block = slot(h, mod4(first + 1), second, jx, h * half + quarter, quarter)
            send(block, block, f1s.at[h, j, 1], f1r.at[h, j, 1], neighbour(rings[h][0], -1))
    for k, step in ((1, -1), (2, 1)):
        for h in (0, 1):
            send_second(h, k, mod4(place[rings[h][0]] + step))
    for n, (shards, expert) in enumerate(experts):
        for step in (1, 3, 2):
            landed = expert.at[xl, mod4(y - step)]
            arrived(landed, er.at[n, step - 1])
            send(landed, landed, ex.at[n, step], ey.at[n, step], neighbour("xl", 1))
    for h in (0, 1):
        first, second = place[rings[h][0]], place[rings[h][1]]
        for j, jx in ((0, xl), (1, other)):
            for p in (0, 1):
                block = slot(h, mod4(first + 2), second, jx, h * half + p * quarter, quarter)
                arrived(block, f1r.at[h, j, p])
        send_second(h, 3, mod4(first + 2))
    steps = ((0, 0), (1, -1), (2, 1), (3, 2))
    for k, step in steps:
        for h in (0, 1):
            first, second = mod4(place[rings[h][0]] + step), place[rings[h][1]]
            arrived(slot(h, first, mod4(second - 1), both, h * half, half), r2m.at[h, k])
            block = slot(h, first, mod4(second - 1), both, h * half, quarter)
            send(block, block, f2s.at[h, k, 0], f2r.at[h, k, 0], neighbour(rings[h][1], 1))
            arrived(slot(h, first, mod4(second + 1), both, h * half, half), r2p.at[h, k])
            block = slot(h, first, mod4(second + 1), both, h * half + quarter, quarter)
            send(block, block, f2s.at[h, k, 1], f2r.at[h, k, 1], neighbour(rings[h][1], -1))
    for k, step in steps:
        for h in (0, 1):
            first, second = mod4(place[rings[h][0]] + step), place[rings[h][1]]
            for p in (0, 1):
                block = slot(h, first, mod4(second + 2), both, h * half + p * quarter, quarter)
                arrived(block, f2r.at[h, k, p])
    for n, (shards, expert) in enumerate(experts):
        for step in (0, 1, 3, 2):
            arrived(expert.at[other, mod4(y - step)], ey.at[n, step])
        kept[n].wait()
    sends.finish()


def gather_dp(shard, ups, downs):
    _, rows, cols = shard.shape
    dma = pltpu.SemaphoreType.DMA
    whole, up, down = pl.pallas_call(
        gather_body,
        out_shape=[
            jax.ShapeDtypeStruct((4, 2, 4, rows, cols), shard.dtype),
            jax.ShapeDtypeStruct((2, *ups.shape), ups.dtype),
            jax.ShapeDtypeStruct((2, *downs.shape), downs.dtype),
        ],
        in_specs=[pl.BlockSpec(memory_space=pl.ANY)] * 3,
        out_specs=[pl.BlockSpec(memory_space=pl.ANY)] * 3,
        scratch_shapes=[
            dma((3,)),
            dma((2,)),
            dma((2,)),
            dma((2, 2, 2)),
            dma((2, 2)),
            dma((2, 2)),
            dma((2, 2, 2)),
            dma((2, 2, 2)),
            dma((2, 4, 2)),
            dma((2, 4)),
            dma((2, 4)),
            dma((2, 4, 2)),
            dma((2, 4, 2)),
            dma((2, 3)),
            dma((2, 3)),
            dma((2, 4)),
            dma((2, 4)),
        ],
        compiler_params=pltpu.CompilerParams(collective_id=0, has_side_effects=True),
        name="gather_weights",
    )(shard, ups, downs)
    return whole.reshape(32 * rows, cols), up, down


def reduce_body(scatter_count, part_refs, core_buf, sum_buf, far_buf, core_s, core_r, far_s, far_r, sends):
    xh, core = lax.axis_index("xh"), lax.axis_index("core")
    rows = part_refs[0].shape[1]
    step = rows // scatter_count
    far, here = 1 - xh, xh
    for n, chunk in enumerate(range(0, rows, step)):
        at = pl.ds(chunk, step)
        for i, part in enumerate(part_refs):
            sends(
                part.at[far * 2 + 1 - core, at],
                core_buf.at[i, 0, at],
                core_s.at[i, n, 0],
                core_r.at[i, n, 0],
                neighbour("core", 1),
            )
    for n, chunk in enumerate(range(0, rows, step)):
        at = pl.ds(chunk, step)
        for i, part in enumerate(part_refs):
            sends(
                part.at[here * 2 + 1 - core, at],
                core_buf.at[i, 1, at],
                core_s.at[i, n, 1],
                core_r.at[i, n, 1],
                neighbour("core", 1),
            )
    for n, chunk in enumerate(range(0, rows, step)):
        at = pl.ds(chunk, step)
        for i, part in enumerate(part_refs):
            arrived(core_buf.at[i, 0, at], core_r.at[i, n, 0])
            mine = part[far * 2 + core, chunk : chunk + step, :].astype(F32)
            sum_buf[i, chunk : chunk + step, :] = (
                mine + core_buf[i, 0, chunk : chunk + step, :].astype(F32)
            ).astype(BF16)
            sends(
                sum_buf.at[i, at],
                far_buf.at[i, at],
                far_s.at[i, n],
                far_r.at[i, n],
                neighbour("xh", 1),
            )

    def total(i, n):
        chunk = n * step
        at = pl.ds(chunk, step)
        arrived(core_buf.at[i, 1, at], core_r.at[i, n, 1])
        near = part_refs[i][here * 2 + core, chunk : chunk + step, :].astype(F32)
        near = near + core_buf[i, 1, chunk : chunk + step, :].astype(F32)
        arrived(far_buf.at[i, at], far_r.at[i, n])
        return near + far_buf[i, chunk : chunk + step, :].astype(F32)

    return total


def ring_reduce_body(part_ref, core_buf, sum_buf, via_buf, far_buf, core_s, core_r, ring_s, ring_r, sends):
    xl, xh, core = lax.axis_index("xl"), lax.axis_index("xh"), lax.axis_index("core")
    rows = part_ref.shape[3]
    half = rows // 2
    at = xh * 2 + xl
    chips = [lax.rem(at + step, 4) for step in (2, 1, 3, 0)]
    chips = [(lax.rem(chip, 2), lax.div(chip, 2)) for chip in chips]
    for n, (pxl, pxh) in enumerate(chips):
        sends(
            part_ref.at[pxl, pxh, 1 - core],
            core_buf.at[n],
            core_s.at[n],
            core_r.at[n],
            neighbour("core", 1),
        )

    def own(n, start):
        pxl, pxh = chips[n]
        return part_ref[pxl, pxh, core, start : start + half, :].astype(F32)

    def both(n, start):
        return own(n, start) + core_buf[n, start : start + half, :].astype(F32)

    first, second = pl.ds(0, half), pl.ds(half, half)
    ahead, behind = chip_along(1), chip_along(-1)
    arrived(core_buf.at[0], core_r.at[0])
    sum_buf[0, :half, :] = both(0, 0).astype(BF16)
    sends(sum_buf.at[0, first], via_buf.at[0], ring_s.at[0], ring_r.at[0], ahead)
    sum_buf[0, half:, :] = both(0, half).astype(BF16)
    sends(sum_buf.at[0, second], via_buf.at[1], ring_s.at[1], ring_r.at[1], behind)
    arrived(core_buf.at[1], core_r.at[1])
    sum_buf[1, half:, :] = both(1, half).astype(BF16)
    sends(sum_buf.at[1, second], far_buf.at[0, second], ring_s.at[2], ring_r.at[2], ahead)
    arrived(core_buf.at[2], core_r.at[2])
    sum_buf[2, :half, :] = both(2, 0).astype(BF16)
    sends(sum_buf.at[2, first], far_buf.at[1, first], ring_s.at[3], ring_r.at[3], behind)
    arrived(via_buf.at[0], ring_r.at[0])
    sum_buf[1, :half, :] = (both(1, 0) + via_buf[0].astype(F32)).astype(BF16)
    sends(sum_buf.at[1, first], far_buf.at[0, first], ring_s.at[4], ring_r.at[4], ahead)
    arrived(via_buf.at[1], ring_r.at[1])
    sum_buf[2, half:, :] = (both(2, half) + via_buf[1].astype(F32)).astype(BF16)
    sends(sum_buf.at[2, second], far_buf.at[1, second], ring_s.at[5], ring_r.at[5], behind)
    arrived(core_buf.at[3], core_r.at[3])

    def total(part):
        rows_at = first if part == 0 else second
        start = part * half
        near = both(3, start)
        arrived(far_buf.at[0, rows_at], ring_r.at[4 if part == 0 else 2])
        near = near + far_buf[0, start : start + half, :].astype(F32)
        arrived(far_buf.at[1, rows_at], ring_r.at[3 if part == 0 else 5])
        return near + far_buf[1, start : start + half, :].astype(F32)

    return total


def ring_reduce_scratch(rows, width):
    dma = pltpu.SemaphoreType.DMA
    return [
        pltpu.VMEM((4, rows, width), BF16),
        pltpu.VMEM((3, rows, width), BF16),
        pltpu.VMEM((2, rows // 2, width), BF16),
        pltpu.VMEM((2, rows, width), BF16),
        dma((4,)),
        dma((4,)),
        dma((6,)),
        dma((6,)),
    ]


def ring_spread(out_ref, part, ring_s, ring_r, core_s, core_r, sends):
    xl, xh, core = lax.axis_index("xl"), lax.axis_index("xh"), lax.axis_index("core")
    half = out_ref.shape[3] // 2
    mine = out_ref.at[xl, xh, core, pl.ds(part * half, half)]
    sends(mine, mine, ring_s.at[part, 0], ring_r.at[part, 0], chip_along(1))
    sends(mine, mine, ring_s.at[part, 1], ring_r.at[part, 1], chip_along(-1))
    sends(mine, mine, core_s.at[part, 0], core_r.at[part, 0], neighbour("core", 1))


def ring_spread_finish(out_ref, ring_s, ring_r, core_s, core_r, sends):
    xl, xh, core = lax.axis_index("xl"), lax.axis_index("xh"), lax.axis_index("core")
    half = out_ref.shape[3] // 2
    at = xh * 2 + xl

    def block(step, part, which):
        chip = lax.rem(at + step + 4, 4)
        return out_ref.at[lax.rem(chip, 2), lax.div(chip, 2), which, pl.ds(part * half, half)]

    for part in (0, 1):
        for n, (step, on) in enumerate(((-1, 1), (1, -1))):
            landed = block(step, part, core)
            arrived(landed, ring_r.at[part, n])
            if part == n:
                sends(landed, landed, ring_s.at[part, 2], ring_r.at[part, 2], chip_along(on))
            sends(landed, landed, core_s.at[part, 1 + n], core_r.at[part, 1 + n], neighbour("core", 1))
    for part in (0, 1):
        landed = block(2, part, core)
        arrived(landed, ring_r.at[part, 2])
        sends(landed, landed, core_s.at[part, 3], core_r.at[part, 3], neighbour("core", 1))
    for part in (0, 1):
        for n, step in enumerate((0, -1, 1, 2)):
            arrived(block(step, part, 1 - core), core_r.at[part, n])


def ring_spread_scratch():
    dma = pltpu.SemaphoreType.DMA
    return [dma((2, 3)), dma((2, 3)), dma((2, 4)), dma((2, 4))]


def along_x():
    return neighbour("core", 1), neighbour("xh", 1), chip_along(1), chip_along(-1)


CHUNKS = 4


def reduce_scratch(count, rows, width):
    dma = pltpu.SemaphoreType.DMA
    return [
        pltpu.VMEM((count, 2, rows, width), BF16),
        pltpu.VMEM((count, rows, width), BF16),
        pltpu.VMEM((count, rows, width), BF16),
        dma((count, CHUNKS, 2)),
        dma((count, CHUNKS, 2)),
        dma((count, CHUNKS)),
        dma((count, CHUNKS)),
    ]


def spread_chunk(out_ref, n, step, sems, sends):
    xh, core = lax.axis_index("xh"), lax.axis_index("core")
    at = pl.ds(n * step, step)
    mine = out_ref.at[xh * 2 + core, at]
    far_s, far_r, core_s, core_r = sems
    sends(mine, mine, far_s.at[n], far_r.at[n], neighbour("xh", 1))
    sends(mine, mine, core_s.at[n, 0], core_r.at[n, 0], neighbour("core", 1))


def spread_finish(out_ref, step, sems, sends):
    xh, core = lax.axis_index("xh"), lax.axis_index("core")
    far_s, far_r, core_s, core_r = sems
    for n in range(CHUNKS):
        at = pl.ds(n * step, step)
        theirs = out_ref.at[(1 - xh) * 2 + core, at]
        arrived(theirs, far_r.at[n])
        sends(theirs, theirs, core_s.at[n, 1], core_r.at[n, 1], neighbour("core", 1))
    for n in range(CHUNKS):
        at = pl.ds(n * step, step)
        arrived(out_ref.at[xh * 2 + 1 - core, at], core_r.at[n, 0])
        arrived(out_ref.at[(1 - xh) * 2 + 1 - core, at], core_r.at[n, 1])


def spread_scratch():
    dma = pltpu.SemaphoreType.DMA
    return [dma((CHUNKS,)), dma((CHUNKS,)), dma((CHUNKS, 2)), dma((CHUNKS, 2))]


def middle_body(part_ref, x_ref, gain_ref, middle_ref, unit_ref, *scratch):
    sends = Sends()
    greet(*along_x())
    total = ring_reduce_body(part_ref, *scratch[:8], sends)
    me = lax.axis_index("xh") * 2 + lax.axis_index("core")
    step = x_ref.shape[0] // CHUNKS
    half = x_ref.shape[0] // 2
    for part in (0, 1):
        rows = slice(part * half, (part + 1) * half)
        middle = x_ref[rows, :].astype(F32) + total(part)
        middle_ref[rows, :] = middle
        inverse = lax.rsqrt(jnp.mean(middle * middle, 1, keepdims=True) + EPSILON)
        unit_ref[me, rows, :] = (middle * inverse * gain_ref[...]).astype(BF16)
        for n in range(part * CHUNKS // 2, (part + 1) * CHUNKS // 2):
            spread_chunk(unit_ref, n, step, scratch[8:], sends)
    spread_finish(unit_ref, step, scratch[8:], sends)
    sends.finish()


def vmem(count):
    return [pl.BlockSpec(memory_space=pltpu.VMEM)] * count


def middle_and_unit(part, x, gain):
    rows, width = x.shape
    middle, unit = pl.pallas_call(
        middle_body,
        out_shape=[
            jax.ShapeDtypeStruct((rows, width), F32),
            jax.ShapeDtypeStruct((4, rows, width), BF16),
        ],
        in_specs=vmem(3),
        out_specs=vmem(2),
        scratch_shapes=ring_reduce_scratch(rows, width) + spread_scratch(),
        compiler_params=pltpu.CompilerParams(
            collective_id=1, has_side_effects=True, vmem_limit_bytes=32 * MIB
        ),
        name="middle_and_unit",
    )(part.reshape(2, 2, 2, rows, width), x, gain[None])
    return middle, unit.reshape(4 * rows, width)


def back_body(part_ref, middle_ref, grad_ref, gain_ref, dmiddle_ref, dgain_ref, spread_ref, *scratch):
    sends = Sends()
    greet(*along_x())
    total = reduce_body(CHUNKS, [part_ref], *scratch[:7], sends)
    xl, xh, core = lax.axis_index("xl"), lax.axis_index("xh"), lax.axis_index("core")
    step = middle_ref.shape[0] // CHUNKS
    for n in range(CHUNKS):
        rows = slice(n * step, (n + 1) * step)
        middle = middle_ref[rows, :]
        inverse = lax.rsqrt(jnp.mean(middle * middle, 1, keepdims=True) + EPSILON)
        normed = middle * inverse
        dunit = total(0, n)
        product = dunit * normed
        dgain = jnp.sum(product, 0, keepdims=True)
        if n == 0:
            dgain_ref[...] = dgain
        else:
            dgain_ref[...] += dgain
        mean = jnp.mean(product * gain_ref[...], 1, keepdims=True)
        dmiddle = grad_ref[rows, :].astype(F32) + inverse * (dunit * gain_ref[...] - normed * mean)
        dmiddle_ref[rows, :] = dmiddle
        spread_ref[xl, xh, core, rows, :] = dmiddle.astype(BF16)
        if n % 2 == 1:
            ring_spread(spread_ref, n // 2, *scratch[7:], sends)
    ring_spread_finish(spread_ref, *scratch[7:], sends)
    sends.finish()


def middle_back(part, middle, grad, gain):
    rows, width = middle.shape
    dmiddle, dgain, spread = pl.pallas_call(
        back_body,
        out_shape=[
            jax.ShapeDtypeStruct((rows, width), F32),
            jax.ShapeDtypeStruct((1, width), F32),
            jax.ShapeDtypeStruct((2, 2, 2, rows, width), BF16),
        ],
        in_specs=vmem(4),
        out_specs=vmem(3),
        scratch_shapes=reduce_scratch(1, rows, width) + ring_spread_scratch(),
        compiler_params=pltpu.CompilerParams(
            collective_id=2, has_side_effects=True, vmem_limit_bytes=32 * MIB
        ),
        name="middle_back",
    )(part.reshape(4, rows, width), middle, grad, gain[None])
    return dmiddle, dgain[0], spread.reshape(8 * rows, width)


def last_body(
    part_ref, feed_ref, x_ref, middle_ref, dmiddle_ref, gain_ref, small_ref,
    output_ref, dinput_ref, small_out, *scratch,
):
    sends = Sends()
    xh, core = lax.axis_index("xh"), lax.axis_index("core")
    peers = ({"xh": xh, "core": 1 - core}, {"xh": 1 - xh, "core": core}, {"xh": 1 - xh, "core": 1 - core})
    greet(*peers, chip_along(1), chip_along(-1))
    small_buf, small_s, small_r = scratch[15:]
    for n, peer in enumerate(peers):
        sends(small_ref, small_buf.at[n], small_s.at[n], small_r.at[n], peer)
    total = ring_reduce_body(part_ref, *scratch[7:15], sends)
    feed = reduce_body(CHUNKS, [feed_ref], *scratch[:7], sends)
    half = x_ref.shape[0] // 2
    for part in (0, 1):
        rows = slice(part * half, (part + 1) * half)
        x = x_ref[rows, :].astype(F32)
        inverse = lax.rsqrt(jnp.mean(x * x, 1, keepdims=True) + EPSILON)
        normed = x * inverse
        dscaled = total(part) * gain_ref[...]
        mean = jnp.mean(dscaled * normed, 1, keepdims=True)
        dinput_ref[rows, :] = dmiddle_ref[rows, :] + inverse * (dscaled - normed * mean)
    step = x_ref.shape[0] // CHUNKS
    for n in range(CHUNKS):
        rows = slice(n * step, (n + 1) * step)
        output_ref[rows, :] = (middle_ref[rows, :] + feed(0, n)).astype(BF16)
    for n in range(3):
        arrived(small_buf.at[n], small_r.at[n])
    small_out[...] = (small_ref[...] + small_buf[1]) + (small_buf[0] + small_buf[2])
    sends.finish()


def last_sums(part, feed, x, middle, dmiddle, gain, small):
    rows, width = x.shape
    dma = pltpu.SemaphoreType.DMA
    return pl.pallas_call(
        last_body,
        out_shape=[
            jax.ShapeDtypeStruct((rows, width), BF16),
            jax.ShapeDtypeStruct((rows, width), F32),
            jax.ShapeDtypeStruct(small.shape, F32),
        ],
        in_specs=vmem(7),
        out_specs=vmem(3),
        scratch_shapes=reduce_scratch(1, rows, width)
        + ring_reduce_scratch(rows, width)
        + [pltpu.VMEM((3, *small.shape), F32), dma((3,)), dma((3,))],
        compiler_params=pltpu.CompilerParams(
            collective_id=3, has_side_effects=True, vmem_limit_bytes=40 * MIB
        ),
        name="last_sums",
    )(
        part.reshape(2, 2, 2, rows, width),
        feed.reshape(4, rows, width),
        x,
        middle,
        dmiddle,
        gain[None],
        small,
    )


def rows_body(rows_ref, out_ref, loc, far_s, far_r, core_s, core_r):
    y, core = lax.axis_index("y"), lax.axis_index("core")
    half = rows_ref.shape[1] // 2
    sends = Sends()
    greet(neighbour("core", 1), *(neighbour("y", step) for step in (1, 2, 3)))
    at = pl.ds(pl.multiple_of(core * half, half), half)
    own = pltpu.make_async_copy(rows_ref.at[y], out_ref.at[y], loc)
    own.start()
    for step in (2, 1, 3):
        target = mod4(y + step)
        sends(
            rows_ref.at[target, at],
            out_ref.at[y, at],
            far_s.at[step - 1],
            far_r.at[step - 1],
            neighbour("y", step),
        )
    for step in (1, 3, 2):
        source = mod4(y - step)
        block = out_ref.at[source, at]
        arrived(block, far_r.at[step - 1])
        sends(block, block, core_s.at[step - 1], core_r.at[step - 1], neighbour("core", 1))
    own.wait()
    other = pl.ds(pl.multiple_of((1 - core) * half, half), half)
    for step in (1, 3, 2):
        arrived(out_ref.at[mod4(y - step), other], core_r.at[step - 1])
    sends.finish()


def rows_to_experts(rows):
    dma = pltpu.SemaphoreType.DMA
    return pl.pallas_call(
        rows_body,
        out_shape=jax.ShapeDtypeStruct(rows.shape, rows.dtype),
        in_specs=[pl.BlockSpec(memory_space=pl.ANY)],
        out_specs=pl.BlockSpec(memory_space=pl.ANY),
        scratch_shapes=[dma, dma((3,)), dma((3,)), dma((3,)), dma((3,))],
        compiler_params=pltpu.CompilerParams(collective_id=4, has_side_effects=True),
        name="rows_to_experts",
    )(rows)


STEPS = (2, 1, -1, 0)


def scatter_body(
    qkv_ref, small_ref, o_ref, up_ref, down_ref, out_ref, up_out, down_out, g_ref, loc, t_buf, r_buf, tb_buf, rb_buf, c_buf,
    t_s, t_r, r_s, r_r, tb_s, tb_r, rb_s, rb_r, c_s, c_r, up_buf, down_buf, up_sum, down_sum, ex, ey, es, er,
):
    xl = lax.axis_index("xl")
    place = {"y": lax.axis_index("y"), "z": lax.axis_index("z")}
    half = g_ref.shape[3] // 2
    quarter = half // 2
    rings = (("z", "y"), ("y", "z"))
    sends = Sends()
    column = 0
    parts = []
    for n, ref in enumerate((qkv_ref, small_ref, o_ref)):
        cols = ref.shape[-1]
        parts.append(pltpu.make_async_copy(ref, g_ref.at[..., pl.ds(column, cols)], loc.at[n]))
        parts[-1].start()
        column += cols
    greet(
        neighbour("xl", 1),
        *(neighbour("y", step) for step in (1, 2, 3)),
        *(neighbour("z", step) for step in (1, -1)),
    )
    both = slice(0, 2)
    experts = ((up_ref, up_buf, up_sum, up_out), (down_ref, down_buf, down_sum, down_out))
    my_y = place["y"]
    for n, (grads, buf, _, _) in enumerate(experts):
        for step in (2, 1, 3, 0):
            target = mod4(my_y + step)
            sends(
                grads.at[1 - xl, target],
                buf.at[step],
                ex.at[n, step],
                ey.at[n, step],
                neighbour("xl", 1),
            )
    for part in parts:
        part.wait()

    def grad_ref(h, first, second, start):
        zz, yy = (first, second) if h == 0 else (second, first)
        return g_ref.at[zz, both, yy, pl.ds(h * half + start, quarter)]

    def grad(h, first, second, j, start, count):
        zz, yy = (first, second) if h == 0 else (second, first)
        return g_ref[zz, j, yy, h * half + start : h * half + start + count, :].astype(F32)

    def firsts(h, k):
        return mod4(place[rings[h][0]] + STEPS[k])

    for k in range(4):
        for h in (0, 1):
            second = place[rings[h][1]]
            for d, way in ((0, 1), (1, -1)):
                sends(
                    grad_ref(h, firsts(h, k), mod4(second + 2), d * quarter),
                    t_buf.at[h, d, k],
                    t_s.at[h, d, k],
                    t_r.at[h, d, k],
                    neighbour(rings[h][1], way),
                )
    for k in range(4):
        for h in (0, 1):
            second = place[rings[h][1]]
            for d, way in ((0, 1), (1, -1)):
                sends(
                    grad_ref(h, firsts(h, k), mod4(second + way), (1 - d) * quarter),
                    r_buf.at[h, d, k, both, pl.ds((1 - d) * quarter, quarter)],
                    r_s.at[h, d, k, 0],
                    r_r.at[h, d, k, 0],
                    neighbour(rings[h][1], way),
                )
    for k in range(4):
        for h in (0, 1):
            second = place[rings[h][1]]
            for d, way in ((0, 1), (1, -1)):
                arrived(t_buf.at[h, d, k], t_r.at[h, d, k])
                for j in (0, 1):
                    t_buf[h, d, k, j] = (
                        t_buf[h, d, k, j].astype(F32)
                        + grad(h, firsts(h, k), mod4(second + way), j, d * quarter, quarter)
                    ).astype(BF16)
                sends(
                    t_buf.at[h, d, k],
                    r_buf.at[h, d, k, both, pl.ds(d * quarter, quarter)],
                    r_s.at[h, d, k, 1],
                    r_r.at[h, d, k, 1],
                    neighbour(rings[h][1], way),
                )
    for n, (grads, buf, total, result) in enumerate(experts):
        for step in (2, 1, 3, 0):
            target = mod4(my_y + step)
            arrived(buf.at[step], ey.at[n, step])
            value = (grads[xl, target].astype(F32) + buf[step].astype(F32)).astype(BF16)
            if step == 0:
                result[my_y] = value
            else:
                total[step - 1] = value
                sends(
                    total.at[step - 1],
                    result.at[my_y],
                    es.at[n, step - 1],
                    er.at[n, step - 1],
                    neighbour("y", step),
                )
    for k in range(4):
        for h in (0, 1):
            second = place[rings[h][1]]
            for d in (0, 1):
                arrived(r_buf.at[h, d, k, both, pl.ds((1 - d) * quarter, quarter)], r_r.at[h, d, k, 0])
                arrived(r_buf.at[h, d, k, both, pl.ds(d * quarter, quarter)], r_r.at[h, d, k, 1])
            for j in (0, 1):
                r_buf[h, 0, k, j] = (
                    r_buf[h, 0, k, j].astype(F32)
                    + r_buf[h, 1, k, j].astype(F32)
                    + grad(h, firsts(h, k), second, j, 0, half)
                ).astype(BF16)
            for d, way in ((0, 1), (1, -1)):
                device = neighbour(rings[h][0], way)
                if k == 0:
                    sends(
                        r_buf.at[h, 0, 0, both, pl.ds(d * quarter, quarter)],
                        tb_buf.at[h, d],
                        tb_s.at[h, d],
                        tb_r.at[h, d],
                        device,
                    )
                if k == 1 + d:
                    sends(
                        r_buf.at[h, 0, k, both, pl.ds((1 - d) * quarter, quarter)],
                        rb_buf.at[h, d, both, pl.ds((1 - d) * quarter, quarter)],
                        rb_s.at[h, d, 0],
                        rb_r.at[h, d, 0],
                        device,
                    )
                    arrived(tb_buf.at[h, d], tb_r.at[h, d])
                    for j in (0, 1):
                        tb_buf[h, d, j] = (
                            tb_buf[h, d, j].astype(F32)
                            + r_buf[h, 0, k, j, d * quarter : (d + 1) * quarter, :].astype(F32)
                        ).astype(BF16)
                    sends(
                        tb_buf.at[h, d],
                        rb_buf.at[h, d, both, pl.ds(d * quarter, quarter)],
                        rb_s.at[h, d, 1],
                        rb_r.at[h, d, 1],
                        device,
                    )
    for h in (0, 1):
        for d in (0, 1):
            arrived(rb_buf.at[h, d, both, pl.ds((1 - d) * quarter, quarter)], rb_r.at[h, d, 0])
            arrived(rb_buf.at[h, d, both, pl.ds(d * quarter, quarter)], rb_r.at[h, d, 1])
        for j in (0, 1):
            rb_buf[h, 0, j] = (
                rb_buf[h, 0, j].astype(F32)
                + rb_buf[h, 1, j].astype(F32)
                + r_buf[h, 0, 3, j].astype(F32)
            ).astype(BF16)
        sends(rb_buf.at[h, 0, 1 - xl], c_buf.at[h], c_s.at[h], c_r.at[h], neighbour("xl", 1))
        out_ref[xl, h * half : (h + 1) * half, :] = rb_buf[h, 0, xl].astype(F32)
    for h in (0, 1):
        arrived(c_buf.at[h], c_r.at[h])
        out_ref[1 - xl, h * half : (h + 1) * half, :] = c_buf[h].astype(F32)
    for n, (_, _, _, result) in enumerate(experts):
        for step in (1, 3, 2):
            arrived(result.at[mod4(my_y - step)], er.at[n, step - 1])
    sends.finish()


def scatter_dp(grads, ups, downs):
    rows, cols = grads[0].shape[0], sum(grad.shape[1] for grad in grads)
    share = rows // 32
    half, quarter = share // 2, share // 4
    dma = pltpu.SemaphoreType.DMA
    up_cols, down_cols = ups.shape[1], downs.shape[1]
    return pl.pallas_call(
        scatter_body,
        out_shape=[
            jax.ShapeDtypeStruct((2, share, cols), F32),
            jax.ShapeDtypeStruct((4, share, up_cols), BF16),
            jax.ShapeDtypeStruct((4, share, down_cols), BF16),
        ],
        in_specs=[pl.BlockSpec(memory_space=pl.ANY)] * 3 + vmem(2),
        out_specs=vmem(3),
        scratch_shapes=[
            pltpu.VMEM((4, 2, 4, share, cols), BF16),
            dma((3,)),
            pltpu.VMEM((2, 2, 4, 2, quarter, cols), BF16),
            pltpu.VMEM((2, 2, 4, 2, half, cols), BF16),
            pltpu.VMEM((2, 2, 2, quarter, cols), BF16),
            pltpu.VMEM((2, 2, 2, half, cols), BF16),
            pltpu.VMEM((2, half, cols), BF16),
            dma((2, 2, 4)),
            dma((2, 2, 4)),
            dma((2, 2, 4, 2)),
            dma((2, 2, 4, 2)),
            dma((2, 2)),
            dma((2, 2)),
            dma((2, 2, 2)),
            dma((2, 2, 2)),
            dma((2,)),
            dma((2,)),
            pltpu.VMEM((4, share, up_cols), BF16),
            pltpu.VMEM((4, share, down_cols), BF16),
            pltpu.VMEM((3, share, up_cols), BF16),
            pltpu.VMEM((3, share, down_cols), BF16),
            dma((2, 4)),
            dma((2, 4)),
            dma((2, 3)),
            dma((2, 3)),
        ],
        compiler_params=pltpu.CompilerParams(
            collective_id=5, has_side_effects=True, vmem_limit_bytes=56 * MIB
        ),
        name="scatter_grads",
    )(
        *(grad.reshape(4, 2, 4, share, grad.shape[1]) for grad in grads),
        ups.reshape(2, 4, share, up_cols),
        downs.reshape(2, 4, share, down_cols),
    )


def dot(a, b, dims):
    return lax.dot_general(a, b, (dims, ((), ())), preferred_element_type=F32)


def attention_body(
    k_ref, v_ref, q0, q1, q2, cos_ref, sin_ref, col_ref, row_ref, gate_ref,
    key_out, val_out, que_out, mix_out, gmix_out, prob_out,
):
    h = pl.program_id(1)
    cosine, sine = cos_ref[...], sin_ref[...]
    scale = 1.0 / math.sqrt(HD)

    def rotated(v):
        return v * cosine + pltpu.roll(v, HD // 2, 1) * sine

    key = rotated(k_ref[...]).astype(BF16)
    val = v_ref[...].astype(BF16)
    key_out[...] = key
    val_out[...] = val
    tokens = key.shape[0]
    seg_col, seg_row = col_ref[...], row_ref[0]
    at_row = lax.broadcasted_iota(jnp.int32, (tokens, tokens), 0)
    at_col = lax.broadcasted_iota(jnp.int32, (tokens, tokens), 1)
    allowed = (at_col <= at_row) & ((seg_row == 0) | (seg_row == seg_col))
    for e, q_ref in enumerate((q0, q1, q2)):
        query = (rotated(q_ref[...]) * scale).astype(BF16)
        scores = jnp.where(allowed, dot(query, key, ((1,), (1,))), NEGATIVE)
        largest = jnp.max(scores, 1, keepdims=True)
        expsum = jnp.exp(scores - largest)
        prob = (expsum * (1.0 / jnp.sum(expsum, 1, keepdims=True))).astype(BF16)
        prob_out[0, 0, e] = prob
        mixed = dot(prob, val, ((1,), (0,))).astype(BF16)
        at = pl.ds(pl.multiple_of((e * HEADS + h) * HD, HD), HD)
        que_out[:, at] = query
        mix_out[:, at] = mixed
        gmix_out[:, at] = (mixed.astype(F32) * gate_ref[:, e : e + 1]).astype(BF16)


def block_specs(tokens):
    def column(n):
        return pl.BlockSpec((tokens, HD), lambda g, h: (g, n * HEADS + h))

    def rows(width):
        return pl.BlockSpec((tokens, width), lambda g, h: (g, 0))

    return column, rows


def prob_spec(tokens):
    return pl.BlockSpec((1, 1, 3, tokens, tokens), lambda g, h: (g, h, 0, 0, 0))


def attention_forward(joined, cosine, sine, segments, gates):
    groups, tokens = segments.shape
    column, rows = block_specs(tokens)
    wide = jax.ShapeDtypeStruct((groups * tokens, 3 * HEADS * HD), BF16)
    narrow = jax.ShapeDtypeStruct((groups * tokens, HEADS * HD), BF16)
    return pl.pallas_call(
        attention_body,
        grid=(groups, HEADS),
        in_specs=[column(n) for n in range(5)]
        + [rows(HD)] * 2
        + [rows(1), pl.BlockSpec((1, 1, tokens), lambda g, h: (g, 0, 0)), rows(gates.shape[1])],
        out_specs=[column(0), column(0)] + [rows(wide.shape[1])] * 3 + [prob_spec(tokens)],
        out_shape=[narrow, narrow, wide, wide, wide]
        + [jax.ShapeDtypeStruct((groups, HEADS, 3, tokens, tokens), BF16)],
        compiler_params=pltpu.CompilerParams(vmem_limit_bytes=48 * MIB),
        name="attention_forward",
    )(
        *[joined] * 5, cosine, sine, segments.reshape(-1, 1), segments[:, None], gates
    )


def attention_back_body(
    key_ref, val_ref, q0, q1, q2, m0, m1, m2, h0, h1, h2, prob_ref, cos_ref, sin_ref, gate_ref,
    grad_out, dgate_out,
):
    h = pl.program_id(1)
    cosine, sine = cos_ref[...], sin_ref[...]
    scale = 1.0 / math.sqrt(HD)

    def rotated_back(v):
        return v * cosine - pltpu.roll(v, HD // 2, 1) * sine

    key, val = key_ref[...], val_ref[...]
    tokens = key.shape[0]
    dkey = jnp.zeros((tokens, HD), F32)
    dval = jnp.zeros((tokens, HD), F32)
    lane = lax.broadcasted_iota(jnp.int32, (tokens, HD), 1)
    dgates = jnp.zeros((tokens, HD), F32)
    for e, (q_ref, m_ref, h_ref) in enumerate(((q0, m0, h0), (q1, m1, h1), (q2, m2, h2))):
        query, mixed, raw = q_ref[...], m_ref[...].astype(F32), h_ref[...]
        inner = jnp.sum(mixed * raw, 1, keepdims=True)
        dgates = dgates + jnp.where(lane == e, inner, 0.0)
        gate = gate_ref[:, e : e + 1]
        dmixed = (raw * gate).astype(BF16)
        prob = prob_ref[0, 0, e]
        dval = dval + dot(prob, dmixed, ((0,), (0,)))
        dprob = dot(dmixed, val, ((1,), (1,)))
        delta = jnp.sum(dmixed.astype(F32) * mixed, 1, keepdims=True)
        dscores = (prob.astype(F32) * (dprob - delta)).astype(BF16)
        dquery = dot(dscores, key, ((1,), (0,)))
        dkey = dkey + dot(dscores, query, ((0,), (0,)))
        at = pl.ds(pl.multiple_of(((2 + e) * HEADS + h) * HD, HD), HD)
        grad_out[:, at] = rotated_back(dquery * scale).astype(BF16)
    grad_out[:, pl.ds(pl.multiple_of(h * HD, HD), HD)] = rotated_back(dkey).astype(BF16)
    grad_out[:, pl.ds(pl.multiple_of((HEADS + h) * HD, HD), HD)] = dval.astype(BF16)

    @pl.when(h == 0)
    def _():
        dgate_out[...] = dgates

    @pl.when(h > 0)
    def _():
        dgate_out[...] += dgates


def attention_back(key, val, que, mix, raw, prob, cosine, sine, gates):
    groups, tokens = prob.shape[0], prob.shape[-1]
    column, rows = block_specs(tokens)
    thirds = [column(n) for n in range(3)]
    grads = jax.ShapeDtypeStruct((groups * tokens, 5 * HEADS * HD), BF16)
    return pl.pallas_call(
        attention_back_body,
        grid=(groups, HEADS),
        in_specs=[column(0), column(0)]
        + thirds * 3
        + [prob_spec(tokens)]
        + [rows(HD)] * 2
        + [rows(gates.shape[1])],
        out_specs=[rows(grads.shape[1]), rows(HD)],
        out_shape=[grads, jax.ShapeDtypeStruct((groups * tokens, HD), F32)],
        compiler_params=pltpu.CompilerParams(vmem_limit_bytes=48 * MIB),
        name="attention_back",
    )(key, val, que, que, que, mix, mix, mix, raw, raw, raw, prob, cosine, sine, gates)


def positions(segments):
    index = jnp.arange(segments.shape[0], dtype=jnp.int32)
    prompt = jnp.sum((segments == 0).astype(jnp.int32))
    first = jnp.sum((segments == 1).astype(jnp.int32))
    before = jnp.where(segments == 0, 0, jnp.where(segments == 1, prompt, prompt + first))
    return jnp.where(segments == 0, index, prompt + index - before)


def route_gates(logits, routes, count):
    onehot = (routes[:, :, None] == jnp.arange(count, dtype=jnp.int32)).astype(F32)
    chosen = jnp.sum(onehot * logits[:, None, :], -1)
    expsum = jnp.exp(chosen - jnp.max(chosen, -1, keepdims=True))
    weights = expsum / jnp.sum(expsum, -1, keepdims=True)
    return weights, onehot, jnp.sum(weights[:, :, None] * onehot, 1)


def router_back(dgate, weights, onehot):
    dchosen = jnp.sum(dgate[:, None, :] * onehot, -1)
    dselect = weights * (dchosen - jnp.sum(weights * dchosen, -1, keepdims=True))
    return jnp.sum(dselect[:, :, None] * onehot, 1).astype(BF16)


def normalize(activations):
    inverse = lax.rsqrt(jnp.mean(activations * activations, -1, keepdims=True) + EPSILON)
    return activations * inverse, inverse


def swiglu_back(dhidden, gate_pre, linear):
    sigmoid_pre = jax.nn.sigmoid(gate_pre)
    dgate_pre = dhidden * linear * sigmoid_pre * (1.0 + gate_pre * (1.0 - sigmoid_pre))
    dlinear = dhidden * gate_pre * sigmoid_pre
    return jnp.concatenate([dgate_pre, dlinear], 1).astype(BF16)


def reorder(rows):
    count, width = rows.shape
    return jnp.transpose(rows.reshape(count, 4, 2, 4, width // 32), (0, 3, 2, 1, 4)).reshape(count, width)


def pad_to(array, width):
    return jnp.pad(array, ((0, 0), (0, width - array.shape[1])))


def on_device(
    inputs,
    segments,
    att_routes,
    mlp_routes,
    key_value,
    query_proj,
    output_proj,
    router_att,
    gain_att,
    gate_up,
    down_proj,
    router_mlp,
    gain_mlp,
    out_grad,
):
    width = inputs.shape[1]
    inner = query_proj.shape[2]
    hidden_local = down_proj.shape[1]
    att_count = query_proj.shape[0]
    mlp_count = gate_up.shape[0]
    share = gate_up.shape[1]
    part = inner // 2
    qkv_cols = (2 + att_count) * part
    small_at = qkv_cols
    out_at = qkv_cols + 128
    small = jnp.concatenate([router_att, router_mlp, gain_att[:, None], gain_mlp[:, None]], 1)
    own_att = jnp.concatenate(
        [
            jnp.transpose(key_value.reshape(share, 2, 2, part), (2, 0, 1, 3)).reshape(2, share, -1),
            jnp.transpose(query_proj.reshape(att_count, share, 2, part), (2, 1, 0, 3)).reshape(
                2, share, -1
            ),
            jnp.broadcast_to(pad_to(small, 128), (2, share, 128)),
            jnp.transpose(output_proj.reshape(att_count, 2, part, share), (1, 3, 0, 2)).reshape(
                2, share, -1
            ),
        ],
        2,
    )
    inputs = reorder(inputs)
    out_grad = reorder(out_grad)
    x_all = lax.all_gather(inputs, ("xl", *TP), axis=0, tiled=True)
    grad_all = lax.all_gather(out_grad, TP, axis=0, tiled=True)
    marks = lax.all_gather(jnp.concatenate([segments[:, None], att_routes], 1), "xl", axis=0)
    weights, up_parts, down_parts = gather_dp(
        own_att, gate_up.reshape(mlp_count, share, -1), jnp.swapaxes(down_proj, 1, 2)
    )
    up_whole = lax.all_gather(
        up_parts.reshape(2 * mlp_count * share, -1), "z", axis=0, tiled=True
    )
    down_whole = lax.all_gather(
        down_parts.reshape(2 * mlp_count * share, -1), "z", axis=0, tiled=True
    )

    tokens = segments.shape[0]
    match = jnp.sum((mlp_routes[:, :, None] == jnp.arange(mlp_count, dtype=jnp.int32)).astype(BF16), 1)
    index = jnp.arange(tokens, dtype=jnp.int32)
    lower = (index[None, :] < index[:, None]).astype(BF16)
    rank = dot(lower, match, ((1,), (0,)))
    slot = jnp.where(match > 0, rank.astype(jnp.int32), -1)
    pick = (slot.T[:, None, :] == jnp.arange(CAP, dtype=jnp.int32)[None, :, None]).astype(BF16)
    pick_rows = pick.reshape(mlp_count * CAP, tokens)
    grad_rows = dot(pick_rows, grad_all, ((1,), (0,))).astype(BF16)
    grad_in = lax.all_to_all(grad_rows.reshape(mlp_count, CAP, width), "y", 0, 0, tiled=True)
    grad_in = grad_in.reshape(mlp_count * CAP, width)

    small_all = weights[:, small_at : small_at + 128].astype(F32)
    gain_one, gain_two = small_all[:, 7], small_all[:, 8]
    segments = marks[:, :, 0]
    att_routes = marks[:, :, 1:].reshape(2 * tokens, 2)
    places = jax.vmap(positions)(segments).reshape(-1).astype(F32)
    frequency = ROPE_BASE ** (-2.0 * jnp.arange(HD // 2, dtype=F32) / HD)
    angles = places[:, None] * frequency[None, :]
    cosine = jnp.concatenate([jnp.cos(angles)] * 2, 1)
    sine = jnp.concatenate([-jnp.sin(angles), jnp.sin(angles)], 1)
    normed_one, _ = normalize(x_all.astype(F32))
    unit_one = (normed_one * gain_one).astype(BF16)
    joined_att = dot(unit_one, weights[:, :out_at], ((1,), (0,)))
    weights_att, onehot_att, gate_att = route_gates(
        joined_att[:, small_at : small_at + att_count], att_routes, att_count
    )
    key_rot, val_rows, queries, mixed, gmixed, prob = attention_forward(
        joined_att, cosine, sine, segments, gate_att
    )
    out_weights = weights[:, out_at:]
    attention = dot(gmixed, out_weights, ((1,), (1,))).astype(BF16)
    middle, unit_two = middle_and_unit(attention, inputs, gain_two)

    router_two = weights[:, small_at + att_count : small_at + att_count + mlp_count]
    logit_mlp = dot(unit_two, router_two, ((1,), (0,)))
    weights_mlp, onehot_mlp, gate_mlp = route_gates(logit_mlp, mlp_routes, mlp_count)
    gate_high = gate_mlp.astype(BF16)
    gate_low = (gate_mlp - gate_high.astype(F32)).astype(BF16)
    extended = jnp.concatenate([unit_two, pad_to(jnp.concatenate([gate_high, gate_low], 1), 128)], 1)
    rows_out = dot(pick_rows, extended, ((1,), (0,))).astype(BF16)
    rows_ext = rows_to_experts(rows_out.reshape(mlp_count, CAP, width + 128))
    rows_ext = rows_ext.reshape(mlp_count * CAP, width + 128)
    rows_in = rows_ext[:, :width]
    gates_ext = rows_ext[:, width : width + 2 * mlp_count].astype(F32)
    mine = (jnp.arange(2 * mlp_count) % mlp_count == lax.axis_index("y")).astype(F32)
    gates_in = jnp.sum(gates_ext * mine, 1, keepdims=True)
    joined = dot(rows_in, up_whole, ((1,), (0,)))
    gate_pre = joined[:, :hidden_local]
    linear = joined[:, hidden_local:]
    hidden_f32 = jax.nn.silu(gate_pre) * linear
    hidden = hidden_f32.astype(BF16)
    dhidden = dot(grad_in, down_whole, ((1,), (0,)))
    dgate_in = jnp.sum(hidden_f32 * dhidden, 1, keepdims=True)
    djoined = swiglu_back(dhidden * gates_in, gate_pre, linear)
    grad_down_whole = dot(
        grad_in, (hidden_f32 * gates_in).astype(BF16), ((0,), (0,))
    ).astype(BF16)
    djoined, grad_down_whole = lax.optimization_barrier((djoined, grad_down_whole))
    grad_down_sum = lax.psum_scatter(grad_down_whole, "z", scatter_dimension=0, tiled=True)
    dunit_part = dot(djoined, up_whole, ((1,), (1,))).astype(BF16)
    dgate_high = dgate_in.astype(BF16)
    dgate_low = (dgate_in - dgate_high.astype(F32)).astype(BF16)
    dunit_ext = jnp.concatenate(
        [dunit_part, pad_to(jnp.concatenate([dgate_high, dgate_low], 1), 128)], 1
    )
    dunit_back = lax.all_to_all(dunit_ext.reshape(mlp_count, CAP, width + 128), "y", 0, 0, tiled=True)
    djoined, dunit_ext = lax.optimization_barrier((djoined, dunit_ext))
    grad_up_whole = dot(rows_in, djoined, ((0,), (0,))).astype(BF16)
    hidden, grad_up_whole = lax.optimization_barrier((hidden, grad_up_whole))
    grad_up_sum = lax.psum_scatter(grad_up_whole, "z", scatter_dimension=0, tiled=True)
    branch_part = dot(hidden, down_whole, ((1,), (1,))).astype(BF16)
    dunit_back, branch_part = lax.optimization_barrier((dunit_back, branch_part))
    branch_back = lax.all_to_all(
        branch_part.reshape(mlp_count, CAP, width), "y", 0, 0, tiled=True
    ).reshape(mlp_count * CAP, width)
    dunit_back = dunit_back.reshape(mlp_count * CAP, width + 128)
    dgate_slots = (
        dunit_back[:, width : width + 1].astype(F32) + dunit_back[:, width + 1 : width + 2].astype(F32)
    ).reshape(mlp_count, CAP, 1)
    dgate_two = jnp.sum(pick.astype(F32) * dgate_slots, 1).T
    dlogit_mlp = router_back(dgate_two, weights_mlp, onehot_mlp)
    dunit_two = dot(pick_rows, dunit_back[:, :width], ((0,), (0,))) + dot(
        dlogit_mlp, router_two, ((1,), (1,))
    )
    grad_rmlp = dot(unit_two, dlogit_mlp, ((0,), (0,)))
    dmiddle, grad_gain_two, dattention = middle_back(
        dunit_two.astype(BF16), middle, out_grad, gain_two
    )

    raw = dot(dattention, out_weights, ((1,), (0,)))
    grad_qkv, dgate_one = attention_back(
        key_rot, val_rows, queries, mixed, raw, prob, cosine, sine, gate_att
    )
    dlogit_att = router_back(dgate_one[:, :att_count], weights_att, onehot_att)
    grad_joined = jnp.concatenate([grad_qkv, pad_to(dlogit_att, 128)], 1)
    dunit_one = dot(grad_joined, weights[:, :out_at], ((1,), (1,)))
    grad_gain_one = jnp.sum(dunit_one * normed_one, 0)
    grad_small = jnp.concatenate(
        [
            dot(unit_one, dlogit_att, ((0,), (0,))),
            grad_rmlp,
            grad_gain_one[:, None],
            grad_gain_two[:, None],
        ],
        1,
    )
    gate_slots = jnp.sum(pick.astype(F32) * gate_mlp.T[:, None, :], -1).reshape(mlp_count * CAP, 1)
    feed = dot(pick_rows, (branch_back.astype(F32) * gate_slots).astype(BF16), ((0,), (0,)))
    summed_att, ups_sum, downs_sum = scatter_dp(
        (
            dot(unit_one, grad_qkv, ((0,), (0,))).astype(BF16),
            pad_to(grad_small, 128).astype(BF16),
            dot(dattention, gmixed, ((0,), (0,))).astype(BF16),
        ),
        grad_up_sum,
        grad_down_sum,
    )
    grad_kv = jnp.transpose(
        summed_att[:, :, : 2 * part].reshape(2, share, 2, part), (1, 2, 0, 3)
    ).reshape(share, 2, inner)
    grad_query = jnp.transpose(
        summed_att[:, :, 2 * part : qkv_cols].reshape(2, share, att_count, part), (2, 1, 0, 3)
    ).reshape(att_count, share, inner)
    grad_output = jnp.transpose(
        summed_att[:, :, out_at:].reshape(2, share, att_count, part), (2, 0, 3, 1)
    ).reshape(att_count, inner, share)
    output, grad_input, small_sum = last_sums(
        dunit_one.astype(BF16),
        feed.astype(BF16),
        inputs,
        middle,
        dmiddle,
        gain_one,
        jnp.sum(summed_att[:, :, small_at:out_at], 0),
    )
    output = reorder(output)
    grad_input = reorder(grad_input)

    grads_up = ups_sum.astype(F32).reshape(mlp_count, share, 2, hidden_local)
    grads_down = jnp.swapaxes(downs_sum.astype(F32), 1, 2)
    return (
        output,
        grad_input,
        grad_kv,
        grad_query,
        grad_output,
        small_sum[:, :3],
        small_sum[:, 7],
        grads_up,
        grads_down,
        small_sum[:, 3:7],
        small_sum[:, 8],
    )


def solution(mesh):
    fine = Mesh(mesh.devices.reshape(4, 2, 4, 2, 2), ALL)
    return jax.shard_map(
        on_device,
        mesh=fine,
        in_specs=(
            P(ALL, None),
            P(DP),
            P(DP, None),
            P(DP, None),
            P(DP, None, TP),
            P(None, DP, TP),
            P(None, TP, DP),
            P(DP, None),
            P(DP),
            P(None, DP, None, TP),
            P(None, TP, DP),
            P(DP, None),
            P(DP),
            P(ALL, None),
        ),
        out_specs=(
            P(ALL, None),
            P(ALL, None),
            P(DP, None, TP),
            P(None, DP, TP),
            P(None, TP, DP),
            P(DP, None),
            P(DP),
            P(None, DP, None, TP),
            P(None, TP, DP),
            P(DP, None),
            P(DP),
        ),
        check_vma=False,
    )
```

```python
import functools
import math

import jax
import jax.numpy as jnp
from jax import lax
from jax.experimental import pallas as pl
from jax.experimental.pallas import tpu as pltpu
from jax.sharding import Mesh, PartitionSpec as P

HD = 128
HEADS = 2
CAP = 320
EPSILON = 1e-06
NEGATIVE = -1e30
ROPE_BASE = 10000.0
MESH_ID = pl.DeviceIdType.MESH
MIB = 1024 * 1024
DP = ("y", "xl", "z")
TP = ("xh", "core")
ALL = DP + TP
F32 = jnp.float32
BF16 = jnp.bfloat16


def mod4(place):
    return lax.rem(place + 4, 4)


def neighbour(axis, step):
    size = 4 if axis in ("y", "z") else 2
    return {axis: lax.rem(lax.axis_index(axis) + step + size, size)}


def chip_along(step):
    at = lax.rem(lax.axis_index("xh") * 2 + lax.axis_index("xl") + step + 4, 4)
    return {"xh": lax.div(at, 2), "xl": lax.rem(at, 2)}


def greet(*devices):
    barrier = pltpu.get_barrier_semaphore()
    for device in devices:
        pl.semaphore_signal(barrier, inc=1, device_id=device, device_id_type=MESH_ID)
    pl.semaphore_wait(barrier, len(devices))


def arrived(ref, sem):
    pltpu.make_async_copy(ref, ref, sem).wait()


class Sends:
    def __init__(self):
        self.copies = []

    def __call__(self, src, dst, send_sem, recv_sem, device):
        copy = pltpu.make_async_remote_copy(
            src_ref=src,
            dst_ref=dst,
            send_sem=send_sem,
            recv_sem=recv_sem,
            device_id=device,
            device_id_type=MESH_ID,
        )
        copy.start()
        self.copies.append(copy)

    def finish(self):
        for copy in self.copies:
            copy.wait_send()


def gather_body(
    x_ref, ups_ref, downs_ref, out_ref, up_ref, down_ref,
    loc, xs, xr, s1, r1m, r1p, f1s, f1r, s2, r2m, r2p, f2s, f2r, es, er, ex, ey,
):
    y, xl, z = lax.axis_index("y"), lax.axis_index("xl"), lax.axis_index("z")
    half = x_ref.shape[1] // 2
    quarter = half // 2
    greet(
        neighbour("xl", 1),
        *(neighbour("y", step) for step in (1, 2, 3)),
        *(neighbour("z", step) for step in (1, -1)),
    )
    rings = (("z", "y"), ("y", "z"))
    place = {"y": y, "z": z}
    other = 1 - xl
    both = pl.ds(0, 2)
    sends = Sends()
    send = sends

    def slot(h, first, second, j, start, count):
        yy, zz = (second, first) if h == 0 else (first, second)
        return out_ref.at[zz, j, yy, pl.ds(start, count)]

    own = pltpu.make_async_copy(x_ref.at[xl], out_ref.at[z, xl, y], loc.at[0])
    own.start()
    experts = ((ups_ref, up_ref), (downs_ref, down_ref))
    kept = []
    for n, (shards, expert) in enumerate(experts):
        kept.append(pltpu.make_async_copy(shards.at[y], expert.at[xl, y], loc.at[1 + n]))
        kept[-1].start()
        send(shards.at[y], expert.at[xl, y], ex.at[n, 0], ey.at[n, 0], neighbour("xl", 1))
        for step in (1, 3, 2):
            send(
                shards.at[mod4(y + step)],
                expert.at[xl, y],
                es.at[n, step - 1],
                er.at[n, step - 1],
                neighbour("y", step),
            )
    for h in (0, 1):
        first, second = place[rings[h][0]], place[rings[h][1]]
        src = x_ref.at[xl, pl.ds(h * half, half)]
        dst = slot(h, first, second, xl, h * half, half)
        send(x_ref.at[other, pl.ds(h * half, half)], dst, xs.at[h], xr.at[h], neighbour("xl", 1))
        send(src, dst, s1.at[h, 0, 0], r1m.at[h, 0], neighbour(rings[h][0], 1))
        send(src, dst, s1.at[h, 0, 1], r1p.at[h, 0], neighbour(rings[h][0], -1))
    own.wait()

    def send_second(h, k, first):
        block = slot(h, first, place[rings[h][1]], both, h * half, half)
        send(block, block, s2.at[h, k, 0], r2m.at[h, k], neighbour(rings[h][1], 1))
        send(block, block, s2.at[h, k, 1], r2p.at[h, k], neighbour(rings[h][1], -1))

    for h in (0, 1):
        first, second = place[rings[h][0]], place[rings[h][1]]
        block = slot(h, first, second, other, h * half, half)
        arrived(block, xr.at[h])
        send(block, block, s1.at[h, 1, 0], r1m.at[h, 1], neighbour(rings[h][0], 1))
        send(block, block, s1.at[h, 1, 1], r1p.at[h, 1], neighbour(rings[h][0], -1))
        send_second(h, 0, first)
    for j, jx in ((0, xl), (1, other)):
        for h in (0, 1):
            first, second = place[rings[h][0]], place[rings[h][1]]
            arrived(slot(h, mod4(first - 1), second, jx, h * half, half), r1m.at[h, j])
            block = slot(h, mod4(first - 1), second, jx, h * half, quarter)
            send(block, block, f1s.at[h, j, 0], f1r.at[h, j, 0], neighbour(rings[h][0], 1))
            arrived(slot(h, mod4(first + 1), second, jx, h * half, half), r1p.at[h, j])
            block = slot(h, mod4(first + 1), second, jx, h * half + quarter, quarter)
            send(block, block, f1s.at[h, j, 1], f1r.at[h, j, 1], neighbour(rings[h][0], -1))
    for k, step in ((1, -1), (2, 1)):
        for h in (0, 1):
            send_second(h, k, mod4(place[rings[h][0]] + step))
    for n, (shards, expert) in enumerate(experts):
        for step in (1, 3, 2):
            landed = expert.at[xl, mod4(y - step)]
            arrived(landed, er.at[n, step - 1])
            send(landed, landed, ex.at[n, step], ey.at[n, step], neighbour("xl", 1))
    for h in (0, 1):
        first, second = place[rings[h][0]], place[rings[h][1]]
        for j, jx in ((0, xl), (1, other)):
            for p in (0, 1):
                block = slot(h, mod4(first + 2), second, jx, h * half + p * quarter, quarter)
                arrived(block, f1r.at[h, j, p])
        send_second(h, 3, mod4(first + 2))
    steps = ((0, 0), (1, -1), (2, 1), (3, 2))
    for k, step in steps:
        for h in (0, 1):
            first, second = mod4(place[rings[h][0]] + step), place[rings[h][1]]
            arrived(slot(h, first, mod4(second - 1), both, h * half, half), r2m.at[h, k])
            block = slot(h, first, mod4(second - 1), both, h * half, quarter)
            send(block, block, f2s.at[h, k, 0], f2r.at[h, k, 0], neighbour(rings[h][1], 1))
            arrived(slot(h, first, mod4(second + 1), both, h * half, half), r2p.at[h, k])
            block = slot(h, first, mod4(second + 1), both, h * half + quarter, quarter)
            send(block, block, f2s.at[h, k, 1], f2r.at[h, k, 1], neighbour(rings[h][1], -1))
    for k, step in steps:
        for h in (0, 1):
            first, second = mod4(place[rings[h][0]] + step), place[rings[h][1]]
            for p in (0, 1):
                block = slot(h, first, mod4(second + 2), both, h * half + p * quarter, quarter)
                arrived(block, f2r.at[h, k, p])
    for n, (shards, expert) in enumerate(experts):
        for step in (0, 1, 3, 2):
            arrived(expert.at[other, mod4(y - step)], ey.at[n, step])
        kept[n].wait()
    sends.finish()


def gather_dp(shard, ups, downs):
    _, rows, cols = shard.shape
    dma = pltpu.SemaphoreType.DMA
    whole, up, down = pl.pallas_call(
        gather_body,
        out_shape=[
            jax.ShapeDtypeStruct((4, 2, 4, rows, cols), shard.dtype),
            jax.ShapeDtypeStruct((2, *ups.shape), ups.dtype),
            jax.ShapeDtypeStruct((2, *downs.shape), downs.dtype),
        ],
        in_specs=[pl.BlockSpec(memory_space=pl.ANY)] * 3,
        out_specs=[pl.BlockSpec(memory_space=pl.ANY)] * 3,
        scratch_shapes=[
            dma((3,)),
            dma((2,)),
            dma((2,)),
            dma((2, 2, 2)),
            dma((2, 2)),
            dma((2, 2)),
            dma((2, 2, 2)),
            dma((2, 2, 2)),
            dma((2, 4, 2)),
            dma((2, 4)),
            dma((2, 4)),
            dma((2, 4, 2)),
            dma((2, 4, 2)),
            dma((2, 3)),
            dma((2, 3)),
            dma((2, 4)),
            dma((2, 4)),
        ],
        compiler_params=pltpu.CompilerParams(collective_id=0, has_side_effects=True),
        name="gather_weights",
    )(shard, ups, downs)
    return whole.reshape(32 * rows, cols), up, down


def reduce_stages(scatter_count, part_refs, core_buf, sum_buf, far_buf, core_s, core_r, far_s, far_r, sends):
    xh, core = lax.axis_index("xh"), lax.axis_index("core")
    rows = part_refs[0].shape[1]
    step = rows // scatter_count
    far, here = 1 - xh, xh
    for n, chunk in enumerate(range(0, rows, step)):
        at = pl.ds(chunk, step)
        for i, part in enumerate(part_refs):
            sends(
                part.at[far * 2 + 1 - core, at],
                core_buf.at[i, 0, at],
                core_s.at[i, n, 0],
                core_r.at[i, n, 0],
                neighbour("core", 1),
            )
    for n, chunk in enumerate(range(0, rows, step)):
        at = pl.ds(chunk, step)
        for i, part in enumerate(part_refs):
            sends(
                part.at[here * 2 + 1 - core, at],
                core_buf.at[i, 1, at],
                core_s.at[i, n, 1],
                core_r.at[i, n, 1],
                neighbour("core", 1),
            )
    yield
    for n, chunk in enumerate(range(0, rows, step)):
        at = pl.ds(chunk, step)
        for i, part in enumerate(part_refs):
            arrived(core_buf.at[i, 0, at], core_r.at[i, n, 0])
            mine = part[far * 2 + core, chunk : chunk + step, :].astype(F32)
            sum_buf[i, chunk : chunk + step, :] = (
                mine + core_buf[i, 0, chunk : chunk + step, :].astype(F32)
            ).astype(BF16)
            sends(
                sum_buf.at[i, at],
                far_buf.at[i, at],
                far_s.at[i, n],
                far_r.at[i, n],
                neighbour("xh", 1),
            )
    yield

    def total(i, n):
        chunk = n * step
        at = pl.ds(chunk, step)
        arrived(core_buf.at[i, 1, at], core_r.at[i, n, 1])
        near = part_refs[i][here * 2 + core, chunk : chunk + step, :].astype(F32)
        near = near + core_buf[i, 1, chunk : chunk + step, :].astype(F32)
        arrived(far_buf.at[i, at], far_r.at[i, n])
        return near + far_buf[i, chunk : chunk + step, :].astype(F32)

    yield total


def ring_reduce_stages(part_ref, core_buf, sum_buf, via_buf, far_buf, core_s, core_r, ring_s, ring_r, sends):
    xl, xh, core = lax.axis_index("xl"), lax.axis_index("xh"), lax.axis_index("core")
    rows = part_ref.shape[3]
    half = rows // 2
    at = xh * 2 + xl
    chips = [lax.rem(at + step, 4) for step in (2, 1, 3, 0)]
    chips = [(lax.rem(chip, 2), lax.div(chip, 2)) for chip in chips]
    for n, (pxl, pxh) in enumerate(chips):
        sends(
            part_ref.at[pxl, pxh, 1 - core],
            core_buf.at[n],
            core_s.at[n],
            core_r.at[n],
            neighbour("core", 1),
        )

    def own(n, start):
        pxl, pxh = chips[n]
        return part_ref[pxl, pxh, core, start : start + half, :].astype(F32)

    def both(n, start):
        return own(n, start) + core_buf[n, start : start + half, :].astype(F32)

    first, second = pl.ds(0, half), pl.ds(half, half)
    ahead, behind = chip_along(1), chip_along(-1)
    yield
    arrived(core_buf.at[0], core_r.at[0])
    sum_buf[0, :half, :] = both(0, 0).astype(BF16)
    sends(sum_buf.at[0, first], via_buf.at[0], ring_s.at[0], ring_r.at[0], ahead)
    sum_buf[0, half:, :] = both(0, half).astype(BF16)
    sends(sum_buf.at[0, second], via_buf.at[1], ring_s.at[1], ring_r.at[1], behind)
    arrived(core_buf.at[1], core_r.at[1])
    sum_buf[1, half:, :] = both(1, half).astype(BF16)
    sends(sum_buf.at[1, second], far_buf.at[0, second], ring_s.at[2], ring_r.at[2], ahead)
    arrived(core_buf.at[2], core_r.at[2])
    sum_buf[2, :half, :] = both(2, 0).astype(BF16)
    sends(sum_buf.at[2, first], far_buf.at[1, first], ring_s.at[3], ring_r.at[3], behind)
    yield
    arrived(via_buf.at[0], ring_r.at[0])
    sum_buf[1, :half, :] = (both(1, 0) + via_buf[0].astype(F32)).astype(BF16)
    sends(sum_buf.at[1, first], far_buf.at[0, first], ring_s.at[4], ring_r.at[4], ahead)
    arrived(via_buf.at[1], ring_r.at[1])
    sum_buf[2, half:, :] = (both(2, half) + via_buf[1].astype(F32)).astype(BF16)
    sends(sum_buf.at[2, second], far_buf.at[1, second], ring_s.at[5], ring_r.at[5], behind)
    arrived(core_buf.at[3], core_r.at[3])

    def total(part):
        rows_at = first if part == 0 else second
        start = part * half
        near = both(3, start)
        arrived(far_buf.at[0, rows_at], ring_r.at[4 if part == 0 else 2])
        near = near + far_buf[0, start : start + half, :].astype(F32)
        arrived(far_buf.at[1, rows_at], ring_r.at[3 if part == 0 else 5])
        return near + far_buf[1, start : start + half, :].astype(F32)

    yield total


def ring_reduce_scratch(rows, width):
    dma = pltpu.SemaphoreType.DMA
    return [
        pltpu.VMEM((4, rows, width), BF16),
        pltpu.VMEM((3, rows, width), BF16),
        pltpu.VMEM((2, rows // 2, width), BF16),
        pltpu.VMEM((2, rows, width), BF16),
        dma((4,)),
        dma((4,)),
        dma((6,)),
        dma((6,)),
    ]


def ring_spread(out_ref, part, ring_s, ring_r, core_s, core_r, sends):
    xl, xh, core = lax.axis_index("xl"), lax.axis_index("xh"), lax.axis_index("core")
    half = out_ref.shape[3] // 2
    mine = out_ref.at[xl, xh, core, pl.ds(part * half, half)]
    sends(mine, mine, ring_s.at[part, 0], ring_r.at[part, 0], chip_along(1))
    sends(mine, mine, ring_s.at[part, 1], ring_r.at[part, 1], chip_along(-1))
    sends(mine, mine, core_s.at[part, 0], core_r.at[part, 0], neighbour("core", 1))


def ring_spread_finish(out_ref, ring_s, ring_r, core_s, core_r, sends):
    xl, xh, core = lax.axis_index("xl"), lax.axis_index("xh"), lax.axis_index("core")
    half = out_ref.shape[3] // 2
    at = xh * 2 + xl

    def block(step, part, which):
        chip = lax.rem(at + step + 4, 4)
        return out_ref.at[lax.rem(chip, 2), lax.div(chip, 2), which, pl.ds(part * half, half)]

    for part in (0, 1):
        for n, (step, on) in enumerate(((-1, 1), (1, -1))):
            landed = block(step, part, core)
            arrived(landed, ring_r.at[part, n])
            if part == n:
                sends(landed, landed, ring_s.at[part, 2], ring_r.at[part, 2], chip_along(on))
            sends(landed, landed, core_s.at[part, 1 + n], core_r.at[part, 1 + n], neighbour("core", 1))
    for part in (0, 1):
        landed = block(2, part, core)
        arrived(landed, ring_r.at[part, 2])
        sends(landed, landed, core_s.at[part, 3], core_r.at[part, 3], neighbour("core", 1))
    for part in (0, 1):
        for n, step in enumerate((0, -1, 1, 2)):
            arrived(block(step, part, 1 - core), core_r.at[part, n])


def ring_spread_scratch():
    dma = pltpu.SemaphoreType.DMA
    return [dma((2, 3)), dma((2, 3)), dma((2, 4)), dma((2, 4))]


def along_x():
    return neighbour("core", 1), neighbour("xh", 1), chip_along(1), chip_along(-1)


CHUNKS = 4


def reduce_scratch(count, rows, width):
    dma = pltpu.SemaphoreType.DMA
    return [
        pltpu.VMEM((count, 2, rows, width), BF16),
        pltpu.VMEM((count, rows, width), BF16),
        pltpu.VMEM((count, rows, width), BF16),
        dma((count, CHUNKS, 2)),
        dma((count, CHUNKS, 2)),
        dma((count, CHUNKS)),
        dma((count, CHUNKS)),
    ]


def spread_chunk(out_ref, n, step, sems, sends):
    xh, core = lax.axis_index("xh"), lax.axis_index("core")
    at = pl.ds(n * step, step)
    mine = out_ref.at[xh * 2 + core, at]
    far_s, far_r, core_s, core_r = sems
    sends(mine, mine, far_s.at[n], far_r.at[n], neighbour("xh", 1))
    sends(mine, mine, core_s.at[n, 0], core_r.at[n, 0], neighbour("core", 1))


def spread_finish(out_ref, step, sems, sends):
    xh, core = lax.axis_index("xh"), lax.axis_index("core")
    far_s, far_r, core_s, core_r = sems
    for n in range(CHUNKS):
        at = pl.ds(n * step, step)
        theirs = out_ref.at[(1 - xh) * 2 + core, at]
        arrived(theirs, far_r.at[n])
        sends(theirs, theirs, core_s.at[n, 1], core_r.at[n, 1], neighbour("core", 1))
    for n in range(CHUNKS):
        at = pl.ds(n * step, step)
        arrived(out_ref.at[xh * 2 + 1 - core, at], core_r.at[n, 0])
        arrived(out_ref.at[(1 - xh) * 2 + 1 - core, at], core_r.at[n, 1])


def spread_scratch():
    dma = pltpu.SemaphoreType.DMA
    return [dma((CHUNKS,)), dma((CHUNKS,)), dma((CHUNKS, 2)), dma((CHUNKS, 2))]


def middle_body(part_ref, x_ref, gain_ref, middle_ref, unit_ref, *scratch):
    sends = Sends()
    greet(*along_x())
    *_, total = ring_reduce_stages(part_ref, *scratch[:8], sends)
    me = lax.axis_index("xh") * 2 + lax.axis_index("core")
    step = x_ref.shape[0] // CHUNKS
    half = x_ref.shape[0] // 2
    for part in (0, 1):
        rows = slice(part * half, (part + 1) * half)
        middle = x_ref[rows, :].astype(F32) + total(part)
        middle_ref[rows, :] = middle
        inverse = lax.rsqrt(jnp.mean(middle * middle, 1, keepdims=True) + EPSILON)
        unit_ref[me, rows, :] = (middle * inverse * gain_ref[...]).astype(BF16)
        for n in range(part * CHUNKS // 2, (part + 1) * CHUNKS // 2):
            spread_chunk(unit_ref, n, step, scratch[8:], sends)
    spread_finish(unit_ref, step, scratch[8:], sends)
    sends.finish()


def vmem(count):
    return [pl.BlockSpec(memory_space=pltpu.VMEM)] * count


def middle_and_unit(part, x, gain):
    rows, width = x.shape
    middle, unit = pl.pallas_call(
        middle_body,
        out_shape=[
            jax.ShapeDtypeStruct((rows, width), F32),
            jax.ShapeDtypeStruct((4, rows, width), BF16),
        ],
        in_specs=vmem(3),
        out_specs=vmem(2),
        scratch_shapes=ring_reduce_scratch(rows, width) + spread_scratch(),
        compiler_params=pltpu.CompilerParams(
            collective_id=1, has_side_effects=True, vmem_limit_bytes=32 * MIB
        ),
        name="middle_and_unit",
    )(part.reshape(2, 2, 2, rows, width), x, gain[None])
    return middle, unit.reshape(4 * rows, width)


def back_body(part_ref, middle_ref, grad_ref, gain_ref, dmiddle_ref, dgain_ref, spread_ref, *scratch):
    sends = Sends()
    greet(*along_x())
    *_, total = reduce_stages(CHUNKS, [part_ref], *scratch[:7], sends)
    xl, xh, core = lax.axis_index("xl"), lax.axis_index("xh"), lax.axis_index("core")
    step = middle_ref.shape[0] // CHUNKS
    for n in range(CHUNKS):
        rows = slice(n * step, (n + 1) * step)
        middle = middle_ref[rows, :]
        inverse = lax.rsqrt(jnp.mean(middle * middle, 1, keepdims=True) + EPSILON)
        normed = middle * inverse
        dunit = total(0, n)
        product = dunit * normed
        dgain = jnp.sum(product, 0, keepdims=True)
        if n == 0:
            dgain_ref[...] = dgain
        else:
            dgain_ref[...] += dgain
        mean = jnp.mean(product * gain_ref[...], 1, keepdims=True)
        dmiddle = grad_ref[rows, :].astype(F32) + inverse * (dunit * gain_ref[...] - normed * mean)
        dmiddle_ref[rows, :] = dmiddle
        spread_ref[xl, xh, core, rows, :] = dmiddle.astype(BF16)
        if n % 2 == 1:
            ring_spread(spread_ref, n // 2, *scratch[7:], sends)
    ring_spread_finish(spread_ref, *scratch[7:], sends)
    sends.finish()


def middle_back(part, middle, grad, gain):
    rows, width = middle.shape
    dmiddle, dgain, spread = pl.pallas_call(
        back_body,
        out_shape=[
            jax.ShapeDtypeStruct((rows, width), F32),
            jax.ShapeDtypeStruct((1, width), F32),
            jax.ShapeDtypeStruct((2, 2, 2, rows, width), BF16),
        ],
        in_specs=vmem(4),
        out_specs=vmem(3),
        scratch_shapes=reduce_scratch(1, rows, width) + ring_spread_scratch(),
        compiler_params=pltpu.CompilerParams(
            collective_id=2, has_side_effects=True, vmem_limit_bytes=32 * MIB
        ),
        name="middle_back",
    )(part.reshape(4, rows, width), middle, grad, gain[None])
    return dmiddle, dgain[0], spread.reshape(8 * rows, width)


def rows_body(rows_ref, out_ref, loc, far_s, far_r, core_s, core_r):
    y, core = lax.axis_index("y"), lax.axis_index("core")
    half = rows_ref.shape[1] // 2
    sends = Sends()
    greet(neighbour("core", 1), *(neighbour("y", step) for step in (1, 2, 3)))
    at = pl.ds(pl.multiple_of(core * half, half), half)
    own = pltpu.make_async_copy(rows_ref.at[y], out_ref.at[y], loc)
    own.start()
    for step in (2, 1, 3):
        target = mod4(y + step)
        sends(
            rows_ref.at[target, at],
            out_ref.at[y, at],
            far_s.at[step - 1],
            far_r.at[step - 1],
            neighbour("y", step),
        )
    for step in (1, 3, 2):
        source = mod4(y - step)
        block = out_ref.at[source, at]
        arrived(block, far_r.at[step - 1])
        sends(block, block, core_s.at[step - 1], core_r.at[step - 1], neighbour("core", 1))
    own.wait()
    other = pl.ds(pl.multiple_of((1 - core) * half, half), half)
    for step in (1, 3, 2):
        arrived(out_ref.at[mod4(y - step), other], core_r.at[step - 1])
    sends.finish()


def rows_to_experts(rows):
    dma = pltpu.SemaphoreType.DMA
    return pl.pallas_call(
        rows_body,
        out_shape=jax.ShapeDtypeStruct(rows.shape, rows.dtype),
        in_specs=[pl.BlockSpec(memory_space=pl.ANY)],
        out_specs=pl.BlockSpec(memory_space=pl.ANY),
        scratch_shapes=[dma, dma((3,)), dma((3,)), dma((3,)), dma((3,))],
        compiler_params=pltpu.CompilerParams(collective_id=4, has_side_effects=True),
        name="rows_to_experts",
    )(rows)


STEPS = (2, 1, -1, 0)


def finish_body(
    qkv_ref, small_ref, o_ref, ups_ref, downs_ref, part_ref, feed_ref, x_ref, middle_ref, dmiddle_ref, gain_ref,
    out_ref, up_out, down_out, output_ref, dinput_ref, small_out,
    g_ref, loc, t_buf, r_buf, tb_buf, rb_buf, c_buf,
    t_s, t_r, r_s, r_r, tb_s, tb_r, rb_s, rb_r, c_s, c_r,
    up_own, down_own, up_buf, down_buf, up_sum, down_sum, ex, ey, es, er,
    small_own, small_buf, small_s, small_r, *scratch,
):
    xl, xh, core = lax.axis_index("xl"), lax.axis_index("xh"), lax.axis_index("core")
    place = {"y": lax.axis_index("y"), "z": lax.axis_index("z")}
    my_y = place["y"]
    half = g_ref.shape[3] // 2
    quarter = half // 2
    rings = (("z", "y"), ("y", "z"))
    sends = Sends()
    column = 0
    parts = []
    for n, ref in enumerate((qkv_ref, small_ref, o_ref)):
        cols = ref.shape[-1]
        parts.append(pltpu.make_async_copy(ref, g_ref.at[..., pl.ds(column, cols)], loc.at[n]))
        parts[-1].start()
        column += cols
    for n, (ref, own) in enumerate(((ups_ref, up_own), (downs_ref, down_own))):
        parts.append(pltpu.make_async_copy(ref.at[xl], own, loc.at[3 + n]))
        parts[-1].start()
    peers = ({"xh": xh, "core": 1 - core}, {"xh": 1 - xh, "core": core}, {"xh": 1 - xh, "core": 1 - core})
    greet(
        *peers,
        chip_along(1),
        chip_along(-1),
        *(neighbour("y", step) for step in (1, 2, 3)),
        *(neighbour("z", step) for step in (1, -1)),
    )
    both = slice(0, 2)
    ring_stages = ring_reduce_stages(part_ref, *scratch[7:15], sends)
    feed_stages = reduce_stages(CHUNKS, [feed_ref], *scratch[:7], sends)
    experts = ((ups_ref, up_own, up_buf, up_sum, up_out), (downs_ref, down_own, down_buf, down_sum, down_out))
    for n, (grads, _, buf, _, _) in enumerate(experts):
        for step in (2, 1, 3, 0):
            sends(
                grads.at[1 - xl, mod4(my_y + step)],
                buf.at[step],
                ex.at[n, step],
                ey.at[n, step],
                neighbour("xl", 1),
            )
    next(ring_stages)
    next(feed_stages)
    for part in parts[:3]:
        part.wait()

    def grad_ref(h, first, second, start):
        zz, yy = (first, second) if h == 0 else (second, first)
        return g_ref.at[zz, both, yy, pl.ds(h * half + start, quarter)]

    def grad(h, first, second, j, start, count):
        zz, yy = (first, second) if h == 0 else (second, first)
        return g_ref[zz, j, yy, h * half + start : h * half + start + count, :].astype(F32)

    def firsts(h, k):
        return mod4(place[rings[h][0]] + STEPS[k])

    for k in range(4):
        for h in (0, 1):
            second = place[rings[h][1]]
            for d, way in ((0, 1), (1, -1)):
                sends(
                    grad_ref(h, firsts(h, k), mod4(second + 2), d * quarter),
                    t_buf.at[h, d, k],
                    t_s.at[h, d, k],
                    t_r.at[h, d, k],
                    neighbour(rings[h][1], way),
                )
    for k in range(4):
        for h in (0, 1):
            second = place[rings[h][1]]
            for d, way in ((0, 1), (1, -1)):
                sends(
                    grad_ref(h, firsts(h, k), mod4(second + way), (1 - d) * quarter),
                    r_buf.at[h, d, k, both, pl.ds((1 - d) * quarter, quarter)],
                    r_s.at[h, d, k, 0],
                    r_r.at[h, d, k, 0],
                    neighbour(rings[h][1], way),
                )
    next(ring_stages)
    next(feed_stages)
    for k in range(4):
        for h in (0, 1):
            second = place[rings[h][1]]
            for d, way in ((0, 1), (1, -1)):
                arrived(t_buf.at[h, d, k], t_r.at[h, d, k])
                for j in (0, 1):
                    t_buf[h, d, k, j] = (
                        t_buf[h, d, k, j].astype(F32)
                        + grad(h, firsts(h, k), mod4(second + way), j, d * quarter, quarter)
                    ).astype(BF16)
                sends(
                    t_buf.at[h, d, k],
                    r_buf.at[h, d, k, both, pl.ds(d * quarter, quarter)],
                    r_s.at[h, d, k, 1],
                    r_r.at[h, d, k, 1],
                    neighbour(rings[h][1], way),
                )
    total = next(ring_stages)
    for part in parts[3:]:
        part.wait()
    for n, (_, own, buf, summed, result) in enumerate(experts):
        for step in (2, 1, 3, 0):
            target = mod4(my_y + step)
            arrived(buf.at[step], ey.at[n, step])
            value = (own[target].astype(F32) + buf[step].astype(F32)).astype(BF16)
            if step == 0:
                result[my_y] = value
            else:
                summed[step - 1] = value
                sends(
                    summed.at[step - 1],
                    result.at[my_y],
                    es.at[n, step - 1],
                    er.at[n, step - 1],
                    neighbour("y", step),
                )
    for k in range(4):
        for h in (0, 1):
            second = place[rings[h][1]]
            for d in (0, 1):
                arrived(r_buf.at[h, d, k, both, pl.ds((1 - d) * quarter, quarter)], r_r.at[h, d, k, 0])
                arrived(r_buf.at[h, d, k, both, pl.ds(d * quarter, quarter)], r_r.at[h, d, k, 1])
            for j in (0, 1):
                r_buf[h, 0, k, j] = (
                    r_buf[h, 0, k, j].astype(F32)
                    + r_buf[h, 1, k, j].astype(F32)
                    + grad(h, firsts(h, k), second, j, 0, half)
                ).astype(BF16)
            for d, way in ((0, 1), (1, -1)):
                device = neighbour(rings[h][0], way)
                if k == 0:
                    sends(
                        r_buf.at[h, 0, 0, both, pl.ds(d * quarter, quarter)],
                        tb_buf.at[h, d],
                        tb_s.at[h, d],
                        tb_r.at[h, d],
                        device,
                    )
                if k == 1 + d:
                    sends(
                        r_buf.at[h, 0, k, both, pl.ds((1 - d) * quarter, quarter)],
                        rb_buf.at[h, d, both, pl.ds((1 - d) * quarter, quarter)],
                        rb_s.at[h, d, 0],
                        rb_r.at[h, d, 0],
                        device,
                    )
                    arrived(tb_buf.at[h, d], tb_r.at[h, d])
                    for j in (0, 1):
                        tb_buf[h, d, j] = (
                            tb_buf[h, d, j].astype(F32)
                            + r_buf[h, 0, k, j, d * quarter : (d + 1) * quarter, :].astype(F32)
                        ).astype(BF16)
                    sends(
                        tb_buf.at[h, d],
                        rb_buf.at[h, d, both, pl.ds(d * quarter, quarter)],
                        rb_s.at[h, d, 1],
                        rb_r.at[h, d, 1],
                        device,
                    )
    rows_half = x_ref.shape[0] // 2
    for part in (0, 1):
        rows = slice(part * rows_half, (part + 1) * rows_half)
        x = x_ref[rows, :].astype(F32)
        inverse = lax.rsqrt(jnp.mean(x * x, 1, keepdims=True) + EPSILON)
        normed = x * inverse
        dscaled = total(part) * gain_ref[...]
        mean = jnp.mean(dscaled * normed, 1, keepdims=True)
        dinput_ref[rows, :] = dmiddle_ref[rows, :] + inverse * (dscaled - normed * mean)
    for h in (0, 1):
        for d in (0, 1):
            arrived(rb_buf.at[h, d, both, pl.ds((1 - d) * quarter, quarter)], rb_r.at[h, d, 0])
            arrived(rb_buf.at[h, d, both, pl.ds(d * quarter, quarter)], rb_r.at[h, d, 1])
        for j in (0, 1):
            rb_buf[h, 0, j] = (
                rb_buf[h, 0, j].astype(F32)
                + rb_buf[h, 1, j].astype(F32)
                + r_buf[h, 0, 3, j].astype(F32)
            ).astype(BF16)
        sends(rb_buf.at[h, 0, 1 - xl], c_buf.at[h], c_s.at[h], c_r.at[h], neighbour("xl", 1))
        out_ref[xl, h * half : (h + 1) * half, :] = rb_buf[h, 0, xl].astype(F32)
    for h in (0, 1):
        arrived(c_buf.at[h], c_r.at[h])
        out_ref[1 - xl, h * half : (h + 1) * half, :] = c_buf[h].astype(F32)
    first, last = qkv_ref.shape[-1], qkv_ref.shape[-1] + small_ref.shape[-1]
    small_own[...] = out_ref[0, :, first:last] + out_ref[1, :, first:last]
    for n, peer in enumerate(peers):
        sends(small_own, small_buf.at[n], small_s.at[n], small_r.at[n], peer)
    feed = next(feed_stages)
    step = x_ref.shape[0] // CHUNKS
    for n in range(CHUNKS):
        rows = slice(n * step, (n + 1) * step)
        output_ref[rows, :] = (middle_ref[rows, :] + feed(0, n)).astype(BF16)
    for n, (_, _, _, _, result) in enumerate(experts):
        for step in (1, 3, 2):
            arrived(result.at[mod4(my_y - step)], er.at[n, step - 1])
    for n in range(3):
        arrived(small_buf.at[n], small_r.at[n])
    small_out[...] = (small_own[...] + small_buf[1]) + (small_buf[0] + small_buf[2])
    sends.finish()


def finish(grads, ups, downs, part, feed, x, middle, dmiddle, gain):
    rows, cols = grads[0].shape[0], sum(grad.shape[1] for grad in grads)
    share = rows // 32
    half, quarter = share // 2, share // 4
    dma = pltpu.SemaphoreType.DMA
    up_cols, down_cols = ups.shape[1], downs.shape[1]
    small = (share, grads[1].shape[1])
    own_rows, width = x.shape
    anywhere = pl.BlockSpec(memory_space=pl.ANY)
    return pl.pallas_call(
        finish_body,
        out_shape=[
            jax.ShapeDtypeStruct((2, share, cols), F32),
            jax.ShapeDtypeStruct((4, share, up_cols), BF16),
            jax.ShapeDtypeStruct((4, share, down_cols), BF16),
            jax.ShapeDtypeStruct((own_rows, width), BF16),
            jax.ShapeDtypeStruct((own_rows, width), F32),
            jax.ShapeDtypeStruct(small, F32),
        ],
        in_specs=[anywhere] * 5 + vmem(6),
        out_specs=vmem(6),
        scratch_shapes=[
            pltpu.VMEM((4, 2, 4, share, cols), BF16),
            dma((5,)),
            pltpu.VMEM((2, 2, 4, 2, quarter, cols), BF16),
            pltpu.VMEM((2, 2, 4, 2, half, cols), BF16),
            pltpu.VMEM((2, 2, 2, quarter, cols), BF16),
            pltpu.VMEM((2, 2, 2, half, cols), BF16),
            pltpu.VMEM((2, half, cols), BF16),
            dma((2, 2, 4)),
            dma((2, 2, 4)),
            dma((2, 2, 4, 2)),
            dma((2, 2, 4, 2)),
            dma((2, 2)),
            dma((2, 2)),
            dma((2, 2, 2)),
            dma((2, 2, 2)),
            dma((2,)),
            dma((2,)),
            pltpu.VMEM((4, share, up_cols), BF16),
            pltpu.VMEM((4, share, down_cols), BF16),
            pltpu.VMEM((4, share, up_cols), BF16),
            pltpu.VMEM((4, share, down_cols), BF16),
            pltpu.VMEM((3, share, up_cols), BF16),
            pltpu.VMEM((3, share, down_cols), BF16),
            dma((2, 4)),
            dma((2, 4)),
            dma((2, 3)),
            dma((2, 3)),
            pltpu.VMEM(small, F32),
            pltpu.VMEM((3, *small), F32),
            dma((3,)),
            dma((3,)),
        ]
        + reduce_scratch(1, own_rows, width)
        + ring_reduce_scratch(own_rows, width),
        compiler_params=pltpu.CompilerParams(
            collective_id=5, has_side_effects=True, vmem_limit_bytes=60 * MIB
        ),
        name="finish",
    )(
        *(grad.reshape(4, 2, 4, share, grad.shape[1]) for grad in grads),
        ups.reshape(2, 4, share, up_cols),
        downs.reshape(2, 4, share, down_cols),
        part.reshape(2, 2, 2, own_rows, width),
        feed.reshape(4, own_rows, width),
        x,
        middle,
        dmiddle,
        gain[None],
    )


def dot(a, b, dims):
    return lax.dot_general(a, b, (dims, ((), ())), preferred_element_type=F32)


LANES = 128
WIDE = 256


def experts_body(
    rows_ref, grad_ref, up_ref, down_ref, gate_ref, up_rows_ref,
    djoined_out, hidden_out, gated_out, dgate_out, dunit_out, raw, djoined,
):
    j = pl.program_id(0)
    chunks = djoined.shape[1] // WIDE

    @pl.when(j == 0)
    def _():
        dgate_out[...] = jnp.zeros_like(dgate_out)

    @pl.when((j < chunks) & (lax.rem(j, 2) == 0))
    def _():
        pair = dot(grad_ref[...], down_ref[...], ((1,), (0,)))
        raw[0] = pair[:, :LANES]
        raw[1] = pair[:, LANES:]

    @pl.when(j < chunks)
    def _():
        joined = dot(rows_ref[...], up_ref[...], ((1,), (0,)))
        gate_pre, linear = joined[:, :LANES], joined[:, LANES:]
        sigmoid = jax.nn.sigmoid(gate_pre)
        silu = gate_pre * sigmoid
        hidden = silu * linear
        dhidden = raw[lax.rem(j, 2)]
        gate = gate_ref[...]
        dgate_out[...] += hidden * dhidden
        dhidden = dhidden * gate
        hidden_out[...] = hidden.astype(BF16)
        gated_out[...] = (hidden * gate).astype(BF16)
        dgate_pre = (dhidden * linear * (sigmoid + silu * (1.0 - sigmoid))).astype(BF16)
        dlinear = (dhidden * silu).astype(BF16)
        djoined_out[:, :LANES] = dgate_pre
        djoined_out[:, LANES:] = dlinear
        at = pl.multiple_of(j * WIDE, WIDE)
        djoined[:, pl.ds(at, LANES)] = dgate_pre
        djoined[:, pl.ds(at + LANES, LANES)] = dlinear

    @pl.when(j >= chunks)
    def _():
        dunit_out[...] = dot(djoined[...], up_rows_ref[...], ((1,), (1,))).astype(BF16)


def experts(rows, grads, up, down, gates):
    count, width = grads.shape
    hidden = down.shape[1]
    chunks = hidden // LANES
    steps = chunks + width // WIDE

    def chunk(j):
        return jnp.minimum(j, chunks - 1)

    def tail(j):
        return jnp.maximum(j - chunks, 0)

    return pl.pallas_call(
        experts_body,
        grid=(steps,),
        in_specs=[
            pl.BlockSpec((count, width), lambda j: (0, 0)),
            pl.BlockSpec((count, width), lambda j: (0, 0)),
            pl.BlockSpec((width, WIDE), lambda j: (0, chunk(j))),
            pl.BlockSpec((width, WIDE), lambda j: (0, chunk(j) // 2)),
            pl.BlockSpec((count, 1), lambda j: (0, 0)),
            pl.BlockSpec((WIDE, 2 * hidden), lambda j: (tail(j), 0)),
        ],
        out_specs=[
            pl.BlockSpec((count, WIDE), lambda j: (0, chunk(j))),
            pl.BlockSpec((count, LANES), lambda j: (0, chunk(j))),
            pl.BlockSpec((count, LANES), lambda j: (0, chunk(j))),
            pl.BlockSpec((count, LANES), lambda j: (0, 0)),
            pl.BlockSpec((count, WIDE), lambda j: (0, tail(j))),
        ],
        out_shape=[
            jax.ShapeDtypeStruct((count, 2 * hidden), BF16),
            jax.ShapeDtypeStruct((count, hidden), BF16),
            jax.ShapeDtypeStruct((count, hidden), BF16),
            jax.ShapeDtypeStruct((count, LANES), F32),
            jax.ShapeDtypeStruct((count, width), BF16),
        ],
        scratch_shapes=[
            pltpu.VMEM((2, count, LANES), F32),
            pltpu.VMEM((count, 2 * hidden), BF16),
        ],
        compiler_params=pltpu.CompilerParams(vmem_limit_bytes=60 * MIB),
        name="experts",
    )(rows, grads, up, down, gates, up)


def return_body(
    dunit_ref, dgate_ref, rows_ref, djoined_ref, hidden_ref, down_ref,
    dunit_out, dgate_out, up_out, branch_out,
    dunit_own, dgate_own, rows, djoined, hidden, down, dunit_buf, dgate_buf, dunit_sum, dgate_sum, block,
    loc, core_s, core_r, far_s, far_r, out_sem,
):
    y, core = lax.axis_index("y"), lax.axis_index("core")
    half = dunit_ref.shape[1] // 2
    sends = Sends()
    greet(neighbour("core", 1), *(neighbour("y", step) for step in (1, 2, 3)))
    mine = pl.ds(pl.multiple_of(core * half, half), half)
    theirs = pl.ds(pl.multiple_of((1 - core) * half, half), half)
    order = (2, 1, 3, 0)
    kinds = (
        (dunit_ref, dunit_own, dunit_buf, dunit_sum, dunit_out),
        (dgate_ref, dgate_own, dgate_buf, dgate_sum, dgate_out),
    )
    for step in order:
        for n, (whole, _, buf, _, _) in enumerate(kinds):
            sends(
                whole.at[mod4(y + step), theirs],
                buf.at[step],
                core_s.at[n, step],
                core_r.at[n, step],
                neighbour("core", 1),
            )
    own = []
    for step in order:
        for n, (whole, kept, _, _, _) in enumerate(kinds):
            copy = pltpu.make_async_copy(whole.at[mod4(y + step), mine], kept.at[step], loc.at[n, step])
            copy.start()
            own.append(copy)
    loads = []
    for n, (src, dst) in enumerate(
        ((rows_ref.at[:, pl.ds(0, rows.shape[1])], rows), (djoined_ref, djoined), (hidden_ref, hidden), (down_ref, down))
    ):
        loads.append(pltpu.make_async_copy(src, dst, loc.at[2, n]))
        loads[-1].start()
    for copy in own:
        copy.wait()
    for step in order:
        for n, (_, kept, buf, summed, result) in enumerate(kinds):
            arrived(buf.at[step], core_r.at[n, step])
            value = (kept[step].astype(F32) + buf[step].astype(F32)).astype(summed.dtype)
            if step == 0:
                result[y] = value
            else:
                summed[step - 1] = value
                sends(
                    summed.at[step - 1],
                    result.at[y],
                    far_s.at[n, step - 1],
                    far_r.at[n, step - 1],
                    neighbour("y", step),
                )
    for load in loads:
        load.wait()
    blocks = up_out.shape[0] // WIDE

    @pl.loop(0, blocks)
    def _(j):
        at = pl.ds(pl.multiple_of(j * WIDE, WIDE), WIDE)
        slot = lax.rem(j, 2)

        @pl.when(j >= 2)
        def _():
            pltpu.make_async_copy(block.at[slot], up_out.at[at], out_sem.at[slot]).wait()

        block[slot] = dot(rows[:, at], djoined[...], ((0,), (0,))).astype(BF16)
        pltpu.make_async_copy(block.at[slot], up_out.at[at], out_sem.at[slot]).start()

    @pl.loop(0, blocks)
    def _(j):
        at = pl.ds(pl.multiple_of(j * WIDE, WIDE), WIDE)
        branch_out[:, at] = dot(hidden[...], down[at, :], ((1,), (1,))).astype(BF16)

    for slot in (0, 1):
        pltpu.make_async_copy(block.at[slot], up_out.at[pl.ds(0, WIDE)], out_sem.at[slot]).wait()
    for n, (_, _, _, _, result) in enumerate(kinds):
        for step in (1, 3, 2):
            arrived(result.at[mod4(y - step)], far_r.at[n, step - 1])
    sends.finish()


def return_rows(dunit, dgate, rows, djoined, hidden, down):
    _, slots, width = dunit.shape
    half = slots // 2
    count, wide = djoined.shape
    hidden_cols = hidden.shape[1]
    dma = pltpu.SemaphoreType.DMA
    anywhere = pl.BlockSpec(memory_space=pl.ANY)

    def pair(places):
        return [
            pltpu.VMEM((places, half, width), BF16),
            pltpu.VMEM((places, half, dgate.shape[2]), F32),
        ]

    return pl.pallas_call(
        return_body,
        out_shape=[
            jax.ShapeDtypeStruct((4, half, width), BF16),
            jax.ShapeDtypeStruct((4, half, dgate.shape[2]), F32),
            jax.ShapeDtypeStruct((width, wide), BF16),
            jax.ShapeDtypeStruct((count, width), BF16),
        ],
        in_specs=[anywhere] * 6,
        out_specs=vmem(2) + [anywhere] + vmem(1),
        scratch_shapes=pair(4)
        + [
            pltpu.VMEM((count, width), BF16),
            pltpu.VMEM((count, wide), BF16),
            pltpu.VMEM((count, hidden_cols), BF16),
            pltpu.VMEM((width, hidden_cols), BF16),
        ]
        + pair(4)
        + pair(3)
        + [
            pltpu.VMEM((2, WIDE, wide), BF16),
            dma((3, 4)),
            dma((2, 4)),
            dma((2, 4)),
            dma((2, 3)),
            dma((2, 3)),
            dma((2,)),
        ],
        compiler_params=pltpu.CompilerParams(
            collective_id=3, has_side_effects=True, vmem_limit_bytes=62 * MIB
        ),
        name="return_rows",
    )(dunit, dgate, rows, djoined, hidden, down)


def attention_body(
    k_ref, v_ref, q0, q1, q2, cos_ref, sin_ref, col_ref, row_ref, gate_ref,
    key_out, val_out, que_out, mix_out, gmix_out, prob_out,
):
    h = pl.program_id(1)
    cosine, sine = cos_ref[...], sin_ref[...]
    scale = 1.0 / math.sqrt(HD)

    def rotated(v):
        return v * cosine + pltpu.roll(v, HD // 2, 1) * sine

    key = rotated(k_ref[...]).astype(BF16)
    val = v_ref[...].astype(BF16)
    key_out[...] = key
    val_out[...] = val
    tokens = key.shape[0]
    seg_col, seg_row = col_ref[...], row_ref[0]
    at_row = lax.broadcasted_iota(jnp.int32, (tokens, tokens), 0)
    at_col = lax.broadcasted_iota(jnp.int32, (tokens, tokens), 1)
    allowed = (at_col <= at_row) & ((seg_row == 0) | (seg_row == seg_col))
    for e, q_ref in enumerate((q0, q1, q2)):
        query = (rotated(q_ref[...]) * scale).astype(BF16)
        scores = jnp.where(allowed, dot(query, key, ((1,), (1,))), NEGATIVE)
        largest = jnp.max(scores, 1, keepdims=True)
        expsum = jnp.exp(scores - largest)
        prob = (expsum * (1.0 / jnp.sum(expsum, 1, keepdims=True))).astype(BF16)
        prob_out[0, 0, e] = prob
        mixed = dot(prob, val, ((1,), (0,))).astype(BF16)
        at = pl.ds(pl.multiple_of((e * HEADS + h) * HD, HD), HD)
        que_out[:, at] = query
        mix_out[:, at] = mixed
        gmix_out[:, at] = (mixed.astype(F32) * gate_ref[:, e : e + 1]).astype(BF16)


def block_specs(tokens):
    def column(n):
        return pl.BlockSpec((tokens, HD), lambda g, h: (g, n * HEADS + h))

    def rows(width):
        return pl.BlockSpec((tokens, width), lambda g, h: (g, 0))

    return column, rows


def prob_spec(tokens):
    return pl.BlockSpec((1, 1, 3, tokens, tokens), lambda g, h: (g, h, 0, 0, 0))


def attention_forward(joined, cosine, sine, segments, gates):
    groups, tokens = segments.shape
    column, rows = block_specs(tokens)
    wide = jax.ShapeDtypeStruct((groups * tokens, 3 * HEADS * HD), BF16)
    narrow = jax.ShapeDtypeStruct((groups * tokens, HEADS * HD), BF16)
    return pl.pallas_call(
        attention_body,
        grid=(groups, HEADS),
        in_specs=[column(n) for n in range(5)]
        + [rows(HD)] * 2
        + [rows(1), pl.BlockSpec((1, 1, tokens), lambda g, h: (g, 0, 0)), rows(gates.shape[1])],
        out_specs=[column(0), column(0)] + [rows(wide.shape[1])] * 3 + [prob_spec(tokens)],
        out_shape=[narrow, narrow, wide, wide, wide]
        + [jax.ShapeDtypeStruct((groups, HEADS, 3, tokens, tokens), BF16)],
        compiler_params=pltpu.CompilerParams(vmem_limit_bytes=48 * MIB),
        name="attention_forward",
    )(
        *[joined] * 5, cosine, sine, segments.reshape(-1, 1), segments[:, None], gates
    )


def attention_back_body(
    key_ref, val_ref, q0, q1, q2, m0, m1, m2, h0, h1, h2, prob_ref, cos_ref, sin_ref, gate_ref,
    grad_out, dgate_out,
):
    h = pl.program_id(1)
    cosine, sine = cos_ref[...], sin_ref[...]
    scale = 1.0 / math.sqrt(HD)

    def rotated_back(v):
        return v * cosine - pltpu.roll(v, HD // 2, 1) * sine

    key, val = key_ref[...], val_ref[...]
    tokens = key.shape[0]
    dkey = jnp.zeros((tokens, HD), F32)
    dval = jnp.zeros((tokens, HD), F32)
    lane = lax.broadcasted_iota(jnp.int32, (tokens, HD), 1)
    dgates = jnp.zeros((tokens, HD), F32)
    for e, (q_ref, m_ref, h_ref) in enumerate(((q0, m0, h0), (q1, m1, h1), (q2, m2, h2))):
        query, mixed, raw = q_ref[...], m_ref[...].astype(F32), h_ref[...]
        inner = jnp.sum(mixed * raw, 1, keepdims=True)
        dgates = dgates + jnp.where(lane == e, inner, 0.0)
        gate = gate_ref[:, e : e + 1]
        dmixed = (raw * gate).astype(BF16)
        prob = prob_ref[0, 0, e]
        dval = dval + dot(prob, dmixed, ((0,), (0,)))
        dprob = dot(dmixed, val, ((1,), (1,)))
        delta = jnp.sum(dmixed.astype(F32) * mixed, 1, keepdims=True)
        dscores = (prob.astype(F32) * (dprob - delta)).astype(BF16)
        dquery = dot(dscores, key, ((1,), (0,)))
        dkey = dkey + dot(dscores, query, ((0,), (0,)))
        at = pl.ds(pl.multiple_of(((2 + e) * HEADS + h) * HD, HD), HD)
        grad_out[:, at] = rotated_back(dquery * scale).astype(BF16)
    grad_out[:, pl.ds(pl.multiple_of(h * HD, HD), HD)] = rotated_back(dkey).astype(BF16)
    grad_out[:, pl.ds(pl.multiple_of((HEADS + h) * HD, HD), HD)] = dval.astype(BF16)

    @pl.when(h == 0)
    def _():
        dgate_out[...] = dgates

    @pl.when(h > 0)
    def _():
        dgate_out[...] += dgates


def attention_back(key, val, que, mix, raw, prob, cosine, sine, gates):
    groups, tokens = prob.shape[0], prob.shape[-1]
    column, rows = block_specs(tokens)
    thirds = [column(n) for n in range(3)]
    grads = jax.ShapeDtypeStruct((groups * tokens, 5 * HEADS * HD), BF16)
    return pl.pallas_call(
        attention_back_body,
        grid=(groups, HEADS),
        in_specs=[column(0), column(0)]
        + thirds * 3
        + [prob_spec(tokens)]
        + [rows(HD)] * 2
        + [rows(gates.shape[1])],
        out_specs=[rows(grads.shape[1]), rows(HD)],
        out_shape=[grads, jax.ShapeDtypeStruct((groups * tokens, HD), F32)],
        compiler_params=pltpu.CompilerParams(vmem_limit_bytes=48 * MIB),
        name="attention_back",
    )(key, val, que, que, que, mix, mix, mix, raw, raw, raw, prob, cosine, sine, gates)


def positions(segments):
    index = jnp.arange(segments.shape[0], dtype=jnp.int32)
    prompt = jnp.sum((segments == 0).astype(jnp.int32))
    first = jnp.sum((segments == 1).astype(jnp.int32))
    before = jnp.where(segments == 0, 0, jnp.where(segments == 1, prompt, prompt + first))
    return jnp.where(segments == 0, index, prompt + index - before)


def route_gates(logits, routes, count):
    onehot = (routes[:, :, None] == jnp.arange(count, dtype=jnp.int32)).astype(F32)
    chosen = jnp.sum(onehot * logits[:, None, :], -1)
    expsum = jnp.exp(chosen - jnp.max(chosen, -1, keepdims=True))
    weights = expsum / jnp.sum(expsum, -1, keepdims=True)
    return weights, onehot, jnp.sum(weights[:, :, None] * onehot, 1)


def router_back(dgate, weights, onehot):
    dchosen = jnp.sum(dgate[:, None, :] * onehot, -1)
    dselect = weights * (dchosen - jnp.sum(weights * dchosen, -1, keepdims=True))
    return jnp.sum(dselect[:, :, None] * onehot, 1).astype(BF16)


def normalize(activations):
    inverse = lax.rsqrt(jnp.mean(activations * activations, -1, keepdims=True) + EPSILON)
    return activations * inverse, inverse


def reorder(rows):
    count, width = rows.shape
    return jnp.transpose(rows.reshape(count, 4, 2, 4, width // 32), (0, 3, 2, 1, 4)).reshape(count, width)


def pad_to(array, width):
    return jnp.pad(array, ((0, 0), (0, width - array.shape[1])))


def on_device(
    inputs,
    segments,
    att_routes,
    mlp_routes,
    key_value,
    query_proj,
    output_proj,
    router_att,
    gain_att,
    gate_up,
    down_proj,
    router_mlp,
    gain_mlp,
    out_grad,
):
    width = inputs.shape[1]
    inner = query_proj.shape[2]
    hidden_local = down_proj.shape[1]
    att_count = query_proj.shape[0]
    mlp_count = gate_up.shape[0]
    share = gate_up.shape[1]
    part = inner // 2
    qkv_cols = (2 + att_count) * part
    small_at = qkv_cols
    out_at = qkv_cols + 128
    small = jnp.concatenate([router_att, router_mlp, gain_att[:, None], gain_mlp[:, None]], 1)
    own_att = jnp.concatenate(
        [
            jnp.transpose(key_value.reshape(share, 2, 2, part), (2, 0, 1, 3)).reshape(2, share, -1),
            jnp.transpose(query_proj.reshape(att_count, share, 2, part), (2, 1, 0, 3)).reshape(
                2, share, -1
            ),
            jnp.broadcast_to(pad_to(small, 128), (2, share, 128)),
            jnp.transpose(output_proj.reshape(att_count, 2, part, share), (1, 3, 0, 2)).reshape(
                2, share, -1
            ),
        ],
        2,
    )
    inputs = reorder(inputs)
    out_grad = reorder(out_grad)
    x_all = lax.all_gather(inputs, ("xl", *TP), axis=0, tiled=True)
    grad_all = lax.all_gather(out_grad, TP, axis=0, tiled=True)
    marks = lax.all_gather(jnp.concatenate([segments[:, None], att_routes], 1), "xl", axis=0)
    weights, up_parts, down_parts = gather_dp(
        own_att,
        jnp.swapaxes(gate_up.reshape(mlp_count, share, 2, -1, LANES), 2, 3).reshape(mlp_count, share, -1),
        jnp.swapaxes(down_proj, 1, 2),
    )
    up_whole = lax.all_gather(
        up_parts.reshape(2 * mlp_count * share, -1), "z", axis=0, tiled=True
    )
    down_whole = lax.all_gather(
        down_parts.reshape(2 * mlp_count * share, -1), "z", axis=0, tiled=True
    )

    tokens = segments.shape[0]
    match = jnp.sum((mlp_routes[:, :, None] == jnp.arange(mlp_count, dtype=jnp.int32)).astype(BF16), 1)
    index = jnp.arange(tokens, dtype=jnp.int32)
    lower = (index[None, :] < index[:, None]).astype(BF16)
    rank = dot(lower, match, ((1,), (0,)))
    slot = jnp.where(match > 0, rank.astype(jnp.int32), -1)
    pick = (slot.T[:, None, :] == jnp.arange(CAP, dtype=jnp.int32)[None, :, None]).astype(BF16)
    pick_rows = pick.reshape(mlp_count * CAP, tokens)
    grad_rows = dot(pick_rows, grad_all, ((1,), (0,))).astype(BF16)
    grad_in = lax.all_to_all(grad_rows.reshape(mlp_count, CAP, width), "y", 0, 0, tiled=True)
    grad_in = grad_in.reshape(mlp_count * CAP, width)

    small_all = weights[:, small_at : small_at + 128].astype(F32)
    gain_one, gain_two = small_all[:, 7], small_all[:, 8]
    segments = marks[:, :, 0]
    att_routes = marks[:, :, 1:].reshape(2 * tokens, 2)
    places = jax.vmap(positions)(segments).reshape(-1).astype(F32)
    frequency = ROPE_BASE ** (-2.0 * jnp.arange(HD // 2, dtype=F32) / HD)
    angles = places[:, None] * frequency[None, :]
    cosine = jnp.concatenate([jnp.cos(angles)] * 2, 1)
    sine = jnp.concatenate([-jnp.sin(angles), jnp.sin(angles)], 1)
    normed_one, _ = normalize(x_all.astype(F32))
    unit_one = (normed_one * gain_one).astype(BF16)
    joined_att = dot(unit_one, weights[:, :out_at], ((1,), (0,)))
    weights_att, onehot_att, gate_att = route_gates(
        joined_att[:, small_at : small_at + att_count], att_routes, att_count
    )
    key_rot, val_rows, queries, mixed, gmixed, prob = attention_forward(
        joined_att, cosine, sine, segments, gate_att
    )
    out_weights = weights[:, out_at:]
    attention = dot(gmixed, out_weights, ((1,), (1,))).astype(BF16)
    middle, unit_two = middle_and_unit(attention, inputs, gain_two)

    router_two = weights[:, small_at + att_count : small_at + att_count + mlp_count]
    logit_mlp = dot(unit_two, router_two, ((1,), (0,)))
    weights_mlp, onehot_mlp, gate_mlp = route_gates(logit_mlp, mlp_routes, mlp_count)
    gate_high = gate_mlp.astype(BF16)
    gate_low = (gate_mlp - gate_high.astype(F32)).astype(BF16)
    extended = jnp.concatenate([unit_two, pad_to(jnp.concatenate([gate_high, gate_low], 1), 128)], 1)
    rows_out = dot(pick_rows, extended, ((1,), (0,))).astype(BF16)
    rows_ext = rows_to_experts(rows_out.reshape(mlp_count, CAP, width + 128))
    rows_ext = rows_ext.reshape(mlp_count * CAP, width + 128)
    gates_ext = rows_ext[:, width : width + 2 * mlp_count].astype(F32)
    mine = (jnp.arange(2 * mlp_count) % mlp_count == lax.axis_index("y")).astype(F32)
    gates_in = jnp.sum(gates_ext * mine, 1, keepdims=True)
    djoined, hidden, gated, dgate_part, dunit_part = experts(
        rows_ext, grad_in, up_whole, down_whole, gates_in
    )
    grad_down_whole = dot(grad_in, gated, ((0,), (0,))).astype(BF16)
    dunit_part, grad_down_whole = lax.optimization_barrier((dunit_part, grad_down_whole))
    grad_down_sum = lax.psum_scatter(grad_down_whole, "z", scatter_dimension=0, tiled=True)
    dunit_back, dgate_back, grad_up_whole, branch_part = return_rows(
        dunit_part.reshape(mlp_count, CAP, width),
        dgate_part.reshape(mlp_count, CAP, LANES),
        rows_ext,
        djoined,
        hidden,
        down_whole,
    )
    grad_up_sum = lax.psum_scatter(grad_up_whole, "z", scatter_dimension=0, tiled=True)
    branch_back = lax.all_to_all(
        branch_part.reshape(mlp_count, CAP, width), "y", 0, 0, tiled=True
    ).reshape(mlp_count * CAP, width)
    pick_half = lax.dynamic_slice_in_dim(pick, lax.axis_index("core") * (CAP // 2), CAP // 2, 1)
    dgate_two = jnp.sum(pick_half.astype(F32) * jnp.sum(dgate_back, -1, keepdims=True), 1).T
    dlogit_mlp = router_back(dgate_two, weights_mlp, onehot_mlp)
    dunit_two = dot(
        pick_half.reshape(-1, tokens), dunit_back.reshape(-1, width), ((0,), (0,))
    ) + dot(dlogit_mlp, router_two, ((1,), (1,)))
    grad_rmlp = dot(unit_two, dlogit_mlp, ((0,), (0,)))
    dmiddle, grad_gain_two, dattention = middle_back(
        dunit_two.astype(BF16), middle, out_grad, gain_two
    )

    raw = dot(dattention, out_weights, ((1,), (0,)))
    grad_qkv, dgate_one = attention_back(
        key_rot, val_rows, queries, mixed, raw, prob, cosine, sine, gate_att
    )
    dlogit_att = router_back(dgate_one[:, :att_count], weights_att, onehot_att)
    grad_joined = jnp.concatenate([grad_qkv, pad_to(dlogit_att, 128)], 1)
    dunit_one = dot(grad_joined, weights[:, :out_at], ((1,), (1,)))
    grad_gain_one = jnp.sum(dunit_one * normed_one, 0)
    grad_small = jnp.concatenate(
        [
            dot(unit_one, dlogit_att, ((0,), (0,))),
            grad_rmlp,
            grad_gain_one[:, None],
            grad_gain_two[:, None],
        ],
        1,
    )
    gate_slots = jnp.sum(pick.astype(F32) * gate_mlp.T[:, None, :], -1).reshape(mlp_count * CAP, 1)
    feed = dot(pick_rows, (branch_back.astype(F32) * gate_slots).astype(BF16), ((0,), (0,)))
    summed_att, ups_sum, downs_sum, output, grad_input, small_sum = finish(
        (
            dot(unit_one, grad_qkv, ((0,), (0,))).astype(BF16),
            pad_to(grad_small, 128).astype(BF16),
            dot(dattention, gmixed, ((0,), (0,))).astype(BF16),
        ),
        grad_up_sum,
        grad_down_sum,
        dunit_one.astype(BF16),
        feed.astype(BF16),
        inputs,
        middle,
        dmiddle,
        gain_one,
    )
    grad_kv = jnp.transpose(
        summed_att[:, :, : 2 * part].reshape(2, share, 2, part), (1, 2, 0, 3)
    ).reshape(share, 2, inner)
    grad_query = jnp.transpose(
        summed_att[:, :, 2 * part : qkv_cols].reshape(2, share, att_count, part), (2, 1, 0, 3)
    ).reshape(att_count, share, inner)
    grad_output = jnp.transpose(
        summed_att[:, :, out_at:].reshape(2, share, att_count, part), (2, 0, 3, 1)
    ).reshape(att_count, inner, share)
    output = reorder(output)
    grad_input = reorder(grad_input)

    grads_up = jnp.swapaxes(
        ups_sum.astype(F32).reshape(mlp_count, share, -1, 2, LANES), 2, 3
    ).reshape(mlp_count, share, 2, hidden_local)
    grads_down = jnp.swapaxes(downs_sum.astype(F32), 1, 2)
    return (
        output,
        grad_input,
        grad_kv,
        grad_query,
        grad_output,
        small_sum[:, :3],
        small_sum[:, 7],
        grads_up,
        grads_down,
        small_sum[:, 3:7],
        small_sum[:, 8],
    )


def solution(mesh):
    fine = Mesh(mesh.devices.reshape(4, 2, 4, 2, 2), ALL)
    return jax.shard_map(
        on_device,
        mesh=fine,
        in_specs=(
            P(ALL, None),
            P(DP),
            P(DP, None),
            P(DP, None),
            P(DP, None, TP),
            P(None, DP, TP),
            P(None, TP, DP),
            P(DP, None),
            P(DP),
            P(None, DP, None, TP),
            P(None, TP, DP),
            P(DP, None),
            P(DP),
            P(ALL, None),
        ),
        out_specs=(
            P(ALL, None),
            P(ALL, None),
            P(DP, None, TP),
            P(None, DP, TP),
            P(None, TP, DP),
            P(DP, None),
            P(DP),
            P(None, DP, None, TP),
            P(None, TP, DP),
            P(DP, None),
            P(DP),
        ),
        check_vma=False,
    )
```

```python
import functools
import math

import jax
import jax.numpy as jnp
from jax import lax
from jax.experimental import pallas as pl
from jax.experimental.pallas import tpu as pltpu
from jax.sharding import Mesh, PartitionSpec as P

HD = 128
HEADS = 2
CAP = 320
EPSILON = 1e-06
NEGATIVE = -1e30
ROPE_BASE = 10000.0
MESH_ID = pl.DeviceIdType.MESH
MIB = 1024 * 1024
DP = ("y", "xl", "z")
TP = ("xh", "core")
ALL = DP + TP
F32 = jnp.float32
BF16 = jnp.bfloat16


def mod4(place):
    return lax.rem(place + 4, 4)


def neighbour(axis, step):
    size = 4 if axis in ("y", "z") else 2
    return {axis: lax.rem(lax.axis_index(axis) + step + size, size)}


def chip_along(step):
    at = lax.rem(lax.axis_index("xh") * 2 + lax.axis_index("xl") + step + 4, 4)
    return {"xh": lax.div(at, 2), "xl": lax.rem(at, 2)}


def greet(*devices):
    barrier = pltpu.get_barrier_semaphore()
    for device in devices:
        pl.semaphore_signal(barrier, inc=1, device_id=device, device_id_type=MESH_ID)
    pl.semaphore_wait(barrier, len(devices))


def arrived(ref, sem):
    pltpu.make_async_copy(ref, ref, sem).wait()


class Sends:
    def __init__(self):
        self.copies = []

    def __call__(self, src, dst, send_sem, recv_sem, device):
        copy = pltpu.make_async_remote_copy(
            src_ref=src,
            dst_ref=dst,
            send_sem=send_sem,
            recv_sem=recv_sem,
            device_id=device,
            device_id_type=MESH_ID,
        )
        copy.start()
        self.copies.append(copy)

    def finish(self):
        for copy in self.copies:
            copy.wait_send()


def gather_body(
    x_ref, ups_ref, downs_ref, marks_ref, out_ref, up_ref, down_ref, marks_out,
    loc, xs, xr, s1, r1m, r1p, f1s, f1r, s2, r2m, r2p, f2s, f2r, es, er, ex, ey, ms, mr,
):
    y, xl, z = lax.axis_index("y"), lax.axis_index("xl"), lax.axis_index("z")
    half = x_ref.shape[1] // 2
    quarter = half // 2
    greet(
        neighbour("xl", 1),
        *(neighbour("y", step) for step in (1, 2, 3)),
        *(neighbour("z", step) for step in (1, -1)),
    )
    rings = (("z", "y"), ("y", "z"))
    place = {"y": y, "z": z}
    other = 1 - xl
    both = pl.ds(0, 2)
    sends = Sends()
    send = sends

    def slot(h, first, second, j, start, count):
        yy, zz = (second, first) if h == 0 else (first, second)
        return out_ref.at[zz, j, yy, pl.ds(start, count)]

    own = pltpu.make_async_copy(x_ref.at[xl], out_ref.at[z, xl, y], loc.at[0])
    own.start()
    own_marks = pltpu.make_async_copy(marks_ref, marks_out.at[xl], loc.at[3])
    own_marks.start()
    send(marks_ref, marks_out.at[xl], ms, mr, neighbour("xl", 1))
    experts = ((ups_ref, up_ref), (downs_ref, down_ref))
    kept = []
    for n, (shards, expert) in enumerate(experts):
        kept.append(pltpu.make_async_copy(shards.at[y], expert.at[xl, y], loc.at[1 + n]))
        kept[-1].start()
        send(shards.at[y], expert.at[xl, y], ex.at[n, 0], ey.at[n, 0], neighbour("xl", 1))
        for step in (1, 3, 2):
            send(
                shards.at[mod4(y + step)],
                expert.at[xl, y],
                es.at[n, step - 1],
                er.at[n, step - 1],
                neighbour("y", step),
            )
    for h in (0, 1):
        first, second = place[rings[h][0]], place[rings[h][1]]
        src = x_ref.at[xl, pl.ds(h * half, half)]
        dst = slot(h, first, second, xl, h * half, half)
        send(x_ref.at[other, pl.ds(h * half, half)], dst, xs.at[h], xr.at[h], neighbour("xl", 1))
        send(src, dst, s1.at[h, 0, 0], r1m.at[h, 0], neighbour(rings[h][0], 1))
        send(src, dst, s1.at[h, 0, 1], r1p.at[h, 0], neighbour(rings[h][0], -1))
    own.wait()

    def send_second(h, k, first):
        block = slot(h, first, place[rings[h][1]], both, h * half, half)
        send(block, block, s2.at[h, k, 0], r2m.at[h, k], neighbour(rings[h][1], 1))
        send(block, block, s2.at[h, k, 1], r2p.at[h, k], neighbour(rings[h][1], -1))

    for h in (0, 1):
        first, second = place[rings[h][0]], place[rings[h][1]]
        block = slot(h, first, second, other, h * half, half)
        arrived(block, xr.at[h])
        send(block, block, s1.at[h, 1, 0], r1m.at[h, 1], neighbour(rings[h][0], 1))
        send(block, block, s1.at[h, 1, 1], r1p.at[h, 1], neighbour(rings[h][0], -1))
        send_second(h, 0, first)
    for j, jx in ((0, xl), (1, other)):
        for h in (0, 1):
            first, second = place[rings[h][0]], place[rings[h][1]]
            arrived(slot(h, mod4(first - 1), second, jx, h * half, half), r1m.at[h, j])
            block = slot(h, mod4(first - 1), second, jx, h * half, quarter)
            send(block, block, f1s.at[h, j, 0], f1r.at[h, j, 0], neighbour(rings[h][0], 1))
            arrived(slot(h, mod4(first + 1), second, jx, h * half, half), r1p.at[h, j])
            block = slot(h, mod4(first + 1), second, jx, h * half + quarter, quarter)
            send(block, block, f1s.at[h, j, 1], f1r.at[h, j, 1], neighbour(rings[h][0], -1))
    for k, step in ((1, -1), (2, 1)):
        for h in (0, 1):
            send_second(h, k, mod4(place[rings[h][0]] + step))
    for n, (shards, expert) in enumerate(experts):
        for step in (1, 3, 2):
            landed = expert.at[xl, mod4(y - step)]
            arrived(landed, er.at[n, step - 1])
            send(landed, landed, ex.at[n, step], ey.at[n, step], neighbour("xl", 1))
    for h in (0, 1):
        first, second = place[rings[h][0]], place[rings[h][1]]
        for j, jx in ((0, xl), (1, other)):
            for p in (0, 1):
                block = slot(h, mod4(first + 2), second, jx, h * half + p * quarter, quarter)
                arrived(block, f1r.at[h, j, p])
        send_second(h, 3, mod4(first + 2))
    steps = ((0, 0), (1, -1), (2, 1), (3, 2))
    for k, step in steps:
        for h in (0, 1):
            first, second = mod4(place[rings[h][0]] + step), place[rings[h][1]]
            arrived(slot(h, first, mod4(second - 1), both, h * half, half), r2m.at[h, k])
            block = slot(h, first, mod4(second - 1), both, h * half, quarter)
            send(block, block, f2s.at[h, k, 0], f2r.at[h, k, 0], neighbour(rings[h][1], 1))
            arrived(slot(h, first, mod4(second + 1), both, h * half, half), r2p.at[h, k])
            block = slot(h, first, mod4(second + 1), both, h * half + quarter, quarter)
            send(block, block, f2s.at[h, k, 1], f2r.at[h, k, 1], neighbour(rings[h][1], -1))
    for k, step in steps:
        for h in (0, 1):
            first, second = mod4(place[rings[h][0]] + step), place[rings[h][1]]
            for p in (0, 1):
                block = slot(h, first, mod4(second + 2), both, h * half + p * quarter, quarter)
                arrived(block, f2r.at[h, k, p])
    for n, (shards, expert) in enumerate(experts):
        for step in (0, 1, 3, 2):
            arrived(expert.at[other, mod4(y - step)], ey.at[n, step])
        kept[n].wait()
    arrived(marks_out.at[other], mr)
    own_marks.wait()
    sends.finish()


def gather_dp(shard, ups, downs, marks):
    _, rows, cols = shard.shape
    dma = pltpu.SemaphoreType.DMA
    whole, up, down, marks = pl.pallas_call(
        gather_body,
        out_shape=[
            jax.ShapeDtypeStruct((4, 2, 4, rows, cols), shard.dtype),
            jax.ShapeDtypeStruct((2, *ups.shape), ups.dtype),
            jax.ShapeDtypeStruct((2, *downs.shape), downs.dtype),
            jax.ShapeDtypeStruct((2, *marks.shape), marks.dtype),
        ],
        in_specs=[pl.BlockSpec(memory_space=pl.ANY)] * 4,
        out_specs=[pl.BlockSpec(memory_space=pl.ANY)] * 4,
        scratch_shapes=[
            dma((4,)),
            dma((2,)),
            dma((2,)),
            dma((2, 2, 2)),
            dma((2, 2)),
            dma((2, 2)),
            dma((2, 2, 2)),
            dma((2, 2, 2)),
            dma((2, 4, 2)),
            dma((2, 4)),
            dma((2, 4)),
            dma((2, 4, 2)),
            dma((2, 4, 2)),
            dma((2, 3)),
            dma((2, 3)),
            dma((2, 4)),
            dma((2, 4)),
            dma,
            dma,
        ],
        compiler_params=pltpu.CompilerParams(collective_id=0, has_side_effects=True),
        name="gather_weights",
    )(shard, ups, downs, marks)
    return whole.reshape(32 * rows, cols), up, down, marks


def reduce_stages(scatter_count, part_refs, core_buf, sum_buf, far_buf, core_s, core_r, far_s, far_r, sends):
    xh, core = lax.axis_index("xh"), lax.axis_index("core")
    rows = part_refs[0].shape[1]
    step = rows // scatter_count
    far, here = 1 - xh, xh
    for n, chunk in enumerate(range(0, rows, step)):
        at = pl.ds(chunk, step)
        for i, part in enumerate(part_refs):
            sends(
                part.at[far * 2 + 1 - core, at],
                core_buf.at[i, 0, at],
                core_s.at[i, n, 0],
                core_r.at[i, n, 0],
                neighbour("core", 1),
            )
    for n, chunk in enumerate(range(0, rows, step)):
        at = pl.ds(chunk, step)
        for i, part in enumerate(part_refs):
            sends(
                part.at[here * 2 + 1 - core, at],
                core_buf.at[i, 1, at],
                core_s.at[i, n, 1],
                core_r.at[i, n, 1],
                neighbour("core", 1),
            )
    yield
    for n, chunk in enumerate(range(0, rows, step)):
        at = pl.ds(chunk, step)
        for i, part in enumerate(part_refs):
            arrived(core_buf.at[i, 0, at], core_r.at[i, n, 0])
            mine = part[far * 2 + core, chunk : chunk + step, :].astype(F32)
            sum_buf[i, chunk : chunk + step, :] = (
                mine + core_buf[i, 0, chunk : chunk + step, :].astype(F32)
            ).astype(BF16)
            sends(
                sum_buf.at[i, at],
                far_buf.at[i, at],
                far_s.at[i, n],
                far_r.at[i, n],
                neighbour("xh", 1),
            )
    yield

    def total(i, n):
        chunk = n * step
        at = pl.ds(chunk, step)
        arrived(core_buf.at[i, 1, at], core_r.at[i, n, 1])
        near = part_refs[i][here * 2 + core, chunk : chunk + step, :].astype(F32)
        near = near + core_buf[i, 1, chunk : chunk + step, :].astype(F32)
        arrived(far_buf.at[i, at], far_r.at[i, n])
        return near + far_buf[i, chunk : chunk + step, :].astype(F32)

    yield total


def ring_reduce_stages(part_ref, core_buf, sum_buf, via_buf, far_buf, core_s, core_r, ring_s, ring_r, sends):
    xl, xh, core = lax.axis_index("xl"), lax.axis_index("xh"), lax.axis_index("core")
    rows = part_ref.shape[3]
    half = rows // 2
    at = xh * 2 + xl
    chips = [lax.rem(at + step, 4) for step in (2, 1, 3, 0)]
    chips = [(lax.rem(chip, 2), lax.div(chip, 2)) for chip in chips]
    for n, (pxl, pxh) in enumerate(chips):
        sends(
            part_ref.at[pxl, pxh, 1 - core],
            core_buf.at[n],
            core_s.at[n],
            core_r.at[n],
            neighbour("core", 1),
        )

    def own(n, start):
        pxl, pxh = chips[n]
        return part_ref[pxl, pxh, core, start : start + half, :].astype(F32)

    def both(n, start):
        return own(n, start) + core_buf[n, start : start + half, :].astype(F32)

    first, second = pl.ds(0, half), pl.ds(half, half)
    ahead, behind = chip_along(1), chip_along(-1)
    yield
    arrived(core_buf.at[0], core_r.at[0])
    sum_buf[0, :half, :] = both(0, 0).astype(BF16)
    sends(sum_buf.at[0, first], via_buf.at[0], ring_s.at[0], ring_r.at[0], ahead)
    sum_buf[0, half:, :] = both(0, half).astype(BF16)
    sends(sum_buf.at[0, second], via_buf.at[1], ring_s.at[1], ring_r.at[1], behind)
    arrived(core_buf.at[1], core_r.at[1])
    sum_buf[1, half:, :] = both(1, half).astype(BF16)
    sends(sum_buf.at[1, second], far_buf.at[0, second], ring_s.at[2], ring_r.at[2], ahead)
    arrived(core_buf.at[2], core_r.at[2])
    sum_buf[2, :half, :] = both(2, 0).astype(BF16)
    sends(sum_buf.at[2, first], far_buf.at[1, first], ring_s.at[3], ring_r.at[3], behind)
    yield
    arrived(via_buf.at[0], ring_r.at[0])
    sum_buf[1, :half, :] = (both(1, 0) + via_buf[0].astype(F32)).astype(BF16)
    sends(sum_buf.at[1, first], far_buf.at[0, first], ring_s.at[4], ring_r.at[4], ahead)
    arrived(via_buf.at[1], ring_r.at[1])
    sum_buf[2, half:, :] = (both(2, half) + via_buf[1].astype(F32)).astype(BF16)
    sends(sum_buf.at[2, second], far_buf.at[1, second], ring_s.at[5], ring_r.at[5], behind)
    arrived(core_buf.at[3], core_r.at[3])

    def total(part):
        rows_at = first if part == 0 else second
        start = part * half
        near = both(3, start)
        arrived(far_buf.at[0, rows_at], ring_r.at[4 if part == 0 else 2])
        near = near + far_buf[0, start : start + half, :].astype(F32)
        arrived(far_buf.at[1, rows_at], ring_r.at[3 if part == 0 else 5])
        return near + far_buf[1, start : start + half, :].astype(F32)

    yield total


def ring_reduce_scratch(rows, width):
    dma = pltpu.SemaphoreType.DMA
    return [
        pltpu.VMEM((4, rows, width), BF16),
        pltpu.VMEM((3, rows, width), BF16),
        pltpu.VMEM((2, rows // 2, width), BF16),
        pltpu.VMEM((2, rows, width), BF16),
        dma((4,)),
        dma((4,)),
        dma((6,)),
        dma((6,)),
    ]


def ring_spread(out_ref, part, ring_s, ring_r, core_s, core_r, sends):
    xl, xh, core = lax.axis_index("xl"), lax.axis_index("xh"), lax.axis_index("core")
    half = out_ref.shape[3] // 2
    mine = out_ref.at[xl, xh, core, pl.ds(part * half, half)]
    sends(mine, mine, ring_s.at[part, 0], ring_r.at[part, 0], chip_along(1))
    sends(mine, mine, ring_s.at[part, 1], ring_r.at[part, 1], chip_along(-1))
    sends(mine, mine, core_s.at[part, 0], core_r.at[part, 0], neighbour("core", 1))


def ring_spread_finish(out_ref, ring_s, ring_r, core_s, core_r, sends):
    xl, xh, core = lax.axis_index("xl"), lax.axis_index("xh"), lax.axis_index("core")
    half = out_ref.shape[3] // 2
    at = xh * 2 + xl

    def block(step, part, which):
        chip = lax.rem(at + step + 4, 4)
        return out_ref.at[lax.rem(chip, 2), lax.div(chip, 2), which, pl.ds(part * half, half)]

    for part in (0, 1):
        for n, (step, on) in enumerate(((-1, 1), (1, -1))):
            landed = block(step, part, core)
            arrived(landed, ring_r.at[part, n])
            if part == n:
                sends(landed, landed, ring_s.at[part, 2], ring_r.at[part, 2], chip_along(on))
            sends(landed, landed, core_s.at[part, 1 + n], core_r.at[part, 1 + n], neighbour("core", 1))
    for part in (0, 1):
        landed = block(2, part, core)
        arrived(landed, ring_r.at[part, 2])
        sends(landed, landed, core_s.at[part, 3], core_r.at[part, 3], neighbour("core", 1))
    for part in (0, 1):
        for n, step in enumerate((0, -1, 1, 2)):
            arrived(block(step, part, 1 - core), core_r.at[part, n])


def ring_spread_scratch():
    dma = pltpu.SemaphoreType.DMA
    return [dma((2, 3)), dma((2, 3)), dma((2, 4)), dma((2, 4))]


def along_x():
    return neighbour("core", 1), neighbour("xh", 1), chip_along(1), chip_along(-1)


CHUNKS = 4


def reduce_scratch(count, rows, width):
    dma = pltpu.SemaphoreType.DMA
    return [
        pltpu.VMEM((count, 2, rows, width), BF16),
        pltpu.VMEM((count, rows, width), BF16),
        pltpu.VMEM((count, rows, width), BF16),
        dma((count, CHUNKS, 2)),
        dma((count, CHUNKS, 2)),
        dma((count, CHUNKS)),
        dma((count, CHUNKS)),
    ]


def spread_chunk(out_ref, n, step, sems, sends):
    xh, core = lax.axis_index("xh"), lax.axis_index("core")
    at = pl.ds(n * step, step)
    mine = out_ref.at[xh * 2 + core, at]
    far_s, far_r, core_s, core_r = sems
    sends(mine, mine, far_s.at[n], far_r.at[n], neighbour("xh", 1))
    sends(mine, mine, core_s.at[n, 0], core_r.at[n, 0], neighbour("core", 1))


def spread_finish(out_ref, step, sems, sends):
    xh, core = lax.axis_index("xh"), lax.axis_index("core")
    far_s, far_r, core_s, core_r = sems
    for n in range(CHUNKS):
        at = pl.ds(n * step, step)
        theirs = out_ref.at[(1 - xh) * 2 + core, at]
        arrived(theirs, far_r.at[n])
        sends(theirs, theirs, core_s.at[n, 1], core_r.at[n, 1], neighbour("core", 1))
    for n in range(CHUNKS):
        at = pl.ds(n * step, step)
        arrived(out_ref.at[xh * 2 + 1 - core, at], core_r.at[n, 0])
        arrived(out_ref.at[(1 - xh) * 2 + 1 - core, at], core_r.at[n, 1])


def spread_scratch():
    dma = pltpu.SemaphoreType.DMA
    return [dma((CHUNKS,)), dma((CHUNKS,)), dma((CHUNKS, 2)), dma((CHUNKS, 2))]


def middle_body(
    part_ref, x_ref, gain_ref, pick_ref, grad_ref, middle_ref, unit_ref, rows_out, rows_buf, loc, ys, yr, cs, cr, *scratch
):
    sends = Sends()
    y, core = lax.axis_index("y"), lax.axis_index("core")
    greet(*along_x(), *(neighbour("y", step) for step in (1, 2, 3)))
    stages = ring_reduce_stages(part_ref, *scratch[:8], sends)
    next(stages)
    slots = pick_ref.shape[1] // 2
    mine = pl.ds(pl.multiple_of(core * slots, slots), slots)

    def pick(step):
        target = mod4(y + step)
        rows_buf[step - 1] = dot(pick_ref[target, mine, :], grad_ref[...], ((1,), (0,))).astype(BF16)
        sends(
            rows_buf.at[step - 1],
            rows_out.at[y, mine],
            ys.at[step - 1],
            yr.at[step - 1],
            neighbour("y", step),
        )

    pick(2)
    next(stages)
    pick(1)
    pick(3)
    rows_buf[3] = dot(pick_ref[y, :slots, :], grad_ref[...], ((1,), (0,))).astype(BF16)
    rows_buf[4] = dot(pick_ref[y, slots:, :], grad_ref[...], ((1,), (0,))).astype(BF16)
    kept = []
    for n in (0, 1):
        kept.append(pltpu.make_async_copy(rows_buf.at[3 + n], rows_out.at[y, pl.ds(n * slots, slots)], loc.at[n]))
        kept[-1].start()
    total = next(stages)
    me = lax.axis_index("xh") * 2 + core
    step = x_ref.shape[0] // CHUNKS
    half = x_ref.shape[0] // 2
    for part in (0, 1):
        rows = slice(part * half, (part + 1) * half)
        middle = x_ref[rows, :].astype(F32) + total(part)
        middle_ref[rows, :] = middle
        inverse = lax.rsqrt(jnp.mean(middle * middle, 1, keepdims=True) + EPSILON)
        unit_ref[me, rows, :] = (middle * inverse * gain_ref[...]).astype(BF16)
        for n in range(part * CHUNKS // 2, (part + 1) * CHUNKS // 2):
            spread_chunk(unit_ref, n, step, scratch[8:], sends)
    spread_finish(unit_ref, step, scratch[8:], sends)
    for step in (1, 3, 2):
        block = rows_out.at[mod4(y - step), mine]
        arrived(block, yr.at[step - 1])
        sends(block, block, cs.at[step - 1], cr.at[step - 1], neighbour("core", 1))
    other = pl.ds(pl.multiple_of((1 - core) * slots, slots), slots)
    for step in (1, 3, 2):
        arrived(rows_out.at[mod4(y - step), other], cr.at[step - 1])
    for copy in kept:
        copy.wait()
    sends.finish()


def vmem(count):
    return [pl.BlockSpec(memory_space=pltpu.VMEM)] * count


def middle_and_unit(part, x, gain, pick, grads):
    rows, width = x.shape
    experts, slots, _ = pick.shape
    dma = pltpu.SemaphoreType.DMA
    middle, unit, rows_in = pl.pallas_call(
        middle_body,
        out_shape=[
            jax.ShapeDtypeStruct((rows, width), F32),
            jax.ShapeDtypeStruct((4, rows, width), BF16),
            jax.ShapeDtypeStruct((experts, slots, width), BF16),
        ],
        in_specs=vmem(5),
        out_specs=vmem(2) + [pl.BlockSpec(memory_space=pl.ANY)],
        scratch_shapes=[
            pltpu.VMEM((5, slots // 2, width), BF16),
            dma((2,)),
            dma((3,)),
            dma((3,)),
            dma((3,)),
            dma((3,)),
        ]
        + ring_reduce_scratch(rows, width)
        + spread_scratch(),
        compiler_params=pltpu.CompilerParams(
            collective_id=1, has_side_effects=True, vmem_limit_bytes=48 * MIB
        ),
        name="middle_and_unit",
    )(part.reshape(2, 2, 2, rows, width), x, gain[None], pick, grads)
    return middle, unit.reshape(4 * rows, width), rows_in.reshape(experts * slots, width)


def back_body(
    part_ref, middle_ref, grad_ref, gain_ref, hidden_ref, down_ref, dmiddle_ref, dgain_ref, spread_ref, branch_out,
    hidden, down, branch, branch_buf, branch_sum, loc, cs, cr, ys, yr, *scratch,
):
    sends = Sends()
    y, core = lax.axis_index("y"), lax.axis_index("core")
    loads = []
    for n, (src, dst) in enumerate(((hidden_ref, hidden), (down_ref, down))):
        loads.append(pltpu.make_async_copy(src, dst, loc.at[n]))
        loads[-1].start()
    greet(*along_x(), *(neighbour("y", step) for step in (1, 2, 3)))
    stages = reduce_stages(CHUNKS, [part_ref], *scratch[:7], sends)
    next(stages)
    slots = branch_out.shape[1]
    mine = pl.ds(pl.multiple_of(core * slots, slots), slots)
    theirs = pl.ds(pl.multiple_of((1 - core) * slots, slots), slots)

    def output(step):
        target = mod4(y + step)
        branch[step] = dot(hidden[target], down[...], ((1,), (1,))).astype(BF16)
        sends(
            branch.at[step, theirs], branch_buf.at[step], cs.at[step], cr.at[step], neighbour("core", 1)
        )

    for load in loads:
        load.wait()
    output(2)
    next(stages)
    for step in (1, 3, 0):
        output(step)
    total = next(stages)
    xl, xh = lax.axis_index("xl"), lax.axis_index("xh")
    step = middle_ref.shape[0] // CHUNKS
    for n in range(CHUNKS):
        rows = slice(n * step, (n + 1) * step)
        middle = middle_ref[rows, :]
        inverse = lax.rsqrt(jnp.mean(middle * middle, 1, keepdims=True) + EPSILON)
        normed = middle * inverse
        dunit = total(0, n)
        product = dunit * normed
        dgain = jnp.sum(product, 0, keepdims=True)
        if n == 0:
            dgain_ref[...] = dgain
        else:
            dgain_ref[...] += dgain
        mean = jnp.mean(product * gain_ref[...], 1, keepdims=True)
        dmiddle = grad_ref[rows, :].astype(F32) + inverse * (dunit * gain_ref[...] - normed * mean)
        dmiddle_ref[rows, :] = dmiddle
        spread_ref[xl, xh, core, rows, :] = dmiddle.astype(BF16)
        if n % 2 == 1:
            ring_spread(spread_ref, n // 2, *scratch[7:], sends)
    for step in (2, 1, 3, 0):
        arrived(branch_buf.at[step], cr.at[step])
        value = (branch[step, mine, :].astype(F32) + branch_buf[step].astype(F32)).astype(BF16)
        if step == 0:
            branch_out[y] = value
        else:
            branch_sum[step - 1] = value
            sends(
                branch_sum.at[step - 1],
                branch_out.at[y],
                ys.at[step - 1],
                yr.at[step - 1],
                neighbour("y", step),
            )
    ring_spread_finish(spread_ref, *scratch[7:], sends)
    for step in (1, 3, 2):
        arrived(branch_out.at[mod4(y - step)], yr.at[step - 1])
    sends.finish()


def middle_back(part, middle, grad, gain, hidden, down):
    rows, width = middle.shape
    count, inner = hidden.shape
    slots = count // 4
    dma = pltpu.SemaphoreType.DMA
    anywhere = pl.BlockSpec(memory_space=pl.ANY)
    dmiddle, dgain, spread, branch = pl.pallas_call(
        back_body,
        out_shape=[
            jax.ShapeDtypeStruct((rows, width), F32),
            jax.ShapeDtypeStruct((1, width), F32),
            jax.ShapeDtypeStruct((2, 2, 2, rows, width), BF16),
            jax.ShapeDtypeStruct((4, slots // 2, width), BF16),
        ],
        in_specs=vmem(4) + [anywhere] * 2,
        out_specs=vmem(4),
        scratch_shapes=[
            pltpu.VMEM((4, slots, inner), BF16),
            pltpu.VMEM(down.shape, BF16),
            pltpu.VMEM((4, slots, width), BF16),
            pltpu.VMEM((4, slots // 2, width), BF16),
            pltpu.VMEM((3, slots // 2, width), BF16),
            dma((2,)),
            dma((4,)),
            dma((4,)),
            dma((3,)),
            dma((3,)),
        ]
        + reduce_scratch(1, rows, width)
        + ring_spread_scratch(),
        compiler_params=pltpu.CompilerParams(
            collective_id=2, has_side_effects=True, vmem_limit_bytes=56 * MIB
        ),
        name="middle_back",
    )(part.reshape(4, rows, width), middle, grad, gain[None], hidden.reshape(4, slots, inner), down)
    return dmiddle, dgain[0], spread.reshape(8 * rows, width), branch


def rows_body(
    rows_ref, grad_ref, down_ref, out_ref, raw_out, grad, down, block, loc, out_sem, far_s, far_r, core_s, core_r
):
    y, core = lax.axis_index("y"), lax.axis_index("core")
    half = rows_ref.shape[1] // 2
    sends = Sends()
    greet(neighbour("core", 1), *(neighbour("y", step) for step in (1, 2, 3)))
    at = pl.ds(pl.multiple_of(core * half, half), half)
    own = pltpu.make_async_copy(rows_ref.at[y], out_ref.at[y], loc.at[0])
    own.start()
    loads = []
    for n, (src, dst) in enumerate(((grad_ref, grad), (down_ref, down))):
        loads.append(pltpu.make_async_copy(src, dst, loc.at[1 + n]))
        loads[-1].start()
    for step in (2, 1, 3):
        target = mod4(y + step)
        sends(
            rows_ref.at[target, at],
            out_ref.at[y, at],
            far_s.at[step - 1],
            far_r.at[step - 1],
            neighbour("y", step),
        )
    for load in loads:
        load.wait()
    outs = []
    columns = raw_out.shape[1]
    for n, start in enumerate(range(0, columns, WIDE)):
        cols = min(WIDE, columns - start)
        if n >= 2:
            outs[n - 2].wait()
        block[n % 2, :, :cols] = dot(grad[...], down[:, start : start + cols], ((1,), (0,)))
        outs.append(
            pltpu.make_async_copy(
                block.at[n % 2, :, pl.ds(0, cols)], raw_out.at[:, pl.ds(start, cols)], out_sem.at[n % 2]
            )
        )
        outs[-1].start()
    for step in (1, 3, 2):
        source = mod4(y - step)
        block = out_ref.at[source, at]
        arrived(block, far_r.at[step - 1])
        sends(block, block, core_s.at[step - 1], core_r.at[step - 1], neighbour("core", 1))
    own.wait()
    other = pl.ds(pl.multiple_of((1 - core) * half, half), half)
    for step in (1, 3, 2):
        arrived(out_ref.at[mod4(y - step), other], core_r.at[step - 1])
    for out in outs[-2:]:
        out.wait()
    sends.finish()


LANES = 128
WIDE = 256


def rows_to_experts(rows, grads, down):
    count, hidden = grads.shape[0], down.shape[1]
    anywhere = pl.BlockSpec(memory_space=pl.ANY)
    dma = pltpu.SemaphoreType.DMA
    return pl.pallas_call(
        rows_body,
        out_shape=[
            jax.ShapeDtypeStruct(rows.shape, rows.dtype),
            jax.ShapeDtypeStruct((count, hidden), F32),
        ],
        in_specs=[anywhere] * 3,
        out_specs=[anywhere] * 2,
        scratch_shapes=[
            pltpu.VMEM(grads.shape, BF16),
            pltpu.VMEM(down.shape, BF16),
            pltpu.VMEM((2, count, WIDE), F32),
            dma((3,)),
            dma((2,)),
            dma((3,)),
            dma((3,)),
            dma((3,)),
            dma((3,)),
        ],
        compiler_params=pltpu.CompilerParams(
            collective_id=4, has_side_effects=True, vmem_limit_bytes=40 * MIB
        ),
        name="rows_to_experts",
    )(rows, grads, down)


STEPS = (2, 1, -1, 0)


def finish_body(
    qkv_ref, small_ref, o_ref, ups_ref, downs_ref, part_ref, feed_ref, x_ref, middle_ref, dmiddle_ref, gain_ref,
    out_ref, up_out, down_out, output_ref, dinput_ref, small_out,
    g_ref, loc, t_buf, r_buf, tb_buf, rb_buf, c_buf,
    t_s, t_r, r_s, r_r, tb_s, tb_r, rb_s, rb_r, c_s, c_r,
    up_own, up_buf, up_sum, ex, ey, es, er,
    small_own, small_buf, small_s, small_r, *scratch,
):
    xl, xh, core = lax.axis_index("xl"), lax.axis_index("xh"), lax.axis_index("core")
    place = {"y": lax.axis_index("y"), "z": lax.axis_index("z")}
    my_y = place["y"]
    half = g_ref.shape[3] // 2
    quarter = half // 2
    rings = (("z", "y"), ("y", "z"))
    sends = Sends()
    column = 0
    parts = []
    for n, ref in enumerate((qkv_ref, small_ref, o_ref)):
        cols = ref.shape[-1]
        parts.append(pltpu.make_async_copy(ref, g_ref.at[..., pl.ds(column, cols)], loc.at[n]))
        parts[-1].start()
        column += cols
    for n, (src, dst) in enumerate(((ups_ref.at[xl], up_own), (downs_ref.at[my_y], down_out.at[my_y]))):
        parts.append(pltpu.make_async_copy(src, dst, loc.at[3 + n]))
        parts[-1].start()
    peers = ({"xh": xh, "core": 1 - core}, {"xh": 1 - xh, "core": core}, {"xh": 1 - xh, "core": 1 - core})
    greet(
        *peers,
        chip_along(1),
        chip_along(-1),
        *(neighbour("y", step) for step in (1, 2, 3)),
        *(neighbour("z", step) for step in (1, -1)),
    )
    both = slice(0, 2)
    ring_stages = ring_reduce_stages(part_ref, *scratch[7:15], sends)
    feed_stages = reduce_stages(CHUNKS, [feed_ref], *scratch[:7], sends)
    for step in (2, 1, 3, 0):
        sends(
            ups_ref.at[1 - xl, mod4(my_y + step)],
            up_buf.at[step],
            ex.at[step],
            ey.at[step],
            neighbour("xl", 1),
        )
    next(ring_stages)
    next(feed_stages)
    for part in parts[:3]:
        part.wait()

    def grad_ref(h, first, second, start):
        zz, yy = (first, second) if h == 0 else (second, first)
        return g_ref.at[zz, both, yy, pl.ds(h * half + start, quarter)]

    def grad(h, first, second, j, start, count):
        zz, yy = (first, second) if h == 0 else (second, first)
        return g_ref[zz, j, yy, h * half + start : h * half + start + count, :].astype(F32)

    def firsts(h, k):
        return mod4(place[rings[h][0]] + STEPS[k])

    for k in range(4):
        for h in (0, 1):
            second = place[rings[h][1]]
            for d, way in ((0, 1), (1, -1)):
                sends(
                    grad_ref(h, firsts(h, k), mod4(second + 2), d * quarter),
                    t_buf.at[h, d, k],
                    t_s.at[h, d, k],
                    t_r.at[h, d, k],
                    neighbour(rings[h][1], way),
                )
    for k in range(4):
        for h in (0, 1):
            second = place[rings[h][1]]
            for d, way in ((0, 1), (1, -1)):
                sends(
                    grad_ref(h, firsts(h, k), mod4(second + way), (1 - d) * quarter),
                    r_buf.at[h, d, k, both, pl.ds((1 - d) * quarter, quarter)],
                    r_s.at[h, d, k, 0],
                    r_r.at[h, d, k, 0],
                    neighbour(rings[h][1], way),
                )
    next(ring_stages)
    next(feed_stages)
    for k in range(4):
        for h in (0, 1):
            second = place[rings[h][1]]
            for d, way in ((0, 1), (1, -1)):
                arrived(t_buf.at[h, d, k], t_r.at[h, d, k])
                for j in (0, 1):
                    t_buf[h, d, k, j] = (
                        t_buf[h, d, k, j].astype(F32)
                        + grad(h, firsts(h, k), mod4(second + way), j, d * quarter, quarter)
                    ).astype(BF16)
                sends(
                    t_buf.at[h, d, k],
                    r_buf.at[h, d, k, both, pl.ds(d * quarter, quarter)],
                    r_s.at[h, d, k, 1],
                    r_r.at[h, d, k, 1],
                    neighbour(rings[h][1], way),
                )
    total = next(ring_stages)
    for step in (2, 1, 3):
        sends(
            downs_ref.at[mod4(my_y + step)],
            down_out.at[my_y],
            es.at[1, step - 1],
            er.at[1, step - 1],
            neighbour("y", step),
        )
    for part in parts[3:]:
        part.wait()
    for step in (2, 1, 3, 0):
        target = mod4(my_y + step)
        arrived(up_buf.at[step], ey.at[step])
        value = (up_own[target].astype(F32) + up_buf[step].astype(F32)).astype(BF16)
        if step == 0:
            up_out[my_y] = value
        else:
            up_sum[step - 1] = value
            sends(
                up_sum.at[step - 1],
                up_out.at[my_y],
                es.at[0, step - 1],
                er.at[0, step - 1],
                neighbour("y", step),
            )
    for k in range(4):
        for h in (0, 1):
            second = place[rings[h][1]]
            for d in (0, 1):
                arrived(r_buf.at[h, d, k, both, pl.ds((1 - d) * quarter, quarter)], r_r.at[h, d, k, 0])
                arrived(r_buf.at[h, d, k, both, pl.ds(d * quarter, quarter)], r_r.at[h, d, k, 1])
            for j in (0, 1):
                r_buf[h, 0, k, j] = (
                    r_buf[h, 0, k, j].astype(F32)
                    + r_buf[h, 1, k, j].astype(F32)
                    + grad(h, firsts(h, k), second, j, 0, half)
                ).astype(BF16)
            for d, way in ((0, 1), (1, -1)):
                device = neighbour(rings[h][0], way)
                if k == 0:
                    sends(
                        r_buf.at[h, 0, 0, both, pl.ds(d * quarter, quarter)],
                        tb_buf.at[h, d],
                        tb_s.at[h, d],
                        tb_r.at[h, d],
                        device,
                    )
                if k == 1 + d:
                    sends(
                        r_buf.at[h, 0, k, both, pl.ds((1 - d) * quarter, quarter)],
                        rb_buf.at[h, d, both, pl.ds((1 - d) * quarter, quarter)],
                        rb_s.at[h, d, 0],
                        rb_r.at[h, d, 0],
                        device,
                    )
                    arrived(tb_buf.at[h, d], tb_r.at[h, d])
                    for j in (0, 1):
                        tb_buf[h, d, j] = (
                            tb_buf[h, d, j].astype(F32)
                            + r_buf[h, 0, k, j, d * quarter : (d + 1) * quarter, :].astype(F32)
                        ).astype(BF16)
                    sends(
                        tb_buf.at[h, d],
                        rb_buf.at[h, d, both, pl.ds(d * quarter, quarter)],
                        rb_s.at[h, d, 1],
                        rb_r.at[h, d, 1],
                        device,
                    )
    rows_half = x_ref.shape[0] // 2
    for part in (0, 1):
        rows = slice(part * rows_half, (part + 1) * rows_half)
        x = x_ref[rows, :].astype(F32)
        inverse = lax.rsqrt(jnp.mean(x * x, 1, keepdims=True) + EPSILON)
        normed = x * inverse
        dscaled = total(part) * gain_ref[...]
        mean = jnp.mean(dscaled * normed, 1, keepdims=True)
        dinput_ref[rows, :] = dmiddle_ref[rows, :] + inverse * (dscaled - normed * mean)
    for h in (0, 1):
        for d in (0, 1):
            arrived(rb_buf.at[h, d, both, pl.ds((1 - d) * quarter, quarter)], rb_r.at[h, d, 0])
            arrived(rb_buf.at[h, d, both, pl.ds(d * quarter, quarter)], rb_r.at[h, d, 1])
        for j in (0, 1):
            rb_buf[h, 0, j] = (
                rb_buf[h, 0, j].astype(F32)
                + rb_buf[h, 1, j].astype(F32)
                + r_buf[h, 0, 3, j].astype(F32)
            ).astype(BF16)
        sends(rb_buf.at[h, 0, 1 - xl], c_buf.at[h], c_s.at[h], c_r.at[h], neighbour("xl", 1))
        out_ref[xl, h * half : (h + 1) * half, :] = rb_buf[h, 0, xl].astype(F32)
    for h in (0, 1):
        arrived(c_buf.at[h], c_r.at[h])
        out_ref[1 - xl, h * half : (h + 1) * half, :] = c_buf[h].astype(F32)
    first, last = qkv_ref.shape[-1], qkv_ref.shape[-1] + small_ref.shape[-1]
    small_own[...] = out_ref[0, :, first:last] + out_ref[1, :, first:last]
    for n, peer in enumerate(peers):
        sends(small_own, small_buf.at[n], small_s.at[n], small_r.at[n], peer)
    feed = next(feed_stages)
    step = x_ref.shape[0] // CHUNKS
    for n in range(CHUNKS):
        rows = slice(n * step, (n + 1) * step)
        output_ref[rows, :] = (middle_ref[rows, :] + feed(0, n)).astype(BF16)
    for n, result in enumerate((up_out, down_out)):
        for step in (1, 3, 2):
            arrived(result.at[mod4(my_y - step)], er.at[n, step - 1])
    for n in range(3):
        arrived(small_buf.at[n], small_r.at[n])
    small_out[...] = (small_own[...] + small_buf[1]) + (small_buf[0] + small_buf[2])
    sends.finish()


def finish(grads, ups, downs, part, feed, x, middle, dmiddle, gain):
    rows, cols = grads[0].shape[0], sum(grad.shape[1] for grad in grads)
    share = rows // 32
    half, quarter = share // 2, share // 4
    dma = pltpu.SemaphoreType.DMA
    up_cols, down_cols = ups.shape[1], downs.shape[1]
    small = (share, grads[1].shape[1])
    own_rows, width = x.shape
    anywhere = pl.BlockSpec(memory_space=pl.ANY)
    return pl.pallas_call(
        finish_body,
        out_shape=[
            jax.ShapeDtypeStruct((2, share, cols), F32),
            jax.ShapeDtypeStruct((4, share, up_cols), BF16),
            jax.ShapeDtypeStruct((4, share, down_cols), BF16),
            jax.ShapeDtypeStruct((own_rows, width), BF16),
            jax.ShapeDtypeStruct((own_rows, width), F32),
            jax.ShapeDtypeStruct(small, F32),
        ],
        in_specs=[anywhere] * 5 + vmem(6),
        out_specs=vmem(6),
        scratch_shapes=[
            pltpu.VMEM((4, 2, 4, share, cols), BF16),
            dma((5,)),
            pltpu.VMEM((2, 2, 4, 2, quarter, cols), BF16),
            pltpu.VMEM((2, 2, 4, 2, half, cols), BF16),
            pltpu.VMEM((2, 2, 2, quarter, cols), BF16),
            pltpu.VMEM((2, 2, 2, half, cols), BF16),
            pltpu.VMEM((2, half, cols), BF16),
            dma((2, 2, 4)),
            dma((2, 2, 4)),
            dma((2, 2, 4, 2)),
            dma((2, 2, 4, 2)),
            dma((2, 2)),
            dma((2, 2)),
            dma((2, 2, 2)),
            dma((2, 2, 2)),
            dma((2,)),
            dma((2,)),
            pltpu.VMEM((4, share, up_cols), BF16),
            pltpu.VMEM((4, share, up_cols), BF16),
            pltpu.VMEM((3, share, up_cols), BF16),
            dma((4,)),
            dma((4,)),
            dma((2, 3)),
            dma((2, 3)),
            pltpu.VMEM(small, F32),
            pltpu.VMEM((3, *small), F32),
            dma((3,)),
            dma((3,)),
        ]
        + reduce_scratch(1, own_rows, width)
        + ring_reduce_scratch(own_rows, width),
        compiler_params=pltpu.CompilerParams(
            collective_id=5, has_side_effects=True, vmem_limit_bytes=60 * MIB
        ),
        name="finish",
    )(
        *(grad.reshape(4, 2, 4, share, grad.shape[1]) for grad in grads),
        ups.reshape(2, 4, share, up_cols),
        downs.reshape(4, share, down_cols),
        part.reshape(2, 2, 2, own_rows, width),
        feed.reshape(4, own_rows, width),
        x,
        middle,
        dmiddle,
        gain[None],
    )


def dot(a, b, dims):
    return lax.dot_general(a, b, (dims, ((), ())), preferred_element_type=F32)


def experts_body(
    rows_ref, raw_ref, gate_up_ref, linear_up_ref, gate_ref,
    dgate_pre_out, dlinear_out, hidden_out, gated_out, dgate_out,
):
    @pl.when(pl.program_id(0) == 0)
    def _():
        dgate_out[...] = jnp.zeros_like(dgate_out)

    up = jnp.concatenate([gate_up_ref[...], linear_up_ref[...]], 1)
    joined = dot(rows_ref[...], up, ((1,), (0,)))
    gate_pre, linear = joined[:, :LANES], joined[:, LANES:]
    sigmoid = jax.nn.sigmoid(gate_pre)
    silu = gate_pre * sigmoid
    hidden = silu * linear
    dhidden = raw_ref[...]
    gate = gate_ref[...]
    dgate_out[...] += hidden * dhidden
    dhidden = dhidden * gate
    hidden_out[...] = hidden.astype(BF16)
    gated_out[...] = (hidden * gate).astype(BF16)
    dgate_pre_out[...] = (dhidden * linear * (sigmoid + silu * (1.0 - sigmoid))).astype(BF16)
    dlinear_out[...] = (dhidden * silu).astype(BF16)


def experts(rows, raw, up, gates):
    count, hidden = raw.shape
    width = up.shape[0]
    chunks = hidden // LANES
    chunk = pl.BlockSpec((count, LANES), lambda j: (0, j))
    some = jax.ShapeDtypeStruct((count, hidden), BF16)
    return pl.pallas_call(
        experts_body,
        grid=(chunks,),
        in_specs=[
            pl.BlockSpec((count, width), lambda j: (0, 0)),
            chunk,
            pl.BlockSpec((width, LANES), lambda j: (0, j)),
            pl.BlockSpec((width, LANES), lambda j: (0, chunks + j)),
            pl.BlockSpec((count, 1), lambda j: (0, 0)),
        ],
        out_specs=[chunk] * 4 + [pl.BlockSpec((count, LANES), lambda j: (0, 0))],
        out_shape=[some] * 4 + [jax.ShapeDtypeStruct((count, LANES), F32)],
        compiler_params=pltpu.CompilerParams(vmem_limit_bytes=56 * MIB),
        name="experts",
    )(rows, raw, up, up, gates)


def return_body(
    dgate_pre_ref, dlinear_ref, up_ref, dgate_ref, rows_ref,
    dunit_out, dgate_out, up_out,
    djoined, up, rows, dunit, dgate_own, dunit_buf, dgate_buf, dunit_sum, dgate_sum, block,
    loc, core_s, core_r, far_s, far_r, out_sem,
):
    y, core = lax.axis_index("y"), lax.axis_index("core")
    slots = dgate_ref.shape[1]
    half = slots // 2
    hidden = dgate_pre_ref.shape[1]
    sends = Sends()
    loads = []
    for n, (src, dst) in enumerate(
        (
            (up_ref, up),
            (dgate_pre_ref, djoined.at[:, pl.ds(0, hidden)]),
            (dlinear_ref, djoined.at[:, pl.ds(hidden, hidden)]),
            (rows_ref.at[:, pl.ds(0, rows.shape[1])], rows),
        )
    ):
        loads.append(pltpu.make_async_copy(src, dst, loc.at[1, n]))
        loads[-1].start()
    greet(neighbour("core", 1), *(neighbour("y", step) for step in (1, 2, 3)))
    mine = pl.ds(pl.multiple_of(core * half, half), half)
    theirs = pl.ds(pl.multiple_of((1 - core) * half, half), half)
    order = (2, 1, 3, 0)
    own = []
    for step in order:
        target = mod4(y + step)
        sends(
            dgate_ref.at[target, theirs],
            dgate_buf.at[step],
            core_s.at[1, step],
            core_r.at[1, step],
            neighbour("core", 1),
        )
        own.append(pltpu.make_async_copy(dgate_ref.at[target, mine], dgate_own.at[step], loc.at[0, step]))
        own[-1].start()
    for load in loads[:3]:
        load.wait()
    for copy in own:
        copy.wait()

    def compute(step):
        at = pl.ds(pl.multiple_of(mod4(y + step) * slots, slots), slots)
        dunit[step] = dot(djoined[at, :], up[...], ((1,), (1,))).astype(BF16)
        sends(
            dunit.at[step, theirs],
            dunit_buf.at[step],
            core_s.at[0, step],
            core_r.at[0, step],
            neighbour("core", 1),
        )

    def pass_on(step):
        arrived(dunit_buf.at[step], core_r.at[0, step])
        arrived(dgate_buf.at[step], core_r.at[1, step])
        dunit_value = (dunit[step, mine, :].astype(F32) + dunit_buf[step].astype(F32)).astype(BF16)
        dgate_value = dgate_own[step] + dgate_buf[step]
        if step == 0:
            dunit_out[y] = dunit_value
            dgate_out[y] = dgate_value
            return
        dunit_sum[step - 1] = dunit_value
        dgate_sum[step - 1] = dgate_value
        for n, (summed, result) in enumerate(((dunit_sum, dunit_out), (dgate_sum, dgate_out))):
            sends(
                summed.at[step - 1],
                result.at[y],
                far_s.at[n, step - 1],
                far_r.at[n, step - 1],
                neighbour("y", step),
            )

    compute(2)
    compute(1)
    pass_on(2)
    compute(3)
    pass_on(1)
    compute(0)
    pass_on(3)
    loads[3].wait()
    blocks = up_out.shape[0] // WIDE

    @pl.loop(0, blocks)
    def _(j):
        at = pl.ds(pl.multiple_of(j * WIDE, WIDE), WIDE)
        slot = lax.rem(j, 2)

        @pl.when(j >= 2)
        def _():
            pltpu.make_async_copy(block.at[slot], up_out.at[at], out_sem.at[slot]).wait()

        block[slot] = dot(rows[:, at], djoined[...], ((0,), (0,))).astype(BF16)
        pltpu.make_async_copy(block.at[slot], up_out.at[at], out_sem.at[slot]).start()

    pass_on(0)
    for slot in (0, 1):
        pltpu.make_async_copy(block.at[slot], up_out.at[pl.ds(0, WIDE)], out_sem.at[slot]).wait()
    for n, result in enumerate((dunit_out, dgate_out)):
        for step in (1, 3, 2):
            arrived(result.at[mod4(y - step)], far_r.at[n, step - 1])
    sends.finish()


def return_rows(dgate_pre, dlinear, up, dgate, rows):
    _, slots, lanes = dgate.shape
    half = slots // 2
    width, wide = up.shape
    count = dlinear.shape[0]
    dma = pltpu.SemaphoreType.DMA
    anywhere = pl.BlockSpec(memory_space=pl.ANY)
    return pl.pallas_call(
        return_body,
        out_shape=[
            jax.ShapeDtypeStruct((4, half, width), BF16),
            jax.ShapeDtypeStruct((4, half, lanes), F32),
            jax.ShapeDtypeStruct((width, wide), BF16),
        ],
        in_specs=[anywhere] * 5,
        out_specs=vmem(2) + [anywhere],
        scratch_shapes=[
            pltpu.VMEM((count, wide), BF16),
            pltpu.VMEM((width, wide), BF16),
            pltpu.VMEM((count, width), BF16),
            pltpu.VMEM((4, slots, width), BF16),
            pltpu.VMEM((4, half, lanes), F32),
            pltpu.VMEM((4, half, width), BF16),
            pltpu.VMEM((4, half, lanes), F32),
            pltpu.VMEM((3, half, width), BF16),
            pltpu.VMEM((3, half, lanes), F32),
            pltpu.VMEM((2, WIDE, wide), BF16),
            dma((2, 4)),
            dma((2, 4)),
            dma((2, 4)),
            dma((2, 3)),
            dma((2, 3)),
            dma((2,)),
        ],
        compiler_params=pltpu.CompilerParams(
            collective_id=3, has_side_effects=True, vmem_limit_bytes=62 * MIB
        ),
        name="return_rows",
    )(dgate_pre, dlinear, up, dgate, rows)


def attention_body(
    k_ref, v_ref, q0, q1, q2, cos_ref, sin_ref, col_ref, row_ref, gate_ref,
    key_out, val_out, que_out, mix_out, gmix_out, prob_out,
):
    h = pl.program_id(1)
    cosine, sine = cos_ref[...], sin_ref[...]
    scale = 1.0 / math.sqrt(HD)

    def rotated(v):
        return v * cosine + pltpu.roll(v, HD // 2, 1) * sine

    key = rotated(k_ref[...]).astype(BF16)
    val = v_ref[...].astype(BF16)
    key_out[...] = key
    val_out[...] = val
    tokens = key.shape[0]
    seg_col, seg_row = col_ref[...], row_ref[0]
    at_row = lax.broadcasted_iota(jnp.int32, (tokens, tokens), 0)
    at_col = lax.broadcasted_iota(jnp.int32, (tokens, tokens), 1)
    allowed = (at_col <= at_row) & ((seg_row == 0) | (seg_row == seg_col))
    for e, q_ref in enumerate((q0, q1, q2)):
        query = (rotated(q_ref[...]) * scale).astype(BF16)
        scores = jnp.where(allowed, dot(query, key, ((1,), (1,))), NEGATIVE)
        largest = jnp.max(scores, 1, keepdims=True)
        expsum = jnp.exp(scores - largest)
        prob = (expsum * (1.0 / jnp.sum(expsum, 1, keepdims=True))).astype(BF16)
        prob_out[0, 0, e] = prob
        mixed = dot(prob, val, ((1,), (0,))).astype(BF16)
        at = pl.ds(pl.multiple_of((e * HEADS + h) * HD, HD), HD)
        que_out[:, at] = query
        mix_out[:, at] = mixed
        gmix_out[:, at] = (mixed.astype(F32) * gate_ref[:, e : e + 1]).astype(BF16)


def block_specs(tokens):
    def column(n):
        return pl.BlockSpec((tokens, HD), lambda g, h: (g, n * HEADS + h))

    def rows(width):
        return pl.BlockSpec((tokens, width), lambda g, h: (g, 0))

    return column, rows


def prob_spec(tokens):
    return pl.BlockSpec((1, 1, 3, tokens, tokens), lambda g, h: (g, h, 0, 0, 0))


def attention_forward(joined, cosine, sine, segments, gates):
    groups, tokens = segments.shape
    column, rows = block_specs(tokens)
    wide = jax.ShapeDtypeStruct((groups * tokens, 3 * HEADS * HD), BF16)
    narrow = jax.ShapeDtypeStruct((groups * tokens, HEADS * HD), BF16)
    return pl.pallas_call(
        attention_body,
        grid=(groups, HEADS),
        in_specs=[column(n) for n in range(5)]
        + [rows(HD)] * 2
        + [rows(1), pl.BlockSpec((1, 1, tokens), lambda g, h: (g, 0, 0)), rows(gates.shape[1])],
        out_specs=[column(0), column(0)] + [rows(wide.shape[1])] * 3 + [prob_spec(tokens)],
        out_shape=[narrow, narrow, wide, wide, wide]
        + [jax.ShapeDtypeStruct((groups, HEADS, 3, tokens, tokens), BF16)],
        compiler_params=pltpu.CompilerParams(vmem_limit_bytes=48 * MIB),
        name="attention_forward",
    )(
        *[joined] * 5, cosine, sine, segments.reshape(-1, 1), segments[:, None], gates
    )


def attention_back_body(
    key_ref, val_ref, q0, q1, q2, m0, m1, m2, h0, h1, h2, prob_ref, cos_ref, sin_ref, gate_ref,
    grad_out, dgate_out,
):
    h = pl.program_id(1)
    cosine, sine = cos_ref[...], sin_ref[...]
    scale = 1.0 / math.sqrt(HD)

    def rotated_back(v):
        return v * cosine - pltpu.roll(v, HD // 2, 1) * sine

    key, val = key_ref[...], val_ref[...]
    tokens = key.shape[0]
    dkey = jnp.zeros((tokens, HD), F32)
    dval = jnp.zeros((tokens, HD), F32)
    lane = lax.broadcasted_iota(jnp.int32, (tokens, HD), 1)
    dgates = jnp.zeros((tokens, HD), F32)
    for e, (q_ref, m_ref, h_ref) in enumerate(((q0, m0, h0), (q1, m1, h1), (q2, m2, h2))):
        query, mixed, raw = q_ref[...], m_ref[...].astype(F32), h_ref[...]
        inner = jnp.sum(mixed * raw, 1, keepdims=True)
        dgates = dgates + jnp.where(lane == e, inner, 0.0)
        gate = gate_ref[:, e : e + 1]
        dmixed = (raw * gate).astype(BF16)
        prob = prob_ref[0, 0, e]
        dval = dval + dot(prob, dmixed, ((0,), (0,)))
        dprob = dot(dmixed, val, ((1,), (1,)))
        delta = jnp.sum(dmixed.astype(F32) * mixed, 1, keepdims=True)
        dscores = (prob.astype(F32) * (dprob - delta)).astype(BF16)
        dquery = dot(dscores, key, ((1,), (0,)))
        dkey = dkey + dot(dscores, query, ((0,), (0,)))
        at = pl.ds(pl.multiple_of(((2 + e) * HEADS + h) * HD, HD), HD)
        grad_out[:, at] = rotated_back(dquery * scale).astype(BF16)
    grad_out[:, pl.ds(pl.multiple_of(h * HD, HD), HD)] = rotated_back(dkey).astype(BF16)
    grad_out[:, pl.ds(pl.multiple_of((HEADS + h) * HD, HD), HD)] = dval.astype(BF16)

    @pl.when(h == 0)
    def _():
        dgate_out[...] = dgates

    @pl.when(h > 0)
    def _():
        dgate_out[...] += dgates


def attention_back(key, val, que, mix, raw, prob, cosine, sine, gates):
    groups, tokens = prob.shape[0], prob.shape[-1]
    column, rows = block_specs(tokens)
    thirds = [column(n) for n in range(3)]
    grads = jax.ShapeDtypeStruct((groups * tokens, 5 * HEADS * HD), BF16)
    return pl.pallas_call(
        attention_back_body,
        grid=(groups, HEADS),
        in_specs=[column(0), column(0)]
        + thirds * 3
        + [prob_spec(tokens)]
        + [rows(HD)] * 2
        + [rows(gates.shape[1])],
        out_specs=[rows(grads.shape[1]), rows(HD)],
        out_shape=[grads, jax.ShapeDtypeStruct((groups * tokens, HD), F32)],
        compiler_params=pltpu.CompilerParams(vmem_limit_bytes=48 * MIB),
        name="attention_back",
    )(key, val, que, que, que, mix, mix, mix, raw, raw, raw, prob, cosine, sine, gates)


def positions(segments):
    index = jnp.arange(segments.shape[0], dtype=jnp.int32)
    prompt = jnp.sum((segments == 0).astype(jnp.int32))
    first = jnp.sum((segments == 1).astype(jnp.int32))
    before = jnp.where(segments == 0, 0, jnp.where(segments == 1, prompt, prompt + first))
    return jnp.where(segments == 0, index, prompt + index - before)


def route_gates(logits, routes, count):
    onehot = (routes[:, :, None] == jnp.arange(count, dtype=jnp.int32)).astype(F32)
    chosen = jnp.sum(onehot * logits[:, None, :], -1)
    expsum = jnp.exp(chosen - jnp.max(chosen, -1, keepdims=True))
    weights = expsum / jnp.sum(expsum, -1, keepdims=True)
    return weights, onehot, jnp.sum(weights[:, :, None] * onehot, 1)


def router_back(dgate, weights, onehot):
    dchosen = jnp.sum(dgate[:, None, :] * onehot, -1)
    dselect = weights * (dchosen - jnp.sum(weights * dchosen, -1, keepdims=True))
    return jnp.sum(dselect[:, :, None] * onehot, 1).astype(BF16)


def normalize(activations):
    inverse = lax.rsqrt(jnp.mean(activations * activations, -1, keepdims=True) + EPSILON)
    return activations * inverse, inverse


def reorder(rows):
    count, width = rows.shape
    return jnp.transpose(rows.reshape(count, 4, 2, 4, width // 32), (0, 3, 2, 1, 4)).reshape(count, width)


def pad_to(array, width):
    return jnp.pad(array, ((0, 0), (0, width - array.shape[1])))


def on_device(
    inputs,
    segments,
    att_routes,
    mlp_routes,
    key_value,
    query_proj,
    output_proj,
    router_att,
    gain_att,
    gate_up,
    down_proj,
    router_mlp,
    gain_mlp,
    out_grad,
):
    width = inputs.shape[1]
    inner = query_proj.shape[2]
    hidden_local = down_proj.shape[1]
    att_count = query_proj.shape[0]
    mlp_count = gate_up.shape[0]
    share = gate_up.shape[1]
    part = inner // 2
    qkv_cols = (2 + att_count) * part
    small_at = qkv_cols
    out_at = qkv_cols + 128
    small = jnp.concatenate([router_att, router_mlp, gain_att[:, None], gain_mlp[:, None]], 1)
    own_att = jnp.concatenate(
        [
            jnp.transpose(key_value.reshape(share, 2, 2, part), (2, 0, 1, 3)).reshape(2, share, -1),
            jnp.transpose(query_proj.reshape(att_count, share, 2, part), (2, 1, 0, 3)).reshape(
                2, share, -1
            ),
            jnp.broadcast_to(pad_to(small, 128), (2, share, 128)),
            jnp.transpose(output_proj.reshape(att_count, 2, part, share), (1, 3, 0, 2)).reshape(
                2, share, -1
            ),
        ],
        2,
    )
    inputs = reorder(inputs)
    out_grad = reorder(out_grad)
    x_all = lax.all_gather(inputs, ("xl", *TP), axis=0, tiled=True)
    grad_all = lax.all_gather(out_grad, TP, axis=0, tiled=True)
    marks = pad_to(jnp.concatenate([segments[:, None], att_routes], 1), LANES).astype(BF16)
    weights, up_parts, down_parts, marks = gather_dp(
        own_att,
        gate_up.reshape(mlp_count, share, -1),
        jnp.swapaxes(down_proj, 1, 2),
        marks,
    )
    marks = marks[:, :, :3].astype(jnp.int32)
    up_whole = lax.all_gather(
        up_parts.reshape(2 * mlp_count * share, -1), "z", axis=0, tiled=True
    )
    down_whole = lax.all_gather(
        down_parts.reshape(2 * mlp_count * share, -1), "z", axis=0, tiled=True
    )

    tokens = segments.shape[0]
    match = jnp.sum((mlp_routes[:, :, None] == jnp.arange(mlp_count, dtype=jnp.int32)).astype(BF16), 1)
    index = jnp.arange(tokens, dtype=jnp.int32)
    lower = (index[None, :] < index[:, None]).astype(BF16)
    rank = dot(lower, match, ((1,), (0,)))
    slot = jnp.where(match > 0, rank.astype(jnp.int32), -1)
    pick = (slot.T[:, None, :] == jnp.arange(CAP, dtype=jnp.int32)[None, :, None]).astype(BF16)
    pick_rows = pick.reshape(mlp_count * CAP, tokens)
    small_all = weights[:, small_at : small_at + 128].astype(F32)
    gain_one, gain_two = small_all[:, 7], small_all[:, 8]
    segments = marks[:, :, 0]
    att_routes = marks[:, :, 1:].reshape(2 * tokens, 2)
    places = jax.vmap(positions)(segments).reshape(-1).astype(F32)
    frequency = ROPE_BASE ** (-2.0 * jnp.arange(HD // 2, dtype=F32) / HD)
    angles = places[:, None] * frequency[None, :]
    cosine = jnp.concatenate([jnp.cos(angles)] * 2, 1)
    sine = jnp.concatenate([-jnp.sin(angles), jnp.sin(angles)], 1)
    normed_one, _ = normalize(x_all.astype(F32))
    unit_one = (normed_one * gain_one).astype(BF16)
    joined_att = dot(unit_one, weights[:, :out_at], ((1,), (0,)))
    weights_att, onehot_att, gate_att = route_gates(
        joined_att[:, small_at : small_at + att_count], att_routes, att_count
    )
    key_rot, val_rows, queries, mixed, gmixed, prob = attention_forward(
        joined_att, cosine, sine, segments, gate_att
    )
    out_weights = weights[:, out_at:]
    attention = dot(gmixed, out_weights, ((1,), (1,))).astype(BF16)
    middle, unit_two, grad_in = middle_and_unit(attention, inputs, gain_two, pick, grad_all)

    router_two = weights[:, small_at + att_count : small_at + att_count + mlp_count]
    logit_mlp = dot(unit_two, router_two, ((1,), (0,)))
    weights_mlp, onehot_mlp, gate_mlp = route_gates(logit_mlp, mlp_routes, mlp_count)
    gate_high = gate_mlp.astype(BF16)
    gate_low = (gate_mlp - gate_high.astype(F32)).astype(BF16)
    extended = jnp.concatenate([unit_two, pad_to(jnp.concatenate([gate_high, gate_low], 1), 128)], 1)
    rows_out = dot(pick_rows, extended, ((1,), (0,))).astype(BF16)
    rows_ext, raw = rows_to_experts(
        rows_out.reshape(mlp_count, CAP, width + 128), grad_in, down_whole
    )
    rows_ext = rows_ext.reshape(mlp_count * CAP, width + 128)
    gates_ext = rows_ext[:, width : width + 2 * mlp_count].astype(F32)
    mine = (jnp.arange(2 * mlp_count) % mlp_count == lax.axis_index("y")).astype(F32)
    gates_in = jnp.sum(gates_ext * mine, 1, keepdims=True)
    dgate_pre, dlinear, hidden, gated, dgate_part = experts(rows_ext, raw, up_whole, gates_in)
    grad_down_whole = dot(grad_in, gated, ((0,), (0,))).astype(BF16)
    dgate_part, grad_down_whole = lax.optimization_barrier((dgate_part, grad_down_whole))
    grad_down_sum = lax.psum_scatter(grad_down_whole, ("z", "xl"), scatter_dimension=0, tiled=True)
    dunit_back, dgate_back, grad_up_whole = return_rows(
        dgate_pre, dlinear, up_whole, dgate_part.reshape(mlp_count, CAP, LANES), rows_ext
    )
    grad_up_sum = lax.psum_scatter(grad_up_whole, "z", scatter_dimension=0, tiled=True)
    pick_half = lax.dynamic_slice_in_dim(pick, lax.axis_index("core") * (CAP // 2), CAP // 2, 1)
    dgate_two = jnp.sum(pick_half.astype(F32) * jnp.sum(dgate_back, -1, keepdims=True), 1).T
    dlogit_mlp = router_back(dgate_two, weights_mlp, onehot_mlp)
    dunit_two = dot(
        pick_half.reshape(-1, tokens), dunit_back.reshape(-1, width), ((0,), (0,))
    ) + dot(dlogit_mlp, router_two, ((1,), (1,)))
    grad_rmlp = dot(unit_two, dlogit_mlp, ((0,), (0,)))
    dmiddle, grad_gain_two, dattention, branch_back = middle_back(
        dunit_two.astype(BF16), middle, out_grad, gain_two, hidden, down_whole
    )

    raw = dot(dattention, out_weights, ((1,), (0,)))
    grad_qkv, dgate_one = attention_back(
        key_rot, val_rows, queries, mixed, raw, prob, cosine, sine, gate_att
    )
    dlogit_att = router_back(dgate_one[:, :att_count], weights_att, onehot_att)
    grad_joined = jnp.concatenate([grad_qkv, pad_to(dlogit_att, 128)], 1)
    dunit_one = dot(grad_joined, weights[:, :out_at], ((1,), (1,)))
    grad_gain_one = jnp.sum(dunit_one * normed_one, 0)
    grad_small = jnp.concatenate(
        [
            dot(unit_one, dlogit_att, ((0,), (0,))),
            grad_rmlp,
            grad_gain_one[:, None],
            grad_gain_two[:, None],
        ],
        1,
    )
    gate_slots = jnp.sum(pick_half.astype(F32) * gate_mlp.T[:, None, :], -1, keepdims=True)
    feed = dot(
        pick_half.reshape(-1, tokens),
        (branch_back.astype(F32) * gate_slots).astype(BF16).reshape(-1, width),
        ((0,), (0,)),
    )
    summed_att, ups_sum, downs_sum, output, grad_input, small_sum = finish(
        (
            dot(unit_one, grad_qkv, ((0,), (0,))).astype(BF16),
            pad_to(grad_small, 128).astype(BF16),
            dot(dattention, gmixed, ((0,), (0,))).astype(BF16),
        ),
        grad_up_sum,
        grad_down_sum,
        dunit_one.astype(BF16),
        feed.astype(BF16),
        inputs,
        middle,
        dmiddle,
        gain_one,
    )
    grad_kv = jnp.transpose(
        summed_att[:, :, : 2 * part].reshape(2, share, 2, part), (1, 2, 0, 3)
    ).reshape(share, 2, inner)
    grad_query = jnp.transpose(
        summed_att[:, :, 2 * part : qkv_cols].reshape(2, share, att_count, part), (2, 1, 0, 3)
    ).reshape(att_count, share, inner)
    grad_output = jnp.transpose(
        summed_att[:, :, out_at:].reshape(2, share, att_count, part), (2, 0, 3, 1)
    ).reshape(att_count, inner, share)
    output = reorder(output)
    grad_input = reorder(grad_input)

    grads_up = ups_sum.astype(F32).reshape(mlp_count, share, 2, hidden_local)
    grads_down = jnp.swapaxes(downs_sum.astype(F32), 1, 2)
    return (
        output,
        grad_input,
        grad_kv,
        grad_query,
        grad_output,
        small_sum[:, :3],
        small_sum[:, 7],
        grads_up,
        grads_down,
        small_sum[:, 3:7],
        small_sum[:, 8],
    )


def solution(mesh):
    fine = Mesh(mesh.devices.reshape(4, 2, 4, 2, 2), ALL)
    return jax.shard_map(
        on_device,
        mesh=fine,
        in_specs=(
            P(ALL, None),
            P(DP),
            P(DP, None),
            P(DP, None),
            P(DP, None, TP),
            P(None, DP, TP),
            P(None, TP, DP),
            P(DP, None),
            P(DP),
            P(None, DP, None, TP),
            P(None, TP, DP),
            P(DP, None),
            P(DP),
            P(ALL, None),
        ),
        out_specs=(
            P(ALL, None),
            P(ALL, None),
            P(DP, None, TP),
            P(None, DP, TP),
            P(None, TP, DP),
            P(DP, None),
            P(DP),
            P(None, DP, None, TP),
            P(None, TP, DP),
            P(DP, None),
            P(DP),
        ),
        check_vma=False,
    )
```

```python
import functools
import math

import jax
import jax.numpy as jnp
from jax import lax
from jax.experimental import pallas as pl
from jax.experimental.pallas import tpu as pltpu
from jax.sharding import Mesh, PartitionSpec as P

LANES = 128
WIDE = 256
HD = 128
HEADS = 2
CAP = 320
EPSILON = 1e-06
NEGATIVE = -1e30
ROPE_BASE = 10000.0
MESH_ID = pl.DeviceIdType.MESH
MIB = 1024 * 1024
DP = ("y", "xl", "z")
TP = ("xh", "core")
ALL = DP + TP
F32 = jnp.float32
BF16 = jnp.bfloat16


def mod4(place):
    return lax.rem(place + 4, 4)


def neighbour(axis, step):
    size = 4 if axis in ("y", "z") else 2
    return {axis: lax.rem(lax.axis_index(axis) + step + size, size)}


def chip_along(step):
    at = lax.rem(lax.axis_index("xh") * 2 + lax.axis_index("xl") + step + 4, 4)
    return {"xh": lax.div(at, 2), "xl": lax.rem(at, 2)}


def greet(*devices):
    barrier = pltpu.get_barrier_semaphore()
    for device in devices:
        pl.semaphore_signal(barrier, inc=1, device_id=device, device_id_type=MESH_ID)
    pl.semaphore_wait(barrier, len(devices))


def arrived(ref, sem):
    pltpu.make_async_copy(ref, ref, sem).wait()


class Sends:
    def __init__(self):
        self.copies = []

    def __call__(self, src, dst, send_sem, recv_sem, device):
        copy = pltpu.make_async_remote_copy(
            src_ref=src,
            dst_ref=dst,
            send_sem=send_sem,
            recv_sem=recv_sem,
            device_id=device,
            device_id_type=MESH_ID,
        )
        copy.start()
        self.copies.append(copy)

    def finish(self):
        for copy in self.copies:
            copy.wait_send()


def gather_body(
    x_ref, ups_ref, downs_ref, marks_ref, out_ref, up_ref, down_ref, marks_out,
    loc, xs, xr, s1, r1m, r1p, f1s, f1r, s2, r2m, r2p, f2s, f2r, es, er, ex, ey, ms, mr,
):
    y, xl, z = lax.axis_index("y"), lax.axis_index("xl"), lax.axis_index("z")
    rows, cols = x_ref.shape[1:]
    half = rows // 2
    split = cols // (3 * LANES) * LANES
    columns = (pl.ds(0, split), pl.ds(split, cols - split))
    greet(
        neighbour("xl", 1),
        *(neighbour("y", step) for step in (1, 2, 3)),
        *(neighbour("z", step) for step in (1, -1)),
    )
    rings = (("z", "y"), ("y", "z"))
    place = {"y": y, "z": z}
    other = 1 - xl
    both = pl.ds(0, 2)
    sends = Sends()
    send = sends

    def slot(h, first, second, j, start, count):
        yy, zz = (second, first) if h == 0 else (first, second)
        return out_ref.at[zz, j, yy, pl.ds(start, count), columns[h]]

    own = pltpu.make_async_copy(x_ref.at[xl], out_ref.at[z, xl, y], loc.at[0])
    own.start()
    own_marks = pltpu.make_async_copy(marks_ref, marks_out.at[xl], loc.at[3])
    own_marks.start()
    send(marks_ref, marks_out.at[xl], ms, mr, neighbour("xl", 1))
    experts = ((ups_ref, up_ref), (downs_ref, down_ref))
    kept = []
    for n, (shards, expert) in enumerate(experts):
        kept.append(pltpu.make_async_copy(shards.at[y], expert.at[xl, y], loc.at[1 + n]))
        kept[-1].start()
        send(shards.at[y], expert.at[xl, y], ex.at[n, 0], ey.at[n, 0], neighbour("xl", 1))
        for step in (1, 3, 2):
            send(
                shards.at[mod4(y + step)],
                expert.at[xl, y],
                es.at[n, step - 1],
                er.at[n, step - 1],
                neighbour("y", step),
            )
    for h in (0, 1):
        first, second = place[rings[h][0]], place[rings[h][1]]
        src = x_ref.at[xl, :, columns[h]]
        dst = slot(h, first, second, xl, 0, rows)
        send(x_ref.at[other, :, columns[h]], dst, xs.at[h], xr.at[h], neighbour("xl", 1))
        send(src, dst, s1.at[h, 0, 0], r1m.at[h, 0], neighbour(rings[h][0], 1))
        send(src, dst, s1.at[h, 0, 1], r1p.at[h, 0], neighbour(rings[h][0], -1))
    own.wait()

    def send_second(h, k, first):
        block = slot(h, first, place[rings[h][1]], both, 0, rows)
        send(block, block, s2.at[h, k, 0], r2m.at[h, k], neighbour(rings[h][1], 1))
        send(block, block, s2.at[h, k, 1], r2p.at[h, k], neighbour(rings[h][1], -1))

    for h in (0, 1):
        first, second = place[rings[h][0]], place[rings[h][1]]
        block = slot(h, first, second, other, 0, rows)
        arrived(block, xr.at[h])
        send(block, block, s1.at[h, 1, 0], r1m.at[h, 1], neighbour(rings[h][0], 1))
        send(block, block, s1.at[h, 1, 1], r1p.at[h, 1], neighbour(rings[h][0], -1))
        send_second(h, 0, first)
    for j, jx in ((0, xl), (1, other)):
        for h in (0, 1):
            first, second = place[rings[h][0]], place[rings[h][1]]
            arrived(slot(h, mod4(first - 1), second, jx, 0, rows), r1m.at[h, j])
            block = slot(h, mod4(first - 1), second, jx, 0, half)
            send(block, block, f1s.at[h, j, 0], f1r.at[h, j, 0], neighbour(rings[h][0], 1))
            arrived(slot(h, mod4(first + 1), second, jx, 0, rows), r1p.at[h, j])
            block = slot(h, mod4(first + 1), second, jx, half, half)
            send(block, block, f1s.at[h, j, 1], f1r.at[h, j, 1], neighbour(rings[h][0], -1))
    for k, step in ((1, -1), (2, 1)):
        for h in (0, 1):
            send_second(h, k, mod4(place[rings[h][0]] + step))
    for h in (0, 1):
        first, second = place[rings[h][0]], place[rings[h][1]]
        for j, jx in ((0, xl), (1, other)):
            for p in (0, 1):
                block = slot(h, mod4(first + 2), second, jx, p * half, half)
                arrived(block, f1r.at[h, j, p])
        send_second(h, 3, mod4(first + 2))
    for n, (shards, expert) in enumerate(experts):
        for step in (1, 3, 2):
            landed = expert.at[xl, mod4(y - step)]
            arrived(landed, er.at[n, step - 1])
            send(landed, landed, ex.at[n, step], ey.at[n, step], neighbour("xl", 1))
    steps = ((0, 0), (1, -1), (2, 1), (3, 2))
    for k, step in steps:
        for h in (0, 1):
            first, second = mod4(place[rings[h][0]] + step), place[rings[h][1]]
            arrived(slot(h, first, mod4(second - 1), both, 0, rows), r2m.at[h, k])
            block = slot(h, first, mod4(second - 1), both, 0, half)
            send(block, block, f2s.at[h, k, 0], f2r.at[h, k, 0], neighbour(rings[h][1], 1))
            arrived(slot(h, first, mod4(second + 1), both, 0, rows), r2p.at[h, k])
            block = slot(h, first, mod4(second + 1), both, half, half)
            send(block, block, f2s.at[h, k, 1], f2r.at[h, k, 1], neighbour(rings[h][1], -1))
    for k, step in steps:
        for h in (0, 1):
            first, second = mod4(place[rings[h][0]] + step), place[rings[h][1]]
            for p in (0, 1):
                block = slot(h, first, mod4(second + 2), both, p * half, half)
                arrived(block, f2r.at[h, k, p])
    for n, (shards, expert) in enumerate(experts):
        for step in (0, 1, 3, 2):
            arrived(expert.at[other, mod4(y - step)], ey.at[n, step])
        kept[n].wait()
    arrived(marks_out.at[other], mr)
    own_marks.wait()
    sends.finish()


def gather_dp(shard, ups, downs, marks):
    _, rows, cols = shard.shape
    dma = pltpu.SemaphoreType.DMA
    whole, up, down, marks = pl.pallas_call(
        gather_body,
        out_shape=[
            jax.ShapeDtypeStruct((4, 2, 4, rows, cols), shard.dtype),
            jax.ShapeDtypeStruct((2, *ups.shape), ups.dtype),
            jax.ShapeDtypeStruct((2, *downs.shape), downs.dtype),
            jax.ShapeDtypeStruct((2, *marks.shape), marks.dtype),
        ],
        in_specs=[pl.BlockSpec(memory_space=pl.ANY)] * 4,
        out_specs=[pl.BlockSpec(memory_space=pl.ANY)] * 4,
        scratch_shapes=[
            dma((4,)),
            dma((2,)),
            dma((2,)),
            dma((2, 2, 2)),
            dma((2, 2)),
            dma((2, 2)),
            dma((2, 2, 2)),
            dma((2, 2, 2)),
            dma((2, 4, 2)),
            dma((2, 4)),
            dma((2, 4)),
            dma((2, 4, 2)),
            dma((2, 4, 2)),
            dma((2, 3)),
            dma((2, 3)),
            dma((2, 4)),
            dma((2, 4)),
            dma,
            dma,
        ],
        compiler_params=pltpu.CompilerParams(collective_id=0, has_side_effects=True),
        name="gather_weights",
    )(shard, ups, downs, marks)
    return whole.reshape(32 * rows, cols), up, down, marks


def reduce_stages(scatter_count, part_refs, core_buf, sum_buf, far_buf, core_s, core_r, far_s, far_r, sends):
    xh, core = lax.axis_index("xh"), lax.axis_index("core")
    rows = part_refs[0].shape[1]
    step = rows // scatter_count
    far, here = 1 - xh, xh
    for n, chunk in enumerate(range(0, rows, step)):
        at = pl.ds(chunk, step)
        for i, part in enumerate(part_refs):
            sends(
                part.at[far * 2 + 1 - core, at],
                core_buf.at[i, 0, at],
                core_s.at[i, n, 0],
                core_r.at[i, n, 0],
                neighbour("core", 1),
            )
    for n, chunk in enumerate(range(0, rows, step)):
        at = pl.ds(chunk, step)
        for i, part in enumerate(part_refs):
            sends(
                part.at[here * 2 + 1 - core, at],
                core_buf.at[i, 1, at],
                core_s.at[i, n, 1],
                core_r.at[i, n, 1],
                neighbour("core", 1),
            )
    yield
    for n, chunk in enumerate(range(0, rows, step)):
        at = pl.ds(chunk, step)
        for i, part in enumerate(part_refs):
            arrived(core_buf.at[i, 0, at], core_r.at[i, n, 0])
            mine = part[far * 2 + core, chunk : chunk + step, :].astype(F32)
            sum_buf[i, chunk : chunk + step, :] = (
                mine + core_buf[i, 0, chunk : chunk + step, :].astype(F32)
            ).astype(BF16)
            sends(
                sum_buf.at[i, at],
                far_buf.at[i, at],
                far_s.at[i, n],
                far_r.at[i, n],
                neighbour("xh", 1),
            )
    yield

    def total(i, n):
        chunk = n * step
        at = pl.ds(chunk, step)
        arrived(core_buf.at[i, 1, at], core_r.at[i, n, 1])
        near = part_refs[i][here * 2 + core, chunk : chunk + step, :].astype(F32)
        near = near + core_buf[i, 1, chunk : chunk + step, :].astype(F32)
        arrived(far_buf.at[i, at], far_r.at[i, n])
        return near + far_buf[i, chunk : chunk + step, :].astype(F32)

    yield total


def ring_reduce_stages(part_ref, core_buf, sum_buf, via_buf, far_buf, core_s, core_r, ring_s, ring_r, sends):
    xl, xh, core = lax.axis_index("xl"), lax.axis_index("xh"), lax.axis_index("core")
    rows = part_ref.shape[3]
    half = rows // 2
    at = xh * 2 + xl
    chips = [lax.rem(at + step, 4) for step in (2, 1, 3, 0)]
    chips = [(lax.rem(chip, 2), lax.div(chip, 2)) for chip in chips]
    for n, (pxl, pxh) in enumerate(chips):
        sends(
            part_ref.at[pxl, pxh, 1 - core],
            core_buf.at[n],
            core_s.at[n],
            core_r.at[n],
            neighbour("core", 1),
        )

    def own(n, start):
        pxl, pxh = chips[n]
        return part_ref[pxl, pxh, core, start : start + half, :].astype(F32)

    def both(n, start):
        return own(n, start) + core_buf[n, start : start + half, :].astype(F32)

    first, second = pl.ds(0, half), pl.ds(half, half)
    ahead, behind = chip_along(1), chip_along(-1)
    yield
    arrived(core_buf.at[0], core_r.at[0])
    sum_buf[0, :half, :] = both(0, 0).astype(BF16)
    sends(sum_buf.at[0, first], via_buf.at[0], ring_s.at[0], ring_r.at[0], ahead)
    sum_buf[0, half:, :] = both(0, half).astype(BF16)
    sends(sum_buf.at[0, second], via_buf.at[1], ring_s.at[1], ring_r.at[1], behind)
    arrived(core_buf.at[1], core_r.at[1])
    sum_buf[1, half:, :] = both(1, half).astype(BF16)
    sends(sum_buf.at[1, second], far_buf.at[0, second], ring_s.at[2], ring_r.at[2], ahead)
    arrived(core_buf.at[2], core_r.at[2])
    sum_buf[2, :half, :] = both(2, 0).astype(BF16)
    sends(sum_buf.at[2, first], far_buf.at[1, first], ring_s.at[3], ring_r.at[3], behind)
    yield
    arrived(via_buf.at[0], ring_r.at[0])
    sum_buf[1, :half, :] = (both(1, 0) + via_buf[0].astype(F32)).astype(BF16)
    sends(sum_buf.at[1, first], far_buf.at[0, first], ring_s.at[4], ring_r.at[4], ahead)
    arrived(via_buf.at[1], ring_r.at[1])
    sum_buf[2, half:, :] = (both(2, half) + via_buf[1].astype(F32)).astype(BF16)
    sends(sum_buf.at[2, second], far_buf.at[1, second], ring_s.at[5], ring_r.at[5], behind)
    arrived(core_buf.at[3], core_r.at[3])

    def total(part):
        rows_at = first if part == 0 else second
        start = part * half
        near = both(3, start)
        arrived(far_buf.at[0, rows_at], ring_r.at[4 if part == 0 else 2])
        near = near + far_buf[0, start : start + half, :].astype(F32)
        arrived(far_buf.at[1, rows_at], ring_r.at[3 if part == 0 else 5])
        return near + far_buf[1, start : start + half, :].astype(F32)

    yield total


def ring_reduce_scratch(rows, width):
    dma = pltpu.SemaphoreType.DMA
    return [
        pltpu.VMEM((4, rows, width), BF16),
        pltpu.VMEM((3, rows, width), BF16),
        pltpu.VMEM((2, rows // 2, width), BF16),
        pltpu.VMEM((2, rows, width), BF16),
        dma((4,)),
        dma((4,)),
        dma((6,)),
        dma((6,)),
    ]


def ring_spread(out_ref, part, ring_s, ring_r, core_s, core_r, sends):
    xl, xh, core = lax.axis_index("xl"), lax.axis_index("xh"), lax.axis_index("core")
    half = out_ref.shape[3] // 2
    mine = out_ref.at[xl, xh, core, pl.ds(part * half, half)]
    sends(mine, mine, ring_s.at[part, 0], ring_r.at[part, 0], chip_along(1))
    sends(mine, mine, ring_s.at[part, 1], ring_r.at[part, 1], chip_along(-1))
    sends(mine, mine, core_s.at[part, 0], core_r.at[part, 0], neighbour("core", 1))


def ring_spread_finish(out_ref, ring_s, ring_r, core_s, core_r, sends):
    xl, xh, core = lax.axis_index("xl"), lax.axis_index("xh"), lax.axis_index("core")
    half = out_ref.shape[3] // 2
    at = xh * 2 + xl

    def block(step, part, which):
        chip = lax.rem(at + step + 4, 4)
        return out_ref.at[lax.rem(chip, 2), lax.div(chip, 2), which, pl.ds(part * half, half)]

    for part in (0, 1):
        for n, (step, on) in enumerate(((-1, 1), (1, -1))):
            landed = block(step, part, core)
            arrived(landed, ring_r.at[part, n])
            if part == n:
                sends(landed, landed, ring_s.at[part, 2], ring_r.at[part, 2], chip_along(on))
            sends(landed, landed, core_s.at[part, 1 + n], core_r.at[part, 1 + n], neighbour("core", 1))
    for part in (0, 1):
        landed = block(2, part, core)
        arrived(landed, ring_r.at[part, 2])
        sends(landed, landed, core_s.at[part, 3], core_r.at[part, 3], neighbour("core", 1))
    for part in (0, 1):
        for n, step in enumerate((0, -1, 1, 2)):
            arrived(block(step, part, 1 - core), core_r.at[part, n])


def ring_spread_scratch():
    dma = pltpu.SemaphoreType.DMA
    return [dma((2, 3)), dma((2, 3)), dma((2, 4)), dma((2, 4))]


def along_x():
    return neighbour("core", 1), neighbour("xh", 1), chip_along(1), chip_along(-1)


CHUNKS = 4


def reduce_scratch(count, rows, width):
    dma = pltpu.SemaphoreType.DMA
    return [
        pltpu.VMEM((count, 2, rows, width), BF16),
        pltpu.VMEM((count, rows, width), BF16),
        pltpu.VMEM((count, rows, width), BF16),
        dma((count, CHUNKS, 2)),
        dma((count, CHUNKS, 2)),
        dma((count, CHUNKS)),
        dma((count, CHUNKS)),
    ]


def spread_chunk(out_ref, n, step, sems, sends):
    xh, core = lax.axis_index("xh"), lax.axis_index("core")
    at = pl.ds(n * step, step)
    mine = out_ref.at[xh * 2 + core, at]
    far_s, far_r, core_s, core_r = sems
    sends(mine, mine, far_s.at[n], far_r.at[n], neighbour("xh", 1))
    sends(mine, mine, core_s.at[n, 0], core_r.at[n, 0], neighbour("core", 1))


def spread_finish(out_ref, step, sems, sends):
    xh, core = lax.axis_index("xh"), lax.axis_index("core")
    far_s, far_r, core_s, core_r = sems
    for n in range(CHUNKS):
        at = pl.ds(n * step, step)
        theirs = out_ref.at[(1 - xh) * 2 + core, at]
        arrived(theirs, far_r.at[n])
        sends(theirs, theirs, core_s.at[n, 1], core_r.at[n, 1], neighbour("core", 1))
    for n in range(CHUNKS):
        at = pl.ds(n * step, step)
        arrived(out_ref.at[xh * 2 + 1 - core, at], core_r.at[n, 0])
        arrived(out_ref.at[(1 - xh) * 2 + 1 - core, at], core_r.at[n, 1])


def spread_scratch():
    dma = pltpu.SemaphoreType.DMA
    return [dma((CHUNKS,)), dma((CHUNKS,)), dma((CHUNKS, 2)), dma((CHUNKS, 2))]


def middle_body(part_ref, x_ref, gain_ref, middle_ref, unit_ref, *scratch):
    sends = Sends()
    greet(*along_x())
    *_, total = ring_reduce_stages(part_ref, *scratch[:8], sends)
    me = lax.axis_index("xh") * 2 + lax.axis_index("core")
    step = x_ref.shape[0] // CHUNKS
    half = x_ref.shape[0] // 2
    for part in (0, 1):
        rows = slice(part * half, (part + 1) * half)
        middle = x_ref[rows, :].astype(F32) + total(part)
        middle_ref[rows, :] = middle
        inverse = lax.rsqrt(jnp.mean(middle * middle, 1, keepdims=True) + EPSILON)
        unit_ref[me, rows, :] = (middle * inverse * gain_ref[...]).astype(BF16)
        for n in range(part * CHUNKS // 2, (part + 1) * CHUNKS // 2):
            spread_chunk(unit_ref, n, step, scratch[8:], sends)
    spread_finish(unit_ref, step, scratch[8:], sends)
    sends.finish()


def vmem(count):
    return [pl.BlockSpec(memory_space=pltpu.VMEM)] * count


def middle_and_unit(part, x, gain):
    rows, width = x.shape
    middle, unit = pl.pallas_call(
        middle_body,
        out_shape=[
            jax.ShapeDtypeStruct((rows, width), F32),
            jax.ShapeDtypeStruct((4, rows, width), BF16),
        ],
        in_specs=vmem(3),
        out_specs=vmem(2),
        scratch_shapes=ring_reduce_scratch(rows, width) + spread_scratch(),
        compiler_params=pltpu.CompilerParams(
            collective_id=1, has_side_effects=True, vmem_limit_bytes=32 * MIB
        ),
        name="middle_and_unit",
    )(part.reshape(2, 2, 2, rows, width), x, gain[None])
    return middle, unit.reshape(4 * rows, width)


def back_body(
    part_ref, middle_ref, grad_ref, gain_ref, hidden_ref, down_ref, dmiddle_ref, dgain_ref, spread_ref, branch_out,
    hidden, down, branch, loc, out_sem, *scratch,
):
    sends = Sends()
    loads = []
    for n, (src, dst) in enumerate(((hidden_ref, hidden), (down_ref, down))):
        loads.append(pltpu.make_async_copy(src, dst, loc.at[n]))
        loads[-1].start()
    greet(*along_x())
    stages = reduce_stages(CHUNKS, [part_ref], *scratch[:7], sends)
    next(stages)
    next(stages)
    for load in loads:
        load.wait()
    slots = branch.shape[1]
    outs = []
    for n in range(4):
        branch[n] = dot(hidden[n * slots : (n + 1) * slots, :], down[...], ((1,), (1,))).astype(BF16)
        outs.append(pltpu.make_async_copy(branch.at[n], branch_out.at[n], out_sem.at[n]))
        outs[-1].start()
    total = next(stages)
    xl, xh, core = lax.axis_index("xl"), lax.axis_index("xh"), lax.axis_index("core")
    step = middle_ref.shape[0] // CHUNKS
    for n in range(CHUNKS):
        rows = slice(n * step, (n + 1) * step)
        middle = middle_ref[rows, :]
        inverse = lax.rsqrt(jnp.mean(middle * middle, 1, keepdims=True) + EPSILON)
        normed = middle * inverse
        dunit = total(0, n)
        product = dunit * normed
        dgain = jnp.sum(product, 0, keepdims=True)
        if n == 0:
            dgain_ref[...] = dgain
        else:
            dgain_ref[...] += dgain
        mean = jnp.mean(product * gain_ref[...], 1, keepdims=True)
        dmiddle = grad_ref[rows, :].astype(F32) + inverse * (dunit * gain_ref[...] - normed * mean)
        dmiddle_ref[rows, :] = dmiddle
        spread_ref[xl, xh, core, rows, :] = dmiddle.astype(BF16)
        if n % 2 == 1:
            ring_spread(spread_ref, n // 2, *scratch[7:], sends)
    ring_spread_finish(spread_ref, *scratch[7:], sends)
    for out in outs:
        out.wait()
    sends.finish()


def middle_back(part, middle, grad, gain, hidden, down):
    rows, width = middle.shape
    count, inner = hidden.shape
    slots = count // 4
    dma = pltpu.SemaphoreType.DMA
    anywhere = pl.BlockSpec(memory_space=pl.ANY)
    dmiddle, dgain, spread, branch = pl.pallas_call(
        back_body,
        out_shape=[
            jax.ShapeDtypeStruct((rows, width), F32),
            jax.ShapeDtypeStruct((1, width), F32),
            jax.ShapeDtypeStruct((2, 2, 2, rows, width), BF16),
            jax.ShapeDtypeStruct((4, slots, width), BF16),
        ],
        in_specs=vmem(4) + [anywhere] * 2,
        out_specs=vmem(3) + [anywhere],
        scratch_shapes=[
            pltpu.VMEM((count, inner), BF16),
            pltpu.VMEM(down.shape, BF16),
            pltpu.VMEM((4, slots, width), BF16),
            dma((2,)),
            dma((4,)),
        ]
        + reduce_scratch(1, rows, width)
        + ring_spread_scratch(),
        compiler_params=pltpu.CompilerParams(
            collective_id=2, has_side_effects=True, vmem_limit_bytes=48 * MIB
        ),
        name="middle_back",
    )(part.reshape(4, rows, width), middle, grad, gain[None], hidden, down)
    return dmiddle, dgain[0], spread.reshape(8 * rows, width), branch


def rows_body(
    rows_ref, grad_ref, down_ref, out_ref, raw_out, grad, down, block, loc, out_sem, far_s, far_r, core_s, core_r
):
    y, core = lax.axis_index("y"), lax.axis_index("core")
    half = rows_ref.shape[1] // 2
    sends = Sends()
    greet(neighbour("core", 1), *(neighbour("y", step) for step in (1, 2, 3)))
    at = pl.ds(pl.multiple_of(core * half, half), half)
    own = pltpu.make_async_copy(rows_ref.at[y], out_ref.at[y], loc.at[0])
    own.start()
    loads = []
    for n, (src, dst) in enumerate(((grad_ref, grad), (down_ref, down))):
        loads.append(pltpu.make_async_copy(src, dst, loc.at[1 + n]))
        loads[-1].start()
    for step in (2, 1, 3):
        target = mod4(y + step)
        sends(
            rows_ref.at[target, at],
            out_ref.at[y, at],
            far_s.at[step - 1],
            far_r.at[step - 1],
            neighbour("y", step),
        )
    for load in loads:
        load.wait()
    outs = []
    columns = raw_out.shape[1]
    for n, start in enumerate(range(0, columns, WIDE)):
        cols = min(WIDE, columns - start)
        if n >= 2:
            outs[n - 2].wait()
        block[n % 2, :, :cols] = dot(grad[...], down[:, start : start + cols], ((1,), (0,)))
        outs.append(
            pltpu.make_async_copy(
                block.at[n % 2, :, pl.ds(0, cols)], raw_out.at[:, pl.ds(start, cols)], out_sem.at[n % 2]
            )
        )
        outs[-1].start()
    for step in (1, 3, 2):
        source = mod4(y - step)
        block = out_ref.at[source, at]
        arrived(block, far_r.at[step - 1])
        sends(block, block, core_s.at[step - 1], core_r.at[step - 1], neighbour("core", 1))
    own.wait()
    other = pl.ds(pl.multiple_of((1 - core) * half, half), half)
    for step in (1, 3, 2):
        arrived(out_ref.at[mod4(y - step), other], core_r.at[step - 1])
    for out in outs[-2:]:
        out.wait()
    sends.finish()


def rows_to_experts(rows, grads, down):
    count, hidden = grads.shape[0], down.shape[1]
    anywhere = pl.BlockSpec(memory_space=pl.ANY)
    dma = pltpu.SemaphoreType.DMA
    return pl.pallas_call(
        rows_body,
        out_shape=[
            jax.ShapeDtypeStruct(rows.shape, rows.dtype),
            jax.ShapeDtypeStruct((count, hidden), F32),
        ],
        in_specs=[anywhere] * 3,
        out_specs=[anywhere] * 2,
        scratch_shapes=[
            pltpu.VMEM(grads.shape, BF16),
            pltpu.VMEM(down.shape, BF16),
            pltpu.VMEM((2, count, WIDE), F32),
            dma((3,)),
            dma((2,)),
            dma((3,)),
            dma((3,)),
            dma((3,)),
            dma((3,)),
        ],
        compiler_params=pltpu.CompilerParams(
            collective_id=4, has_side_effects=True, vmem_limit_bytes=40 * MIB
        ),
        name="rows_to_experts",
    )(rows, grads, down)


STEPS = (2, 1, -1, 0)


def finish_body(
    qkv_ref, small_ref, o_ref, ups_ref, downs_ref, part_ref, feed_ref, x_ref, middle_ref, dmiddle_ref, gain_ref,
    out_ref, up_out, down_out, output_ref, dinput_ref, small_out,
    g_ref, loc, t_buf, r_buf, tb_buf, rb_buf, c_buf,
    t_s, t_r, r_s, r_r, tb_s, tb_r, rb_s, rb_r, c_s, c_r,
    up_own, down_own, up_buf, down_buf, up_sum, down_sum, ex, ey, es, er,
    small_own, small_buf, small_s, small_r, *scratch,
):
    xl, xh, core = lax.axis_index("xl"), lax.axis_index("xh"), lax.axis_index("core")
    place = {"y": lax.axis_index("y"), "z": lax.axis_index("z")}
    my_y = place["y"]
    half = g_ref.shape[3] // 2
    quarter = half // 2
    rings = (("z", "y"), ("y", "z"))
    sends = Sends()
    column = 0
    parts = []
    for n, ref in enumerate((qkv_ref, small_ref, o_ref)):
        cols = ref.shape[-1]
        parts.append(pltpu.make_async_copy(ref, g_ref.at[..., pl.ds(column, cols)], loc.at[n]))
        parts[-1].start()
        column += cols
    for n, (ref, own) in enumerate(((ups_ref, up_own), (downs_ref, down_own))):
        parts.append(pltpu.make_async_copy(ref.at[xl], own, loc.at[3 + n]))
        parts[-1].start()
    peers = ({"xh": xh, "core": 1 - core}, {"xh": 1 - xh, "core": core}, {"xh": 1 - xh, "core": 1 - core})
    greet(
        *peers,
        chip_along(1),
        chip_along(-1),
        *(neighbour("y", step) for step in (1, 2, 3)),
        *(neighbour("z", step) for step in (1, -1)),
    )
    both = slice(0, 2)
    ring_stages = ring_reduce_stages(part_ref, *scratch[7:15], sends)
    feed_stages = reduce_stages(CHUNKS, [feed_ref], *scratch[:7], sends)
    experts = ((ups_ref, up_own, up_buf, up_sum, up_out), (downs_ref, down_own, down_buf, down_sum, down_out))
    for n, (grads, _, buf, _, _) in enumerate(experts):
        for step in (2, 1, 3, 0):
            sends(
                grads.at[1 - xl, mod4(my_y + step)],
                buf.at[step],
                ex.at[n, step],
                ey.at[n, step],
                neighbour("xl", 1),
            )
    next(ring_stages)
    next(feed_stages)
    for part in parts[:3]:
        part.wait()

    def grad_ref(h, first, second, start):
        zz, yy = (first, second) if h == 0 else (second, first)
        return g_ref.at[zz, both, yy, pl.ds(h * half + start, quarter)]

    def grad(h, first, second, j, start, count):
        zz, yy = (first, second) if h == 0 else (second, first)
        return g_ref[zz, j, yy, h * half + start : h * half + start + count, :].astype(F32)

    def firsts(h, k):
        return mod4(place[rings[h][0]] + STEPS[k])

    for k in range(4):
        for h in (0, 1):
            second = place[rings[h][1]]
            for d, way in ((0, 1), (1, -1)):
                sends(
                    grad_ref(h, firsts(h, k), mod4(second + 2), d * quarter),
                    t_buf.at[h, d, k],
                    t_s.at[h, d, k],
                    t_r.at[h, d, k],
                    neighbour(rings[h][1], way),
                )
    for k in range(4):
        for h in (0, 1):
            second = place[rings[h][1]]
            for d, way in ((0, 1), (1, -1)):
                sends(
                    grad_ref(h, firsts(h, k), mod4(second + way), (1 - d) * quarter),
                    r_buf.at[h, d, k, both, pl.ds((1 - d) * quarter, quarter)],
                    r_s.at[h, d, k, 0],
                    r_r.at[h, d, k, 0],
                    neighbour(rings[h][1], way),
                )
    next(ring_stages)
    next(feed_stages)
    for k in range(4):
        for h in (0, 1):
            second = place[rings[h][1]]
            for d, way in ((0, 1), (1, -1)):
                arrived(t_buf.at[h, d, k], t_r.at[h, d, k])
                for j in (0, 1):
                    t_buf[h, d, k, j] = (
                        t_buf[h, d, k, j].astype(F32)
                        + grad(h, firsts(h, k), mod4(second + way), j, d * quarter, quarter)
                    ).astype(BF16)
                sends(
                    t_buf.at[h, d, k],
                    r_buf.at[h, d, k, both, pl.ds(d * quarter, quarter)],
                    r_s.at[h, d, k, 1],
                    r_r.at[h, d, k, 1],
                    neighbour(rings[h][1], way),
                )
    total = next(ring_stages)
    for part in parts[3:]:
        part.wait()
    for n, (_, own, buf, summed, result) in enumerate(experts):
        for step in (2, 1, 3, 0):
            target = mod4(my_y + step)
            arrived(buf.at[step], ey.at[n, step])
            value = (own[target].astype(F32) + buf[step].astype(F32)).astype(BF16)
            if step == 0:
                result[my_y] = value
            else:
                summed[step - 1] = value
                sends(
                    summed.at[step - 1],
                    result.at[my_y],
                    es.at[n, step - 1],
                    er.at[n, step - 1],
                    neighbour("y", step),
                )
    for k in range(4):
        for h in (0, 1):
            second = place[rings[h][1]]
            for d in (0, 1):
                arrived(r_buf.at[h, d, k, both, pl.ds((1 - d) * quarter, quarter)], r_r.at[h, d, k, 0])
                arrived(r_buf.at[h, d, k, both, pl.ds(d * quarter, quarter)], r_r.at[h, d, k, 1])
            for j in (0, 1):
                r_buf[h, 0, k, j] = (
                    r_buf[h, 0, k, j].astype(F32)
                    + r_buf[h, 1, k, j].astype(F32)
                    + grad(h, firsts(h, k), second, j, 0, half)
                ).astype(BF16)
            for d, way in ((0, 1), (1, -1)):
                device = neighbour(rings[h][0], way)
                if k == 0:
                    sends(
                        r_buf.at[h, 0, 0, both, pl.ds(d * quarter, quarter)],
                        tb_buf.at[h, d],
                        tb_s.at[h, d],
                        tb_r.at[h, d],
                        device,
                    )
                if k == 1 + d:
                    sends(
                        r_buf.at[h, 0, k, both, pl.ds((1 - d) * quarter, quarter)],
                        rb_buf.at[h, d, both, pl.ds((1 - d) * quarter, quarter)],
                        rb_s.at[h, d, 0],
                        rb_r.at[h, d, 0],
                        device,
                    )
                    arrived(tb_buf.at[h, d], tb_r.at[h, d])
                    for j in (0, 1):
                        tb_buf[h, d, j] = (
                            tb_buf[h, d, j].astype(F32)
                            + r_buf[h, 0, k, j, d * quarter : (d + 1) * quarter, :].astype(F32)
                        ).astype(BF16)
                    sends(
                        tb_buf.at[h, d],
                        rb_buf.at[h, d, both, pl.ds(d * quarter, quarter)],
                        rb_s.at[h, d, 1],
                        rb_r.at[h, d, 1],
                        device,
                    )
    rows_half = x_ref.shape[0] // 2
    for part in (0, 1):
        rows = slice(part * rows_half, (part + 1) * rows_half)
        x = x_ref[rows, :].astype(F32)
        inverse = lax.rsqrt(jnp.mean(x * x, 1, keepdims=True) + EPSILON)
        normed = x * inverse
        dscaled = total(part) * gain_ref[...]
        mean = jnp.mean(dscaled * normed, 1, keepdims=True)
        dinput_ref[rows, :] = dmiddle_ref[rows, :] + inverse * (dscaled - normed * mean)
    for h in (0, 1):
        for d in (0, 1):
            arrived(rb_buf.at[h, d, both, pl.ds((1 - d) * quarter, quarter)], rb_r.at[h, d, 0])
            arrived(rb_buf.at[h, d, both, pl.ds(d * quarter, quarter)], rb_r.at[h, d, 1])
        for j in (0, 1):
            rb_buf[h, 0, j] = (
                rb_buf[h, 0, j].astype(F32)
                + rb_buf[h, 1, j].astype(F32)
                + r_buf[h, 0, 3, j].astype(F32)
            ).astype(BF16)
        sends(rb_buf.at[h, 0, 1 - xl], c_buf.at[h], c_s.at[h], c_r.at[h], neighbour("xl", 1))
        out_ref[xl, h * half : (h + 1) * half, :] = rb_buf[h, 0, xl].astype(F32)
    for h in (0, 1):
        arrived(c_buf.at[h], c_r.at[h])
        out_ref[1 - xl, h * half : (h + 1) * half, :] = c_buf[h].astype(F32)
    first, last = qkv_ref.shape[-1], qkv_ref.shape[-1] + small_ref.shape[-1]
    small_own[...] = out_ref[0, :, first:last] + out_ref[1, :, first:last]
    for n, peer in enumerate(peers):
        sends(small_own, small_buf.at[n], small_s.at[n], small_r.at[n], peer)
    feed = next(feed_stages)
    step = x_ref.shape[0] // CHUNKS
    for n in range(CHUNKS):
        rows = slice(n * step, (n + 1) * step)
        output_ref[rows, :] = (middle_ref[rows, :] + feed(0, n)).astype(BF16)
    for n, (_, _, _, _, result) in enumerate(experts):
        for step in (1, 3, 2):
            arrived(result.at[mod4(my_y - step)], er.at[n, step - 1])
    for n in range(3):
        arrived(small_buf.at[n], small_r.at[n])
    small_out[...] = (small_own[...] + small_buf[1]) + (small_buf[0] + small_buf[2])
    sends.finish()


def finish(grads, ups, downs, part, feed, x, middle, dmiddle, gain):
    rows, cols = grads[0].shape[0], sum(grad.shape[1] for grad in grads)
    share = rows // 32
    half, quarter = share // 2, share // 4
    dma = pltpu.SemaphoreType.DMA
    up_cols, down_cols = ups.shape[1], downs.shape[1]
    small = (share, grads[1].shape[1])
    own_rows, width = x.shape
    anywhere = pl.BlockSpec(memory_space=pl.ANY)
    return pl.pallas_call(
        finish_body,
        out_shape=[
            jax.ShapeDtypeStruct((2, share, cols), F32),
            jax.ShapeDtypeStruct((4, share, up_cols), BF16),
            jax.ShapeDtypeStruct((4, share, down_cols), BF16),
            jax.ShapeDtypeStruct((own_rows, width), BF16),
            jax.ShapeDtypeStruct((own_rows, width), F32),
            jax.ShapeDtypeStruct(small, F32),
        ],
        in_specs=[anywhere] * 5 + vmem(6),
        out_specs=vmem(6),
        scratch_shapes=[
            pltpu.VMEM((4, 2, 4, share, cols), BF16),
            dma((5,)),
            pltpu.VMEM((2, 2, 4, 2, quarter, cols), BF16),
            pltpu.VMEM((2, 2, 4, 2, half, cols), BF16),
            pltpu.VMEM((2, 2, 2, quarter, cols), BF16),
            pltpu.VMEM((2, 2, 2, half, cols), BF16),
            pltpu.VMEM((2, half, cols), BF16),
            dma((2, 2, 4)),
            dma((2, 2, 4)),
            dma((2, 2, 4, 2)),
            dma((2, 2, 4, 2)),
            dma((2, 2)),
            dma((2, 2)),
            dma((2, 2, 2)),
            dma((2, 2, 2)),
            dma((2,)),
            dma((2,)),
            pltpu.VMEM((4, share, up_cols), BF16),
            pltpu.VMEM((4, share, down_cols), BF16),
            pltpu.VMEM((4, share, up_cols), BF16),
            pltpu.VMEM((4, share, down_cols), BF16),
            pltpu.VMEM((3, share, up_cols), BF16),
            pltpu.VMEM((3, share, down_cols), BF16),
            dma((2, 4)),
            dma((2, 4)),
            dma((2, 3)),
            dma((2, 3)),
            pltpu.VMEM(small, F32),
            pltpu.VMEM((3, *small), F32),
            dma((3,)),
            dma((3,)),
        ]
        + reduce_scratch(1, own_rows, width)
        + ring_reduce_scratch(own_rows, width),
        compiler_params=pltpu.CompilerParams(
            collective_id=5, has_side_effects=True, vmem_limit_bytes=60 * MIB
        ),
        name="finish",
    )(
        *(grad.reshape(4, 2, 4, share, grad.shape[1]) for grad in grads),
        ups.reshape(2, 4, share, up_cols),
        downs.reshape(2, 4, share, down_cols),
        part.reshape(2, 2, 2, own_rows, width),
        feed.reshape(4, own_rows, width),
        x,
        middle,
        dmiddle,
        gain[None],
    )


def dot(a, b, dims):
    return lax.dot_general(a, b, (dims, ((), ())), preferred_element_type=F32)


def experts_body(
    rows_ref, raw_ref, gate_up_ref, linear_up_ref, gate_ref,
    dgate_pre_out, dlinear_out, hidden_out, gated_out, dgate_out,
):
    @pl.when(pl.program_id(0) == 0)
    def _():
        dgate_out[...] = jnp.zeros_like(dgate_out)

    up = jnp.concatenate([gate_up_ref[...], linear_up_ref[...]], 1)
    joined = dot(rows_ref[...], up, ((1,), (0,)))
    gate_pre, linear = joined[:, :LANES], joined[:, LANES:]
    sigmoid = jax.nn.sigmoid(gate_pre)
    silu = gate_pre * sigmoid
    hidden = silu * linear
    dhidden = raw_ref[...]
    gate = gate_ref[...]
    dgate_out[...] += hidden * dhidden
    dhidden = dhidden * gate
    hidden_out[...] = hidden.astype(BF16)
    gated_out[...] = (hidden * gate).astype(BF16)
    dgate_pre_out[...] = (dhidden * linear * (sigmoid + silu * (1.0 - sigmoid))).astype(BF16)
    dlinear_out[...] = (dhidden * silu).astype(BF16)


def experts(rows, raw, up, gates):
    count, hidden = raw.shape
    width = up.shape[0]
    chunks = hidden // LANES
    chunk = pl.BlockSpec((count, LANES), lambda j: (0, j))
    some = jax.ShapeDtypeStruct((count, hidden), BF16)
    return pl.pallas_call(
        experts_body,
        grid=(chunks,),
        in_specs=[
            pl.BlockSpec((count, width), lambda j: (0, 0)),
            chunk,
            pl.BlockSpec((width, LANES), lambda j: (0, j)),
            pl.BlockSpec((width, LANES), lambda j: (0, chunks + j)),
            pl.BlockSpec((count, 1), lambda j: (0, 0)),
        ],
        out_specs=[chunk] * 4 + [pl.BlockSpec((count, LANES), lambda j: (0, 0))],
        out_shape=[some] * 4 + [jax.ShapeDtypeStruct((count, LANES), F32)],
        compiler_params=pltpu.CompilerParams(vmem_limit_bytes=56 * MIB),
        name="experts",
    )(rows, raw, up, up, gates)


def return_body(
    dgate_pre_ref, dlinear_ref, up_ref, dgate_ref, rows_ref,
    dunit_out, dgate_out, up_out,
    djoined, up, rows, dunit, dgate_own, dunit_buf, dgate_buf, dunit_sum, dgate_sum, block,
    loc, core_s, core_r, far_s, far_r, out_sem,
):
    y, core = lax.axis_index("y"), lax.axis_index("core")
    slots = dgate_ref.shape[1]
    half = slots // 2
    hidden = dgate_pre_ref.shape[1]
    sends = Sends()
    loads = []
    for n, (src, dst) in enumerate(
        (
            (up_ref, up),
            (dgate_pre_ref, djoined.at[:, pl.ds(0, hidden)]),
            (dlinear_ref, djoined.at[:, pl.ds(hidden, hidden)]),
            (rows_ref.at[:, pl.ds(0, rows.shape[1])], rows),
        )
    ):
        loads.append(pltpu.make_async_copy(src, dst, loc.at[1, n]))
        loads[-1].start()
    greet(neighbour("core", 1), *(neighbour("y", step) for step in (1, 2, 3)))
    mine = pl.ds(pl.multiple_of(core * half, half), half)
    theirs = pl.ds(pl.multiple_of((1 - core) * half, half), half)
    order = (2, 1, 3, 0)
    own = []
    for step in order:
        target = mod4(y + step)
        sends(
            dgate_ref.at[target, theirs],
            dgate_buf.at[step],
            core_s.at[1, step],
            core_r.at[1, step],
            neighbour("core", 1),
        )
        own.append(pltpu.make_async_copy(dgate_ref.at[target, mine], dgate_own.at[step], loc.at[0, step]))
        own[-1].start()
    for load in loads[:3]:
        load.wait()
    for copy in own:
        copy.wait()

    def compute(step):
        at = pl.ds(pl.multiple_of(mod4(y + step) * slots, slots), slots)
        dunit[step] = dot(djoined[at, :], up[...], ((1,), (1,))).astype(BF16)
        sends(
            dunit.at[step, theirs],
            dunit_buf.at[step],
            core_s.at[0, step],
            core_r.at[0, step],
            neighbour("core", 1),
        )

    def pass_on(step):
        arrived(dunit_buf.at[step], core_r.at[0, step])
        arrived(dgate_buf.at[step], core_r.at[1, step])
        dunit_value = (dunit[step, mine, :].astype(F32) + dunit_buf[step].astype(F32)).astype(BF16)
        dgate_value = dgate_own[step] + dgate_buf[step]
        if step == 0:
            dunit_out[y] = dunit_value
            dgate_out[y] = dgate_value
            return
        dunit_sum[step - 1] = dunit_value
        dgate_sum[step - 1] = dgate_value
        for n, (summed, result) in enumerate(((dunit_sum, dunit_out), (dgate_sum, dgate_out))):
            sends(
                summed.at[step - 1],
                result.at[y],
                far_s.at[n, step - 1],
                far_r.at[n, step - 1],
                neighbour("y", step),
            )

    compute(2)
    compute(1)
    pass_on(2)
    compute(3)
    pass_on(1)
    compute(0)
    pass_on(3)
    loads[3].wait()
    blocks = up_out.shape[0] // WIDE

    @pl.loop(0, blocks)
    def _(j):
        at = pl.ds(pl.multiple_of(j * WIDE, WIDE), WIDE)
        slot = lax.rem(j, 2)

        @pl.when(j >= 2)
        def _():
            pltpu.make_async_copy(block.at[slot], up_out.at[at], out_sem.at[slot]).wait()

        block[slot] = dot(rows[:, at], djoined[...], ((0,), (0,))).astype(BF16)
        pltpu.make_async_copy(block.at[slot], up_out.at[at], out_sem.at[slot]).start()

    pass_on(0)
    for slot in (0, 1):
        pltpu.make_async_copy(block.at[slot], up_out.at[pl.ds(0, WIDE)], out_sem.at[slot]).wait()
    for n, result in enumerate((dunit_out, dgate_out)):
        for step in (1, 3, 2):
            arrived(result.at[mod4(y - step)], far_r.at[n, step - 1])
    sends.finish()


def return_rows(dgate_pre, dlinear, up, dgate, rows):
    _, slots, lanes = dgate.shape
    half = slots // 2
    width, wide = up.shape
    count = dlinear.shape[0]
    dma = pltpu.SemaphoreType.DMA
    anywhere = pl.BlockSpec(memory_space=pl.ANY)
    return pl.pallas_call(
        return_body,
        out_shape=[
            jax.ShapeDtypeStruct((4, half, width), BF16),
            jax.ShapeDtypeStruct((4, half, lanes), F32),
            jax.ShapeDtypeStruct((width, wide), BF16),
        ],
        in_specs=[anywhere] * 5,
        out_specs=vmem(2) + [anywhere],
        scratch_shapes=[
            pltpu.VMEM((count, wide), BF16),
            pltpu.VMEM((width, wide), BF16),
            pltpu.VMEM((count, width), BF16),
            pltpu.VMEM((4, slots, width), BF16),
            pltpu.VMEM((4, half, lanes), F32),
            pltpu.VMEM((4, half, width), BF16),
            pltpu.VMEM((4, half, lanes), F32),
            pltpu.VMEM((3, half, width), BF16),
            pltpu.VMEM((3, half, lanes), F32),
            pltpu.VMEM((2, WIDE, wide), BF16),
            dma((2, 4)),
            dma((2, 4)),
            dma((2, 4)),
            dma((2, 3)),
            dma((2, 3)),
            dma((2,)),
        ],
        compiler_params=pltpu.CompilerParams(
            collective_id=3, has_side_effects=True, vmem_limit_bytes=62 * MIB
        ),
        name="return_rows",
    )(dgate_pre, dlinear, up, dgate, rows)


def attention_body(
    k_ref, v_ref, q0, q1, q2, cos_ref, sin_ref, col_ref, row_ref, gate_ref,
    key_out, val_out, que_out, mix_out, gmix_out, prob_out,
):
    h = pl.program_id(1)
    cosine, sine = cos_ref[...], sin_ref[...]
    scale = 1.0 / math.sqrt(HD)

    def rotated(v):
        return v * cosine + pltpu.roll(v, HD // 2, 1) * sine

    key = rotated(k_ref[...]).astype(BF16)
    val = v_ref[...].astype(BF16)
    key_out[...] = key
    val_out[...] = val
    tokens = key.shape[0]
    half = tokens // 2
    allowed = []
    for start in (0, half):
        seen = start + half
        at_row = start + lax.broadcasted_iota(jnp.int32, (half, seen), 0)
        at_col = lax.broadcasted_iota(jnp.int32, (half, seen), 1)
        seg_row, seg_col = row_ref[0, :, :seen], col_ref[start : start + half, :]
        allowed.append((at_col <= at_row) & ((seg_row == 0) | (seg_row == seg_col)))
    for e, q_ref in enumerate((q0, q1, q2)):
        query = (rotated(q_ref[...]) * scale).astype(BF16)
        at = pl.ds(pl.multiple_of((e * HEADS + h) * HD, HD), HD)
        que_out[:, at] = query
        for n, start in enumerate((0, half)):
            rows, seen = slice(start, start + half), start + half
            scores = jnp.where(allowed[n], dot(query[rows], key[:seen], ((1,), (1,))), NEGATIVE)
            largest = jnp.max(scores, 1, keepdims=True)
            expsum = jnp.exp(scores - largest)
            prob = (expsum * (1.0 / jnp.sum(expsum, 1, keepdims=True))).astype(BF16)
            prob_out[0, 0, e, rows, :seen] = prob
            mixed = dot(prob, val[:seen], ((1,), (0,))).astype(BF16)
            mix_out[rows, at] = mixed
            gmix_out[rows, at] = (mixed.astype(F32) * gate_ref[rows, e : e + 1]).astype(BF16)


def block_specs(tokens):
    def column(n):
        return pl.BlockSpec((tokens, HD), lambda g, h: (g, n * HEADS + h))

    def rows(width):
        return pl.BlockSpec((tokens, width), lambda g, h: (g, 0))

    return column, rows


def prob_spec(tokens):
    return pl.BlockSpec((1, 1, 3, tokens, tokens), lambda g, h: (g, h, 0, 0, 0))


def attention_forward(joined, cosine, sine, segments, gates):
    groups, tokens = segments.shape
    column, rows = block_specs(tokens)
    wide = jax.ShapeDtypeStruct((groups * tokens, 3 * HEADS * HD), BF16)
    narrow = jax.ShapeDtypeStruct((groups * tokens, HEADS * HD), BF16)
    return pl.pallas_call(
        attention_body,
        grid=(groups, HEADS),
        in_specs=[column(n) for n in range(5)]
        + [rows(HD)] * 2
        + [rows(1), pl.BlockSpec((1, 1, tokens), lambda g, h: (g, 0, 0)), rows(gates.shape[1])],
        out_specs=[column(0), column(0)] + [rows(wide.shape[1])] * 3 + [prob_spec(tokens)],
        out_shape=[narrow, narrow, wide, wide, wide]
        + [jax.ShapeDtypeStruct((groups, HEADS, 3, tokens, tokens), BF16)],
        compiler_params=pltpu.CompilerParams(vmem_limit_bytes=48 * MIB),
        name="attention_forward",
    )(
        *[joined] * 5, cosine, sine, segments.reshape(-1, 1), segments[:, None], gates
    )


def attention_back_body(
    key_ref, val_ref, q0, q1, q2, m0, m1, m2, h0, h1, h2, prob_ref, cos_ref, sin_ref, gate_ref,
    grad_out, dgate_out,
):
    h = pl.program_id(1)
    cosine, sine = cos_ref[...], sin_ref[...]
    scale = 1.0 / math.sqrt(HD)

    def rotated_back(v):
        return v * cosine - pltpu.roll(v, HD // 2, 1) * sine

    key, val = key_ref[...], val_ref[...]
    tokens = key.shape[0]
    half = tokens // 2
    dkeys = [jnp.zeros((half, HD), F32)] * 2
    dvals = [jnp.zeros((half, HD), F32)] * 2
    lane = lax.broadcasted_iota(jnp.int32, (tokens, HD), 1)
    dgates = jnp.zeros((tokens, HD), F32)
    for e, (q_ref, m_ref, h_ref) in enumerate(((q0, m0, h0), (q1, m1, h1), (q2, m2, h2))):
        query, mixed, raw = q_ref[...], m_ref[...].astype(F32), h_ref[...]
        inner = jnp.sum(mixed * raw, 1, keepdims=True)
        dgates = dgates + jnp.where(lane == e, inner, 0.0)
        gate = gate_ref[:, e : e + 1]
        dmixed = (raw * gate).astype(BF16)
        delta = jnp.sum(dmixed.astype(F32) * mixed, 1, keepdims=True)
        dqueries = []
        for start in (0, half):
            rows, seen = slice(start, start + half), start + half
            prob = prob_ref[0, 0, e, rows, :seen]
            dprob = dot(dmixed[rows], val[:seen], ((1,), (1,)))
            dscores = (prob.astype(F32) * (dprob - delta[rows])).astype(BF16)
            dqueries.append(dot(dscores, key[:seen], ((1,), (0,))))
            dval = dot(prob, dmixed[rows], ((0,), (0,)))
            dkey = dot(dscores, query[rows], ((0,), (0,)))
            dvals[0] = dvals[0] + dval[:half]
            dkeys[0] = dkeys[0] + dkey[:half]
            if start:
                dvals[1] = dvals[1] + dval[half:]
                dkeys[1] = dkeys[1] + dkey[half:]
        dquery = jnp.concatenate(dqueries, 0)
        at = pl.ds(pl.multiple_of(((2 + e) * HEADS + h) * HD, HD), HD)
        grad_out[:, at] = rotated_back(dquery * scale).astype(BF16)
    dkey, dval = jnp.concatenate(dkeys, 0), jnp.concatenate(dvals, 0)
    grad_out[:, pl.ds(pl.multiple_of(h * HD, HD), HD)] = rotated_back(dkey).astype(BF16)
    grad_out[:, pl.ds(pl.multiple_of((HEADS + h) * HD, HD), HD)] = dval.astype(BF16)

    @pl.when(h == 0)
    def _():
        dgate_out[...] = dgates

    @pl.when(h > 0)
    def _():
        dgate_out[...] += dgates


def attention_back(key, val, que, mix, raw, prob, cosine, sine, gates):
    groups, tokens = prob.shape[0], prob.shape[-1]
    column, rows = block_specs(tokens)
    thirds = [column(n) for n in range(3)]
    grads = jax.ShapeDtypeStruct((groups * tokens, 5 * HEADS * HD), BF16)
    return pl.pallas_call(
        attention_back_body,
        grid=(groups, HEADS),
        in_specs=[column(0), column(0)]
        + thirds * 3
        + [prob_spec(tokens)]
        + [rows(HD)] * 2
        + [rows(gates.shape[1])],
        out_specs=[rows(grads.shape[1]), rows(HD)],
        out_shape=[grads, jax.ShapeDtypeStruct((groups * tokens, HD), F32)],
        compiler_params=pltpu.CompilerParams(vmem_limit_bytes=48 * MIB),
        name="attention_back",
    )(key, val, que, que, que, mix, mix, mix, raw, raw, raw, prob, cosine, sine, gates)


def positions(segments):
    index = jnp.arange(segments.shape[0], dtype=jnp.int32)
    prompt = jnp.sum((segments == 0).astype(jnp.int32))
    first = jnp.sum((segments == 1).astype(jnp.int32))
    before = jnp.where(segments == 0, 0, jnp.where(segments == 1, prompt, prompt + first))
    return jnp.where(segments == 0, index, prompt + index - before)


def route_gates(logits, routes, count):
    onehot = (routes[:, :, None] == jnp.arange(count, dtype=jnp.int32)).astype(F32)
    chosen = jnp.sum(onehot * logits[:, None, :], -1)
    expsum = jnp.exp(chosen - jnp.max(chosen, -1, keepdims=True))
    weights = expsum / jnp.sum(expsum, -1, keepdims=True)
    return weights, onehot, jnp.sum(weights[:, :, None] * onehot, 1)


def router_back(dgate, weights, onehot):
    dchosen = jnp.sum(dgate[:, None, :] * onehot, -1)
    dselect = weights * (dchosen - jnp.sum(weights * dchosen, -1, keepdims=True))
    return jnp.sum(dselect[:, :, None] * onehot, 1).astype(BF16)


def normalize(activations):
    inverse = lax.rsqrt(jnp.mean(activations * activations, -1, keepdims=True) + EPSILON)
    return activations * inverse, inverse


def reorder(rows):
    count, width = rows.shape
    return jnp.transpose(rows.reshape(count, 4, 2, 4, width // 32), (0, 3, 2, 1, 4)).reshape(count, width)


def pad_to(array, width):
    return jnp.pad(array, ((0, 0), (0, width - array.shape[1])))


def on_device(
    inputs,
    segments,
    att_routes,
    mlp_routes,
    key_value,
    query_proj,
    output_proj,
    router_att,
    gain_att,
    gate_up,
    down_proj,
    router_mlp,
    gain_mlp,
    out_grad,
):
    width = inputs.shape[1]
    inner = query_proj.shape[2]
    hidden_local = down_proj.shape[1]
    att_count = query_proj.shape[0]
    mlp_count = gate_up.shape[0]
    share = gate_up.shape[1]
    part = inner // 2
    qkv_cols = (2 + att_count) * part
    small_at = qkv_cols
    out_at = qkv_cols + 128
    small = jnp.concatenate([router_att, router_mlp, gain_att[:, None], gain_mlp[:, None]], 1)
    own_att = jnp.concatenate(
        [
            jnp.transpose(key_value.reshape(share, 2, 2, part), (2, 0, 1, 3)).reshape(2, share, -1),
            jnp.transpose(query_proj.reshape(att_count, share, 2, part), (2, 1, 0, 3)).reshape(
                2, share, -1
            ),
            jnp.broadcast_to(pad_to(small, 128), (2, share, 128)),
            jnp.transpose(output_proj.reshape(att_count, 2, part, share), (1, 3, 0, 2)).reshape(
                2, share, -1
            ),
        ],
        2,
    )
    inputs = reorder(inputs)
    out_grad = reorder(out_grad)
    x_all = lax.all_gather(inputs, ("xl", *TP), axis=0, tiled=True)
    grad_all = lax.all_gather(out_grad, TP, axis=0, tiled=True)
    marks = pad_to(jnp.concatenate([segments[:, None], att_routes], 1), LANES).astype(BF16)
    weights, up_parts, down_parts, marks = gather_dp(
        own_att,
        gate_up.reshape(mlp_count, share, -1),
        jnp.swapaxes(down_proj, 1, 2),
        marks,
    )
    marks = marks[:, :, :3].astype(jnp.int32)
    up_whole = lax.all_gather(
        up_parts.reshape(2 * mlp_count * share, -1), "z", axis=0, tiled=True
    )
    down_whole = lax.all_gather(
        down_parts.reshape(2 * mlp_count * share, -1), "z", axis=0, tiled=True
    )

    tokens = segments.shape[0]
    match = jnp.sum((mlp_routes[:, :, None] == jnp.arange(mlp_count, dtype=jnp.int32)).astype(BF16), 1)
    index = jnp.arange(tokens, dtype=jnp.int32)
    lower = (index[None, :] < index[:, None]).astype(BF16)
    rank = dot(lower, match, ((1,), (0,)))
    slot = jnp.where(match > 0, rank.astype(jnp.int32), -1)
    pick = (slot.T[:, None, :] == jnp.arange(CAP, dtype=jnp.int32)[None, :, None]).astype(BF16)
    pick_rows = pick.reshape(mlp_count * CAP, tokens)
    grad_rows = dot(pick_rows, grad_all, ((1,), (0,))).astype(BF16)
    grad_in = lax.all_to_all(grad_rows.reshape(mlp_count, CAP, width), "y", 0, 0, tiled=True)
    grad_in = grad_in.reshape(mlp_count * CAP, width)

    small_all = weights[:, small_at : small_at + 128].astype(F32)
    gain_one, gain_two = small_all[:, 7], small_all[:, 8]
    segments = marks[:, :, 0]
    att_routes = marks[:, :, 1:].reshape(2 * tokens, 2)
    places = jax.vmap(positions)(segments).reshape(-1).astype(F32)
    frequency = ROPE_BASE ** (-2.0 * jnp.arange(HD // 2, dtype=F32) / HD)
    angles = places[:, None] * frequency[None, :]
    cosine = jnp.concatenate([jnp.cos(angles)] * 2, 1)
    sine = jnp.concatenate([-jnp.sin(angles), jnp.sin(angles)], 1)
    normed_one, _ = normalize(x_all.astype(F32))
    unit_one = (normed_one * gain_one).astype(BF16)
    joined_att = dot(unit_one, weights[:, :out_at], ((1,), (0,)))
    weights_att, onehot_att, gate_att = route_gates(
        joined_att[:, small_at : small_at + att_count], att_routes, att_count
    )
    key_rot, val_rows, queries, mixed, gmixed, prob = attention_forward(
        joined_att, cosine, sine, segments, gate_att
    )
    out_weights = weights[:, out_at:]
    attention = dot(gmixed, out_weights, ((1,), (1,))).astype(BF16)
    middle, unit_two = middle_and_unit(attention, inputs, gain_two)

    router_two = weights[:, small_at + att_count : small_at + att_count + mlp_count]
    logit_mlp = dot(unit_two, router_two, ((1,), (0,)))
    weights_mlp, onehot_mlp, gate_mlp = route_gates(logit_mlp, mlp_routes, mlp_count)
    gate_high = gate_mlp.astype(BF16)
    gate_low = (gate_mlp - gate_high.astype(F32)).astype(BF16)
    extended = jnp.concatenate([unit_two, pad_to(jnp.concatenate([gate_high, gate_low], 1), 128)], 1)
    rows_out = dot(pick_rows, extended, ((1,), (0,))).astype(BF16)
    rows_ext, raw = rows_to_experts(
        rows_out.reshape(mlp_count, CAP, width + 128), grad_in, down_whole
    )
    rows_ext = rows_ext.reshape(mlp_count * CAP, width + 128)
    gates_ext = rows_ext[:, width : width + 2 * mlp_count].astype(F32)
    mine = (jnp.arange(2 * mlp_count) % mlp_count == lax.axis_index("y")).astype(F32)
    gates_in = jnp.sum(gates_ext * mine, 1, keepdims=True)
    dgate_pre, dlinear, hidden, gated, dgate_part = experts(rows_ext, raw, up_whole, gates_in)
    grad_down_whole = dot(grad_in, gated, ((0,), (0,))).astype(BF16)
    dgate_part, grad_down_whole = lax.optimization_barrier((dgate_part, grad_down_whole))
    grad_down_sum = lax.psum_scatter(grad_down_whole, "z", scatter_dimension=0, tiled=True)
    dunit_back, dgate_back, grad_up_whole = return_rows(
        dgate_pre, dlinear, up_whole, dgate_part.reshape(mlp_count, CAP, LANES), rows_ext
    )
    grad_up_sum = lax.psum_scatter(grad_up_whole, "z", scatter_dimension=0, tiled=True)
    pick_half = lax.dynamic_slice_in_dim(pick, lax.axis_index("core") * (CAP // 2), CAP // 2, 1)
    dgate_two = jnp.sum(pick_half.astype(F32) * jnp.sum(dgate_back, -1, keepdims=True), 1).T
    dlogit_mlp = router_back(dgate_two, weights_mlp, onehot_mlp)
    dunit_two = dot(
        pick_half.reshape(-1, tokens), dunit_back.reshape(-1, width), ((0,), (0,))
    ) + dot(dlogit_mlp, router_two, ((1,), (1,)))
    grad_rmlp = dot(unit_two, dlogit_mlp, ((0,), (0,)))
    dmiddle, grad_gain_two, dattention, branch_part = middle_back(
        dunit_two.astype(BF16), middle, out_grad, gain_two, hidden, down_whole
    )
    branch_back = lax.all_to_all(branch_part, "y", 0, 0, tiled=True)

    raw = dot(dattention, out_weights, ((1,), (0,)))
    grad_qkv, dgate_one = attention_back(
        key_rot, val_rows, queries, mixed, raw, prob, cosine, sine, gate_att
    )
    dlogit_att = router_back(dgate_one[:, :att_count], weights_att, onehot_att)
    grad_joined = jnp.concatenate([grad_qkv, pad_to(dlogit_att, 128)], 1)
    dunit_one = dot(grad_joined, weights[:, :out_at], ((1,), (1,)))
    grad_gain_one = jnp.sum(dunit_one * normed_one, 0)
    grad_small = jnp.concatenate(
        [
            dot(unit_one, dlogit_att, ((0,), (0,))),
            grad_rmlp,
            grad_gain_one[:, None],
            grad_gain_two[:, None],
        ],
        1,
    )
    gate_slots = jnp.sum(pick.astype(F32) * gate_mlp.T[:, None, :], -1, keepdims=True)
    feed = dot(
        pick_rows,
        (branch_back.astype(F32) * gate_slots).astype(BF16).reshape(-1, width),
        ((0,), (0,)),
    )
    summed_att, ups_sum, downs_sum, output, grad_input, small_sum = finish(
        (
            dot(unit_one, grad_qkv, ((0,), (0,))).astype(BF16),
            pad_to(grad_small, 128).astype(BF16),
            dot(dattention, gmixed, ((0,), (0,))).astype(BF16),
        ),
        grad_up_sum,
        grad_down_sum,
        dunit_one.astype(BF16),
        feed.astype(BF16),
        inputs,
        middle,
        dmiddle,
        gain_one,
    )
    grad_kv = jnp.transpose(
        summed_att[:, :, : 2 * part].reshape(2, share, 2, part), (1, 2, 0, 3)
    ).reshape(share, 2, inner)
    grad_query = jnp.transpose(
        summed_att[:, :, 2 * part : qkv_cols].reshape(2, share, att_count, part), (2, 1, 0, 3)
    ).reshape(att_count, share, inner)
    grad_output = jnp.transpose(
        summed_att[:, :, out_at:].reshape(2, share, att_count, part), (2, 0, 3, 1)
    ).reshape(att_count, inner, share)
    output = reorder(output)
    grad_input = reorder(grad_input)

    grads_up = ups_sum.astype(F32).reshape(mlp_count, share, 2, hidden_local)
    grads_down = jnp.swapaxes(downs_sum.astype(F32), 1, 2)
    return (
        output,
        grad_input,
        grad_kv,
        grad_query,
        grad_output,
        small_sum[:, :3],
        small_sum[:, 7],
        grads_up,
        grads_down,
        small_sum[:, 3:7],
        small_sum[:, 8],
    )


def solution(mesh):
    fine = Mesh(mesh.devices.reshape(4, 2, 4, 2, 2), ALL)
    return jax.shard_map(
        on_device,
        mesh=fine,
        in_specs=(
            P(ALL, None),
            P(DP),
            P(DP, None),
            P(DP, None),
            P(DP, None, TP),
            P(None, DP, TP),
            P(None, TP, DP),
            P(DP, None),
            P(DP),
            P(None, DP, None, TP),
            P(None, TP, DP),
            P(DP, None),
            P(DP),
            P(ALL, None),
        ),
        out_specs=(
            P(ALL, None),
            P(ALL, None),
            P(DP, None, TP),
            P(None, DP, TP),
            P(None, TP, DP),
            P(DP, None),
            P(DP),
            P(None, DP, None, TP),
            P(None, TP, DP),
            P(DP, None),
            P(DP),
        ),
        check_vma=False,
    )
```

```python
import functools
import math

import jax
import jax.numpy as jnp
from jax import lax
from jax.experimental import pallas as pl
from jax.experimental.pallas import tpu as pltpu
from jax.sharding import Mesh, PartitionSpec as P

LANES = 128
WIDE = 256
HD = 128
HEADS = 2
CAP = 320
EPSILON = 1e-06
NEGATIVE = -1e30
ROPE_BASE = 10000.0
MESH_ID = pl.DeviceIdType.MESH
MIB = 1024 * 1024
DP = ("y", "xl", "z")
TP = ("xh", "core")
ALL = DP + TP
F32 = jnp.float32
BF16 = jnp.bfloat16


def mod4(place):
    return lax.rem(place + 4, 4)


def neighbour(axis, step):
    size = 4 if axis in ("y", "z") else 2
    return {axis: lax.rem(lax.axis_index(axis) + step + size, size)}


def chip_along(step):
    at = lax.rem(lax.axis_index("xh") * 2 + lax.axis_index("xl") + step + 4, 4)
    return {"xh": lax.div(at, 2), "xl": lax.rem(at, 2)}


def greet(*devices):
    barrier = pltpu.get_barrier_semaphore()
    for device in devices:
        pl.semaphore_signal(barrier, inc=1, device_id=device, device_id_type=MESH_ID)
    pl.semaphore_wait(barrier, len(devices))


def arrived(ref, sem):
    pltpu.make_async_copy(ref, ref, sem).wait()


class Sends:
    def __init__(self):
        self.copies = []

    def __call__(self, src, dst, send_sem, recv_sem, device):
        copy = pltpu.make_async_remote_copy(
            src_ref=src,
            dst_ref=dst,
            send_sem=send_sem,
            recv_sem=recv_sem,
            device_id=device,
            device_id_type=MESH_ID,
        )
        copy.start()
        self.copies.append(copy)

    def finish(self):
        for copy in self.copies:
            copy.wait_send()


def gather_body(
    x_ref, ups_ref, downs_ref, marks_ref, out_ref, up_ref, down_ref, marks_out,
    loc, xs, xr, s1, r1m, r1p, f1s, f1r, s2, r2m, r2p, f2s, f2r, es, er, ex, ey, ms, mr,
):
    y, xl, z = lax.axis_index("y"), lax.axis_index("xl"), lax.axis_index("z")
    half = x_ref.shape[1] // 2
    quarter = half // 2
    greet(
        neighbour("xl", 1),
        *(neighbour("y", step) for step in (1, 2, 3)),
        *(neighbour("z", step) for step in (1, -1)),
    )
    rings = (("z", "y"), ("y", "z"))
    place = {"y": y, "z": z}
    other = 1 - xl
    both = pl.ds(0, 2)
    sends = Sends()
    send = sends

    def slot(h, first, second, j, start, count):
        yy, zz = (second, first) if h == 0 else (first, second)
        return out_ref.at[zz, j, yy, pl.ds(start, count)]

    own = pltpu.make_async_copy(x_ref.at[xl], out_ref.at[z, xl, y], loc.at[0])
    own.start()
    own_marks = pltpu.make_async_copy(marks_ref, marks_out.at[xl], loc.at[3])
    own_marks.start()
    send(marks_ref, marks_out.at[xl], ms, mr, neighbour("xl", 1))
    experts = ((ups_ref, up_ref), (downs_ref, down_ref))
    kept = []
    for n, (shards, expert) in enumerate(experts):
        kept.append(pltpu.make_async_copy(shards.at[y], expert.at[xl, y], loc.at[1 + n]))
        kept[-1].start()
        send(shards.at[y], expert.at[xl, y], ex.at[n, 0], ey.at[n, 0], neighbour("xl", 1))
        for step in (1, 3, 2):
            send(
                shards.at[mod4(y + step)],
                expert.at[xl, y],
                es.at[n, step - 1],
                er.at[n, step - 1],
                neighbour("y", step),
            )
    for h in (0, 1):
        first, second = place[rings[h][0]], place[rings[h][1]]
        src = x_ref.at[xl, pl.ds(h * half, half)]
        dst = slot(h, first, second, xl, h * half, half)
        send(x_ref.at[other, pl.ds(h * half, half)], dst, xs.at[h], xr.at[h], neighbour("xl", 1))
        send(src, dst, s1.at[h, 0, 0], r1m.at[h, 0], neighbour(rings[h][0], 1))
        send(src, dst, s1.at[h, 0, 1], r1p.at[h, 0], neighbour(rings[h][0], -1))
    own.wait()

    def send_second(h, k, first):
        block = slot(h, first, place[rings[h][1]], both, h * half, half)
        send(block, block, s2.at[k, 0], r2m.at[k], neighbour(rings[h][1], 1))
        send(block, block, s2.at[k, 1], r2p.at[k], neighbour(rings[h][1], -1))

    for h in (0, 1):
        first, second = place[rings[h][0]], place[rings[h][1]]
        block = slot(h, first, second, other, h * half, half)
        arrived(block, xr.at[h])
        send(block, block, s1.at[h, 1, 0], r1m.at[h, 1], neighbour(rings[h][0], 1))
        send(block, block, s1.at[h, 1, 1], r1p.at[h, 1], neighbour(rings[h][0], -1))
        if h == 1:
            send_second(h, 0, first)
    for j, jx in ((0, xl), (1, other)):
        for h in (0, 1):
            first, second = place[rings[h][0]], place[rings[h][1]]
            arrived(slot(h, mod4(first - 1), second, jx, h * half, half), r1m.at[h, j])
            block = slot(h, mod4(first - 1), second, jx, h * half, quarter)
            send(block, block, f1s.at[h, j, 0], f1r.at[h, j, 0], neighbour(rings[h][0], 1))
            arrived(slot(h, mod4(first + 1), second, jx, h * half, half), r1p.at[h, j])
            block = slot(h, mod4(first + 1), second, jx, h * half + quarter, quarter)
            send(block, block, f1s.at[h, j, 1], f1r.at[h, j, 1], neighbour(rings[h][0], -1))
    for k, step in ((1, -1), (2, 1)):
        send_second(1, k, mod4(place[rings[1][0]] + step))
    for n, (shards, expert) in enumerate(experts):
        for step in (1, 3, 2):
            landed = expert.at[xl, mod4(y - step)]
            arrived(landed, er.at[n, step - 1])
            send(landed, landed, ex.at[n, step], ey.at[n, step], neighbour("xl", 1))
    for h in (0, 1):
        first, second = place[rings[h][0]], place[rings[h][1]]
        for j, jx in ((0, xl), (1, other)):
            for p in (0, 1):
                block = slot(h, mod4(first + 2), second, jx, h * half + p * quarter, quarter)
                arrived(block, f1r.at[h, j, p])
        if h == 1:
            send_second(h, 3, mod4(first + 2))
    steps = ((0, 0), (1, -1), (2, 1), (3, 2))
    h = 1
    second = place[rings[h][1]]
    for k, step in steps:
        first = mod4(place[rings[h][0]] + step)
        arrived(slot(h, first, mod4(second - 1), both, half, half), r2m.at[k])
        block = slot(h, first, mod4(second - 1), both, half, quarter)
        send(block, block, f2s.at[k, 0], f2r.at[k, 0], neighbour(rings[h][1], 1))
        arrived(slot(h, first, mod4(second + 1), both, half, half), r2p.at[k])
        block = slot(h, first, mod4(second + 1), both, half + quarter, quarter)
        send(block, block, f2s.at[k, 1], f2r.at[k, 1], neighbour(rings[h][1], -1))
    for k, step in steps:
        first = mod4(place[rings[h][0]] + step)
        for p in (0, 1):
            block = slot(h, first, mod4(second + 2), both, half + p * quarter, quarter)
            arrived(block, f2r.at[k, p])
    for n, (shards, expert) in enumerate(experts):
        for step in (0, 1, 3, 2):
            arrived(expert.at[other, mod4(y - step)], ey.at[n, step])
        kept[n].wait()
    arrived(marks_out.at[other], mr)
    own_marks.wait()
    sends.finish()


def gather_rest_body(start_ref, out_ref, s2, r2m, r2p, f2s, f2r):
    y, z = lax.axis_index("y"), lax.axis_index("z")
    half = out_ref.shape[3] // 2
    quarter = half // 2
    ahead, behind = neighbour("y", 1), neighbour("y", -1)
    greet(ahead, behind)
    sends = Sends()
    both = pl.ds(0, 2)

    def slot(ref, zz, yy, start, count):
        return ref.at[zz, both, yy, pl.ds(start, count)]

    steps = ((0, 0), (1, -1), (2, 1), (3, 2))
    for k, step in steps:
        zz = mod4(z + step)
        src, dst = slot(start_ref, zz, y, 0, half), slot(out_ref, zz, y, 0, half)
        sends(src, dst, s2.at[k, 0], r2m.at[k], ahead)
        sends(src, dst, s2.at[k, 1], r2p.at[k], behind)
    for k, step in steps:
        zz = mod4(z + step)
        arrived(slot(out_ref, zz, mod4(y - 1), 0, half), r2m.at[k])
        block = slot(out_ref, zz, mod4(y - 1), 0, quarter)
        sends(block, block, f2s.at[k, 0], f2r.at[k, 0], ahead)
        arrived(slot(out_ref, zz, mod4(y + 1), 0, half), r2p.at[k])
        block = slot(out_ref, zz, mod4(y + 1), quarter, quarter)
        sends(block, block, f2s.at[k, 1], f2r.at[k, 1], behind)
    for k, step in steps:
        for p in (0, 1):
            arrived(slot(out_ref, mod4(z + step), mod4(y + 2), p * quarter, quarter), f2r.at[k, p])
    sends.finish()


def gather_rest(whole, rows):
    dma = pltpu.SemaphoreType.DMA
    cols = whole.shape[1]
    anywhere = pl.BlockSpec(memory_space=pl.ANY)
    out = pl.pallas_call(
        gather_rest_body,
        out_shape=jax.ShapeDtypeStruct((4, 2, 4, rows, cols), whole.dtype),
        in_specs=[anywhere],
        out_specs=anywhere,
        scratch_shapes=[dma((4, 2)), dma((4,)), dma((4,)), dma((4, 2)), dma((4, 2))],
        input_output_aliases={0: 0},
        compiler_params=pltpu.CompilerParams(collective_id=6, has_side_effects=True),
        name="gather_rest",
    )(whole.reshape(4, 2, 4, rows, cols))
    return out.reshape(whole.shape)


def gather_dp(shard, ups, downs, marks):
    _, rows, cols = shard.shape
    dma = pltpu.SemaphoreType.DMA
    whole, up, down, marks = pl.pallas_call(
        gather_body,
        out_shape=[
            jax.ShapeDtypeStruct((4, 2, 4, rows, cols), shard.dtype),
            jax.ShapeDtypeStruct((2, *ups.shape), ups.dtype),
            jax.ShapeDtypeStruct((2, *downs.shape), downs.dtype),
            jax.ShapeDtypeStruct((2, *marks.shape), marks.dtype),
        ],
        in_specs=[pl.BlockSpec(memory_space=pl.ANY)] * 4,
        out_specs=[pl.BlockSpec(memory_space=pl.ANY)] * 4,
        scratch_shapes=[
            dma((4,)),
            dma((2,)),
            dma((2,)),
            dma((2, 2, 2)),
            dma((2, 2)),
            dma((2, 2)),
            dma((2, 2, 2)),
            dma((2, 2, 2)),
            dma((4, 2)),
            dma((4,)),
            dma((4,)),
            dma((4, 2)),
            dma((4, 2)),
            dma((2, 3)),
            dma((2, 3)),
            dma((2, 4)),
            dma((2, 4)),
            dma,
            dma,
        ],
        compiler_params=pltpu.CompilerParams(collective_id=0, has_side_effects=True),
        name="gather_weights",
    )(shard, ups, downs, marks)
    return whole.reshape(32 * rows, cols), up, down, marks


def reduce_stages(scatter_count, part_refs, core_buf, sum_buf, far_buf, core_s, core_r, far_s, far_r, sends):
    xh, core = lax.axis_index("xh"), lax.axis_index("core")
    rows = part_refs[0].shape[1]
    step = rows // scatter_count
    far, here = 1 - xh, xh
    for n, chunk in enumerate(range(0, rows, step)):
        at = pl.ds(chunk, step)
        for i, part in enumerate(part_refs):
            sends(
                part.at[far * 2 + 1 - core, at],
                core_buf.at[i, 0, at],
                core_s.at[i, n, 0],
                core_r.at[i, n, 0],
                neighbour("core", 1),
            )
    for n, chunk in enumerate(range(0, rows, step)):
        at = pl.ds(chunk, step)
        for i, part in enumerate(part_refs):
            sends(
                part.at[here * 2 + 1 - core, at],
                core_buf.at[i, 1, at],
                core_s.at[i, n, 1],
                core_r.at[i, n, 1],
                neighbour("core", 1),
            )
    yield
    for n, chunk in enumerate(range(0, rows, step)):
        at = pl.ds(chunk, step)
        for i, part in enumerate(part_refs):
            arrived(core_buf.at[i, 0, at], core_r.at[i, n, 0])
            mine = part[far * 2 + core, chunk : chunk + step, :].astype(F32)
            sum_buf[i, chunk : chunk + step, :] = (
                mine + core_buf[i, 0, chunk : chunk + step, :].astype(F32)
            ).astype(BF16)
            sends(
                sum_buf.at[i, at],
                far_buf.at[i, at],
                far_s.at[i, n],
                far_r.at[i, n],
                neighbour("xh", 1),
            )
    yield

    def total(i, n):
        chunk = n * step
        at = pl.ds(chunk, step)
        arrived(core_buf.at[i, 1, at], core_r.at[i, n, 1])
        near = part_refs[i][here * 2 + core, chunk : chunk + step, :].astype(F32)
        near = near + core_buf[i, 1, chunk : chunk + step, :].astype(F32)
        arrived(far_buf.at[i, at], far_r.at[i, n])
        return near + far_buf[i, chunk : chunk + step, :].astype(F32)

    yield total


def ring_reduce_stages(part_ref, core_buf, sum_buf, via_buf, far_buf, core_s, core_r, ring_s, ring_r, sends):
    xl, xh, core = lax.axis_index("xl"), lax.axis_index("xh"), lax.axis_index("core")
    rows = part_ref.shape[3]
    half = rows // 2
    at = xh * 2 + xl
    chips = [lax.rem(at + step, 4) for step in (2, 1, 3, 0)]
    chips = [(lax.rem(chip, 2), lax.div(chip, 2)) for chip in chips]
    for n, (pxl, pxh) in enumerate(chips):
        sends(
            part_ref.at[pxl, pxh, 1 - core],
            core_buf.at[n],
            core_s.at[n],
            core_r.at[n],
            neighbour("core", 1),
        )

    def own(n, start):
        pxl, pxh = chips[n]
        return part_ref[pxl, pxh, core, start : start + half, :].astype(F32)

    def both(n, start):
        return own(n, start) + core_buf[n, start : start + half, :].astype(F32)

    first, second = pl.ds(0, half), pl.ds(half, half)
    ahead, behind = chip_along(1), chip_along(-1)
    yield
    arrived(core_buf.at[0], core_r.at[0])
    sum_buf[0, :half, :] = both(0, 0).astype(BF16)
    sends(sum_buf.at[0, first], via_buf.at[0], ring_s.at[0], ring_r.at[0], ahead)
    sum_buf[0, half:, :] = both(0, half).astype(BF16)
    sends(sum_buf.at[0, second], via_buf.at[1], ring_s.at[1], ring_r.at[1], behind)
    arrived(core_buf.at[1], core_r.at[1])
    sum_buf[1, half:, :] = both(1, half).astype(BF16)
    sends(sum_buf.at[1, second], far_buf.at[0, second], ring_s.at[2], ring_r.at[2], ahead)
    arrived(core_buf.at[2], core_r.at[2])
    sum_buf[2, :half, :] = both(2, 0).astype(BF16)
    sends(sum_buf.at[2, first], far_buf.at[1, first], ring_s.at[3], ring_r.at[3], behind)
    yield
    arrived(via_buf.at[0], ring_r.at[0])
    sum_buf[1, :half, :] = (both(1, 0) + via_buf[0].astype(F32)).astype(BF16)
    sends(sum_buf.at[1, first], far_buf.at[0, first], ring_s.at[4], ring_r.at[4], ahead)
    arrived(via_buf.at[1], ring_r.at[1])
    sum_buf[2, half:, :] = (both(2, half) + via_buf[1].astype(F32)).astype(BF16)
    sends(sum_buf.at[2, second], far_buf.at[1, second], ring_s.at[5], ring_r.at[5], behind)
    arrived(core_buf.at[3], core_r.at[3])

    def total(part):
        rows_at = first if part == 0 else second
        start = part * half
        near = both(3, start)
        arrived(far_buf.at[0, rows_at], ring_r.at[4 if part == 0 else 2])
        near = near + far_buf[0, start : start + half, :].astype(F32)
        arrived(far_buf.at[1, rows_at], ring_r.at[3 if part == 0 else 5])
        return near + far_buf[1, start : start + half, :].astype(F32)

    yield total


def ring_reduce_scratch(rows, width):
    dma = pltpu.SemaphoreType.DMA
    return [
        pltpu.VMEM((4, rows, width), BF16),
        pltpu.VMEM((3, rows, width), BF16),
        pltpu.VMEM((2, rows // 2, width), BF16),
        pltpu.VMEM((2, rows, width), BF16),
        dma((4,)),
        dma((4,)),
        dma((6,)),
        dma((6,)),
    ]


def ring_spread(out_ref, part, ring_s, ring_r, core_s, core_r, sends):
    xl, xh, core = lax.axis_index("xl"), lax.axis_index("xh"), lax.axis_index("core")
    half = out_ref.shape[3] // 2
    mine = out_ref.at[xl, xh, core, pl.ds(part * half, half)]
    sends(mine, mine, ring_s.at[part, 0], ring_r.at[part, 0], chip_along(1))
    sends(mine, mine, ring_s.at[part, 1], ring_r.at[part, 1], chip_along(-1))
    sends(mine, mine, core_s.at[part, 0], core_r.at[part, 0], neighbour("core", 1))


def ring_spread_finish(out_ref, ring_s, ring_r, core_s, core_r, sends):
    xl, xh, core = lax.axis_index("xl"), lax.axis_index("xh"), lax.axis_index("core")
    half = out_ref.shape[3] // 2
    at = xh * 2 + xl

    def block(step, part, which):
        chip = lax.rem(at + step + 4, 4)
        return out_ref.at[lax.rem(chip, 2), lax.div(chip, 2), which, pl.ds(part * half, half)]

    for part in (0, 1):
        for n, (step, on) in enumerate(((-1, 1), (1, -1))):
            landed = block(step, part, core)
            arrived(landed, ring_r.at[part, n])
            if part == n:
                sends(landed, landed, ring_s.at[part, 2], ring_r.at[part, 2], chip_along(on))
            sends(landed, landed, core_s.at[part, 1 + n], core_r.at[part, 1 + n], neighbour("core", 1))
    for part in (0, 1):
        landed = block(2, part, core)
        arrived(landed, ring_r.at[part, 2])
        sends(landed, landed, core_s.at[part, 3], core_r.at[part, 3], neighbour("core", 1))
    for part in (0, 1):
        for n, step in enumerate((0, -1, 1, 2)):
            arrived(block(step, part, 1 - core), core_r.at[part, n])


def ring_spread_scratch():
    dma = pltpu.SemaphoreType.DMA
    return [dma((2, 3)), dma((2, 3)), dma((2, 4)), dma((2, 4))]


def along_x():
    return neighbour("core", 1), neighbour("xh", 1), chip_along(1), chip_along(-1)


CHUNKS = 4


def reduce_scratch(count, rows, width):
    dma = pltpu.SemaphoreType.DMA
    return [
        pltpu.VMEM((count, 2, rows, width), BF16),
        pltpu.VMEM((count, rows, width), BF16),
        pltpu.VMEM((count, rows, width), BF16),
        dma((count, CHUNKS, 2)),
        dma((count, CHUNKS, 2)),
        dma((count, CHUNKS)),
        dma((count, CHUNKS)),
    ]


def spread_chunk(out_ref, n, step, sems, sends):
    xh, core = lax.axis_index("xh"), lax.axis_index("core")
    at = pl.ds(n * step, step)
    mine = out_ref.at[xh * 2 + core, at]
    far_s, far_r, core_s, core_r = sems
    sends(mine, mine, far_s.at[n], far_r.at[n], neighbour("xh", 1))
    sends(mine, mine, core_s.at[n, 0], core_r.at[n, 0], neighbour("core", 1))


def spread_finish(out_ref, step, sems, sends):
    xh, core = lax.axis_index("xh"), lax.axis_index("core")
    far_s, far_r, core_s, core_r = sems
    for n in range(CHUNKS):
        at = pl.ds(n * step, step)
        theirs = out_ref.at[(1 - xh) * 2 + core, at]
        arrived(theirs, far_r.at[n])
        sends(theirs, theirs, core_s.at[n, 1], core_r.at[n, 1], neighbour("core", 1))
    for n in range(CHUNKS):
        at = pl.ds(n * step, step)
        arrived(out_ref.at[xh * 2 + 1 - core, at], core_r.at[n, 0])
        arrived(out_ref.at[(1 - xh) * 2 + 1 - core, at], core_r.at[n, 1])


def spread_scratch():
    dma = pltpu.SemaphoreType.DMA
    return [dma((CHUNKS,)), dma((CHUNKS,)), dma((CHUNKS, 2)), dma((CHUNKS, 2))]


def middle_body(part_ref, x_ref, gain_ref, middle_ref, unit_ref, *scratch):
    sends = Sends()
    greet(*along_x())
    *_, total = ring_reduce_stages(part_ref, *scratch[:8], sends)
    me = lax.axis_index("xh") * 2 + lax.axis_index("core")
    step = x_ref.shape[0] // CHUNKS
    half = x_ref.shape[0] // 2
    for part in (0, 1):
        rows = slice(part * half, (part + 1) * half)
        middle = x_ref[rows, :].astype(F32) + total(part)
        middle_ref[rows, :] = middle
        inverse = lax.rsqrt(jnp.mean(middle * middle, 1, keepdims=True) + EPSILON)
        unit_ref[me, rows, :] = (middle * inverse * gain_ref[...]).astype(BF16)
        for n in range(part * CHUNKS // 2, (part + 1) * CHUNKS // 2):
            spread_chunk(unit_ref, n, step, scratch[8:], sends)
    spread_finish(unit_ref, step, scratch[8:], sends)
    sends.finish()


def vmem(count):
    return [pl.BlockSpec(memory_space=pltpu.VMEM)] * count


def middle_and_unit(part, x, gain):
    rows, width = x.shape
    middle, unit = pl.pallas_call(
        middle_body,
        out_shape=[
            jax.ShapeDtypeStruct((rows, width), F32),
            jax.ShapeDtypeStruct((4, rows, width), BF16),
        ],
        in_specs=vmem(3),
        out_specs=vmem(2),
        scratch_shapes=ring_reduce_scratch(rows, width) + spread_scratch(),
        compiler_params=pltpu.CompilerParams(
            collective_id=1, has_side_effects=True, vmem_limit_bytes=32 * MIB
        ),
        name="middle_and_unit",
    )(part.reshape(2, 2, 2, rows, width), x, gain[None])
    return middle, unit.reshape(4 * rows, width)


def back_body(
    part_ref, middle_ref, grad_ref, gain_ref, hidden_ref, down_ref, dmiddle_ref, dgain_ref, spread_ref, branch_out,
    hidden, down, branch, loc, out_sem, *scratch,
):
    sends = Sends()
    loads = []
    for n, (src, dst) in enumerate(((hidden_ref, hidden), (down_ref, down))):
        loads.append(pltpu.make_async_copy(src, dst, loc.at[n]))
        loads[-1].start()
    greet(*along_x())
    stages = reduce_stages(CHUNKS, [part_ref], *scratch[:7], sends)
    next(stages)
    next(stages)
    for load in loads:
        load.wait()
    slots = branch.shape[1]
    outs = []
    for n in range(4):
        branch[n] = dot(hidden[n * slots : (n + 1) * slots, :], down[...], ((1,), (1,))).astype(BF16)
        outs.append(pltpu.make_async_copy(branch.at[n], branch_out.at[n], out_sem.at[n]))
        outs[-1].start()
    total = next(stages)
    xl, xh, core = lax.axis_index("xl"), lax.axis_index("xh"), lax.axis_index("core")
    step = middle_ref.shape[0] // CHUNKS
    for n in range(CHUNKS):
        rows = slice(n * step, (n + 1) * step)
        middle = middle_ref[rows, :]
        inverse = lax.rsqrt(jnp.mean(middle * middle, 1, keepdims=True) + EPSILON)
        normed = middle * inverse
        dunit = total(0, n)
        product = dunit * normed
        dgain = jnp.sum(product, 0, keepdims=True)
        if n == 0:
            dgain_ref[...] = dgain
        else:
            dgain_ref[...] += dgain
        mean = jnp.mean(product * gain_ref[...], 1, keepdims=True)
        dmiddle = grad_ref[rows, :].astype(F32) + inverse * (dunit * gain_ref[...] - normed * mean)
        dmiddle_ref[rows, :] = dmiddle
        spread_ref[xl, xh, core, rows, :] = dmiddle.astype(BF16)
        if n % 2 == 1:
            ring_spread(spread_ref, n // 2, *scratch[7:], sends)
    ring_spread_finish(spread_ref, *scratch[7:], sends)
    for out in outs:
        out.wait()
    sends.finish()


def middle_back(part, middle, grad, gain, hidden, down):
    rows, width = middle.shape
    count, inner = hidden.shape
    slots = count // 4
    dma = pltpu.SemaphoreType.DMA
    anywhere = pl.BlockSpec(memory_space=pl.ANY)
    dmiddle, dgain, spread, branch = pl.pallas_call(
        back_body,
        out_shape=[
            jax.ShapeDtypeStruct((rows, width), F32),
            jax.ShapeDtypeStruct((1, width), F32),
            jax.ShapeDtypeStruct((2, 2, 2, rows, width), BF16),
            jax.ShapeDtypeStruct((4, slots, width), BF16),
        ],
        in_specs=vmem(4) + [anywhere] * 2,
        out_specs=vmem(3) + [anywhere],
        scratch_shapes=[
            pltpu.VMEM((count, inner), BF16),
            pltpu.VMEM(down.shape, BF16),
            pltpu.VMEM((4, slots, width), BF16),
            dma((2,)),
            dma((4,)),
        ]
        + reduce_scratch(1, rows, width)
        + ring_spread_scratch(),
        compiler_params=pltpu.CompilerParams(
            collective_id=2, has_side_effects=True, vmem_limit_bytes=48 * MIB
        ),
        name="middle_back",
    )(part.reshape(4, rows, width), middle, grad, gain[None], hidden, down)
    return dmiddle, dgain[0], spread.reshape(8 * rows, width), branch


def rows_body(
    rows_ref, grad_ref, down_ref, out_ref, raw_out, grad, down, block, loc, out_sem, far_s, far_r, core_s, core_r
):
    y, core = lax.axis_index("y"), lax.axis_index("core")
    half = rows_ref.shape[1] // 2
    sends = Sends()
    greet(neighbour("core", 1), *(neighbour("y", step) for step in (1, 2, 3)))
    at = pl.ds(pl.multiple_of(core * half, half), half)
    own = pltpu.make_async_copy(rows_ref.at[y], out_ref.at[y], loc.at[0])
    own.start()
    loads = []
    for n, (src, dst) in enumerate(((grad_ref, grad), (down_ref, down))):
        loads.append(pltpu.make_async_copy(src, dst, loc.at[1 + n]))
        loads[-1].start()
    for step in (2, 1, 3):
        target = mod4(y + step)
        sends(
            rows_ref.at[target, at],
            out_ref.at[y, at],
            far_s.at[step - 1],
            far_r.at[step - 1],
            neighbour("y", step),
        )
    for load in loads:
        load.wait()
    outs = []
    columns = raw_out.shape[1]
    for n, start in enumerate(range(0, columns, WIDE)):
        cols = min(WIDE, columns - start)
        if n >= 2:
            outs[n - 2].wait()
        block[n % 2, :, :cols] = dot(grad[...], down[:, start : start + cols], ((1,), (0,)))
        outs.append(
            pltpu.make_async_copy(
                block.at[n % 2, :, pl.ds(0, cols)], raw_out.at[:, pl.ds(start, cols)], out_sem.at[n % 2]
            )
        )
        outs[-1].start()
    for step in (1, 3, 2):
        source = mod4(y - step)
        block = out_ref.at[source, at]
        arrived(block, far_r.at[step - 1])
        sends(block, block, core_s.at[step - 1], core_r.at[step - 1], neighbour("core", 1))
    own.wait()
    other = pl.ds(pl.multiple_of((1 - core) * half, half), half)
    for step in (1, 3, 2):
        arrived(out_ref.at[mod4(y - step), other], core_r.at[step - 1])
    for out in outs[-2:]:
        out.wait()
    sends.finish()


def rows_to_experts(rows, grads, down):
    count, hidden = grads.shape[0], down.shape[1]
    anywhere = pl.BlockSpec(memory_space=pl.ANY)
    dma = pltpu.SemaphoreType.DMA
    return pl.pallas_call(
        rows_body,
        out_shape=[
            jax.ShapeDtypeStruct(rows.shape, rows.dtype),
            jax.ShapeDtypeStruct((count, hidden), F32),
        ],
        in_specs=[anywhere] * 3,
        out_specs=[anywhere] * 2,
        scratch_shapes=[
            pltpu.VMEM(grads.shape, BF16),
            pltpu.VMEM(down.shape, BF16),
            pltpu.VMEM((2, count, WIDE), F32),
            dma((3,)),
            dma((2,)),
            dma((3,)),
            dma((3,)),
            dma((3,)),
            dma((3,)),
        ],
        compiler_params=pltpu.CompilerParams(
            collective_id=4, has_side_effects=True, vmem_limit_bytes=40 * MIB
        ),
        name="rows_to_experts",
    )(rows, grads, down)


STEPS = (2, 1, -1, 0)


def finish_body(
    qkv_ref, small_ref, o_ref, ups_ref, downs_ref, part_ref, feed_ref, x_ref, middle_ref, dmiddle_ref, gain_ref,
    out_ref, up_out, down_out, output_ref, dinput_ref, small_out,
    g_ref, loc, t_buf, r_buf, tb_buf, rb_buf, c_buf,
    t_s, t_r, r_s, r_r, tb_s, tb_r, rb_s, rb_r, c_s, c_r,
    up_own, up_buf, up_sum, ex, ey, es, er,
    small_own, small_buf, small_s, small_r, *scratch,
):
    xl, xh, core = lax.axis_index("xl"), lax.axis_index("xh"), lax.axis_index("core")
    place = {"y": lax.axis_index("y"), "z": lax.axis_index("z")}
    my_y = place["y"]
    half = g_ref.shape[3] // 2
    quarter = half // 2
    rings = (("z", "y"), ("y", "z"))
    sends = Sends()
    column = 0
    parts = []
    for n, ref in enumerate((qkv_ref, small_ref, o_ref)):
        cols = ref.shape[-1]
        parts.append(pltpu.make_async_copy(ref, g_ref.at[..., pl.ds(column, cols)], loc.at[n]))
        parts[-1].start()
        column += cols
    for n, (src, dst) in enumerate(((ups_ref.at[xl], up_own), (downs_ref.at[my_y], down_out.at[my_y]))):
        parts.append(pltpu.make_async_copy(src, dst, loc.at[3 + n]))
        parts[-1].start()
    peers = ({"xh": xh, "core": 1 - core}, {"xh": 1 - xh, "core": core}, {"xh": 1 - xh, "core": 1 - core})
    greet(
        *peers,
        chip_along(1),
        chip_along(-1),
        *(neighbour("y", step) for step in (1, 2, 3)),
        *(neighbour("z", step) for step in (1, -1)),
    )
    both = slice(0, 2)
    ring_stages = ring_reduce_stages(part_ref, *scratch[7:15], sends)
    feed_stages = reduce_stages(CHUNKS, [feed_ref], *scratch[:7], sends)
    for step in (2, 1, 3, 0):
        sends(
            ups_ref.at[1 - xl, mod4(my_y + step)],
            up_buf.at[step],
            ex.at[step],
            ey.at[step],
            neighbour("xl", 1),
        )
    next(ring_stages)
    next(feed_stages)
    for part in parts[:3]:
        part.wait()

    def grad_ref(h, first, second, start):
        zz, yy = (first, second) if h == 0 else (second, first)
        return g_ref.at[zz, both, yy, pl.ds(h * half + start, quarter)]

    def grad(h, first, second, j, start, count):
        zz, yy = (first, second) if h == 0 else (second, first)
        return g_ref[zz, j, yy, h * half + start : h * half + start + count, :].astype(F32)

    def firsts(h, k):
        return mod4(place[rings[h][0]] + STEPS[k])

    for k in range(4):
        for h in (0, 1):
            second = place[rings[h][1]]
            for d, way in ((0, 1), (1, -1)):
                sends(
                    grad_ref(h, firsts(h, k), mod4(second + 2), d * quarter),
                    t_buf.at[h, d, k],
                    t_s.at[h, d, k],
                    t_r.at[h, d, k],
                    neighbour(rings[h][1], way),
                )
    for k in range(4):
        for h in (0, 1):
            second = place[rings[h][1]]
            for d, way in ((0, 1), (1, -1)):
                sends(
                    grad_ref(h, firsts(h, k), mod4(second + way), (1 - d) * quarter),
                    r_buf.at[h, d, k, both, pl.ds((1 - d) * quarter, quarter)],
                    r_s.at[h, d, k, 0],
                    r_r.at[h, d, k, 0],
                    neighbour(rings[h][1], way),
                )
    next(ring_stages)
    next(feed_stages)
    for k in range(4):
        for h in (0, 1):
            second = place[rings[h][1]]
            for d, way in ((0, 1), (1, -1)):
                arrived(t_buf.at[h, d, k], t_r.at[h, d, k])
                for j in (0, 1):
                    t_buf[h, d, k, j] = (
                        t_buf[h, d, k, j].astype(F32)
                        + grad(h, firsts(h, k), mod4(second + way), j, d * quarter, quarter)
                    ).astype(BF16)
                sends(
                    t_buf.at[h, d, k],
                    r_buf.at[h, d, k, both, pl.ds(d * quarter, quarter)],
                    r_s.at[h, d, k, 1],
                    r_r.at[h, d, k, 1],
                    neighbour(rings[h][1], way),
                )
    total = next(ring_stages)
    for step in (2, 1, 3):
        sends(
            downs_ref.at[mod4(my_y + step)],
            down_out.at[my_y],
            es.at[1, step - 1],
            er.at[1, step - 1],
            neighbour("y", step),
        )
    for part in parts[3:]:
        part.wait()
    for step in (2, 1, 3, 0):
        target = mod4(my_y + step)
        arrived(up_buf.at[step], ey.at[step])
        value = (up_own[target].astype(F32) + up_buf[step].astype(F32)).astype(BF16)
        if step == 0:
            up_out[my_y] = value
        else:
            up_sum[step - 1] = value
            sends(
                up_sum.at[step - 1],
                up_out.at[my_y],
                es.at[0, step - 1],
                er.at[0, step - 1],
                neighbour("y", step),
            )
    for k in range(4):
        for h in (0, 1):
            second = place[rings[h][1]]
            for d in (0, 1):
                arrived(r_buf.at[h, d, k, both, pl.ds((1 - d) * quarter, quarter)], r_r.at[h, d, k, 0])
                arrived(r_buf.at[h, d, k, both, pl.ds(d * quarter, quarter)], r_r.at[h, d, k, 1])
            for j in (0, 1):
                r_buf[h, 0, k, j] = (
                    r_buf[h, 0, k, j].astype(F32)
                    + r_buf[h, 1, k, j].astype(F32)
                    + grad(h, firsts(h, k), second, j, 0, half)
                ).astype(BF16)
            for d, way in ((0, 1), (1, -1)):
                device = neighbour(rings[h][0], way)
                if k == 0:
                    sends(
                        r_buf.at[h, 0, 0, both, pl.ds(d * quarter, quarter)],
                        tb_buf.at[h, d],
                        tb_s.at[h, d],
                        tb_r.at[h, d],
                        device,
                    )
                if k == 1 + d:
                    sends(
                        r_buf.at[h, 0, k, both, pl.ds((1 - d) * quarter, quarter)],
                        rb_buf.at[h, d, both, pl.ds((1 - d) * quarter, quarter)],
                        rb_s.at[h, d, 0],
                        rb_r.at[h, d, 0],
                        device,
                    )
                    arrived(tb_buf.at[h, d], tb_r.at[h, d])
                    for j in (0, 1):
                        tb_buf[h, d, j] = (
                            tb_buf[h, d, j].astype(F32)
                            + r_buf[h, 0, k, j, d * quarter : (d + 1) * quarter, :].astype(F32)
                        ).astype(BF16)
                    sends(
                        tb_buf.at[h, d],
                        rb_buf.at[h, d, both, pl.ds(d * quarter, quarter)],
                        rb_s.at[h, d, 1],
                        rb_r.at[h, d, 1],
                        device,
                    )
    rows_half = x_ref.shape[0] // 2
    for part in (0, 1):
        rows = slice(part * rows_half, (part + 1) * rows_half)
        x = x_ref[rows, :].astype(F32)
        inverse = lax.rsqrt(jnp.mean(x * x, 1, keepdims=True) + EPSILON)
        normed = x * inverse
        dscaled = total(part) * gain_ref[...]
        mean = jnp.mean(dscaled * normed, 1, keepdims=True)
        dinput_ref[rows, :] = dmiddle_ref[rows, :] + inverse * (dscaled - normed * mean)
    for h in (0, 1):
        for d in (0, 1):
            arrived(rb_buf.at[h, d, both, pl.ds((1 - d) * quarter, quarter)], rb_r.at[h, d, 0])
            arrived(rb_buf.at[h, d, both, pl.ds(d * quarter, quarter)], rb_r.at[h, d, 1])
        for j in (0, 1):
            rb_buf[h, 0, j] = (
                rb_buf[h, 0, j].astype(F32)
                + rb_buf[h, 1, j].astype(F32)
                + r_buf[h, 0, 3, j].astype(F32)
            ).astype(BF16)
        sends(rb_buf.at[h, 0, 1 - xl], c_buf.at[h], c_s.at[h], c_r.at[h], neighbour("xl", 1))
        out_ref[xl, h * half : (h + 1) * half, :] = rb_buf[h, 0, xl].astype(F32)
    for h in (0, 1):
        arrived(c_buf.at[h], c_r.at[h])
        out_ref[1 - xl, h * half : (h + 1) * half, :] = c_buf[h].astype(F32)
    first, last = qkv_ref.shape[-1], qkv_ref.shape[-1] + small_ref.shape[-1]
    small_own[...] = out_ref[0, :, first:last] + out_ref[1, :, first:last]
    for n, peer in enumerate(peers):
        sends(small_own, small_buf.at[n], small_s.at[n], small_r.at[n], peer)
    feed = next(feed_stages)
    step = x_ref.shape[0] // CHUNKS
    for n in range(CHUNKS):
        rows = slice(n * step, (n + 1) * step)
        output_ref[rows, :] = (middle_ref[rows, :] + feed(0, n)).astype(BF16)
    for n, result in enumerate((up_out, down_out)):
        for step in (1, 3, 2):
            arrived(result.at[mod4(my_y - step)], er.at[n, step - 1])
    for n in range(3):
        arrived(small_buf.at[n], small_r.at[n])
    small_out[...] = (small_own[...] + small_buf[1]) + (small_buf[0] + small_buf[2])
    sends.finish()


def finish(grads, ups, downs, part, feed, x, middle, dmiddle, gain):
    rows, cols = grads[0].shape[0], sum(grad.shape[1] for grad in grads)
    share = rows // 32
    half, quarter = share // 2, share // 4
    dma = pltpu.SemaphoreType.DMA
    up_cols, down_cols = ups.shape[1], downs.shape[1]
    small = (share, grads[1].shape[1])
    own_rows, width = x.shape
    anywhere = pl.BlockSpec(memory_space=pl.ANY)
    return pl.pallas_call(
        finish_body,
        out_shape=[
            jax.ShapeDtypeStruct((2, share, cols), F32),
            jax.ShapeDtypeStruct((4, share, up_cols), BF16),
            jax.ShapeDtypeStruct((4, share, down_cols), BF16),
            jax.ShapeDtypeStruct((own_rows, width), BF16),
            jax.ShapeDtypeStruct((own_rows, width), F32),
            jax.ShapeDtypeStruct(small, F32),
        ],
        in_specs=[anywhere] * 5 + vmem(6),
        out_specs=vmem(6),
        scratch_shapes=[
            pltpu.VMEM((4, 2, 4, share, cols), BF16),
            dma((5,)),
            pltpu.VMEM((2, 2, 4, 2, quarter, cols), BF16),
            pltpu.VMEM((2, 2, 4, 2, half, cols), BF16),
            pltpu.VMEM((2, 2, 2, quarter, cols), BF16),
            pltpu.VMEM((2, 2, 2, half, cols), BF16),
            pltpu.VMEM((2, half, cols), BF16),
            dma((2, 2, 4)),
            dma((2, 2, 4)),
            dma((2, 2, 4, 2)),
            dma((2, 2, 4, 2)),
            dma((2, 2)),
            dma((2, 2)),
            dma((2, 2, 2)),
            dma((2, 2, 2)),
            dma((2,)),
            dma((2,)),
            pltpu.VMEM((4, share, up_cols), BF16),
            pltpu.VMEM((4, share, up_cols), BF16),
            pltpu.VMEM((3, share, up_cols), BF16),
            dma((4,)),
            dma((4,)),
            dma((2, 3)),
            dma((2, 3)),
            pltpu.VMEM(small, F32),
            pltpu.VMEM((3, *small), F32),
            dma((3,)),
            dma((3,)),
        ]
        + reduce_scratch(1, own_rows, width)
        + ring_reduce_scratch(own_rows, width),
        compiler_params=pltpu.CompilerParams(
            collective_id=5, has_side_effects=True, vmem_limit_bytes=60 * MIB
        ),
        name="finish",
    )(
        *(grad.reshape(4, 2, 4, share, grad.shape[1]) for grad in grads),
        ups.reshape(2, 4, share, up_cols),
        downs.reshape(4, share, down_cols),
        part.reshape(2, 2, 2, own_rows, width),
        feed.reshape(4, own_rows, width),
        x,
        middle,
        dmiddle,
        gain[None],
    )


def dot(a, b, dims):
    return lax.dot_general(a, b, (dims, ((), ())), preferred_element_type=F32)


def experts_body(
    rows_ref, raw_ref, gate_up_ref, linear_up_ref, gate_ref,
    dgate_pre_out, dlinear_out, hidden_out, gated_out, dgate_out,
):
    @pl.when(pl.program_id(0) == 0)
    def _():
        dgate_out[...] = jnp.zeros_like(dgate_out)

    up = jnp.concatenate([gate_up_ref[...], linear_up_ref[...]], 1)
    joined = dot(rows_ref[...], up, ((1,), (0,)))
    gate_pre, linear = joined[:, :LANES], joined[:, LANES:]
    sigmoid = jax.nn.sigmoid(gate_pre)
    silu = gate_pre * sigmoid
    hidden = silu * linear
    dhidden = raw_ref[...]
    gate = gate_ref[...]
    dgate_out[...] += hidden * dhidden
    dhidden = dhidden * gate
    hidden_out[...] = hidden.astype(BF16)
    gated_out[...] = (hidden * gate).astype(BF16)
    dgate_pre_out[...] = (dhidden * linear * (sigmoid + silu * (1.0 - sigmoid))).astype(BF16)
    dlinear_out[...] = (dhidden * silu).astype(BF16)


def experts(rows, raw, up, gates):
    count, hidden = raw.shape
    width = up.shape[0]
    chunks = hidden // LANES
    chunk = pl.BlockSpec((count, LANES), lambda j: (0, j))
    some = jax.ShapeDtypeStruct((count, hidden), BF16)
    return pl.pallas_call(
        experts_body,
        grid=(chunks,),
        in_specs=[
            pl.BlockSpec((count, width), lambda j: (0, 0)),
            chunk,
            pl.BlockSpec((width, LANES), lambda j: (0, j)),
            pl.BlockSpec((width, LANES), lambda j: (0, chunks + j)),
            pl.BlockSpec((count, 1), lambda j: (0, 0)),
        ],
        out_specs=[chunk] * 4 + [pl.BlockSpec((count, LANES), lambda j: (0, 0))],
        out_shape=[some] * 4 + [jax.ShapeDtypeStruct((count, LANES), F32)],
        compiler_params=pltpu.CompilerParams(vmem_limit_bytes=56 * MIB),
        name="experts",
    )(rows, raw, up, up, gates)


def return_body(
    dgate_pre_ref, dlinear_ref, up_ref, dgate_ref, rows_ref,
    dunit_out, dgate_out, up_out,
    djoined, up, rows, dunit, dgate_own, dunit_buf, dgate_buf, dunit_sum, dgate_sum, block,
    loc, core_s, core_r, far_s, far_r, out_sem,
):
    y, core = lax.axis_index("y"), lax.axis_index("core")
    slots = dgate_ref.shape[1]
    half = slots // 2
    hidden = dgate_pre_ref.shape[1]
    sends = Sends()
    loads = []
    for n, (src, dst) in enumerate(
        (
            (up_ref, up),
            (dgate_pre_ref, djoined.at[:, pl.ds(0, hidden)]),
            (dlinear_ref, djoined.at[:, pl.ds(hidden, hidden)]),
            (rows_ref.at[:, pl.ds(0, rows.shape[1])], rows),
        )
    ):
        loads.append(pltpu.make_async_copy(src, dst, loc.at[1, n]))
        loads[-1].start()
    greet(neighbour("core", 1), *(neighbour("y", step) for step in (1, 2, 3)))
    mine = pl.ds(pl.multiple_of(core * half, half), half)
    theirs = pl.ds(pl.multiple_of((1 - core) * half, half), half)
    order = (2, 1, 3, 0)
    own = []
    for step in order:
        target = mod4(y + step)
        sends(
            dgate_ref.at[target, theirs],
            dgate_buf.at[step],
            core_s.at[1, step],
            core_r.at[1, step],
            neighbour("core", 1),
        )
        own.append(pltpu.make_async_copy(dgate_ref.at[target, mine], dgate_own.at[step], loc.at[0, step]))
        own[-1].start()
    for load in loads[:3]:
        load.wait()
    for copy in own:
        copy.wait()

    def compute(step):
        at = pl.ds(pl.multiple_of(mod4(y + step) * slots, slots), slots)
        dunit[step] = dot(djoined[at, :], up[...], ((1,), (1,))).astype(BF16)
        sends(
            dunit.at[step, theirs],
            dunit_buf.at[step],
            core_s.at[0, step],
            core_r.at[0, step],
            neighbour("core", 1),
        )

    def pass_on(step):
        arrived(dunit_buf.at[step], core_r.at[0, step])
        arrived(dgate_buf.at[step], core_r.at[1, step])
        dunit_value = (dunit[step, mine, :].astype(F32) + dunit_buf[step].astype(F32)).astype(BF16)
        dgate_value = dgate_own[step] + dgate_buf[step]
        if step == 0:
            dunit_out[y] = dunit_value
            dgate_out[y] = dgate_value
            return
        dunit_sum[step - 1] = dunit_value
        dgate_sum[step - 1] = dgate_value
        for n, (summed, result) in enumerate(((dunit_sum, dunit_out), (dgate_sum, dgate_out))):
            sends(
                summed.at[step - 1],
                result.at[y],
                far_s.at[n, step - 1],
                far_r.at[n, step - 1],
                neighbour("y", step),
            )

    compute(2)
    compute(1)
    pass_on(2)
    compute(3)
    pass_on(1)
    compute(0)
    pass_on(3)
    loads[3].wait()
    blocks = up_out.shape[0] // WIDE

    @pl.loop(0, blocks)
    def _(j):
        at = pl.ds(pl.multiple_of(j * WIDE, WIDE), WIDE)
        slot = lax.rem(j, 2)

        @pl.when(j >= 2)
        def _():
            pltpu.make_async_copy(block.at[slot], up_out.at[at], out_sem.at[slot]).wait()

        block[slot] = dot(rows[:, at], djoined[...], ((0,), (0,))).astype(BF16)
        pltpu.make_async_copy(block.at[slot], up_out.at[at], out_sem.at[slot]).start()

    pass_on(0)
    for slot in (0, 1):
        pltpu.make_async_copy(block.at[slot], up_out.at[pl.ds(0, WIDE)], out_sem.at[slot]).wait()
    for n, result in enumerate((dunit_out, dgate_out)):
        for step in (1, 3, 2):
            arrived(result.at[mod4(y - step)], far_r.at[n, step - 1])
    sends.finish()


def return_rows(dgate_pre, dlinear, up, dgate, rows):
    _, slots, lanes = dgate.shape
    half = slots // 2
    width, wide = up.shape
    count = dlinear.shape[0]
    dma = pltpu.SemaphoreType.DMA
    anywhere = pl.BlockSpec(memory_space=pl.ANY)
    return pl.pallas_call(
        return_body,
        out_shape=[
            jax.ShapeDtypeStruct((4, half, width), BF16),
            jax.ShapeDtypeStruct((4, half, lanes), F32),
            jax.ShapeDtypeStruct((width, wide), BF16),
        ],
        in_specs=[anywhere] * 5,
        out_specs=vmem(2) + [anywhere],
        scratch_shapes=[
            pltpu.VMEM((count, wide), BF16),
            pltpu.VMEM((width, wide), BF16),
            pltpu.VMEM((count, width), BF16),
            pltpu.VMEM((4, slots, width), BF16),
            pltpu.VMEM((4, half, lanes), F32),
            pltpu.VMEM((4, half, width), BF16),
            pltpu.VMEM((4, half, lanes), F32),
            pltpu.VMEM((3, half, width), BF16),
            pltpu.VMEM((3, half, lanes), F32),
            pltpu.VMEM((2, WIDE, wide), BF16),
            dma((2, 4)),
            dma((2, 4)),
            dma((2, 4)),
            dma((2, 3)),
            dma((2, 3)),
            dma((2,)),
        ],
        compiler_params=pltpu.CompilerParams(
            collective_id=3, has_side_effects=True, vmem_limit_bytes=62 * MIB
        ),
        name="return_rows",
    )(dgate_pre, dlinear, up, dgate, rows)


def attention_body(
    k_ref, v_ref, q0, q1, q2, cos_ref, sin_ref, col_ref, row_ref, gate_ref,
    key_out, val_out, que_out, mix_out, gmix_out, prob_out,
):
    h = pl.program_id(1)
    cosine, sine = cos_ref[...], sin_ref[...]
    scale = 1.0 / math.sqrt(HD)

    def rotated(v):
        return v * cosine + pltpu.roll(v, HD // 2, 1) * sine

    key = rotated(k_ref[...]).astype(BF16)
    val = v_ref[...].astype(BF16)
    key_out[...] = key
    val_out[...] = val
    tokens = key.shape[0]
    half = tokens // 2
    allowed = []
    for start in (0, half):
        seen = start + half
        at_row = start + lax.broadcasted_iota(jnp.int32, (half, seen), 0)
        at_col = lax.broadcasted_iota(jnp.int32, (half, seen), 1)
        seg_row, seg_col = row_ref[0, :, :seen], col_ref[start : start + half, :]
        allowed.append((at_col <= at_row) & ((seg_row == 0) | (seg_row == seg_col)))
    for e, q_ref in enumerate((q0, q1, q2)):
        query = (rotated(q_ref[...]) * scale).astype(BF16)
        at = pl.ds(pl.multiple_of((e * HEADS + h) * HD, HD), HD)
        que_out[:, at] = query
        for n, start in enumerate((0, half)):
            rows, seen = slice(start, start + half), start + half
            scores = jnp.where(allowed[n], dot(query[rows], key[:seen], ((1,), (1,))), NEGATIVE)
            largest = jnp.max(scores, 1, keepdims=True)
            expsum = jnp.exp(scores - largest)
            prob = (expsum * (1.0 / jnp.sum(expsum, 1, keepdims=True))).astype(BF16)
            prob_out[0, 0, e, rows, :seen] = prob
            mixed = dot(prob, val[:seen], ((1,), (0,))).astype(BF16)
            mix_out[rows, at] = mixed
            gmix_out[rows, at] = (mixed.astype(F32) * gate_ref[rows, e : e + 1]).astype(BF16)


def block_specs(tokens):
    def column(n):
        return pl.BlockSpec((tokens, HD), lambda g, h: (g, n * HEADS + h))

    def rows(width):
        return pl.BlockSpec((tokens, width), lambda g, h: (g, 0))

    return column, rows


def prob_spec(tokens):
    return pl.BlockSpec((1, 1, 3, tokens, tokens), lambda g, h: (g, h, 0, 0, 0))


def attention_forward(joined, cosine, sine, segments, gates):
    groups, tokens = segments.shape
    column, rows = block_specs(tokens)
    wide = jax.ShapeDtypeStruct((groups * tokens, 3 * HEADS * HD), BF16)
    narrow = jax.ShapeDtypeStruct((groups * tokens, HEADS * HD), BF16)
    return pl.pallas_call(
        attention_body,
        grid=(groups, HEADS),
        in_specs=[column(n) for n in range(5)]
        + [rows(HD)] * 2
        + [rows(1), pl.BlockSpec((1, 1, tokens), lambda g, h: (g, 0, 0)), rows(gates.shape[1])],
        out_specs=[column(0), column(0)] + [rows(wide.shape[1])] * 3 + [prob_spec(tokens)],
        out_shape=[narrow, narrow, wide, wide, wide]
        + [jax.ShapeDtypeStruct((groups, HEADS, 3, tokens, tokens), BF16)],
        compiler_params=pltpu.CompilerParams(vmem_limit_bytes=48 * MIB),
        name="attention_forward",
    )(
        *[joined] * 5, cosine, sine, segments.reshape(-1, 1), segments[:, None], gates
    )


def attention_back_body(
    key_ref, val_ref, q0, q1, q2, m0, m1, m2, h0, h1, h2, prob_ref, cos_ref, sin_ref, gate_ref,
    grad_out, dgate_out,
):
    h = pl.program_id(1)
    cosine, sine = cos_ref[...], sin_ref[...]
    scale = 1.0 / math.sqrt(HD)

    def rotated_back(v):
        return v * cosine - pltpu.roll(v, HD // 2, 1) * sine

    key, val = key_ref[...], val_ref[...]
    tokens = key.shape[0]
    half = tokens // 2
    dkeys = [jnp.zeros((half, HD), F32)] * 2
    dvals = [jnp.zeros((half, HD), F32)] * 2
    lane = lax.broadcasted_iota(jnp.int32, (tokens, HD), 1)
    dgates = jnp.zeros((tokens, HD), F32)
    for e, (q_ref, m_ref, h_ref) in enumerate(((q0, m0, h0), (q1, m1, h1), (q2, m2, h2))):
        query, mixed, raw = q_ref[...], m_ref[...].astype(F32), h_ref[...]
        inner = jnp.sum(mixed * raw, 1, keepdims=True)
        dgates = dgates + jnp.where(lane == e, inner, 0.0)
        gate = gate_ref[:, e : e + 1]
        dmixed = (raw * gate).astype(BF16)
        delta = jnp.sum(dmixed.astype(F32) * mixed, 1, keepdims=True)
        dqueries = []
        for start in (0, half):
            rows, seen = slice(start, start + half), start + half
            prob = prob_ref[0, 0, e, rows, :seen]
            dprob = dot(dmixed[rows], val[:seen], ((1,), (1,)))
            dscores = (prob.astype(F32) * (dprob - delta[rows])).astype(BF16)
            dqueries.append(dot(dscores, key[:seen], ((1,), (0,))))
            dval = dot(prob, dmixed[rows], ((0,), (0,)))
            dkey = dot(dscores, query[rows], ((0,), (0,)))
            dvals[0] = dvals[0] + dval[:half]
            dkeys[0] = dkeys[0] + dkey[:half]
            if start:
                dvals[1] = dvals[1] + dval[half:]
                dkeys[1] = dkeys[1] + dkey[half:]
        dquery = jnp.concatenate(dqueries, 0)
        at = pl.ds(pl.multiple_of(((2 + e) * HEADS + h) * HD, HD), HD)
        grad_out[:, at] = rotated_back(dquery * scale).astype(BF16)
    dkey, dval = jnp.concatenate(dkeys, 0), jnp.concatenate(dvals, 0)
    grad_out[:, pl.ds(pl.multiple_of(h * HD, HD), HD)] = rotated_back(dkey).astype(BF16)
    grad_out[:, pl.ds(pl.multiple_of((HEADS + h) * HD, HD), HD)] = dval.astype(BF16)

    @pl.when(h == 0)
    def _():
        dgate_out[...] = dgates

    @pl.when(h > 0)
    def _():
        dgate_out[...] += dgates


def attention_back(key, val, que, mix, raw, prob, cosine, sine, gates):
    groups, tokens = prob.shape[0], prob.shape[-1]
    column, rows = block_specs(tokens)
    thirds = [column(n) for n in range(3)]
    grads = jax.ShapeDtypeStruct((groups * tokens, 5 * HEADS * HD), BF16)
    return pl.pallas_call(
        attention_back_body,
        grid=(groups, HEADS),
        in_specs=[column(0), column(0)]
        + thirds * 3
        + [prob_spec(tokens)]
        + [rows(HD)] * 2
        + [rows(gates.shape[1])],
        out_specs=[rows(grads.shape[1]), rows(HD)],
        out_shape=[grads, jax.ShapeDtypeStruct((groups * tokens, HD), F32)],
        compiler_params=pltpu.CompilerParams(vmem_limit_bytes=48 * MIB),
        name="attention_back",
    )(key, val, que, que, que, mix, mix, mix, raw, raw, raw, prob, cosine, sine, gates)


def positions(segments):
    index = jnp.arange(segments.shape[0], dtype=jnp.int32)
    prompt = jnp.sum((segments == 0).astype(jnp.int32))
    first = jnp.sum((segments == 1).astype(jnp.int32))
    before = jnp.where(segments == 0, 0, jnp.where(segments == 1, prompt, prompt + first))
    return jnp.where(segments == 0, index, prompt + index - before)


def route_gates(logits, routes, count):
    onehot = (routes[:, :, None] == jnp.arange(count, dtype=jnp.int32)).astype(F32)
    chosen = jnp.sum(onehot * logits[:, None, :], -1)
    expsum = jnp.exp(chosen - jnp.max(chosen, -1, keepdims=True))
    weights = expsum / jnp.sum(expsum, -1, keepdims=True)
    return weights, onehot, jnp.sum(weights[:, :, None] * onehot, 1)


def router_back(dgate, weights, onehot):
    dchosen = jnp.sum(dgate[:, None, :] * onehot, -1)
    dselect = weights * (dchosen - jnp.sum(weights * dchosen, -1, keepdims=True))
    return jnp.sum(dselect[:, :, None] * onehot, 1).astype(BF16)


def normalize(activations):
    inverse = lax.rsqrt(jnp.mean(activations * activations, -1, keepdims=True) + EPSILON)
    return activations * inverse, inverse


def reorder(rows):
    count, width = rows.shape
    return jnp.transpose(rows.reshape(count, 4, 2, 4, width // 32), (0, 3, 2, 1, 4)).reshape(count, width)


def pad_to(array, width):
    return jnp.pad(array, ((0, 0), (0, width - array.shape[1])))


def on_device(
    inputs,
    segments,
    att_routes,
    mlp_routes,
    key_value,
    query_proj,
    output_proj,
    router_att,
    gain_att,
    gate_up,
    down_proj,
    router_mlp,
    gain_mlp,
    out_grad,
):
    width = inputs.shape[1]
    inner = query_proj.shape[2]
    hidden_local = down_proj.shape[1]
    att_count = query_proj.shape[0]
    mlp_count = gate_up.shape[0]
    share = gate_up.shape[1]
    part = inner // 2
    qkv_cols = (2 + att_count) * part
    small_at = qkv_cols
    out_at = qkv_cols + 128
    small = jnp.concatenate([router_att, router_mlp, gain_att[:, None], gain_mlp[:, None]], 1)
    own_att = jnp.concatenate(
        [
            jnp.transpose(key_value.reshape(share, 2, 2, part), (2, 0, 1, 3)).reshape(2, share, -1),
            jnp.transpose(query_proj.reshape(att_count, share, 2, part), (2, 1, 0, 3)).reshape(
                2, share, -1
            ),
            jnp.broadcast_to(pad_to(small, 128), (2, share, 128)),
            jnp.transpose(output_proj.reshape(att_count, 2, part, share), (1, 3, 0, 2)).reshape(
                2, share, -1
            ),
        ],
        2,
    )
    inputs = reorder(inputs)
    out_grad = reorder(out_grad)
    x_all = lax.all_gather(inputs, ("xl", *TP), axis=0, tiled=True)
    grad_all = lax.all_gather(out_grad, TP, axis=0, tiled=True)
    marks = pad_to(jnp.concatenate([segments[:, None], att_routes], 1), LANES).astype(BF16)
    weights, up_parts, down_parts, marks = gather_dp(
        own_att,
        gate_up.reshape(mlp_count, share, -1),
        jnp.swapaxes(down_proj, 1, 2),
        marks,
    )
    weights, up_parts, down_parts = lax.optimization_barrier((weights, up_parts, down_parts))
    marks = marks[:, :, :3].astype(jnp.int32)
    up_whole = lax.all_gather(
        up_parts.reshape(2 * mlp_count * share, -1), "z", axis=0, tiled=True
    )
    down_whole = lax.all_gather(
        down_parts.reshape(2 * mlp_count * share, -1), "z", axis=0, tiled=True
    )

    weights = gather_rest(weights, share)

    tokens = segments.shape[0]
    match = jnp.sum((mlp_routes[:, :, None] == jnp.arange(mlp_count, dtype=jnp.int32)).astype(BF16), 1)
    index = jnp.arange(tokens, dtype=jnp.int32)
    lower = (index[None, :] < index[:, None]).astype(BF16)
    rank = dot(lower, match, ((1,), (0,)))
    slot = jnp.where(match > 0, rank.astype(jnp.int32), -1)
    pick = (slot.T[:, None, :] == jnp.arange(CAP, dtype=jnp.int32)[None, :, None]).astype(BF16)
    pick_rows = pick.reshape(mlp_count * CAP, tokens)
    grad_rows = dot(pick_rows, grad_all, ((1,), (0,))).astype(BF16)
    grad_in = lax.all_to_all(grad_rows.reshape(mlp_count, CAP, width), "y", 0, 0, tiled=True)
    grad_in = grad_in.reshape(mlp_count * CAP, width)

    small_all = weights[:, small_at : small_at + 128].astype(F32)
    gain_one, gain_two = small_all[:, 7], small_all[:, 8]
    segments = marks[:, :, 0]
    att_routes = marks[:, :, 1:].reshape(2 * tokens, 2)
    places = jax.vmap(positions)(segments).reshape(-1).astype(F32)
    frequency = ROPE_BASE ** (-2.0 * jnp.arange(HD // 2, dtype=F32) / HD)
    angles = places[:, None] * frequency[None, :]
    cosine = jnp.concatenate([jnp.cos(angles)] * 2, 1)
    sine = jnp.concatenate([-jnp.sin(angles), jnp.sin(angles)], 1)
    normed_one, _ = normalize(x_all.astype(F32))
    unit_one = (normed_one * gain_one).astype(BF16)
    joined_att = dot(unit_one, weights[:, :out_at], ((1,), (0,)))
    weights_att, onehot_att, gate_att = route_gates(
        joined_att[:, small_at : small_at + att_count], att_routes, att_count
    )
    key_rot, val_rows, queries, mixed, gmixed, prob = attention_forward(
        joined_att, cosine, sine, segments, gate_att
    )
    out_weights = weights[:, out_at:]
    attention = dot(gmixed, out_weights, ((1,), (1,))).astype(BF16)
    middle, unit_two = middle_and_unit(attention, inputs, gain_two)

    router_two = weights[:, small_at + att_count : small_at + att_count + mlp_count]
    logit_mlp = dot(unit_two, router_two, ((1,), (0,)))
    weights_mlp, onehot_mlp, gate_mlp = route_gates(logit_mlp, mlp_routes, mlp_count)
    gate_high = gate_mlp.astype(BF16)
    gate_low = (gate_mlp - gate_high.astype(F32)).astype(BF16)
    extended = jnp.concatenate([unit_two, pad_to(jnp.concatenate([gate_high, gate_low], 1), 128)], 1)
    rows_out = dot(pick_rows, extended, ((1,), (0,))).astype(BF16)
    rows_ext, raw = rows_to_experts(
        rows_out.reshape(mlp_count, CAP, width + 128), grad_in, down_whole
    )
    rows_ext = rows_ext.reshape(mlp_count * CAP, width + 128)
    gates_ext = rows_ext[:, width : width + 2 * mlp_count].astype(F32)
    mine = (jnp.arange(2 * mlp_count) % mlp_count == lax.axis_index("y")).astype(F32)
    gates_in = jnp.sum(gates_ext * mine, 1, keepdims=True)
    dgate_pre, dlinear, hidden, gated, dgate_part = experts(rows_ext, raw, up_whole, gates_in)
    grad_down_whole = dot(grad_in, gated, ((0,), (0,))).astype(BF16)
    dgate_part, grad_down_whole = lax.optimization_barrier((dgate_part, grad_down_whole))
    grad_down_sum = lax.psum_scatter(grad_down_whole, "z", scatter_dimension=0, tiled=True)
    dunit_back, dgate_back, grad_up_whole = return_rows(
        dgate_pre, dlinear, up_whole, dgate_part.reshape(mlp_count, CAP, LANES), rows_ext
    )
    grad_up_sum = lax.psum_scatter(grad_up_whole, "z", scatter_dimension=0, tiled=True)
    halves = grad_down_sum.reshape(2, mlp_count * share, hidden_local)
    xl = lax.axis_index("xl")
    theirs = lax.ppermute(
        lax.dynamic_index_in_dim(halves, 1 - xl, 0, keepdims=False), "xl", ((0, 1), (1, 0))
    )
    grad_down_sum = (
        lax.dynamic_index_in_dim(halves, xl, 0, keepdims=False).astype(F32) + theirs.astype(F32)
    ).astype(BF16)
    pick_half = lax.dynamic_slice_in_dim(pick, lax.axis_index("core") * (CAP // 2), CAP // 2, 1)
    dgate_two = jnp.sum(pick_half.astype(F32) * jnp.sum(dgate_back, -1, keepdims=True), 1).T
    dlogit_mlp = router_back(dgate_two, weights_mlp, onehot_mlp)
    dunit_two = dot(
        pick_half.reshape(-1, tokens), dunit_back.reshape(-1, width), ((0,), (0,))
    ) + dot(dlogit_mlp, router_two, ((1,), (1,)))
    grad_rmlp = dot(unit_two, dlogit_mlp, ((0,), (0,)))
    dmiddle, grad_gain_two, dattention, branch_part = middle_back(
        dunit_two.astype(BF16), middle, out_grad, gain_two, hidden, down_whole
    )
    branch_back = lax.all_to_all(branch_part, "y", 0, 0, tiled=True)

    raw = dot(dattention, out_weights, ((1,), (0,)))
    grad_qkv, dgate_one = attention_back(
        key_rot, val_rows, queries, mixed, raw, prob, cosine, sine, gate_att
    )
    dlogit_att = router_back(dgate_one[:, :att_count], weights_att, onehot_att)
    grad_joined = jnp.concatenate([grad_qkv, pad_to(dlogit_att, 128)], 1)
    dunit_one = dot(grad_joined, weights[:, :out_at], ((1,), (1,)))
    grad_gain_one = jnp.sum(dunit_one * normed_one, 0)
    grad_small = jnp.concatenate(
        [
            dot(unit_one, dlogit_att, ((0,), (0,))),
            grad_rmlp,
            grad_gain_one[:, None],
            grad_gain_two[:, None],
        ],
        1,
    )
    gate_slots = jnp.sum(pick.astype(F32) * gate_mlp.T[:, None, :], -1, keepdims=True)
    feed = dot(
        pick_rows,
        (branch_back.astype(F32) * gate_slots).astype(BF16).reshape(-1, width),
        ((0,), (0,)),
    )
    summed_att, ups_sum, downs_sum, output, grad_input, small_sum = finish(
        (
            dot(unit_one, grad_qkv, ((0,), (0,))).astype(BF16),
            pad_to(grad_small, 128).astype(BF16),
            dot(dattention, gmixed, ((0,), (0,))).astype(BF16),
        ),
        grad_up_sum,
        grad_down_sum,
        dunit_one.astype(BF16),
        feed.astype(BF16),
        inputs,
        middle,
        dmiddle,
        gain_one,
    )
    grad_kv = jnp.transpose(
        summed_att[:, :, : 2 * part].reshape(2, share, 2, part), (1, 2, 0, 3)
    ).reshape(share, 2, inner)
    grad_query = jnp.transpose(
        summed_att[:, :, 2 * part : qkv_cols].reshape(2, share, att_count, part), (2, 1, 0, 3)
    ).reshape(att_count, share, inner)
    grad_output = jnp.transpose(
        summed_att[:, :, out_at:].reshape(2, share, att_count, part), (2, 0, 3, 1)
    ).reshape(att_count, inner, share)
    output = reorder(output)
    grad_input = reorder(grad_input)

    grads_up = ups_sum.astype(F32).reshape(mlp_count, share, 2, hidden_local)
    grads_down = jnp.swapaxes(downs_sum.astype(F32), 1, 2)
    return (
        output,
        grad_input,
        grad_kv,
        grad_query,
        grad_output,
        small_sum[:, :3],
        small_sum[:, 7],
        grads_up,
        grads_down,
        small_sum[:, 3:7],
        small_sum[:, 8],
    )


def solution(mesh):
    fine = Mesh(mesh.devices.reshape(4, 2, 4, 2, 2), ALL)
    return jax.shard_map(
        on_device,
        mesh=fine,
        in_specs=(
            P(ALL, None),
            P(DP),
            P(DP, None),
            P(DP, None),
            P(DP, None, TP),
            P(None, DP, TP),
            P(None, TP, DP),
            P(DP, None),
            P(DP),
            P(None, DP, None, TP),
            P(None, TP, DP),
            P(DP, None),
            P(DP),
            P(ALL, None),
        ),
        out_specs=(
            P(ALL, None),
            P(ALL, None),
            P(DP, None, TP),
            P(None, DP, TP),
            P(None, TP, DP),
            P(DP, None),
            P(DP),
            P(None, DP, None, TP),
            P(None, TP, DP),
            P(DP, None),
            P(DP),
        ),
        check_vma=False,
    )
```

```python
import functools
import math

import jax
import jax.numpy as jnp
from jax import lax
from jax.experimental import pallas as pl
from jax.experimental.pallas import tpu as pltpu
from jax.sharding import Mesh, PartitionSpec as P

LANES = 128
WIDE = 256
HD = 128
HEADS = 2
CAP = 320
EPSILON = 1e-06
NEGATIVE = -1e30
ROPE_BASE = 10000.0
MESH_ID = pl.DeviceIdType.MESH
MIB = 1024 * 1024
DP = ("y", "xl", "z")
TP = ("xh", "core")
ALL = DP + TP
F32 = jnp.float32
BF16 = jnp.bfloat16


def mod4(place):
    return lax.rem(place + 4, 4)


def neighbour(axis, step):
    size = 4 if axis in ("y", "z") else 2
    return {axis: lax.rem(lax.axis_index(axis) + step + size, size)}


def chip_along(step):
    at = lax.rem(lax.axis_index("xh") * 2 + lax.axis_index("xl") + step + 4, 4)
    return {"xh": lax.div(at, 2), "xl": lax.rem(at, 2)}


def greet(*devices):
    barrier = pltpu.get_barrier_semaphore()
    for device in devices:
        pl.semaphore_signal(barrier, inc=1, device_id=device, device_id_type=MESH_ID)
    pl.semaphore_wait(barrier, len(devices))


def arrived(ref, sem):
    pltpu.make_async_copy(ref, ref, sem).wait()


class Sends:
    def __init__(self):
        self.copies = []

    def __call__(self, src, dst, send_sem, recv_sem, device):
        copy = pltpu.make_async_remote_copy(
            src_ref=src,
            dst_ref=dst,
            send_sem=send_sem,
            recv_sem=recv_sem,
            device_id=device,
            device_id_type=MESH_ID,
        )
        copy.start()
        self.copies.append(copy)

    def finish(self):
        for copy in self.copies:
            copy.wait_send()


def gather_body(
    x_ref, ups_ref, downs_ref, marks_ref, out_ref, up_ref, down_ref, marks_out,
    loc, xs, xr, s1, r1m, r1p, f1s, f1r, s2, r2m, r2p, f2s, f2r, es, er, ex, ey, ms, mr,
):
    y, xl, z = lax.axis_index("y"), lax.axis_index("xl"), lax.axis_index("z")
    half = x_ref.shape[1] // 2
    quarter = half // 2
    greet(
        neighbour("xl", 1),
        *(neighbour("y", step) for step in (1, 2, 3)),
        *(neighbour("z", step) for step in (1, -1)),
    )
    rings = (("z", "y"), ("y", "z"))
    place = {"y": y, "z": z}
    other = 1 - xl
    both = pl.ds(0, 2)
    sends = Sends()
    send = sends

    def slot(h, first, second, j, start, count):
        yy, zz = (second, first) if h == 0 else (first, second)
        return out_ref.at[zz, j, yy, pl.ds(start, count)]

    own = pltpu.make_async_copy(x_ref.at[xl], out_ref.at[z, xl, y], loc.at[0])
    own.start()
    own_marks = pltpu.make_async_copy(marks_ref, marks_out.at[xl], loc.at[3])
    own_marks.start()
    send(marks_ref, marks_out.at[xl], ms, mr, neighbour("xl", 1))
    experts = ((ups_ref, up_ref), (downs_ref, down_ref))
    kept = []
    for n, (shards, expert) in enumerate(experts):
        place_of = expert.at[xl] if n == 0 else expert
        kept.append(pltpu.make_async_copy(shards.at[y], place_of.at[y], loc.at[1 + n]))
        kept[-1].start()
        if n == 0:
            send(shards.at[y], place_of.at[y], ex.at[0], ey.at[0], neighbour("xl", 1))
        for step in (1, 3, 2):
            send(
                shards.at[mod4(y + step)],
                place_of.at[y],
                es.at[n, step - 1],
                er.at[n, step - 1],
                neighbour("y", step),
            )
    for h in (0, 1):
        first, second = place[rings[h][0]], place[rings[h][1]]
        src = x_ref.at[xl, pl.ds(h * half, half)]
        dst = slot(h, first, second, xl, h * half, half)
        send(x_ref.at[other, pl.ds(h * half, half)], dst, xs.at[h], xr.at[h], neighbour("xl", 1))
        send(src, dst, s1.at[h, 0, 0], r1m.at[h, 0], neighbour(rings[h][0], 1))
        send(src, dst, s1.at[h, 0, 1], r1p.at[h, 0], neighbour(rings[h][0], -1))
    own.wait()

    def send_second(h, k, first):
        block = slot(h, first, place[rings[h][1]], both, h * half, half)
        send(block, block, s2.at[h, k, 0], r2m.at[h, k], neighbour(rings[h][1], 1))
        send(block, block, s2.at[h, k, 1], r2p.at[h, k], neighbour(rings[h][1], -1))

    for h in (0, 1):
        first, second = place[rings[h][0]], place[rings[h][1]]
        block = slot(h, first, second, other, h * half, half)
        arrived(block, xr.at[h])
        send(block, block, s1.at[h, 1, 0], r1m.at[h, 1], neighbour(rings[h][0], 1))
        send(block, block, s1.at[h, 1, 1], r1p.at[h, 1], neighbour(rings[h][0], -1))
        send_second(h, 0, first)
    for j, jx in ((0, xl), (1, other)):
        for h in (0, 1):
            first, second = place[rings[h][0]], place[rings[h][1]]
            arrived(slot(h, mod4(first - 1), second, jx, h * half, half), r1m.at[h, j])
            block = slot(h, mod4(first - 1), second, jx, h * half, quarter)
            send(block, block, f1s.at[h, j, 0], f1r.at[h, j, 0], neighbour(rings[h][0], 1))
            arrived(slot(h, mod4(first + 1), second, jx, h * half, half), r1p.at[h, j])
            block = slot(h, mod4(first + 1), second, jx, h * half + quarter, quarter)
            send(block, block, f1s.at[h, j, 1], f1r.at[h, j, 1], neighbour(rings[h][0], -1))
    for k, step in ((1, -1), (2, 1)):
        for h in (0, 1):
            send_second(h, k, mod4(place[rings[h][0]] + step))
    for h in (0, 1):
        first, second = place[rings[h][0]], place[rings[h][1]]
        for j, jx in ((0, xl), (1, other)):
            for p in (0, 1):
                block = slot(h, mod4(first + 2), second, jx, h * half + p * quarter, quarter)
                arrived(block, f1r.at[h, j, p])
        send_second(h, 3, mod4(first + 2))
    for step in (1, 3, 2):
        landed = up_ref.at[xl, mod4(y - step)]
        arrived(landed, er.at[0, step - 1])
        send(landed, landed, ex.at[step], ey.at[step], neighbour("xl", 1))
    steps = ((0, 0), (1, -1), (2, 1), (3, 2))
    for k, step in steps:
        for h in (0, 1):
            first, second = mod4(place[rings[h][0]] + step), place[rings[h][1]]
            arrived(slot(h, first, mod4(second - 1), both, h * half, half), r2m.at[h, k])
            block = slot(h, first, mod4(second - 1), both, h * half, quarter)
            send(block, block, f2s.at[h, k, 0], f2r.at[h, k, 0], neighbour(rings[h][1], 1))
            arrived(slot(h, first, mod4(second + 1), both, h * half, half), r2p.at[h, k])
            block = slot(h, first, mod4(second + 1), both, h * half + quarter, quarter)
            send(block, block, f2s.at[h, k, 1], f2r.at[h, k, 1], neighbour(rings[h][1], -1))
    for k, step in steps:
        for h in (0, 1):
            first, second = mod4(place[rings[h][0]] + step), place[rings[h][1]]
            for p in (0, 1):
                block = slot(h, first, mod4(second + 2), both, h * half + p * quarter, quarter)
                arrived(block, f2r.at[h, k, p])
    for step in (0, 1, 3, 2):
        arrived(up_ref.at[other, mod4(y - step)], ey.at[step])
    for step in (1, 3, 2):
        arrived(down_ref.at[mod4(y - step)], er.at[1, step - 1])
    for copy in kept:
        copy.wait()
    arrived(marks_out.at[other], mr)
    own_marks.wait()
    sends.finish()


def gather_dp(shard, ups, downs, marks):
    _, rows, cols = shard.shape
    dma = pltpu.SemaphoreType.DMA
    whole, up, down, marks = pl.pallas_call(
        gather_body,
        out_shape=[
            jax.ShapeDtypeStruct((4, 2, 4, rows, cols), shard.dtype),
            jax.ShapeDtypeStruct((2, *ups.shape), ups.dtype),
            jax.ShapeDtypeStruct(downs.shape, downs.dtype),
            jax.ShapeDtypeStruct((2, *marks.shape), marks.dtype),
        ],
        in_specs=[pl.BlockSpec(memory_space=pl.ANY)] * 4,
        out_specs=[pl.BlockSpec(memory_space=pl.ANY)] * 4,
        scratch_shapes=[
            dma((4,)),
            dma((2,)),
            dma((2,)),
            dma((2, 2, 2)),
            dma((2, 2)),
            dma((2, 2)),
            dma((2, 2, 2)),
            dma((2, 2, 2)),
            dma((2, 4, 2)),
            dma((2, 4)),
            dma((2, 4)),
            dma((2, 4, 2)),
            dma((2, 4, 2)),
            dma((2, 3)),
            dma((2, 3)),
            dma((4,)),
            dma((4,)),
            dma,
            dma,
        ],
        compiler_params=pltpu.CompilerParams(collective_id=0, has_side_effects=True),
        name="gather_weights",
    )(shard, ups, downs, marks)
    return whole.reshape(32 * rows, cols), up, down, marks


def reduce_stages(scatter_count, part_refs, core_buf, sum_buf, far_buf, core_s, core_r, far_s, far_r, sends):
    xh, core = lax.axis_index("xh"), lax.axis_index("core")
    rows = part_refs[0].shape[1]
    step = rows // scatter_count
    far, here = 1 - xh, xh
    for n, chunk in enumerate(range(0, rows, step)):
        at = pl.ds(chunk, step)
        for i, part in enumerate(part_refs):
            sends(
                part.at[far * 2 + 1 - core, at],
                core_buf.at[i, 0, at],
                core_s.at[i, n, 0],
                core_r.at[i, n, 0],
                neighbour("core", 1),
            )
    for n, chunk in enumerate(range(0, rows, step)):
        at = pl.ds(chunk, step)
        for i, part in enumerate(part_refs):
            sends(
                part.at[here * 2 + 1 - core, at],
                core_buf.at[i, 1, at],
                core_s.at[i, n, 1],
                core_r.at[i, n, 1],
                neighbour("core", 1),
            )
    yield
    for n, chunk in enumerate(range(0, rows, step)):
        at = pl.ds(chunk, step)
        for i, part in enumerate(part_refs):
            arrived(core_buf.at[i, 0, at], core_r.at[i, n, 0])
            mine = part[far * 2 + core, chunk : chunk + step, :].astype(F32)
            sum_buf[i, chunk : chunk + step, :] = (
                mine + core_buf[i, 0, chunk : chunk + step, :].astype(F32)
            ).astype(BF16)
            sends(
                sum_buf.at[i, at],
                far_buf.at[i, at],
                far_s.at[i, n],
                far_r.at[i, n],
                neighbour("xh", 1),
            )
    yield

    def total(i, n):
        chunk = n * step
        at = pl.ds(chunk, step)
        arrived(core_buf.at[i, 1, at], core_r.at[i, n, 1])
        near = part_refs[i][here * 2 + core, chunk : chunk + step, :].astype(F32)
        near = near + core_buf[i, 1, chunk : chunk + step, :].astype(F32)
        arrived(far_buf.at[i, at], far_r.at[i, n])
        return near + far_buf[i, chunk : chunk + step, :].astype(F32)

    yield total


def ring_reduce_stages(part_ref, core_buf, sum_buf, via_buf, far_buf, core_s, core_r, ring_s, ring_r, sends):
    xl, xh, core = lax.axis_index("xl"), lax.axis_index("xh"), lax.axis_index("core")
    rows = part_ref.shape[3]
    half = rows // 2
    at = xh * 2 + xl
    chips = [lax.rem(at + step, 4) for step in (2, 1, 3, 0)]
    chips = [(lax.rem(chip, 2), lax.div(chip, 2)) for chip in chips]
    for n, (pxl, pxh) in enumerate(chips):
        sends(
            part_ref.at[pxl, pxh, 1 - core],
            core_buf.at[n],
            core_s.at[n],
            core_r.at[n],
            neighbour("core", 1),
        )

    def own(n, start):
        pxl, pxh = chips[n]
        return part_ref[pxl, pxh, core, start : start + half, :].astype(F32)

    def both(n, start):
        return own(n, start) + core_buf[n, start : start + half, :].astype(F32)

    first, second = pl.ds(0, half), pl.ds(half, half)
    ahead, behind = chip_along(1), chip_along(-1)
    yield
    arrived(core_buf.at[0], core_r.at[0])
    sum_buf[0, :half, :] = both(0, 0).astype(BF16)
    sends(sum_buf.at[0, first], via_buf.at[0], ring_s.at[0], ring_r.at[0], ahead)
    sum_buf[0, half:, :] = both(0, half).astype(BF16)
    sends(sum_buf.at[0, second], via_buf.at[1], ring_s.at[1], ring_r.at[1], behind)
    arrived(core_buf.at[1], core_r.at[1])
    sum_buf[1, half:, :] = both(1, half).astype(BF16)
    sends(sum_buf.at[1, second], far_buf.at[0, second], ring_s.at[2], ring_r.at[2], ahead)
    arrived(core_buf.at[2], core_r.at[2])
    sum_buf[2, :half, :] = both(2, 0).astype(BF16)
    sends(sum_buf.at[2, first], far_buf.at[1, first], ring_s.at[3], ring_r.at[3], behind)
    yield
    arrived(via_buf.at[0], ring_r.at[0])
    sum_buf[1, :half, :] = (both(1, 0) + via_buf[0].astype(F32)).astype(BF16)
    sends(sum_buf.at[1, first], far_buf.at[0, first], ring_s.at[4], ring_r.at[4], ahead)
    arrived(via_buf.at[1], ring_r.at[1])
    sum_buf[2, half:, :] = (both(2, half) + via_buf[1].astype(F32)).astype(BF16)
    sends(sum_buf.at[2, second], far_buf.at[1, second], ring_s.at[5], ring_r.at[5], behind)
    arrived(core_buf.at[3], core_r.at[3])

    def total(part):
        rows_at = first if part == 0 else second
        start = part * half
        near = both(3, start)
        arrived(far_buf.at[0, rows_at], ring_r.at[4 if part == 0 else 2])
        near = near + far_buf[0, start : start + half, :].astype(F32)
        arrived(far_buf.at[1, rows_at], ring_r.at[3 if part == 0 else 5])
        return near + far_buf[1, start : start + half, :].astype(F32)

    yield total


def ring_reduce_scratch(rows, width):
    dma = pltpu.SemaphoreType.DMA
    return [
        pltpu.VMEM((4, rows, width), BF16),
        pltpu.VMEM((3, rows, width), BF16),
        pltpu.VMEM((2, rows // 2, width), BF16),
        pltpu.VMEM((2, rows, width), BF16),
        dma((4,)),
        dma((4,)),
        dma((6,)),
        dma((6,)),
    ]


def ring_spread(out_ref, part, ring_s, ring_r, core_s, core_r, sends):
    xl, xh, core = lax.axis_index("xl"), lax.axis_index("xh"), lax.axis_index("core")
    half = out_ref.shape[3] // 2
    mine = out_ref.at[xl, xh, core, pl.ds(part * half, half)]
    sends(mine, mine, ring_s.at[part, 0], ring_r.at[part, 0], chip_along(1))
    sends(mine, mine, ring_s.at[part, 1], ring_r.at[part, 1], chip_along(-1))
    sends(mine, mine, core_s.at[part, 0], core_r.at[part, 0], neighbour("core", 1))


def ring_spread_finish(out_ref, ring_s, ring_r, core_s, core_r, sends):
    xl, xh, core = lax.axis_index("xl"), lax.axis_index("xh"), lax.axis_index("core")
    half = out_ref.shape[3] // 2
    at = xh * 2 + xl

    def block(step, part, which):
        chip = lax.rem(at + step + 4, 4)
        return out_ref.at[lax.rem(chip, 2), lax.div(chip, 2), which, pl.ds(part * half, half)]

    for part in (0, 1):
        for n, (step, on) in enumerate(((-1, 1), (1, -1))):
            landed = block(step, part, core)
            arrived(landed, ring_r.at[part, n])
            if part == n:
                sends(landed, landed, ring_s.at[part, 2], ring_r.at[part, 2], chip_along(on))
            sends(landed, landed, core_s.at[part, 1 + n], core_r.at[part, 1 + n], neighbour("core", 1))
    for part in (0, 1):
        landed = block(2, part, core)
        arrived(landed, ring_r.at[part, 2])
        sends(landed, landed, core_s.at[part, 3], core_r.at[part, 3], neighbour("core", 1))
    for part in (0, 1):
        for n, step in enumerate((0, -1, 1, 2)):
            arrived(block(step, part, 1 - core), core_r.at[part, n])


def ring_spread_scratch():
    dma = pltpu.SemaphoreType.DMA
    return [dma((2, 3)), dma((2, 3)), dma((2, 4)), dma((2, 4))]


def along_x():
    return neighbour("core", 1), neighbour("xh", 1), chip_along(1), chip_along(-1)


CHUNKS = 4


def reduce_scratch(count, rows, width):
    dma = pltpu.SemaphoreType.DMA
    return [
        pltpu.VMEM((count, 2, rows, width), BF16),
        pltpu.VMEM((count, rows, width), BF16),
        pltpu.VMEM((count, rows, width), BF16),
        dma((count, CHUNKS, 2)),
        dma((count, CHUNKS, 2)),
        dma((count, CHUNKS)),
        dma((count, CHUNKS)),
    ]


def spread_chunk(out_ref, n, step, sems, sends):
    xh, core = lax.axis_index("xh"), lax.axis_index("core")
    at = pl.ds(n * step, step)
    mine = out_ref.at[xh * 2 + core, at]
    far_s, far_r, core_s, core_r = sems
    sends(mine, mine, far_s.at[n], far_r.at[n], neighbour("xh", 1))
    sends(mine, mine, core_s.at[n, 0], core_r.at[n, 0], neighbour("core", 1))


def spread_finish(out_ref, step, sems, sends):
    xh, core = lax.axis_index("xh"), lax.axis_index("core")
    far_s, far_r, core_s, core_r = sems
    for n in range(CHUNKS):
        at = pl.ds(n * step, step)
        theirs = out_ref.at[(1 - xh) * 2 + core, at]
        arrived(theirs, far_r.at[n])
        sends(theirs, theirs, core_s.at[n, 1], core_r.at[n, 1], neighbour("core", 1))
    for n in range(CHUNKS):
        at = pl.ds(n * step, step)
        arrived(out_ref.at[xh * 2 + 1 - core, at], core_r.at[n, 0])
        arrived(out_ref.at[(1 - xh) * 2 + 1 - core, at], core_r.at[n, 1])


def spread_scratch():
    dma = pltpu.SemaphoreType.DMA
    return [dma((CHUNKS,)), dma((CHUNKS,)), dma((CHUNKS, 2)), dma((CHUNKS, 2))]


def middle_body(part_ref, x_ref, gain_ref, middle_ref, unit_ref, *scratch):
    sends = Sends()
    greet(*along_x())
    *_, total = ring_reduce_stages(part_ref, *scratch[:8], sends)
    me = lax.axis_index("xh") * 2 + lax.axis_index("core")
    step = x_ref.shape[0] // CHUNKS
    half = x_ref.shape[0] // 2
    for part in (0, 1):
        rows = slice(part * half, (part + 1) * half)
        middle = x_ref[rows, :].astype(F32) + total(part)
        middle_ref[rows, :] = middle
        inverse = lax.rsqrt(jnp.mean(middle * middle, 1, keepdims=True) + EPSILON)
        unit_ref[me, rows, :] = (middle * inverse * gain_ref[...]).astype(BF16)
        for n in range(part * CHUNKS // 2, (part + 1) * CHUNKS // 2):
            spread_chunk(unit_ref, n, step, scratch[8:], sends)
    spread_finish(unit_ref, step, scratch[8:], sends)
    sends.finish()


def vmem(count):
    return [pl.BlockSpec(memory_space=pltpu.VMEM)] * count


def middle_and_unit(part, x, gain):
    rows, width = x.shape
    middle, unit = pl.pallas_call(
        middle_body,
        out_shape=[
            jax.ShapeDtypeStruct((rows, width), F32),
            jax.ShapeDtypeStruct((4, rows, width), BF16),
        ],
        in_specs=vmem(3),
        out_specs=vmem(2),
        scratch_shapes=ring_reduce_scratch(rows, width) + spread_scratch(),
        compiler_params=pltpu.CompilerParams(
            collective_id=1, has_side_effects=True, vmem_limit_bytes=32 * MIB
        ),
        name="middle_and_unit",
    )(part.reshape(2, 2, 2, rows, width), x, gain[None])
    return middle, unit.reshape(4 * rows, width)


def back_body(
    part_ref, middle_ref, grad_ref, gain_ref, hidden_ref, down_ref, dmiddle_ref, dgain_ref, spread_ref, branch_out,
    hidden, down, branch, loc, out_sem, *scratch,
):
    sends = Sends()
    loads = []
    for n, (src, dst) in enumerate(((hidden_ref, hidden), (down_ref, down))):
        loads.append(pltpu.make_async_copy(src, dst, loc.at[n]))
        loads[-1].start()
    greet(*along_x())
    stages = reduce_stages(CHUNKS, [part_ref], *scratch[:7], sends)
    next(stages)
    next(stages)
    for load in loads:
        load.wait()
    slots = branch.shape[1]
    outs = []
    for n in range(4):
        branch[n] = dot(hidden[n * slots : (n + 1) * slots, :], down[...], ((1,), (1,))).astype(BF16)
        outs.append(pltpu.make_async_copy(branch.at[n], branch_out.at[n], out_sem.at[n]))
        outs[-1].start()
    total = next(stages)
    xl, xh, core = lax.axis_index("xl"), lax.axis_index("xh"), lax.axis_index("core")
    step = middle_ref.shape[0] // CHUNKS
    for n in range(CHUNKS):
        rows = slice(n * step, (n + 1) * step)
        middle = middle_ref[rows, :]
        inverse = lax.rsqrt(jnp.mean(middle * middle, 1, keepdims=True) + EPSILON)
        normed = middle * inverse
        dunit = total(0, n)
        product = dunit * normed
        dgain = jnp.sum(product, 0, keepdims=True)
        if n == 0:
            dgain_ref[...] = dgain
        else:
            dgain_ref[...] += dgain
        mean = jnp.mean(product * gain_ref[...], 1, keepdims=True)
        dmiddle = grad_ref[rows, :].astype(F32) + inverse * (dunit * gain_ref[...] - normed * mean)
        dmiddle_ref[rows, :] = dmiddle
        spread_ref[xl, xh, core, rows, :] = dmiddle.astype(BF16)
        if n % 2 == 1:
            ring_spread(spread_ref, n // 2, *scratch[7:], sends)
    ring_spread_finish(spread_ref, *scratch[7:], sends)
    for out in outs:
        out.wait()
    sends.finish()


def middle_back(part, middle, grad, gain, hidden, down):
    rows, width = middle.shape
    count, inner = hidden.shape
    slots = count // 4
    dma = pltpu.SemaphoreType.DMA
    anywhere = pl.BlockSpec(memory_space=pl.ANY)
    dmiddle, dgain, spread, branch = pl.pallas_call(
        back_body,
        out_shape=[
            jax.ShapeDtypeStruct((rows, width), F32),
            jax.ShapeDtypeStruct((1, width), F32),
            jax.ShapeDtypeStruct((2, 2, 2, rows, width), BF16),
            jax.ShapeDtypeStruct((4, slots, width), BF16),
        ],
        in_specs=vmem(4) + [anywhere] * 2,
        out_specs=vmem(3) + [anywhere],
        scratch_shapes=[
            pltpu.VMEM((count, inner), BF16),
            pltpu.VMEM(down.shape, BF16),
            pltpu.VMEM((4, slots, width), BF16),
            dma((2,)),
            dma((4,)),
        ]
        + reduce_scratch(1, rows, width)
        + ring_spread_scratch(),
        compiler_params=pltpu.CompilerParams(
            collective_id=2, has_side_effects=True, vmem_limit_bytes=48 * MIB
        ),
        name="middle_back",
    )(part.reshape(4, rows, width), middle, grad, gain[None], hidden, down)
    return dmiddle, dgain[0], spread.reshape(8 * rows, width), branch


def rows_body(rows_ref, out_ref, loc, far_s, far_r, core_s, core_r):
    y, core = lax.axis_index("y"), lax.axis_index("core")
    half = rows_ref.shape[1] // 2
    sends = Sends()
    greet(neighbour("core", 1), *(neighbour("y", step) for step in (1, 2, 3)))
    at = pl.ds(pl.multiple_of(core * half, half), half)
    own = pltpu.make_async_copy(rows_ref.at[y], out_ref.at[y], loc)
    own.start()
    for step in (2, 1, 3):
        target = mod4(y + step)
        sends(
            rows_ref.at[target, at],
            out_ref.at[y, at],
            far_s.at[step - 1],
            far_r.at[step - 1],
            neighbour("y", step),
        )
    for step in (1, 3, 2):
        source = mod4(y - step)
        block = out_ref.at[source, at]
        arrived(block, far_r.at[step - 1])
        sends(block, block, core_s.at[step - 1], core_r.at[step - 1], neighbour("core", 1))
    own.wait()
    other = pl.ds(pl.multiple_of((1 - core) * half, half), half)
    for step in (1, 3, 2):
        arrived(out_ref.at[mod4(y - step), other], core_r.at[step - 1])
    sends.finish()


def rows_to_experts(rows):
    dma = pltpu.SemaphoreType.DMA
    return pl.pallas_call(
        rows_body,
        out_shape=jax.ShapeDtypeStruct(rows.shape, rows.dtype),
        in_specs=[pl.BlockSpec(memory_space=pl.ANY)],
        out_specs=pl.BlockSpec(memory_space=pl.ANY),
        scratch_shapes=[dma, dma((3,)), dma((3,)), dma((3,)), dma((3,))],
        compiler_params=pltpu.CompilerParams(collective_id=4, has_side_effects=True),
        name="rows_to_experts",
    )(rows)


STEPS = (2, 1, -1, 0)


def finish_body(
    qkv_ref, small_ref, o_ref, ups_ref, downs_ref, part_ref, feed_ref, x_ref, middle_ref, dmiddle_ref, gain_ref,
    out_ref, up_out, down_out, output_ref, dinput_ref, small_out,
    g_ref, loc, t_buf, r_buf, tb_buf, rb_buf, c_buf,
    t_s, t_r, r_s, r_r, tb_s, tb_r, rb_s, rb_r, c_s, c_r,
    up_own, up_buf, up_sum, ex, ey, es, er,
    small_own, small_buf, small_s, small_r, *scratch,
):
    xl, xh, core = lax.axis_index("xl"), lax.axis_index("xh"), lax.axis_index("core")
    place = {"y": lax.axis_index("y"), "z": lax.axis_index("z")}
    my_y = place["y"]
    half = g_ref.shape[3] // 2
    quarter = half // 2
    rings = (("z", "y"), ("y", "z"))
    sends = Sends()
    column = 0
    parts = []
    for n, ref in enumerate((qkv_ref, small_ref, o_ref)):
        cols = ref.shape[-1]
        parts.append(pltpu.make_async_copy(ref, g_ref.at[..., pl.ds(column, cols)], loc.at[n]))
        parts[-1].start()
        column += cols
    for n, (src, dst) in enumerate(((ups_ref.at[xl], up_own), (downs_ref.at[my_y], down_out.at[my_y]))):
        parts.append(pltpu.make_async_copy(src, dst, loc.at[3 + n]))
        parts[-1].start()
    peers = ({"xh": xh, "core": 1 - core}, {"xh": 1 - xh, "core": core}, {"xh": 1 - xh, "core": 1 - core})
    greet(
        *peers,
        chip_along(1),
        chip_along(-1),
        *(neighbour("y", step) for step in (1, 2, 3)),
        *(neighbour("z", step) for step in (1, -1)),
    )
    both = slice(0, 2)
    ring_stages = ring_reduce_stages(part_ref, *scratch[7:15], sends)
    feed_stages = reduce_stages(CHUNKS, [feed_ref], *scratch[:7], sends)
    for step in (2, 1, 3, 0):
        sends(
            ups_ref.at[1 - xl, mod4(my_y + step)],
            up_buf.at[step],
            ex.at[step],
            ey.at[step],
            neighbour("xl", 1),
        )
    next(ring_stages)
    next(feed_stages)
    for part in parts[:3]:
        part.wait()

    def grad_ref(h, first, second, start):
        zz, yy = (first, second) if h == 0 else (second, first)
        return g_ref.at[zz, both, yy, pl.ds(h * half + start, quarter)]

    def grad(h, first, second, j, start, count):
        zz, yy = (first, second) if h == 0 else (second, first)
        return g_ref[zz, j, yy, h * half + start : h * half + start + count, :].astype(F32)

    def firsts(h, k):
        return mod4(place[rings[h][0]] + STEPS[k])

    for k in range(4):
        for h in (0, 1):
            second = place[rings[h][1]]
            for d, way in ((0, 1), (1, -1)):
                sends(
                    grad_ref(h, firsts(h, k), mod4(second + 2), d * quarter),
                    t_buf.at[h, d, k],
                    t_s.at[h, d, k],
                    t_r.at[h, d, k],
                    neighbour(rings[h][1], way),
                )
    for k in range(4):
        for h in (0, 1):
            second = place[rings[h][1]]
            for d, way in ((0, 1), (1, -1)):
                sends(
                    grad_ref(h, firsts(h, k), mod4(second + way), (1 - d) * quarter),
                    r_buf.at[h, d, k, both, pl.ds((1 - d) * quarter, quarter)],
                    r_s.at[h, d, k, 0],
                    r_r.at[h, d, k, 0],
                    neighbour(rings[h][1], way),
                )
    next(ring_stages)
    next(feed_stages)
    for k in range(4):
        for h in (0, 1):
            second = place[rings[h][1]]
            for d, way in ((0, 1), (1, -1)):
                arrived(t_buf.at[h, d, k], t_r.at[h, d, k])
                for j in (0, 1):
                    t_buf[h, d, k, j] = (
                        t_buf[h, d, k, j].astype(F32)
                        + grad(h, firsts(h, k), mod4(second + way), j, d * quarter, quarter)
                    ).astype(BF16)
                sends(
                    t_buf.at[h, d, k],
                    r_buf.at[h, d, k, both, pl.ds(d * quarter, quarter)],
                    r_s.at[h, d, k, 1],
                    r_r.at[h, d, k, 1],
                    neighbour(rings[h][1], way),
                )
    total = next(ring_stages)
    for step in (2, 1, 3):
        sends(
            downs_ref.at[mod4(my_y + step)],
            down_out.at[my_y],
            es.at[1, step - 1],
            er.at[1, step - 1],
            neighbour("y", step),
        )
    for part in parts[3:]:
        part.wait()
    for step in (2, 1, 3, 0):
        target = mod4(my_y + step)
        arrived(up_buf.at[step], ey.at[step])
        value = (up_own[target].astype(F32) + up_buf[step].astype(F32)).astype(BF16)
        if step == 0:
            up_out[my_y] = value
        else:
            up_sum[step - 1] = value
            sends(
                up_sum.at[step - 1],
                up_out.at[my_y],
                es.at[0, step - 1],
                er.at[0, step - 1],
                neighbour("y", step),
            )
    for k in range(4):
        for h in (0, 1):
            second = place[rings[h][1]]
            for d in (0, 1):
                arrived(r_buf.at[h, d, k, both, pl.ds((1 - d) * quarter, quarter)], r_r.at[h, d, k, 0])
                arrived(r_buf.at[h, d, k, both, pl.ds(d * quarter, quarter)], r_r.at[h, d, k, 1])
            for j in (0, 1):
                r_buf[h, 0, k, j] = (
                    r_buf[h, 0, k, j].astype(F32)
                    + r_buf[h, 1, k, j].astype(F32)
                    + grad(h, firsts(h, k), second, j, 0, half)
                ).astype(BF16)
            for d, way in ((0, 1), (1, -1)):
                device = neighbour(rings[h][0], way)
                if k == 0:
                    sends(
                        r_buf.at[h, 0, 0, both, pl.ds(d * quarter, quarter)],
                        tb_buf.at[h, d],
                        tb_s.at[h, d],
                        tb_r.at[h, d],
                        device,
                    )
                if k == 1 + d:
                    sends(
                        r_buf.at[h, 0, k, both, pl.ds((1 - d) * quarter, quarter)],
                        rb_buf.at[h, d, both, pl.ds((1 - d) * quarter, quarter)],
                        rb_s.at[h, d, 0],
                        rb_r.at[h, d, 0],
                        device,
                    )
                    arrived(tb_buf.at[h, d], tb_r.at[h, d])
                    for j in (0, 1):
                        tb_buf[h, d, j] = (
                            tb_buf[h, d, j].astype(F32)
                            + r_buf[h, 0, k, j, d * quarter : (d + 1) * quarter, :].astype(F32)
                        ).astype(BF16)
                    sends(
                        tb_buf.at[h, d],
                        rb_buf.at[h, d, both, pl.ds(d * quarter, quarter)],
                        rb_s.at[h, d, 1],
                        rb_r.at[h, d, 1],
                        device,
                    )
    rows_half = x_ref.shape[0] // 2
    for part in (0, 1):
        rows = slice(part * rows_half, (part + 1) * rows_half)
        x = x_ref[rows, :].astype(F32)
        inverse = lax.rsqrt(jnp.mean(x * x, 1, keepdims=True) + EPSILON)
        normed = x * inverse
        dscaled = total(part) * gain_ref[...]
        mean = jnp.mean(dscaled * normed, 1, keepdims=True)
        dinput_ref[rows, :] = dmiddle_ref[rows, :] + inverse * (dscaled - normed * mean)
    for h in (0, 1):
        for d in (0, 1):
            arrived(rb_buf.at[h, d, both, pl.ds((1 - d) * quarter, quarter)], rb_r.at[h, d, 0])
            arrived(rb_buf.at[h, d, both, pl.ds(d * quarter, quarter)], rb_r.at[h, d, 1])
        for j in (0, 1):
            rb_buf[h, 0, j] = (
                rb_buf[h, 0, j].astype(F32)
                + rb_buf[h, 1, j].astype(F32)
                + r_buf[h, 0, 3, j].astype(F32)
            ).astype(BF16)
        sends(rb_buf.at[h, 0, 1 - xl], c_buf.at[h], c_s.at[h], c_r.at[h], neighbour("xl", 1))
        out_ref[xl, h * half : (h + 1) * half, :] = rb_buf[h, 0, xl].astype(F32)
    for h in (0, 1):
        arrived(c_buf.at[h], c_r.at[h])
        out_ref[1 - xl, h * half : (h + 1) * half, :] = c_buf[h].astype(F32)
    first, last = qkv_ref.shape[-1], qkv_ref.shape[-1] + small_ref.shape[-1]
    small_own[...] = out_ref[0, :, first:last] + out_ref[1, :, first:last]
    for n, peer in enumerate(peers):
        sends(small_own, small_buf.at[n], small_s.at[n], small_r.at[n], peer)
    feed = next(feed_stages)
    step = x_ref.shape[0] // CHUNKS
    for n in range(CHUNKS):
        rows = slice(n * step, (n + 1) * step)
        output_ref[rows, :] = (middle_ref[rows, :] + feed(0, n)).astype(BF16)
    for n, result in enumerate((up_out, down_out)):
        for step in (1, 3, 2):
            arrived(result.at[mod4(my_y - step)], er.at[n, step - 1])
    for n in range(3):
        arrived(small_buf.at[n], small_r.at[n])
    small_out[...] = (small_own[...] + small_buf[1]) + (small_buf[0] + small_buf[2])
    sends.finish()


def finish(grads, ups, downs, part, feed, x, middle, dmiddle, gain):
    rows, cols = grads[0].shape[0], sum(grad.shape[1] for grad in grads)
    share = rows // 32
    half, quarter = share // 2, share // 4
    dma = pltpu.SemaphoreType.DMA
    up_cols, down_cols = ups.shape[1], downs.shape[1]
    small = (share, grads[1].shape[1])
    own_rows, width = x.shape
    anywhere = pl.BlockSpec(memory_space=pl.ANY)
    return pl.pallas_call(
        finish_body,
        out_shape=[
            jax.ShapeDtypeStruct((2, share, cols), F32),
            jax.ShapeDtypeStruct((4, share, up_cols), BF16),
            jax.ShapeDtypeStruct((4, share, down_cols), BF16),
            jax.ShapeDtypeStruct((own_rows, width), BF16),
            jax.ShapeDtypeStruct((own_rows, width), F32),
            jax.ShapeDtypeStruct(small, F32),
        ],
        in_specs=[anywhere] * 5 + vmem(6),
        out_specs=vmem(6),
        scratch_shapes=[
            pltpu.VMEM((4, 2, 4, share, cols), BF16),
            dma((5,)),
            pltpu.VMEM((2, 2, 4, 2, quarter, cols), BF16),
            pltpu.VMEM((2, 2, 4, 2, half, cols), BF16),
            pltpu.VMEM((2, 2, 2, quarter, cols), BF16),
            pltpu.VMEM((2, 2, 2, half, cols), BF16),
            pltpu.VMEM((2, half, cols), BF16),
            dma((2, 2, 4)),
            dma((2, 2, 4)),
            dma((2, 2, 4, 2)),
            dma((2, 2, 4, 2)),
            dma((2, 2)),
            dma((2, 2)),
            dma((2, 2, 2)),
            dma((2, 2, 2)),
            dma((2,)),
            dma((2,)),
            pltpu.VMEM((4, share, up_cols), BF16),
            pltpu.VMEM((4, share, up_cols), BF16),
            pltpu.VMEM((3, share, up_cols), BF16),
            dma((4,)),
            dma((4,)),
            dma((2, 3)),
            dma((2, 3)),
            pltpu.VMEM(small, F32),
            pltpu.VMEM((3, *small), F32),
            dma((3,)),
            dma((3,)),
        ]
        + reduce_scratch(1, own_rows, width)
        + ring_reduce_scratch(own_rows, width),
        compiler_params=pltpu.CompilerParams(
            collective_id=5, has_side_effects=True, vmem_limit_bytes=60 * MIB
        ),
        name="finish",
    )(
        *(grad.reshape(4, 2, 4, share, grad.shape[1]) for grad in grads),
        ups.reshape(2, 4, share, up_cols),
        downs.reshape(4, share, down_cols),
        part.reshape(2, 2, 2, own_rows, width),
        feed.reshape(4, own_rows, width),
        x,
        middle,
        dmiddle,
        gain[None],
    )


def dot(a, b, dims):
    return lax.dot_general(a, b, (dims, ((), ())), preferred_element_type=F32)


def joined_body(rows_ref, gate_up_ref, linear_up_ref, gate_out, linear_out):
    up = jnp.concatenate([gate_up_ref[...], linear_up_ref[...]], 1)
    joined = dot(rows_ref[...], up, ((1,), (0,)))
    gate_out[...] = joined[:, :LANES]
    linear_out[...] = joined[:, LANES:]


def joined_rows(rows, up):
    count, width, hidden = rows.shape[0], up.shape[0], up.shape[1] // 2
    chunks = hidden // LANES
    chunk = pl.BlockSpec((count, LANES), lambda j: (0, j))
    return pl.pallas_call(
        joined_body,
        grid=(chunks,),
        in_specs=[
            pl.BlockSpec((count, width), lambda j: (0, 0)),
            pl.BlockSpec((width, LANES), lambda j: (0, j)),
            pl.BlockSpec((width, LANES), lambda j: (0, chunks + j)),
        ],
        out_specs=[chunk] * 2,
        out_shape=[jax.ShapeDtypeStruct((count, hidden), F32)] * 2,
        compiler_params=pltpu.CompilerParams(vmem_limit_bytes=48 * MIB),
        name="joined_rows",
    )(rows, up, up)


def experts_body(
    grad_ref, down_ref, gate_pre_ref, linear_ref, gate_ref,
    dgate_pre_out, dlinear_out, hidden_out, gated_out, dgate_out, *, units,
):
    j = pl.program_id(0)

    @pl.when(j == 0)
    def _():
        dgate_out[...] = jnp.zeros_like(dgate_out)

    dhidden = dot(grad_ref[...], down_ref[...], ((1,), (0,)))
    gate_pre, linear = gate_pre_ref[...], linear_ref[...]
    sigmoid = jax.nn.sigmoid(gate_pre)
    silu = gate_pre * sigmoid
    hidden = silu * linear
    gate = gate_ref[...]
    product = hidden * dhidden
    dgate_out[...] += product[:, :LANES] + jnp.where(j * WIDE + LANES < units, product[:, LANES:], 0.0)
    dhidden = dhidden * gate
    hidden_out[...] = hidden.astype(BF16)
    gated_out[...] = (hidden * gate).astype(BF16)
    dgate_pre_out[...] = (dhidden * linear * (sigmoid + silu * (1.0 - sigmoid))).astype(BF16)
    dlinear_out[...] = (dhidden * silu).astype(BF16)


def experts(grads, down, gate_pre, linear, gates):
    count, hidden = gate_pre.shape
    width = down.shape[0]
    chunk = pl.BlockSpec((count, WIDE), lambda j: (0, j))
    some = jax.ShapeDtypeStruct((count, hidden), BF16)
    return pl.pallas_call(
        functools.partial(experts_body, units=hidden),
        grid=(pl.cdiv(hidden, WIDE),),
        in_specs=[
            pl.BlockSpec((count, width), lambda j: (0, 0)),
            pl.BlockSpec((width, WIDE), lambda j: (0, j)),
            chunk,
            chunk,
            pl.BlockSpec((count, 1), lambda j: (0, 0)),
        ],
        out_specs=[chunk] * 4 + [pl.BlockSpec((count, LANES), lambda j: (0, 0))],
        out_shape=[some] * 4 + [jax.ShapeDtypeStruct((count, LANES), F32)],
        compiler_params=pltpu.CompilerParams(vmem_limit_bytes=56 * MIB),
        name="experts",
    )(grads, down, gate_pre, linear, gates)


def return_body(
    dgate_pre_ref, dlinear_ref, up_ref, dgate_ref, rows_ref,
    dunit_out, dgate_out, up_out,
    djoined, up, rows, dunit, dgate_own, dunit_buf, dgate_buf, dunit_sum, dgate_sum, block,
    loc, core_s, core_r, far_s, far_r, out_sem,
):
    y, core = lax.axis_index("y"), lax.axis_index("core")
    slots = dgate_ref.shape[1]
    half = slots // 2
    hidden = dgate_pre_ref.shape[1]
    sends = Sends()
    loads = []
    for n, (src, dst) in enumerate(
        (
            (up_ref, up),
            (dgate_pre_ref, djoined.at[:, pl.ds(0, hidden)]),
            (dlinear_ref, djoined.at[:, pl.ds(hidden, hidden)]),
            (rows_ref.at[:, pl.ds(0, rows.shape[1])], rows),
        )
    ):
        loads.append(pltpu.make_async_copy(src, dst, loc.at[1, n]))
        loads[-1].start()
    greet(neighbour("core", 1), *(neighbour("y", step) for step in (1, 2, 3)))
    mine = pl.ds(pl.multiple_of(core * half, half), half)
    theirs = pl.ds(pl.multiple_of((1 - core) * half, half), half)
    order = (2, 1, 3, 0)
    own = []
    for step in order:
        target = mod4(y + step)
        sends(
            dgate_ref.at[target, theirs],
            dgate_buf.at[step],
            core_s.at[1, step],
            core_r.at[1, step],
            neighbour("core", 1),
        )
        own.append(pltpu.make_async_copy(dgate_ref.at[target, mine], dgate_own.at[step], loc.at[0, step]))
        own[-1].start()
    for load in loads[:3]:
        load.wait()
    for copy in own:
        copy.wait()

    def compute(step):
        at = pl.ds(pl.multiple_of(mod4(y + step) * slots, slots), slots)
        dunit[step] = dot(djoined[at, :], up[...], ((1,), (1,))).astype(BF16)
        sends(
            dunit.at[step, theirs],
            dunit_buf.at[step],
            core_s.at[0, step],
            core_r.at[0, step],
            neighbour("core", 1),
        )

    def pass_on(step):
        arrived(dunit_buf.at[step], core_r.at[0, step])
        arrived(dgate_buf.at[step], core_r.at[1, step])
        dunit_value = (dunit[step, mine, :].astype(F32) + dunit_buf[step].astype(F32)).astype(BF16)
        dgate_value = dgate_own[step] + dgate_buf[step]
        if step == 0:
            dunit_out[y] = dunit_value
            dgate_out[y] = dgate_value
            return
        dunit_sum[step - 1] = dunit_value
        dgate_sum[step - 1] = dgate_value
        for n, (summed, result) in enumerate(((dunit_sum, dunit_out), (dgate_sum, dgate_out))):
            sends(
                summed.at[step - 1],
                result.at[y],
                far_s.at[n, step - 1],
                far_r.at[n, step - 1],
                neighbour("y", step),
            )

    compute(2)
    compute(1)
    pass_on(2)
    compute(3)
    pass_on(1)
    compute(0)
    pass_on(3)
    loads[3].wait()
    blocks = up_out.shape[0] // WIDE

    @pl.loop(0, blocks)
    def _(j):
        at = pl.ds(pl.multiple_of(j * WIDE, WIDE), WIDE)
        slot = lax.rem(j, 2)

        @pl.when(j >= 2)
        def _():
            pltpu.make_async_copy(block.at[slot], up_out.at[at], out_sem.at[slot]).wait()

        block[slot] = dot(rows[:, at], djoined[...], ((0,), (0,))).astype(BF16)
        pltpu.make_async_copy(block.at[slot], up_out.at[at], out_sem.at[slot]).start()

    pass_on(0)
    for slot in (0, 1):
        pltpu.make_async_copy(block.at[slot], up_out.at[pl.ds(0, WIDE)], out_sem.at[slot]).wait()
    for n, result in enumerate((dunit_out, dgate_out)):
        for step in (1, 3, 2):
            arrived(result.at[mod4(y - step)], far_r.at[n, step - 1])
    sends.finish()


def return_rows(dgate_pre, dlinear, up, dgate, rows):
    _, slots, lanes = dgate.shape
    half = slots // 2
    width, wide = up.shape
    count = dlinear.shape[0]
    dma = pltpu.SemaphoreType.DMA
    anywhere = pl.BlockSpec(memory_space=pl.ANY)
    return pl.pallas_call(
        return_body,
        out_shape=[
            jax.ShapeDtypeStruct((4, half, width), BF16),
            jax.ShapeDtypeStruct((4, half, lanes), F32),
            jax.ShapeDtypeStruct((width, wide), BF16),
        ],
        in_specs=[anywhere] * 5,
        out_specs=vmem(2) + [anywhere],
        scratch_shapes=[
            pltpu.VMEM((count, wide), BF16),
            pltpu.VMEM((width, wide), BF16),
            pltpu.VMEM((count, width), BF16),
            pltpu.VMEM((4, slots, width), BF16),
            pltpu.VMEM((4, half, lanes), F32),
            pltpu.VMEM((4, half, width), BF16),
            pltpu.VMEM((4, half, lanes), F32),
            pltpu.VMEM((3, half, width), BF16),
            pltpu.VMEM((3, half, lanes), F32),
            pltpu.VMEM((2, WIDE, wide), BF16),
            dma((2, 4)),
            dma((2, 4)),
            dma((2, 4)),
            dma((2, 3)),
            dma((2, 3)),
            dma((2,)),
        ],
        compiler_params=pltpu.CompilerParams(
            collective_id=3, has_side_effects=True, vmem_limit_bytes=62 * MIB
        ),
        name="return_rows",
    )(dgate_pre, dlinear, up, dgate, rows)


def attention_body(
    k_ref, v_ref, q0, q1, q2, cos_ref, sin_ref, col_ref, row_ref, gate_ref,
    key_out, val_out, que_out, mix_out, gmix_out, prob_out,
):
    h = pl.program_id(1)
    cosine, sine = cos_ref[...], sin_ref[...]
    scale = 1.0 / math.sqrt(HD)

    def rotated(v):
        return v * cosine + pltpu.roll(v, HD // 2, 1) * sine

    key = rotated(k_ref[...]).astype(BF16)
    val = v_ref[...].astype(BF16)
    key_out[...] = key
    val_out[...] = val
    tokens = key.shape[0]
    half = tokens // 2
    allowed = []
    for start in (0, half):
        seen = start + half
        at_row = start + lax.broadcasted_iota(jnp.int32, (half, seen), 0)
        at_col = lax.broadcasted_iota(jnp.int32, (half, seen), 1)
        seg_row, seg_col = row_ref[0, :, :seen], col_ref[start : start + half, :]
        allowed.append((at_col <= at_row) & ((seg_row == 0) | (seg_row == seg_col)))
    for e, q_ref in enumerate((q0, q1, q2)):
        query = (rotated(q_ref[...]) * scale).astype(BF16)
        at = pl.ds(pl.multiple_of((e * HEADS + h) * HD, HD), HD)
        que_out[:, at] = query
        for n, start in enumerate((0, half)):
            rows, seen = slice(start, start + half), start + half
            scores = jnp.where(allowed[n], dot(query[rows], key[:seen], ((1,), (1,))), NEGATIVE)
            largest = jnp.max(scores, 1, keepdims=True)
            expsum = jnp.exp(scores - largest)
            prob = (expsum * (1.0 / jnp.sum(expsum, 1, keepdims=True))).astype(BF16)
            prob_out[0, 0, e, rows, :seen] = prob
            mixed = dot(prob, val[:seen], ((1,), (0,))).astype(BF16)
            mix_out[rows, at] = mixed
            gmix_out[rows, at] = (mixed.astype(F32) * gate_ref[rows, e : e + 1]).astype(BF16)


def block_specs(tokens):
    def column(n):
        return pl.BlockSpec((tokens, HD), lambda g, h: (g, n * HEADS + h))

    def rows(width):
        return pl.BlockSpec((tokens, width), lambda g, h: (g, 0))

    return column, rows


def prob_spec(tokens):
    return pl.BlockSpec((1, 1, 3, tokens, tokens), lambda g, h: (g, h, 0, 0, 0))


def attention_forward(joined, cosine, sine, segments, gates):
    groups, tokens = segments.shape
    column, rows = block_specs(tokens)
    wide = jax.ShapeDtypeStruct((groups * tokens, 3 * HEADS * HD), BF16)
    narrow = jax.ShapeDtypeStruct((groups * tokens, HEADS * HD), BF16)
    return pl.pallas_call(
        attention_body,
        grid=(groups, HEADS),
        in_specs=[column(n) for n in range(5)]
        + [rows(HD)] * 2
        + [rows(1), pl.BlockSpec((1, 1, tokens), lambda g, h: (g, 0, 0)), rows(gates.shape[1])],
        out_specs=[column(0), column(0)] + [rows(wide.shape[1])] * 3 + [prob_spec(tokens)],
        out_shape=[narrow, narrow, wide, wide, wide]
        + [jax.ShapeDtypeStruct((groups, HEADS, 3, tokens, tokens), BF16)],
        compiler_params=pltpu.CompilerParams(vmem_limit_bytes=48 * MIB),
        name="attention_forward",
    )(
        *[joined] * 5, cosine, sine, segments.reshape(-1, 1), segments[:, None], gates
    )


def attention_back_body(
    key_ref, val_ref, q0, q1, q2, m0, m1, m2, h0, h1, h2, prob_ref, cos_ref, sin_ref, gate_ref,
    grad_out, dgate_out,
):
    h = pl.program_id(1)
    cosine, sine = cos_ref[...], sin_ref[...]
    scale = 1.0 / math.sqrt(HD)

    def rotated_back(v):
        return v * cosine - pltpu.roll(v, HD // 2, 1) * sine

    key, val = key_ref[...], val_ref[...]
    tokens = key.shape[0]
    half = tokens // 2
    dkeys = [jnp.zeros((half, HD), F32)] * 2
    dvals = [jnp.zeros((half, HD), F32)] * 2
    lane = lax.broadcasted_iota(jnp.int32, (tokens, HD), 1)
    dgates = jnp.zeros((tokens, HD), F32)
    for e, (q_ref, m_ref, h_ref) in enumerate(((q0, m0, h0), (q1, m1, h1), (q2, m2, h2))):
        query, mixed, raw = q_ref[...], m_ref[...].astype(F32), h_ref[...]
        inner = jnp.sum(mixed * raw, 1, keepdims=True)
        dgates = dgates + jnp.where(lane == e, inner, 0.0)
        gate = gate_ref[:, e : e + 1]
        dmixed = (raw * gate).astype(BF16)
        delta = jnp.sum(dmixed.astype(F32) * mixed, 1, keepdims=True)
        dqueries = []
        for start in (0, half):
            rows, seen = slice(start, start + half), start + half
            prob = prob_ref[0, 0, e, rows, :seen]
            dprob = dot(dmixed[rows], val[:seen], ((1,), (1,)))
            dscores = (prob.astype(F32) * (dprob - delta[rows])).astype(BF16)
            dqueries.append(dot(dscores, key[:seen], ((1,), (0,))))
            dval = dot(prob, dmixed[rows], ((0,), (0,)))
            dkey = dot(dscores, query[rows], ((0,), (0,)))
            dvals[0] = dvals[0] + dval[:half]
            dkeys[0] = dkeys[0] + dkey[:half]
            if start:
                dvals[1] = dvals[1] + dval[half:]
                dkeys[1] = dkeys[1] + dkey[half:]
        dquery = jnp.concatenate(dqueries, 0)
        at = pl.ds(pl.multiple_of(((2 + e) * HEADS + h) * HD, HD), HD)
        grad_out[:, at] = rotated_back(dquery * scale).astype(BF16)
    dkey, dval = jnp.concatenate(dkeys, 0), jnp.concatenate(dvals, 0)
    grad_out[:, pl.ds(pl.multiple_of(h * HD, HD), HD)] = rotated_back(dkey).astype(BF16)
    grad_out[:, pl.ds(pl.multiple_of((HEADS + h) * HD, HD), HD)] = dval.astype(BF16)

    @pl.when(h == 0)
    def _():
        dgate_out[...] = dgates

    @pl.when(h > 0)
    def _():
        dgate_out[...] += dgates


def attention_back(key, val, que, mix, raw, prob, cosine, sine, gates):
    groups, tokens = prob.shape[0], prob.shape[-1]
    column, rows = block_specs(tokens)
    thirds = [column(n) for n in range(3)]
    grads = jax.ShapeDtypeStruct((groups * tokens, 5 * HEADS * HD), BF16)
    return pl.pallas_call(
        attention_back_body,
        grid=(groups, HEADS),
        in_specs=[column(0), column(0)]
        + thirds * 3
        + [prob_spec(tokens)]
        + [rows(HD)] * 2
        + [rows(gates.shape[1])],
        out_specs=[rows(grads.shape[1]), rows(HD)],
        out_shape=[grads, jax.ShapeDtypeStruct((groups * tokens, HD), F32)],
        compiler_params=pltpu.CompilerParams(vmem_limit_bytes=48 * MIB),
        name="attention_back",
    )(key, val, que, que, que, mix, mix, mix, raw, raw, raw, prob, cosine, sine, gates)


def positions(segments):
    index = jnp.arange(segments.shape[0], dtype=jnp.int32)
    prompt = jnp.sum((segments == 0).astype(jnp.int32))
    first = jnp.sum((segments == 1).astype(jnp.int32))
    before = jnp.where(segments == 0, 0, jnp.where(segments == 1, prompt, prompt + first))
    return jnp.where(segments == 0, index, prompt + index - before)


def route_gates(logits, routes, count):
    onehot = (routes[:, :, None] == jnp.arange(count, dtype=jnp.int32)).astype(F32)
    chosen = jnp.sum(onehot * logits[:, None, :], -1)
    expsum = jnp.exp(chosen - jnp.max(chosen, -1, keepdims=True))
    weights = expsum / jnp.sum(expsum, -1, keepdims=True)
    return weights, onehot, jnp.sum(weights[:, :, None] * onehot, 1)


def router_back(dgate, weights, onehot):
    dchosen = jnp.sum(dgate[:, None, :] * onehot, -1)
    dselect = weights * (dchosen - jnp.sum(weights * dchosen, -1, keepdims=True))
    return jnp.sum(dselect[:, :, None] * onehot, 1).astype(BF16)


def normalize(activations):
    inverse = lax.rsqrt(jnp.mean(activations * activations, -1, keepdims=True) + EPSILON)
    return activations * inverse, inverse


def reorder(rows):
    count, width = rows.shape
    return jnp.transpose(rows.reshape(count, 4, 2, 4, width // 32), (0, 3, 2, 1, 4)).reshape(count, width)


def pad_to(array, width):
    return jnp.pad(array, ((0, 0), (0, width - array.shape[1])))


def on_device(
    inputs,
    segments,
    att_routes,
    mlp_routes,
    key_value,
    query_proj,
    output_proj,
    router_att,
    gain_att,
    gate_up,
    down_proj,
    router_mlp,
    gain_mlp,
    out_grad,
):
    width = inputs.shape[1]
    inner = query_proj.shape[2]
    hidden_local = down_proj.shape[1]
    att_count = query_proj.shape[0]
    mlp_count = gate_up.shape[0]
    share = gate_up.shape[1]
    part = inner // 2
    qkv_cols = (2 + att_count) * part
    small_at = qkv_cols
    out_at = qkv_cols + 128
    small = jnp.concatenate([router_att, router_mlp, gain_att[:, None], gain_mlp[:, None]], 1)
    own_att = jnp.concatenate(
        [
            jnp.transpose(key_value.reshape(share, 2, 2, part), (2, 0, 1, 3)).reshape(2, share, -1),
            jnp.transpose(query_proj.reshape(att_count, share, 2, part), (2, 1, 0, 3)).reshape(
                2, share, -1
            ),
            jnp.broadcast_to(pad_to(small, 128), (2, share, 128)),
            jnp.transpose(output_proj.reshape(att_count, 2, part, share), (1, 3, 0, 2)).reshape(
                2, share, -1
            ),
        ],
        2,
    )
    inputs = reorder(inputs)
    out_grad = reorder(out_grad)
    x_all = lax.all_gather(inputs, ("xl", *TP), axis=0, tiled=True)
    grad_all = lax.all_gather(out_grad, TP, axis=0, tiled=True)
    marks = pad_to(jnp.concatenate([segments[:, None], att_routes], 1), LANES).astype(BF16)
    weights, up_parts, down_parts, marks = gather_dp(
        own_att,
        gate_up.reshape(mlp_count, share, -1),
        jnp.swapaxes(down_proj, 1, 2),
        marks,
    )
    marks = marks[:, :, :3].astype(jnp.int32)
    up_whole = lax.all_gather(
        up_parts.reshape(2 * mlp_count * share, -1), "z", axis=0, tiled=True
    )
    up_parts, down_parts = lax.optimization_barrier((up_parts, down_parts))
    down_whole = lax.all_gather(
        down_parts.reshape(mlp_count * share, -1), ("z", "xl"), axis=0, tiled=True
    )

    tokens = segments.shape[0]
    match = jnp.sum((mlp_routes[:, :, None] == jnp.arange(mlp_count, dtype=jnp.int32)).astype(BF16), 1)
    index = jnp.arange(tokens, dtype=jnp.int32)
    lower = (index[None, :] < index[:, None]).astype(BF16)
    rank = dot(lower, match, ((1,), (0,)))
    slot = jnp.where(match > 0, rank.astype(jnp.int32), -1)
    pick = (slot.T[:, None, :] == jnp.arange(CAP, dtype=jnp.int32)[None, :, None]).astype(BF16)
    pick_rows = pick.reshape(mlp_count * CAP, tokens)
    grad_rows = dot(pick_rows, grad_all, ((1,), (0,))).astype(BF16)
    grad_in = lax.all_to_all(grad_rows.reshape(mlp_count, CAP, width), "y", 0, 0, tiled=True)
    grad_in = grad_in.reshape(mlp_count * CAP, width)

    small_all = weights[:, small_at : small_at + 128].astype(F32)
    gain_one, gain_two = small_all[:, 7], small_all[:, 8]
    segments = marks[:, :, 0]
    att_routes = marks[:, :, 1:].reshape(2 * tokens, 2)
    places = jax.vmap(positions)(segments).reshape(-1).astype(F32)
    frequency = ROPE_BASE ** (-2.0 * jnp.arange(HD // 2, dtype=F32) / HD)
    angles = places[:, None] * frequency[None, :]
    cosine = jnp.concatenate([jnp.cos(angles)] * 2, 1)
    sine = jnp.concatenate([-jnp.sin(angles), jnp.sin(angles)], 1)
    normed_one, _ = normalize(x_all.astype(F32))
    unit_one = (normed_one * gain_one).astype(BF16)
    joined_att = dot(unit_one, weights[:, :out_at], ((1,), (0,)))
    weights_att, onehot_att, gate_att = route_gates(
        joined_att[:, small_at : small_at + att_count], att_routes, att_count
    )
    key_rot, val_rows, queries, mixed, gmixed, prob = attention_forward(
        joined_att, cosine, sine, segments, gate_att
    )
    out_weights = weights[:, out_at:]
    attention = dot(gmixed, out_weights, ((1,), (1,))).astype(BF16)
    middle, unit_two = middle_and_unit(attention, inputs, gain_two)

    router_two = weights[:, small_at + att_count : small_at + att_count + mlp_count]
    logit_mlp = dot(unit_two, router_two, ((1,), (0,)))
    weights_mlp, onehot_mlp, gate_mlp = route_gates(logit_mlp, mlp_routes, mlp_count)
    gate_high = gate_mlp.astype(BF16)
    gate_low = (gate_mlp - gate_high.astype(F32)).astype(BF16)
    extended = jnp.concatenate([unit_two, pad_to(jnp.concatenate([gate_high, gate_low], 1), 128)], 1)
    rows_out = dot(pick_rows, extended, ((1,), (0,))).astype(BF16)
    rows_ext = rows_to_experts(rows_out.reshape(mlp_count, CAP, width + 128))
    rows_ext = rows_ext.reshape(mlp_count * CAP, width + 128)
    gates_ext = rows_ext[:, width : width + 2 * mlp_count].astype(F32)
    mine = (jnp.arange(2 * mlp_count) % mlp_count == lax.axis_index("y")).astype(F32)
    gates_in = jnp.sum(gates_ext * mine, 1, keepdims=True)
    gate_pre, linear = joined_rows(rows_ext, up_whole)
    dgate_pre, dlinear, hidden, gated, dgate_part = experts(
        grad_in, down_whole, gate_pre, linear, gates_in
    )
    grad_down_whole = dot(grad_in, gated, ((0,), (0,))).astype(BF16)
    dgate_part, grad_down_whole = lax.optimization_barrier((dgate_part, grad_down_whole))
    grad_down_sum = lax.psum_scatter(grad_down_whole, "z", scatter_dimension=0, tiled=True)
    dunit_back, dgate_back, grad_up_whole = return_rows(
        dgate_pre, dlinear, up_whole, dgate_part.reshape(mlp_count, CAP, LANES), rows_ext
    )
    grad_up_sum = lax.psum_scatter(grad_up_whole, "z", scatter_dimension=0, tiled=True)
    halves = grad_down_sum.reshape(2, mlp_count * share, hidden_local)
    xl = lax.axis_index("xl")
    theirs = lax.ppermute(
        lax.dynamic_index_in_dim(halves, 1 - xl, 0, keepdims=False), "xl", ((0, 1), (1, 0))
    )
    grad_down_sum = (
        lax.dynamic_index_in_dim(halves, xl, 0, keepdims=False).astype(F32) + theirs.astype(F32)
    ).astype(BF16)
    pick_half = lax.dynamic_slice_in_dim(pick, lax.axis_index("core") * (CAP // 2), CAP // 2, 1)
    dgate_two = jnp.sum(pick_half.astype(F32) * jnp.sum(dgate_back, -1, keepdims=True), 1).T
    dlogit_mlp = router_back(dgate_two, weights_mlp, onehot_mlp)
    dunit_two = dot(
        pick_half.reshape(-1, tokens), dunit_back.reshape(-1, width), ((0,), (0,))
    ) + dot(dlogit_mlp, router_two, ((1,), (1,)))
    grad_rmlp = dot(unit_two, dlogit_mlp, ((0,), (0,)))
    dmiddle, grad_gain_two, dattention, branch_part = middle_back(
        dunit_two.astype(BF16), middle, out_grad, gain_two, hidden, down_whole
    )
    branch_back = lax.all_to_all(branch_part, "y", 0, 0, tiled=True)

    raw = dot(dattention, out_weights, ((1,), (0,)))
    grad_qkv, dgate_one = attention_back(
        key_rot, val_rows, queries, mixed, raw, prob, cosine, sine, gate_att
    )
    dlogit_att = router_back(dgate_one[:, :att_count], weights_att, onehot_att)
    grad_joined = jnp.concatenate([grad_qkv, pad_to(dlogit_att, 128)], 1)
    dunit_one = dot(grad_joined, weights[:, :out_at], ((1,), (1,)))
    grad_gain_one = jnp.sum(dunit_one * normed_one, 0)
    grad_small = jnp.concatenate(
        [
            dot(unit_one, dlogit_att, ((0,), (0,))),
            grad_rmlp,
            grad_gain_one[:, None],
            grad_gain_two[:, None],
        ],
        1,
    )
    gate_slots = jnp.sum(pick.astype(F32) * gate_mlp.T[:, None, :], -1, keepdims=True)
    feed = dot(
        pick_rows,
        (branch_back.astype(F32) * gate_slots).astype(BF16).reshape(-1, width),
        ((0,), (0,)),
    )
    summed_att, ups_sum, downs_sum, output, grad_input, small_sum = finish(
        (
            dot(unit_one, grad_qkv, ((0,), (0,))).astype(BF16),
            pad_to(grad_small, 128).astype(BF16),
            dot(dattention, gmixed, ((0,), (0,))).astype(BF16),
        ),
        grad_up_sum,
        grad_down_sum,
        dunit_one.astype(BF16),
        feed.astype(BF16),
        inputs,
        middle,
        dmiddle,
        gain_one,
    )
    grad_kv = jnp.transpose(
        summed_att[:, :, : 2 * part].reshape(2, share, 2, part), (1, 2, 0, 3)
    ).reshape(share, 2, inner)
    grad_query = jnp.transpose(
        summed_att[:, :, 2 * part : qkv_cols].reshape(2, share, att_count, part), (2, 1, 0, 3)
    ).reshape(att_count, share, inner)
    grad_output = jnp.transpose(
        summed_att[:, :, out_at:].reshape(2, share, att_count, part), (2, 0, 3, 1)
    ).reshape(att_count, inner, share)
    output = reorder(output)
    grad_input = reorder(grad_input)

    grads_up = ups_sum.astype(F32).reshape(mlp_count, share, 2, hidden_local)
    grads_down = jnp.swapaxes(downs_sum.astype(F32), 1, 2)
    return (
        output,
        grad_input,
        grad_kv,
        grad_query,
        grad_output,
        small_sum[:, :3],
        small_sum[:, 7],
        grads_up,
        grads_down,
        small_sum[:, 3:7],
        small_sum[:, 8],
    )


def solution(mesh):
    fine = Mesh(mesh.devices.reshape(4, 2, 4, 2, 2), ALL)
    return jax.shard_map(
        on_device,
        mesh=fine,
        in_specs=(
            P(ALL, None),
            P(DP),
            P(DP, None),
            P(DP, None),
            P(DP, None, TP),
            P(None, DP, TP),
            P(None, TP, DP),
            P(DP, None),
            P(DP),
            P(None, DP, None, TP),
            P(None, TP, DP),
            P(DP, None),
            P(DP),
            P(ALL, None),
        ),
        out_specs=(
            P(ALL, None),
            P(ALL, None),
            P(DP, None, TP),
            P(None, DP, TP),
            P(None, TP, DP),
            P(DP, None),
            P(DP),
            P(None, DP, None, TP),
            P(None, TP, DP),
            P(DP, None),
            P(DP),
        ),
        check_vma=False,
    )
```

```python
import functools
import math

import jax
import jax.numpy as jnp
from jax import lax
from jax.experimental import pallas as pl
from jax.experimental.pallas import tpu as pltpu
from jax.sharding import Mesh, PartitionSpec as P

LANES = 128
WIDE = 256
HD = 128
HEADS = 2
CAP = 320
EPSILON = 1e-06
NEGATIVE = -1e30
ROPE_BASE = 10000.0
MESH_ID = pl.DeviceIdType.MESH
MIB = 1024 * 1024
DP = ("y", "xl", "z")
TP = ("xh", "core")
ALL = DP + TP
F32 = jnp.float32
BF16 = jnp.bfloat16


def mod4(place):
    return lax.rem(place + 4, 4)


def neighbour(axis, step):
    size = 4 if axis in ("y", "z") else 2
    return {axis: lax.rem(lax.axis_index(axis) + step + size, size)}


def chip_along(step):
    at = lax.rem(lax.axis_index("xh") * 2 + lax.axis_index("xl") + step + 4, 4)
    return {"xh": lax.div(at, 2), "xl": lax.rem(at, 2)}


def greet(*devices):
    barrier = pltpu.get_barrier_semaphore()
    for device in devices:
        pl.semaphore_signal(barrier, inc=1, device_id=device, device_id_type=MESH_ID)
    pl.semaphore_wait(barrier, len(devices))


def arrived(ref, sem):
    pltpu.make_async_copy(ref, ref, sem).wait()


class Sends:
    def __init__(self):
        self.copies = []

    def __call__(self, src, dst, send_sem, recv_sem, device):
        copy = pltpu.make_async_remote_copy(
            src_ref=src,
            dst_ref=dst,
            send_sem=send_sem,
            recv_sem=recv_sem,
            device_id=device,
            device_id_type=MESH_ID,
        )
        copy.start()
        self.copies.append(copy)

    def finish(self):
        for copy in self.copies:
            copy.wait_send()


def gather_body(
    x_ref, ups_ref, downs_ref, marks_ref, out_ref, up_ref, down_ref, marks_out,
    loc, xs, xr, s1, r1m, r1p, f1s, f1r, s2, r2m, r2p, f2s, f2r, es, er, ex, ey, ms, mr,
):
    y, xl, z = lax.axis_index("y"), lax.axis_index("xl"), lax.axis_index("z")
    half = x_ref.shape[1] // 2
    quarter = half // 2
    greet(
        neighbour("xl", 1),
        *(neighbour("y", step) for step in (1, 2, 3)),
        *(neighbour("z", step) for step in (1, -1)),
    )
    rings = (("z", "y"), ("y", "z"))
    place = {"y": y, "z": z}
    other = 1 - xl
    both = pl.ds(0, 2)
    sends = Sends()
    send = sends

    def slot(h, first, second, j, start, count):
        yy, zz = (second, first) if h == 0 else (first, second)
        return out_ref.at[zz, j, yy, pl.ds(start, count)]

    own = pltpu.make_async_copy(x_ref.at[xl], out_ref.at[z, xl, y], loc.at[0])
    own.start()
    own_marks = pltpu.make_async_copy(marks_ref, marks_out.at[xl], loc.at[3])
    own_marks.start()
    send(marks_ref, marks_out.at[xl], ms, mr, neighbour("xl", 1))
    experts = ((ups_ref, up_ref), (downs_ref, down_ref))
    kept = []
    for n, (shards, expert) in enumerate(experts):
        kept.append(pltpu.make_async_copy(shards.at[y], expert.at[xl, y], loc.at[1 + n]))
        kept[-1].start()
        send(shards.at[y], expert.at[xl, y], ex.at[n, 0], ey.at[n, 0], neighbour("xl", 1))
        for step in (1, 3, 2):
            send(
                shards.at[mod4(y + step)],
                expert.at[xl, y],
                es.at[n, step - 1],
                er.at[n, step - 1],
                neighbour("y", step),
            )
    for h in (0, 1):
        first, second = place[rings[h][0]], place[rings[h][1]]
        src = x_ref.at[xl, pl.ds(h * half, half)]
        dst = slot(h, first, second, xl, h * half, half)
        send(x_ref.at[other, pl.ds(h * half, half)], dst, xs.at[h], xr.at[h], neighbour("xl", 1))
        send(src, dst, s1.at[h, 0, 0], r1m.at[h, 0], neighbour(rings[h][0], 1))
        send(src, dst, s1.at[h, 0, 1], r1p.at[h, 0], neighbour(rings[h][0], -1))
    own.wait()

    def send_second(h, k, first):
        block = slot(h, first, place[rings[h][1]], both, h * half, half)
        send(block, block, s2.at[h, k, 0], r2m.at[h, k], neighbour(rings[h][1], 1))
        send(block, block, s2.at[h, k, 1], r2p.at[h, k], neighbour(rings[h][1], -1))

    for h in (0, 1):
        first, second = place[rings[h][0]], place[rings[h][1]]
        block = slot(h, first, second, other, h * half, half)
        arrived(block, xr.at[h])
        send(block, block, s1.at[h, 1, 0], r1m.at[h, 1], neighbour(rings[h][0], 1))
        send(block, block, s1.at[h, 1, 1], r1p.at[h, 1], neighbour(rings[h][0], -1))
        send_second(h, 0, first)
    for j, jx in ((0, xl), (1, other)):
        for h in (0, 1):
            first, second = place[rings[h][0]], place[rings[h][1]]
            arrived(slot(h, mod4(first - 1), second, jx, h * half, half), r1m.at[h, j])
            block = slot(h, mod4(first - 1), second, jx, h * half, quarter)
            send(block, block, f1s.at[h, j, 0], f1r.at[h, j, 0], neighbour(rings[h][0], 1))
            arrived(slot(h, mod4(first + 1), second, jx, h * half, half), r1p.at[h, j])
            block = slot(h, mod4(first + 1), second, jx, h * half + quarter, quarter)
            send(block, block, f1s.at[h, j, 1], f1r.at[h, j, 1], neighbour(rings[h][0], -1))
    for k, step in ((1, -1), (2, 1)):
        for h in (0, 1):
            send_second(h, k, mod4(place[rings[h][0]] + step))
    for n, (shards, expert) in enumerate(experts):
        for step in (1, 3, 2):
            landed = expert.at[xl, mod4(y - step)]
            arrived(landed, er.at[n, step - 1])
            send(landed, landed, ex.at[n, step], ey.at[n, step], neighbour("xl", 1))
    for h in (0, 1):
        first, second = place[rings[h][0]], place[rings[h][1]]
        for j, jx in ((0, xl), (1, other)):
            for p in (0, 1):
                block = slot(h, mod4(first + 2), second, jx, h * half + p * quarter, quarter)
                arrived(block, f1r.at[h, j, p])
        send_second(h, 3, mod4(first + 2))
    steps = ((0, 0), (1, -1), (2, 1), (3, 2))
    for k, step in steps:
        for h in (0, 1):
            first, second = mod4(place[rings[h][0]] + step), place[rings[h][1]]
            arrived(slot(h, first, mod4(second - 1), both, h * half, half), r2m.at[h, k])
            block = slot(h, first, mod4(second - 1), both, h * half, quarter)
            send(block, block, f2s.at[h, k, 0], f2r.at[h, k, 0], neighbour(rings[h][1], 1))
            arrived(slot(h, first, mod4(second + 1), both, h * half, half), r2p.at[h, k])
            block = slot(h, first, mod4(second + 1), both, h * half + quarter, quarter)
            send(block, block, f2s.at[h, k, 1], f2r.at[h, k, 1], neighbour(rings[h][1], -1))
    for k, step in steps:
        for h in (0, 1):
            first, second = mod4(place[rings[h][0]] + step), place[rings[h][1]]
            for p in (0, 1):
                block = slot(h, first, mod4(second + 2), both, h * half + p * quarter, quarter)
                arrived(block, f2r.at[h, k, p])
    for n, (shards, expert) in enumerate(experts):
        for step in (0, 1, 3, 2):
            arrived(expert.at[other, mod4(y - step)], ey.at[n, step])
        kept[n].wait()
    arrived(marks_out.at[other], mr)
    own_marks.wait()
    sends.finish()


def gather_dp(shard, ups, downs, marks):
    _, rows, cols = shard.shape
    dma = pltpu.SemaphoreType.DMA
    whole, up, down, marks = pl.pallas_call(
        gather_body,
        out_shape=[
            jax.ShapeDtypeStruct((4, 2, 4, rows, cols), shard.dtype),
            jax.ShapeDtypeStruct((2, *ups.shape), ups.dtype),
            jax.ShapeDtypeStruct((2, *downs.shape), downs.dtype),
            jax.ShapeDtypeStruct((2, *marks.shape), marks.dtype),
        ],
        in_specs=[pl.BlockSpec(memory_space=pl.ANY)] * 4,
        out_specs=[pl.BlockSpec(memory_space=pl.ANY)] * 4,
        scratch_shapes=[
            dma((4,)),
            dma((2,)),
            dma((2,)),
            dma((2, 2, 2)),
            dma((2, 2)),
            dma((2, 2)),
            dma((2, 2, 2)),
            dma((2, 2, 2)),
            dma((2, 4, 2)),
            dma((2, 4)),
            dma((2, 4)),
            dma((2, 4, 2)),
            dma((2, 4, 2)),
            dma((2, 3)),
            dma((2, 3)),
            dma((2, 4)),
            dma((2, 4)),
            dma,
            dma,
        ],
        compiler_params=pltpu.CompilerParams(collective_id=0, has_side_effects=True),
        name="gather_weights",
    )(shard, ups, downs, marks)
    return whole.reshape(32 * rows, cols), up, down, marks


def reduce_stages(scatter_count, part_refs, core_buf, sum_buf, far_buf, core_s, core_r, far_s, far_r, sends):
    xh, core = lax.axis_index("xh"), lax.axis_index("core")
    rows = part_refs[0].shape[1]
    step = rows // scatter_count
    far, here = 1 - xh, xh
    for n, chunk in enumerate(range(0, rows, step)):
        at = pl.ds(chunk, step)
        for i, part in enumerate(part_refs):
            sends(
                part.at[far * 2 + 1 - core, at],
                core_buf.at[i, 0, at],
                core_s.at[i, n, 0],
                core_r.at[i, n, 0],
                neighbour("core", 1),
            )
    for n, chunk in enumerate(range(0, rows, step)):
        at = pl.ds(chunk, step)
        for i, part in enumerate(part_refs):
            sends(
                part.at[here * 2 + 1 - core, at],
                core_buf.at[i, 1, at],
                core_s.at[i, n, 1],
                core_r.at[i, n, 1],
                neighbour("core", 1),
            )
    yield
    for n, chunk in enumerate(range(0, rows, step)):
        at = pl.ds(chunk, step)
        for i, part in enumerate(part_refs):
            arrived(core_buf.at[i, 0, at], core_r.at[i, n, 0])
            mine = part[far * 2 + core, chunk : chunk + step, :].astype(F32)
            sum_buf[i, chunk : chunk + step, :] = (
                mine + core_buf[i, 0, chunk : chunk + step, :].astype(F32)
            ).astype(BF16)
            sends(
                sum_buf.at[i, at],
                far_buf.at[i, at],
                far_s.at[i, n],
                far_r.at[i, n],
                neighbour("xh", 1),
            )
    yield

    def total(i, n):
        chunk = n * step
        at = pl.ds(chunk, step)
        arrived(core_buf.at[i, 1, at], core_r.at[i, n, 1])
        near = part_refs[i][here * 2 + core, chunk : chunk + step, :].astype(F32)
        near = near + core_buf[i, 1, chunk : chunk + step, :].astype(F32)
        arrived(far_buf.at[i, at], far_r.at[i, n])
        return near + far_buf[i, chunk : chunk + step, :].astype(F32)

    yield total


def ring_reduce_stages(part_ref, core_buf, sum_buf, via_buf, far_buf, core_s, core_r, ring_s, ring_r, sends):
    xl, xh, core = lax.axis_index("xl"), lax.axis_index("xh"), lax.axis_index("core")
    rows = part_ref.shape[3]
    half = rows // 2
    at = xh * 2 + xl
    chips = [lax.rem(at + step, 4) for step in (2, 1, 3, 0)]
    chips = [(lax.rem(chip, 2), lax.div(chip, 2)) for chip in chips]
    for n, (pxl, pxh) in enumerate(chips):
        sends(
            part_ref.at[pxl, pxh, 1 - core],
            core_buf.at[n],
            core_s.at[n],
            core_r.at[n],
            neighbour("core", 1),
        )

    def own(n, start):
        pxl, pxh = chips[n]
        return part_ref[pxl, pxh, core, start : start + half, :].astype(F32)

    def both(n, start):
        return own(n, start) + core_buf[n, start : start + half, :].astype(F32)

    first, second = pl.ds(0, half), pl.ds(half, half)
    ahead, behind = chip_along(1), chip_along(-1)
    yield
    arrived(core_buf.at[0], core_r.at[0])
    sum_buf[0, :half, :] = both(0, 0).astype(BF16)
    sends(sum_buf.at[0, first], via_buf.at[0], ring_s.at[0], ring_r.at[0], ahead)
    sum_buf[0, half:, :] = both(0, half).astype(BF16)
    sends(sum_buf.at[0, second], via_buf.at[1], ring_s.at[1], ring_r.at[1], behind)
    arrived(core_buf.at[1], core_r.at[1])
    sum_buf[1, half:, :] = both(1, half).astype(BF16)
    sends(sum_buf.at[1, second], far_buf.at[0, second], ring_s.at[2], ring_r.at[2], ahead)
    arrived(core_buf.at[2], core_r.at[2])
    sum_buf[2, :half, :] = both(2, 0).astype(BF16)
    sends(sum_buf.at[2, first], far_buf.at[1, first], ring_s.at[3], ring_r.at[3], behind)
    yield
    arrived(via_buf.at[0], ring_r.at[0])
    sum_buf[1, :half, :] = (both(1, 0) + via_buf[0].astype(F32)).astype(BF16)
    sends(sum_buf.at[1, first], far_buf.at[0, first], ring_s.at[4], ring_r.at[4], ahead)
    arrived(via_buf.at[1], ring_r.at[1])
    sum_buf[2, half:, :] = (both(2, half) + via_buf[1].astype(F32)).astype(BF16)
    sends(sum_buf.at[2, second], far_buf.at[1, second], ring_s.at[5], ring_r.at[5], behind)
    arrived(core_buf.at[3], core_r.at[3])

    def total(part):
        rows_at = first if part == 0 else second
        start = part * half
        near = both(3, start)
        arrived(far_buf.at[0, rows_at], ring_r.at[4 if part == 0 else 2])
        near = near + far_buf[0, start : start + half, :].astype(F32)
        arrived(far_buf.at[1, rows_at], ring_r.at[3 if part == 0 else 5])
        return near + far_buf[1, start : start + half, :].astype(F32)

    yield total


def ring_reduce_scratch(rows, width):
    dma = pltpu.SemaphoreType.DMA
    return [
        pltpu.VMEM((4, rows, width), BF16),
        pltpu.VMEM((3, rows, width), BF16),
        pltpu.VMEM((2, rows // 2, width), BF16),
        pltpu.VMEM((2, rows, width), BF16),
        dma((4,)),
        dma((4,)),
        dma((6,)),
        dma((6,)),
    ]


def ring_spread(out_ref, part, ring_s, ring_r, core_s, core_r, sends):
    xl, xh, core = lax.axis_index("xl"), lax.axis_index("xh"), lax.axis_index("core")
    half = out_ref.shape[3] // 2
    mine = out_ref.at[xl, xh, core, pl.ds(part * half, half)]
    sends(mine, mine, ring_s.at[part, 0], ring_r.at[part, 0], chip_along(1))
    sends(mine, mine, ring_s.at[part, 1], ring_r.at[part, 1], chip_along(-1))
    sends(mine, mine, core_s.at[part, 0], core_r.at[part, 0], neighbour("core", 1))


def ring_spread_finish(out_ref, ring_s, ring_r, core_s, core_r, sends):
    xl, xh, core = lax.axis_index("xl"), lax.axis_index("xh"), lax.axis_index("core")
    half = out_ref.shape[3] // 2
    at = xh * 2 + xl

    def block(step, part, which):
        chip = lax.rem(at + step + 4, 4)
        return out_ref.at[lax.rem(chip, 2), lax.div(chip, 2), which, pl.ds(part * half, half)]

    for part in (0, 1):
        for n, (step, on) in enumerate(((-1, 1), (1, -1))):
            landed = block(step, part, core)
            arrived(landed, ring_r.at[part, n])
            if part == n:
                sends(landed, landed, ring_s.at[part, 2], ring_r.at[part, 2], chip_along(on))
            sends(landed, landed, core_s.at[part, 1 + n], core_r.at[part, 1 + n], neighbour("core", 1))
    for part in (0, 1):
        landed = block(2, part, core)
        arrived(landed, ring_r.at[part, 2])
        sends(landed, landed, core_s.at[part, 3], core_r.at[part, 3], neighbour("core", 1))
    for part in (0, 1):
        for n, step in enumerate((0, -1, 1, 2)):
            arrived(block(step, part, 1 - core), core_r.at[part, n])


def ring_spread_scratch():
    dma = pltpu.SemaphoreType.DMA
    return [dma((2, 3)), dma((2, 3)), dma((2, 4)), dma((2, 4))]


def along_x():
    return neighbour("core", 1), neighbour("xh", 1), chip_along(1), chip_along(-1)


CHUNKS = 4


def reduce_scratch(count, rows, width):
    dma = pltpu.SemaphoreType.DMA
    return [
        pltpu.VMEM((count, 2, rows, width), BF16),
        pltpu.VMEM((count, rows, width), BF16),
        pltpu.VMEM((count, rows, width), BF16),
        dma((count, CHUNKS, 2)),
        dma((count, CHUNKS, 2)),
        dma((count, CHUNKS)),
        dma((count, CHUNKS)),
    ]


def spread_chunk(out_ref, n, step, sems, sends):
    xh, core = lax.axis_index("xh"), lax.axis_index("core")
    at = pl.ds(n * step, step)
    mine = out_ref.at[xh * 2 + core, at]
    far_s, far_r, core_s, core_r = sems
    sends(mine, mine, far_s.at[n], far_r.at[n], neighbour("xh", 1))
    sends(mine, mine, core_s.at[n, 0], core_r.at[n, 0], neighbour("core", 1))


def spread_finish(out_ref, step, sems, sends):
    xh, core = lax.axis_index("xh"), lax.axis_index("core")
    far_s, far_r, core_s, core_r = sems
    for n in range(CHUNKS):
        at = pl.ds(n * step, step)
        theirs = out_ref.at[(1 - xh) * 2 + core, at]
        arrived(theirs, far_r.at[n])
        sends(theirs, theirs, core_s.at[n, 1], core_r.at[n, 1], neighbour("core", 1))
    for n in range(CHUNKS):
        at = pl.ds(n * step, step)
        arrived(out_ref.at[xh * 2 + 1 - core, at], core_r.at[n, 0])
        arrived(out_ref.at[(1 - xh) * 2 + 1 - core, at], core_r.at[n, 1])


def spread_scratch():
    dma = pltpu.SemaphoreType.DMA
    return [dma((CHUNKS,)), dma((CHUNKS,)), dma((CHUNKS, 2)), dma((CHUNKS, 2))]


def middle_body(part_ref, x_ref, gain_ref, middle_ref, unit_ref, *scratch):
    sends = Sends()
    greet(*along_x())
    *_, total = ring_reduce_stages(part_ref, *scratch[:8], sends)
    me = lax.axis_index("xh") * 2 + lax.axis_index("core")
    step = x_ref.shape[0] // CHUNKS
    half = x_ref.shape[0] // 2
    for part in (0, 1):
        rows = slice(part * half, (part + 1) * half)
        middle = x_ref[rows, :].astype(F32) + total(part)
        middle_ref[rows, :] = middle
        inverse = lax.rsqrt(jnp.mean(middle * middle, 1, keepdims=True) + EPSILON)
        unit_ref[me, rows, :] = (middle * inverse * gain_ref[...]).astype(BF16)
        for n in range(part * CHUNKS // 2, (part + 1) * CHUNKS // 2):
            spread_chunk(unit_ref, n, step, scratch[8:], sends)
    spread_finish(unit_ref, step, scratch[8:], sends)
    sends.finish()


def vmem(count):
    return [pl.BlockSpec(memory_space=pltpu.VMEM)] * count


def middle_and_unit(part, x, gain):
    rows, width = x.shape
    middle, unit = pl.pallas_call(
        middle_body,
        out_shape=[
            jax.ShapeDtypeStruct((rows, width), F32),
            jax.ShapeDtypeStruct((4, rows, width), BF16),
        ],
        in_specs=vmem(3),
        out_specs=vmem(2),
        scratch_shapes=ring_reduce_scratch(rows, width) + spread_scratch(),
        compiler_params=pltpu.CompilerParams(
            collective_id=1, has_side_effects=True, vmem_limit_bytes=32 * MIB
        ),
        name="middle_and_unit",
    )(part.reshape(2, 2, 2, rows, width), x, gain[None])
    return middle, unit.reshape(4 * rows, width)


def back_body(
    part_ref, middle_ref, grad_ref, gain_ref, hidden_ref, down_ref, dmiddle_ref, dgain_ref, spread_ref, branch_out,
    hidden, down, branch, branch_buf, branch_sum, loc, cs, cr, ys, yr, *scratch,
):
    sends = Sends()
    y, core = lax.axis_index("y"), lax.axis_index("core")
    loads = []
    for n, (src, dst) in enumerate(((hidden_ref, hidden), (down_ref, down))):
        loads.append(pltpu.make_async_copy(src, dst, loc.at[n]))
        loads[-1].start()
    greet(*along_x(), *(neighbour("y", step) for step in (1, 2, 3)))
    stages = reduce_stages(CHUNKS, [part_ref], *scratch[:7], sends)
    next(stages)
    slots = branch_out.shape[1]
    mine = pl.ds(pl.multiple_of(core * slots, slots), slots)
    theirs = pl.ds(pl.multiple_of((1 - core) * slots, slots), slots)

    def output(step):
        target = mod4(y + step)
        branch[step] = dot(hidden[target], down[...], ((1,), (1,))).astype(BF16)
        sends(
            branch.at[step, theirs], branch_buf.at[step], cs.at[step], cr.at[step], neighbour("core", 1)
        )

    def pass_on(step):
        arrived(branch_buf.at[step], cr.at[step])
        value = (branch[step, mine, :].astype(F32) + branch_buf[step].astype(F32)).astype(BF16)
        if step == 0:
            branch_out[y] = value
        else:
            branch_sum[step - 1] = value
            sends(
                branch_sum.at[step - 1],
                branch_out.at[y],
                ys.at[step - 1],
                yr.at[step - 1],
                neighbour("y", step),
            )

    next(stages)
    for load in loads:
        load.wait()
    output(2)
    output(1)
    pass_on(2)
    output(3)
    pass_on(1)
    output(0)
    pass_on(3)
    total = next(stages)
    xl, xh = lax.axis_index("xl"), lax.axis_index("xh")
    step = middle_ref.shape[0] // CHUNKS
    for n in range(CHUNKS):
        rows = slice(n * step, (n + 1) * step)
        middle = middle_ref[rows, :]
        inverse = lax.rsqrt(jnp.mean(middle * middle, 1, keepdims=True) + EPSILON)
        normed = middle * inverse
        dunit = total(0, n)
        product = dunit * normed
        dgain = jnp.sum(product, 0, keepdims=True)
        if n == 0:
            dgain_ref[...] = dgain
        else:
            dgain_ref[...] += dgain
        mean = jnp.mean(product * gain_ref[...], 1, keepdims=True)
        dmiddle = grad_ref[rows, :].astype(F32) + inverse * (dunit * gain_ref[...] - normed * mean)
        dmiddle_ref[rows, :] = dmiddle
        spread_ref[xl, xh, core, rows, :] = dmiddle.astype(BF16)
        if n % 2 == 1:
            ring_spread(spread_ref, n // 2, *scratch[7:], sends)
    pass_on(0)
    ring_spread_finish(spread_ref, *scratch[7:], sends)
    for step in (1, 3, 2):
        arrived(branch_out.at[mod4(y - step)], yr.at[step - 1])
    sends.finish()


def middle_back(part, middle, grad, gain, hidden, down):
    rows, width = middle.shape
    count, inner = hidden.shape
    slots = count // 4
    dma = pltpu.SemaphoreType.DMA
    anywhere = pl.BlockSpec(memory_space=pl.ANY)
    dmiddle, dgain, spread, branch = pl.pallas_call(
        back_body,
        out_shape=[
            jax.ShapeDtypeStruct((rows, width), F32),
            jax.ShapeDtypeStruct((1, width), F32),
            jax.ShapeDtypeStruct((2, 2, 2, rows, width), BF16),
            jax.ShapeDtypeStruct((4, slots // 2, width), BF16),
        ],
        in_specs=vmem(4) + [anywhere] * 2,
        out_specs=vmem(4),
        scratch_shapes=[
            pltpu.VMEM((4, slots, inner), BF16),
            pltpu.VMEM(down.shape, BF16),
            pltpu.VMEM((4, slots, width), BF16),
            pltpu.VMEM((4, slots // 2, width), BF16),
            pltpu.VMEM((3, slots // 2, width), BF16),
            dma((2,)),
            dma((4,)),
            dma((4,)),
            dma((3,)),
            dma((3,)),
        ]
        + reduce_scratch(1, rows, width)
        + ring_spread_scratch(),
        compiler_params=pltpu.CompilerParams(
            collective_id=2, has_side_effects=True, vmem_limit_bytes=56 * MIB
        ),
        name="middle_back",
    )(part.reshape(4, rows, width), middle, grad, gain[None], hidden.reshape(4, slots, inner), down)
    return dmiddle, dgain[0], spread.reshape(8 * rows, width), branch


def rows_body(
    rows_ref, grad_ref, down_ref, out_ref, raw_out, grad, down, block, loc, out_sem, far_s, far_r, core_s, core_r
):
    y, core = lax.axis_index("y"), lax.axis_index("core")
    half = rows_ref.shape[1] // 2
    sends = Sends()
    greet(neighbour("core", 1), *(neighbour("y", step) for step in (1, 2, 3)))
    at = pl.ds(pl.multiple_of(core * half, half), half)
    own = pltpu.make_async_copy(rows_ref.at[y], out_ref.at[y], loc.at[0])
    own.start()
    loads = []
    for n, (src, dst) in enumerate(((grad_ref, grad), (down_ref, down))):
        loads.append(pltpu.make_async_copy(src, dst, loc.at[1 + n]))
        loads[-1].start()
    for step in (2, 1, 3):
        target = mod4(y + step)
        sends(
            rows_ref.at[target, at],
            out_ref.at[y, at],
            far_s.at[step - 1],
            far_r.at[step - 1],
            neighbour("y", step),
        )
    for load in loads:
        load.wait()
    outs = []
    columns = raw_out.shape[1]
    for n, start in enumerate(range(0, columns, WIDE)):
        cols = min(WIDE, columns - start)
        if n >= 2:
            outs[n - 2].wait()
        block[n % 2, :, :cols] = dot(grad[...], down[:, start : start + cols], ((1,), (0,)))
        outs.append(
            pltpu.make_async_copy(
                block.at[n % 2, :, pl.ds(0, cols)], raw_out.at[:, pl.ds(start, cols)], out_sem.at[n % 2]
            )
        )
        outs[-1].start()
    for step in (1, 3, 2):
        source = mod4(y - step)
        block = out_ref.at[source, at]
        arrived(block, far_r.at[step - 1])
        sends(block, block, core_s.at[step - 1], core_r.at[step - 1], neighbour("core", 1))
    own.wait()
    other = pl.ds(pl.multiple_of((1 - core) * half, half), half)
    for step in (1, 3, 2):
        arrived(out_ref.at[mod4(y - step), other], core_r.at[step - 1])
    for out in outs[-2:]:
        out.wait()
    sends.finish()


def rows_to_experts(rows, grads, down):
    count, hidden = grads.shape[0], down.shape[1]
    anywhere = pl.BlockSpec(memory_space=pl.ANY)
    dma = pltpu.SemaphoreType.DMA
    return pl.pallas_call(
        rows_body,
        out_shape=[
            jax.ShapeDtypeStruct(rows.shape, rows.dtype),
            jax.ShapeDtypeStruct((count, hidden), F32),
        ],
        in_specs=[anywhere] * 3,
        out_specs=[anywhere] * 2,
        scratch_shapes=[
            pltpu.VMEM(grads.shape, BF16),
            pltpu.VMEM(down.shape, BF16),
            pltpu.VMEM((2, count, WIDE), F32),
            dma((3,)),
            dma((2,)),
            dma((3,)),
            dma((3,)),
            dma((3,)),
            dma((3,)),
        ],
        compiler_params=pltpu.CompilerParams(
            collective_id=4, has_side_effects=True, vmem_limit_bytes=40 * MIB
        ),
        name="rows_to_experts",
    )(rows, grads, down)


STEPS = (2, 1, -1, 0)


def finish_body(
    qkv_ref, small_ref, o_ref, ups_ref, downs_ref, part_ref, feed_ref, x_ref, middle_ref, dmiddle_ref, gain_ref,
    out_ref, up_out, down_out, output_ref, dinput_ref, small_out,
    g_ref, loc, t_buf, r_buf, tb_buf, rb_buf, c_buf,
    t_s, t_r, r_s, r_r, tb_s, tb_r, rb_s, rb_r, c_s, c_r,
    up_own, up_buf, up_sum, ex, ey, es, er,
    small_own, small_buf, small_s, small_r, *scratch,
):
    xl, xh, core = lax.axis_index("xl"), lax.axis_index("xh"), lax.axis_index("core")
    place = {"y": lax.axis_index("y"), "z": lax.axis_index("z")}
    my_y = place["y"]
    half = g_ref.shape[3] // 2
    quarter = half // 2
    rings = (("z", "y"), ("y", "z"))
    sends = Sends()
    column = 0
    parts = []
    for n, ref in enumerate((qkv_ref, small_ref, o_ref)):
        cols = ref.shape[-1]
        parts.append(pltpu.make_async_copy(ref, g_ref.at[..., pl.ds(column, cols)], loc.at[n]))
        parts[-1].start()
        column += cols
    for n, (src, dst) in enumerate(((ups_ref.at[xl], up_own), (downs_ref.at[my_y], down_out.at[my_y]))):
        parts.append(pltpu.make_async_copy(src, dst, loc.at[3 + n]))
        parts[-1].start()
    peers = ({"xh": xh, "core": 1 - core}, {"xh": 1 - xh, "core": core}, {"xh": 1 - xh, "core": 1 - core})
    greet(
        *peers,
        chip_along(1),
        chip_along(-1),
        *(neighbour("y", step) for step in (1, 2, 3)),
        *(neighbour("z", step) for step in (1, -1)),
    )
    both = slice(0, 2)
    ring_stages = ring_reduce_stages(part_ref, *scratch[7:15], sends)
    feed_stages = reduce_stages(CHUNKS, [feed_ref], *scratch[:7], sends)
    for step in (2, 1, 3, 0):
        sends(
            ups_ref.at[1 - xl, mod4(my_y + step)],
            up_buf.at[step],
            ex.at[step],
            ey.at[step],
            neighbour("xl", 1),
        )
    next(ring_stages)
    next(feed_stages)
    for part in parts[:3]:
        part.wait()

    def grad_ref(h, first, second, start):
        zz, yy = (first, second) if h == 0 else (second, first)
        return g_ref.at[zz, both, yy, pl.ds(h * half + start, quarter)]

    def grad(h, first, second, j, start, count):
        zz, yy = (first, second) if h == 0 else (second, first)
        return g_ref[zz, j, yy, h * half + start : h * half + start + count, :].astype(F32)

    def firsts(h, k):
        return mod4(place[rings[h][0]] + STEPS[k])

    for k in range(4):
        for h in (0, 1):
            second = place[rings[h][1]]
            for d, way in ((0, 1), (1, -1)):
                sends(
                    grad_ref(h, firsts(h, k), mod4(second + 2), d * quarter),
                    t_buf.at[h, d, k],
                    t_s.at[h, d, k],
                    t_r.at[h, d, k],
                    neighbour(rings[h][1], way),
                )
    for k in range(4):
        for h in (0, 1):
            second = place[rings[h][1]]
            for d, way in ((0, 1), (1, -1)):
                sends(
                    grad_ref(h, firsts(h, k), mod4(second + way), (1 - d) * quarter),
                    r_buf.at[h, d, k, both, pl.ds((1 - d) * quarter, quarter)],
                    r_s.at[h, d, k, 0],
                    r_r.at[h, d, k, 0],
                    neighbour(rings[h][1], way),
                )
    next(ring_stages)
    next(feed_stages)
    for k in range(4):
        for h in (0, 1):
            second = place[rings[h][1]]
            for d, way in ((0, 1), (1, -1)):
                arrived(t_buf.at[h, d, k], t_r.at[h, d, k])
                for j in (0, 1):
                    t_buf[h, d, k, j] = (
                        t_buf[h, d, k, j].astype(F32)
                        + grad(h, firsts(h, k), mod4(second + way), j, d * quarter, quarter)
                    ).astype(BF16)
                sends(
                    t_buf.at[h, d, k],
                    r_buf.at[h, d, k, both, pl.ds(d * quarter, quarter)],
                    r_s.at[h, d, k, 1],
                    r_r.at[h, d, k, 1],
                    neighbour(rings[h][1], way),
                )
    total = next(ring_stages)
    for step in (2, 1, 3):
        sends(
            downs_ref.at[mod4(my_y + step)],
            down_out.at[my_y],
            es.at[1, step - 1],
            er.at[1, step - 1],
            neighbour("y", step),
        )
    for part in parts[3:]:
        part.wait()
    for step in (2, 1, 3, 0):
        target = mod4(my_y + step)
        arrived(up_buf.at[step], ey.at[step])
        value = (up_own[target].astype(F32) + up_buf[step].astype(F32)).astype(BF16)
        if step == 0:
            up_out[my_y] = value
        else:
            up_sum[step - 1] = value
            sends(
                up_sum.at[step - 1],
                up_out.at[my_y],
                es.at[0, step - 1],
                er.at[0, step - 1],
                neighbour("y", step),
            )
    for k in range(4):
        for h in (0, 1):
            second = place[rings[h][1]]
            for d in (0, 1):
                arrived(r_buf.at[h, d, k, both, pl.ds((1 - d) * quarter, quarter)], r_r.at[h, d, k, 0])
                arrived(r_buf.at[h, d, k, both, pl.ds(d * quarter, quarter)], r_r.at[h, d, k, 1])
            for j in (0, 1):
                r_buf[h, 0, k, j] = (
                    r_buf[h, 0, k, j].astype(F32)
                    + r_buf[h, 1, k, j].astype(F32)
                    + grad(h, firsts(h, k), second, j, 0, half)
                ).astype(BF16)
            for d, way in ((0, 1), (1, -1)):
                device = neighbour(rings[h][0], way)
                if k == 0:
                    sends(
                        r_buf.at[h, 0, 0, both, pl.ds(d * quarter, quarter)],
                        tb_buf.at[h, d],
                        tb_s.at[h, d],
                        tb_r.at[h, d],
                        device,
                    )
                if k == 1 + d:
                    sends(
                        r_buf.at[h, 0, k, both, pl.ds((1 - d) * quarter, quarter)],
                        rb_buf.at[h, d, both, pl.ds((1 - d) * quarter, quarter)],
                        rb_s.at[h, d, 0],
                        rb_r.at[h, d, 0],
                        device,
                    )
                    arrived(tb_buf.at[h, d], tb_r.at[h, d])
                    for j in (0, 1):
                        tb_buf[h, d, j] = (
                            tb_buf[h, d, j].astype(F32)
                            + r_buf[h, 0, k, j, d * quarter : (d + 1) * quarter, :].astype(F32)
                        ).astype(BF16)
                    sends(
                        tb_buf.at[h, d],
                        rb_buf.at[h, d, both, pl.ds(d * quarter, quarter)],
                        rb_s.at[h, d, 1],
                        rb_r.at[h, d, 1],
                        device,
                    )
    rows_half = x_ref.shape[0] // 2
    for part in (0, 1):
        rows = slice(part * rows_half, (part + 1) * rows_half)
        x = x_ref[rows, :].astype(F32)
        inverse = lax.rsqrt(jnp.mean(x * x, 1, keepdims=True) + EPSILON)
        normed = x * inverse
        dscaled = total(part) * gain_ref[...]
        mean = jnp.mean(dscaled * normed, 1, keepdims=True)
        dinput_ref[rows, :] = dmiddle_ref[rows, :] + inverse * (dscaled - normed * mean)
    for h in (0, 1):
        for d in (0, 1):
            arrived(rb_buf.at[h, d, both, pl.ds((1 - d) * quarter, quarter)], rb_r.at[h, d, 0])
            arrived(rb_buf.at[h, d, both, pl.ds(d * quarter, quarter)], rb_r.at[h, d, 1])
        for j in (0, 1):
            rb_buf[h, 0, j] = (
                rb_buf[h, 0, j].astype(F32)
                + rb_buf[h, 1, j].astype(F32)
                + r_buf[h, 0, 3, j].astype(F32)
            ).astype(BF16)
        sends(rb_buf.at[h, 0, 1 - xl], c_buf.at[h], c_s.at[h], c_r.at[h], neighbour("xl", 1))
        out_ref[xl, h * half : (h + 1) * half, :] = rb_buf[h, 0, xl].astype(F32)
    for h in (0, 1):
        arrived(c_buf.at[h], c_r.at[h])
        out_ref[1 - xl, h * half : (h + 1) * half, :] = c_buf[h].astype(F32)
    first, last = qkv_ref.shape[-1], qkv_ref.shape[-1] + small_ref.shape[-1]
    small_own[...] = out_ref[0, :, first:last] + out_ref[1, :, first:last]
    for n, peer in enumerate(peers):
        sends(small_own, small_buf.at[n], small_s.at[n], small_r.at[n], peer)
    feed = next(feed_stages)
    step = x_ref.shape[0] // CHUNKS
    for n in range(CHUNKS):
        rows = slice(n * step, (n + 1) * step)
        output_ref[rows, :] = (middle_ref[rows, :] + feed(0, n)).astype(BF16)
    for n, result in enumerate((up_out, down_out)):
        for step in (1, 3, 2):
            arrived(result.at[mod4(my_y - step)], er.at[n, step - 1])
    for n in range(3):
        arrived(small_buf.at[n], small_r.at[n])
    small_out[...] = (small_own[...] + small_buf[1]) + (small_buf[0] + small_buf[2])
    sends.finish()


def finish(grads, ups, downs, part, feed, x, middle, dmiddle, gain):
    rows, cols = grads[0].shape[0], sum(grad.shape[1] for grad in grads)
    share = rows // 32
    half, quarter = share // 2, share // 4
    dma = pltpu.SemaphoreType.DMA
    up_cols, down_cols = ups.shape[1], downs.shape[1]
    small = (share, grads[1].shape[1])
    own_rows, width = x.shape
    anywhere = pl.BlockSpec(memory_space=pl.ANY)
    return pl.pallas_call(
        finish_body,
        out_shape=[
            jax.ShapeDtypeStruct((2, share, cols), F32),
            jax.ShapeDtypeStruct((4, share, up_cols), BF16),
            jax.ShapeDtypeStruct((4, share, down_cols), BF16),
            jax.ShapeDtypeStruct((own_rows, width), BF16),
            jax.ShapeDtypeStruct((own_rows, width), F32),
            jax.ShapeDtypeStruct(small, F32),
        ],
        in_specs=[anywhere] * 5 + vmem(6),
        out_specs=vmem(6),
        scratch_shapes=[
            pltpu.VMEM((4, 2, 4, share, cols), BF16),
            dma((5,)),
            pltpu.VMEM((2, 2, 4, 2, quarter, cols), BF16),
            pltpu.VMEM((2, 2, 4, 2, half, cols), BF16),
            pltpu.VMEM((2, 2, 2, quarter, cols), BF16),
            pltpu.VMEM((2, 2, 2, half, cols), BF16),
            pltpu.VMEM((2, half, cols), BF16),
            dma((2, 2, 4)),
            dma((2, 2, 4)),
            dma((2, 2, 4, 2)),
            dma((2, 2, 4, 2)),
            dma((2, 2)),
            dma((2, 2)),
            dma((2, 2, 2)),
            dma((2, 2, 2)),
            dma((2,)),
            dma((2,)),
            pltpu.VMEM((4, share, up_cols), BF16),
            pltpu.VMEM((4, share, up_cols), BF16),
            pltpu.VMEM((3, share, up_cols), BF16),
            dma((4,)),
            dma((4,)),
            dma((2, 3)),
            dma((2, 3)),
            pltpu.VMEM(small, F32),
            pltpu.VMEM((3, *small), F32),
            dma((3,)),
            dma((3,)),
        ]
        + reduce_scratch(1, own_rows, width)
        + ring_reduce_scratch(own_rows, width),
        compiler_params=pltpu.CompilerParams(
            collective_id=5, has_side_effects=True, vmem_limit_bytes=60 * MIB
        ),
        name="finish",
    )(
        *(grad.reshape(4, 2, 4, share, grad.shape[1]) for grad in grads),
        ups.reshape(2, 4, share, up_cols),
        downs.reshape(4, share, down_cols),
        part.reshape(2, 2, 2, own_rows, width),
        feed.reshape(4, own_rows, width),
        x,
        middle,
        dmiddle,
        gain[None],
    )


def dot(a, b, dims):
    return lax.dot_general(a, b, (dims, ((), ())), preferred_element_type=F32)


def experts_body(
    rows_ref, raw_ref, gate_up_ref, linear_up_ref, gate_ref,
    dgate_pre_out, dlinear_out, hidden_out, gated_out, dgate_out,
):
    @pl.when(pl.program_id(0) == 0)
    def _():
        dgate_out[...] = jnp.zeros_like(dgate_out)

    up = jnp.concatenate([gate_up_ref[...], linear_up_ref[...]], 1)
    joined = dot(rows_ref[...], up, ((1,), (0,)))
    gate_pre, linear = joined[:, :LANES], joined[:, LANES:]
    sigmoid = jax.nn.sigmoid(gate_pre)
    silu = gate_pre * sigmoid
    hidden = silu * linear
    dhidden = raw_ref[...]
    gate = gate_ref[...]
    dgate_out[...] += hidden * dhidden
    dhidden = dhidden * gate
    hidden_out[...] = hidden.astype(BF16)
    gated_out[...] = (hidden * gate).astype(BF16)
    dgate_pre_out[...] = (dhidden * linear * (sigmoid + silu * (1.0 - sigmoid))).astype(BF16)
    dlinear_out[...] = (dhidden * silu).astype(BF16)


def experts(rows, raw, up, gates):
    count, hidden = raw.shape
    width = up.shape[0]
    chunks = hidden // LANES
    chunk = pl.BlockSpec((count, LANES), lambda j: (0, j))
    some = jax.ShapeDtypeStruct((count, hidden), BF16)
    return pl.pallas_call(
        experts_body,
        grid=(chunks,),
        in_specs=[
            pl.BlockSpec((count, width), lambda j: (0, 0)),
            chunk,
            pl.BlockSpec((width, LANES), lambda j: (0, j)),
            pl.BlockSpec((width, LANES), lambda j: (0, chunks + j)),
            pl.BlockSpec((count, 1), lambda j: (0, 0)),
        ],
        out_specs=[chunk] * 4 + [pl.BlockSpec((count, LANES), lambda j: (0, 0))],
        out_shape=[some] * 4 + [jax.ShapeDtypeStruct((count, LANES), F32)],
        compiler_params=pltpu.CompilerParams(vmem_limit_bytes=56 * MIB),
        name="experts",
    )(rows, raw, up, up, gates)


def return_body(
    dgate_pre_ref, dlinear_ref, up_ref, dgate_ref, rows_ref,
    dunit_out, dgate_out, up_out,
    djoined, up, rows, dunit, dgate_own, dunit_buf, dgate_buf, dunit_sum, dgate_sum, block,
    loc, core_s, core_r, far_s, far_r, out_sem,
):
    y, core = lax.axis_index("y"), lax.axis_index("core")
    slots = dgate_ref.shape[1]
    half = slots // 2
    hidden = dgate_pre_ref.shape[1]
    sends = Sends()
    loads = []
    for n, (src, dst) in enumerate(
        (
            (up_ref, up),
            (dgate_pre_ref, djoined.at[:, pl.ds(0, hidden)]),
            (dlinear_ref, djoined.at[:, pl.ds(hidden, hidden)]),
            (rows_ref.at[:, pl.ds(0, rows.shape[1])], rows),
        )
    ):
        loads.append(pltpu.make_async_copy(src, dst, loc.at[1, n]))
        loads[-1].start()
    greet(neighbour("core", 1), *(neighbour("y", step) for step in (1, 2, 3)))
    mine = pl.ds(pl.multiple_of(core * half, half), half)
    theirs = pl.ds(pl.multiple_of((1 - core) * half, half), half)
    order = (2, 1, 3, 0)
    own = []
    for step in order:
        target = mod4(y + step)
        sends(
            dgate_ref.at[target, theirs],
            dgate_buf.at[step],
            core_s.at[1, step],
            core_r.at[1, step],
            neighbour("core", 1),
        )
        own.append(pltpu.make_async_copy(dgate_ref.at[target, mine], dgate_own.at[step], loc.at[0, step]))
        own[-1].start()
    for load in loads[:3]:
        load.wait()
    for copy in own:
        copy.wait()

    def compute(step):
        at = pl.ds(pl.multiple_of(mod4(y + step) * slots, slots), slots)
        dunit[step] = dot(djoined[at, :], up[...], ((1,), (1,))).astype(BF16)
        sends(
            dunit.at[step, theirs],
            dunit_buf.at[step],
            core_s.at[0, step],
            core_r.at[0, step],
            neighbour("core", 1),
        )

    def pass_on(step):
        arrived(dunit_buf.at[step], core_r.at[0, step])
        arrived(dgate_buf.at[step], core_r.at[1, step])
        dunit_value = (dunit[step, mine, :].astype(F32) + dunit_buf[step].astype(F32)).astype(BF16)
        dgate_value = dgate_own[step] + dgate_buf[step]
        if step == 0:
            dunit_out[y] = dunit_value
            dgate_out[y] = dgate_value
            return
        dunit_sum[step - 1] = dunit_value
        dgate_sum[step - 1] = dgate_value
        for n, (summed, result) in enumerate(((dunit_sum, dunit_out), (dgate_sum, dgate_out))):
            sends(
                summed.at[step - 1],
                result.at[y],
                far_s.at[n, step - 1],
                far_r.at[n, step - 1],
                neighbour("y", step),
            )

    compute(2)
    compute(1)
    pass_on(2)
    compute(3)
    pass_on(1)
    compute(0)
    pass_on(3)
    loads[3].wait()
    blocks = up_out.shape[0] // WIDE

    @pl.loop(0, blocks)
    def _(j):
        at = pl.ds(pl.multiple_of(j * WIDE, WIDE), WIDE)
        slot = lax.rem(j, 2)

        @pl.when(j >= 2)
        def _():
            pltpu.make_async_copy(block.at[slot], up_out.at[at], out_sem.at[slot]).wait()

        block[slot] = dot(rows[:, at], djoined[...], ((0,), (0,))).astype(BF16)
        pltpu.make_async_copy(block.at[slot], up_out.at[at], out_sem.at[slot]).start()

    pass_on(0)
    for slot in (0, 1):
        pltpu.make_async_copy(block.at[slot], up_out.at[pl.ds(0, WIDE)], out_sem.at[slot]).wait()
    for n, result in enumerate((dunit_out, dgate_out)):
        for step in (1, 3, 2):
            arrived(result.at[mod4(y - step)], far_r.at[n, step - 1])
    sends.finish()


def return_rows(dgate_pre, dlinear, up, dgate, rows):
    _, slots, lanes = dgate.shape
    half = slots // 2
    width, wide = up.shape
    count = dlinear.shape[0]
    dma = pltpu.SemaphoreType.DMA
    anywhere = pl.BlockSpec(memory_space=pl.ANY)
    return pl.pallas_call(
        return_body,
        out_shape=[
            jax.ShapeDtypeStruct((4, half, width), BF16),
            jax.ShapeDtypeStruct((4, half, lanes), F32),
            jax.ShapeDtypeStruct((width, wide), BF16),
        ],
        in_specs=[anywhere] * 5,
        out_specs=vmem(2) + [anywhere],
        scratch_shapes=[
            pltpu.VMEM((count, wide), BF16),
            pltpu.VMEM((width, wide), BF16),
            pltpu.VMEM((count, width), BF16),
            pltpu.VMEM((4, slots, width), BF16),
            pltpu.VMEM((4, half, lanes), F32),
            pltpu.VMEM((4, half, width), BF16),
            pltpu.VMEM((4, half, lanes), F32),
            pltpu.VMEM((3, half, width), BF16),
            pltpu.VMEM((3, half, lanes), F32),
            pltpu.VMEM((2, WIDE, wide), BF16),
            dma((2, 4)),
            dma((2, 4)),
            dma((2, 4)),
            dma((2, 3)),
            dma((2, 3)),
            dma((2,)),
        ],
        compiler_params=pltpu.CompilerParams(
            collective_id=3, has_side_effects=True, vmem_limit_bytes=62 * MIB
        ),
        name="return_rows",
    )(dgate_pre, dlinear, up, dgate, rows)


def attention_body(
    k_ref, v_ref, q0, q1, q2, cos_ref, sin_ref, col_ref, row_ref, gate_ref,
    key_out, val_out, que_out, mix_out, gmix_out, prob_out,
):
    h = pl.program_id(1)
    cosine, sine = cos_ref[...], sin_ref[...]
    scale = 1.0 / math.sqrt(HD)

    def rotated(v):
        return v * cosine + pltpu.roll(v, HD // 2, 1) * sine

    key = rotated(k_ref[...]).astype(BF16)
    val = v_ref[...].astype(BF16)
    key_out[...] = key
    val_out[...] = val
    tokens = key.shape[0]
    half = tokens // 2
    allowed = []
    for start in (0, half):
        seen = start + half
        at_row = start + lax.broadcasted_iota(jnp.int32, (half, seen), 0)
        at_col = lax.broadcasted_iota(jnp.int32, (half, seen), 1)
        seg_row, seg_col = row_ref[0, :, :seen], col_ref[start : start + half, :]
        allowed.append((at_col <= at_row) & ((seg_row == 0) | (seg_row == seg_col)))
    for e, q_ref in enumerate((q0, q1, q2)):
        query = (rotated(q_ref[...]) * scale).astype(BF16)
        at = pl.ds(pl.multiple_of((e * HEADS + h) * HD, HD), HD)
        que_out[:, at] = query
        for n, start in enumerate((0, half)):
            rows, seen = slice(start, start + half), start + half
            scores = jnp.where(allowed[n], dot(query[rows], key[:seen], ((1,), (1,))), NEGATIVE)
            largest = jnp.max(scores, 1, keepdims=True)
            expsum = jnp.exp(scores - largest)
            prob = (expsum * (1.0 / jnp.sum(expsum, 1, keepdims=True))).astype(BF16)
            prob_out[0, 0, e, rows, :seen] = prob
            mixed = dot(prob, val[:seen], ((1,), (0,))).astype(BF16)
            mix_out[rows, at] = mixed
            gmix_out[rows, at] = (mixed.astype(F32) * gate_ref[rows, e : e + 1]).astype(BF16)


def block_specs(tokens):
    def column(n):
        return pl.BlockSpec((tokens, HD), lambda g, h: (g, n * HEADS + h))

    def rows(width):
        return pl.BlockSpec((tokens, width), lambda g, h: (g, 0))

    return column, rows


def prob_spec(tokens):
    return pl.BlockSpec((1, 1, 3, tokens, tokens), lambda g, h: (g, h, 0, 0, 0))


def attention_forward(joined, cosine, sine, segments, gates):
    groups, tokens = segments.shape
    column, rows = block_specs(tokens)
    wide = jax.ShapeDtypeStruct((groups * tokens, 3 * HEADS * HD), BF16)
    narrow = jax.ShapeDtypeStruct((groups * tokens, HEADS * HD), BF16)
    return pl.pallas_call(
        attention_body,
        grid=(groups, HEADS),
        in_specs=[column(n) for n in range(5)]
        + [rows(HD)] * 2
        + [rows(1), pl.BlockSpec((1, 1, tokens), lambda g, h: (g, 0, 0)), rows(gates.shape[1])],
        out_specs=[column(0), column(0)] + [rows(wide.shape[1])] * 3 + [prob_spec(tokens)],
        out_shape=[narrow, narrow, wide, wide, wide]
        + [jax.ShapeDtypeStruct((groups, HEADS, 3, tokens, tokens), BF16)],
        compiler_params=pltpu.CompilerParams(vmem_limit_bytes=48 * MIB),
        name="attention_forward",
    )(
        *[joined] * 5, cosine, sine, segments.reshape(-1, 1), segments[:, None], gates
    )


def attention_back_body(
    key_ref, val_ref, q0, q1, q2, m0, m1, m2, h0, h1, h2, prob_ref, cos_ref, sin_ref, gate_ref,
    grad_out, dgate_out,
):
    h = pl.program_id(1)
    cosine, sine = cos_ref[...], sin_ref[...]
    scale = 1.0 / math.sqrt(HD)

    def rotated_back(v):
        return v * cosine - pltpu.roll(v, HD // 2, 1) * sine

    key, val = key_ref[...], val_ref[...]
    tokens = key.shape[0]
    half = tokens // 2
    dkeys = [jnp.zeros((half, HD), F32)] * 2
    dvals = [jnp.zeros((half, HD), F32)] * 2
    lane = lax.broadcasted_iota(jnp.int32, (tokens, HD), 1)
    dgates = jnp.zeros((tokens, HD), F32)
    for e, (q_ref, m_ref, h_ref) in enumerate(((q0, m0, h0), (q1, m1, h1), (q2, m2, h2))):
        query, mixed, raw = q_ref[...], m_ref[...].astype(F32), h_ref[...]
        inner = jnp.sum(mixed * raw, 1, keepdims=True)
        dgates = dgates + jnp.where(lane == e, inner, 0.0)
        gate = gate_ref[:, e : e + 1]
        dmixed = (raw * gate).astype(BF16)
        delta = jnp.sum(dmixed.astype(F32) * mixed, 1, keepdims=True)
        dqueries = []
        for start in (0, half):
            rows, seen = slice(start, start + half), start + half
            prob = prob_ref[0, 0, e, rows, :seen]
            dprob = dot(dmixed[rows], val[:seen], ((1,), (1,)))
            dscores = (prob.astype(F32) * (dprob - delta[rows])).astype(BF16)
            dqueries.append(dot(dscores, key[:seen], ((1,), (0,))))
            dval = dot(prob, dmixed[rows], ((0,), (0,)))
            dkey = dot(dscores, query[rows], ((0,), (0,)))
            dvals[0] = dvals[0] + dval[:half]
            dkeys[0] = dkeys[0] + dkey[:half]
            if start:
                dvals[1] = dvals[1] + dval[half:]
                dkeys[1] = dkeys[1] + dkey[half:]
        dquery = jnp.concatenate(dqueries, 0)
        at = pl.ds(pl.multiple_of(((2 + e) * HEADS + h) * HD, HD), HD)
        grad_out[:, at] = rotated_back(dquery * scale).astype(BF16)
    dkey, dval = jnp.concatenate(dkeys, 0), jnp.concatenate(dvals, 0)
    grad_out[:, pl.ds(pl.multiple_of(h * HD, HD), HD)] = rotated_back(dkey).astype(BF16)
    grad_out[:, pl.ds(pl.multiple_of((HEADS + h) * HD, HD), HD)] = dval.astype(BF16)

    @pl.when(h == 0)
    def _():
        dgate_out[...] = dgates

    @pl.when(h > 0)
    def _():
        dgate_out[...] += dgates


def attention_back(key, val, que, mix, raw, prob, cosine, sine, gates):
    groups, tokens = prob.shape[0], prob.shape[-1]
    column, rows = block_specs(tokens)
    thirds = [column(n) for n in range(3)]
    grads = jax.ShapeDtypeStruct((groups * tokens, 5 * HEADS * HD), BF16)
    return pl.pallas_call(
        attention_back_body,
        grid=(groups, HEADS),
        in_specs=[column(0), column(0)]
        + thirds * 3
        + [prob_spec(tokens)]
        + [rows(HD)] * 2
        + [rows(gates.shape[1])],
        out_specs=[rows(grads.shape[1]), rows(HD)],
        out_shape=[grads, jax.ShapeDtypeStruct((groups * tokens, HD), F32)],
        compiler_params=pltpu.CompilerParams(vmem_limit_bytes=48 * MIB),
        name="attention_back",
    )(key, val, que, que, que, mix, mix, mix, raw, raw, raw, prob, cosine, sine, gates)


def positions(segments):
    index = jnp.arange(segments.shape[0], dtype=jnp.int32)
    prompt = jnp.sum((segments == 0).astype(jnp.int32))
    first = jnp.sum((segments == 1).astype(jnp.int32))
    before = jnp.where(segments == 0, 0, jnp.where(segments == 1, prompt, prompt + first))
    return jnp.where(segments == 0, index, prompt + index - before)


def route_gates(logits, routes, count):
    onehot = (routes[:, :, None] == jnp.arange(count, dtype=jnp.int32)).astype(F32)
    chosen = jnp.sum(onehot * logits[:, None, :], -1)
    expsum = jnp.exp(chosen - jnp.max(chosen, -1, keepdims=True))
    weights = expsum / jnp.sum(expsum, -1, keepdims=True)
    return weights, onehot, jnp.sum(weights[:, :, None] * onehot, 1)


def router_back(dgate, weights, onehot):
    dchosen = jnp.sum(dgate[:, None, :] * onehot, -1)
    dselect = weights * (dchosen - jnp.sum(weights * dchosen, -1, keepdims=True))
    return jnp.sum(dselect[:, :, None] * onehot, 1).astype(BF16)


def normalize(activations):
    inverse = lax.rsqrt(jnp.mean(activations * activations, -1, keepdims=True) + EPSILON)
    return activations * inverse, inverse


def reorder(rows):
    count, width = rows.shape
    return jnp.transpose(rows.reshape(count, 4, 2, 4, width // 32), (0, 3, 2, 1, 4)).reshape(count, width)


def pad_to(array, width):
    return jnp.pad(array, ((0, 0), (0, width - array.shape[1])))


def on_device(
    inputs,
    segments,
    att_routes,
    mlp_routes,
    key_value,
    query_proj,
    output_proj,
    router_att,
    gain_att,
    gate_up,
    down_proj,
    router_mlp,
    gain_mlp,
    out_grad,
):
    width = inputs.shape[1]
    inner = query_proj.shape[2]
    hidden_local = down_proj.shape[1]
    att_count = query_proj.shape[0]
    mlp_count = gate_up.shape[0]
    share = gate_up.shape[1]
    part = inner // 2
    qkv_cols = (2 + att_count) * part
    small_at = qkv_cols
    out_at = qkv_cols + 128
    small = jnp.concatenate([router_att, router_mlp, gain_att[:, None], gain_mlp[:, None]], 1)
    own_att = jnp.concatenate(
        [
            jnp.transpose(key_value.reshape(share, 2, 2, part), (2, 0, 1, 3)).reshape(2, share, -1),
            jnp.transpose(query_proj.reshape(att_count, share, 2, part), (2, 1, 0, 3)).reshape(
                2, share, -1
            ),
            jnp.broadcast_to(pad_to(small, 128), (2, share, 128)),
            jnp.transpose(output_proj.reshape(att_count, 2, part, share), (1, 3, 0, 2)).reshape(
                2, share, -1
            ),
        ],
        2,
    )
    inputs = reorder(inputs)
    out_grad = reorder(out_grad)
    x_all = lax.all_gather(inputs, ("xl", *TP), axis=0, tiled=True)
    grad_all = lax.all_gather(out_grad, TP, axis=0, tiled=True)
    marks = pad_to(jnp.concatenate([segments[:, None], att_routes], 1), LANES).astype(BF16)
    weights, up_parts, down_parts, marks = gather_dp(
        own_att,
        gate_up.reshape(mlp_count, share, -1),
        jnp.swapaxes(down_proj, 1, 2),
        marks,
    )
    marks = marks[:, :, :3].astype(jnp.int32)
    up_whole = lax.all_gather(
        up_parts.reshape(2 * mlp_count * share, -1), "z", axis=0, tiled=True
    )
    down_whole = lax.all_gather(
        down_parts.reshape(2 * mlp_count * share, -1), "z", axis=0, tiled=True
    )

    tokens = segments.shape[0]
    match = jnp.sum((mlp_routes[:, :, None] == jnp.arange(mlp_count, dtype=jnp.int32)).astype(BF16), 1)
    index = jnp.arange(tokens, dtype=jnp.int32)
    lower = (index[None, :] < index[:, None]).astype(BF16)
    rank = dot(lower, match, ((1,), (0,)))
    slot = jnp.where(match > 0, rank.astype(jnp.int32), -1)
    pick = (slot.T[:, None, :] == jnp.arange(CAP, dtype=jnp.int32)[None, :, None]).astype(BF16)
    pick_rows = pick.reshape(mlp_count * CAP, tokens)
    grad_rows = dot(pick_rows, grad_all, ((1,), (0,))).astype(BF16)
    grad_in = lax.all_to_all(grad_rows.reshape(mlp_count, CAP, width), "y", 0, 0, tiled=True)
    grad_in = grad_in.reshape(mlp_count * CAP, width)

    small_all = weights[:, small_at : small_at + 128].astype(F32)
    gain_one, gain_two = small_all[:, 7], small_all[:, 8]
    segments = marks[:, :, 0]
    att_routes = marks[:, :, 1:].reshape(2 * tokens, 2)
    places = jax.vmap(positions)(segments).reshape(-1).astype(F32)
    frequency = ROPE_BASE ** (-2.0 * jnp.arange(HD // 2, dtype=F32) / HD)
    angles = places[:, None] * frequency[None, :]
    cosine = jnp.concatenate([jnp.cos(angles)] * 2, 1)
    sine = jnp.concatenate([-jnp.sin(angles), jnp.sin(angles)], 1)
    normed_one, _ = normalize(x_all.astype(F32))
    unit_one = (normed_one * gain_one).astype(BF16)
    joined_att = dot(unit_one, weights[:, :out_at], ((1,), (0,)))
    weights_att, onehot_att, gate_att = route_gates(
        joined_att[:, small_at : small_at + att_count], att_routes, att_count
    )
    key_rot, val_rows, queries, mixed, gmixed, prob = attention_forward(
        joined_att, cosine, sine, segments, gate_att
    )
    out_weights = weights[:, out_at:]
    attention = dot(gmixed, out_weights, ((1,), (1,))).astype(BF16)
    middle, unit_two = middle_and_unit(attention, inputs, gain_two)

    router_two = weights[:, small_at + att_count : small_at + att_count + mlp_count]
    logit_mlp = dot(unit_two, router_two, ((1,), (0,)))
    weights_mlp, onehot_mlp, gate_mlp = route_gates(logit_mlp, mlp_routes, mlp_count)
    gate_high = gate_mlp.astype(BF16)
    gate_low = (gate_mlp - gate_high.astype(F32)).astype(BF16)
    extended = jnp.concatenate([unit_two, pad_to(jnp.concatenate([gate_high, gate_low], 1), 128)], 1)
    rows_out = dot(pick_rows, extended, ((1,), (0,))).astype(BF16)
    rows_ext, raw = rows_to_experts(
        rows_out.reshape(mlp_count, CAP, width + 128), grad_in, down_whole
    )
    rows_ext = rows_ext.reshape(mlp_count * CAP, width + 128)
    gates_ext = rows_ext[:, width : width + 2 * mlp_count].astype(F32)
    mine = (jnp.arange(2 * mlp_count) % mlp_count == lax.axis_index("y")).astype(F32)
    gates_in = jnp.sum(gates_ext * mine, 1, keepdims=True)
    dgate_pre, dlinear, hidden, gated, dgate_part = experts(rows_ext, raw, up_whole, gates_in)
    grad_down_whole = dot(grad_in, gated, ((0,), (0,))).astype(BF16)
    dgate_part, grad_down_whole = lax.optimization_barrier((dgate_part, grad_down_whole))
    grad_down_sum = lax.psum_scatter(grad_down_whole, "z", scatter_dimension=0, tiled=True)
    dunit_back, dgate_back, grad_up_whole = return_rows(
        dgate_pre, dlinear, up_whole, dgate_part.reshape(mlp_count, CAP, LANES), rows_ext
    )
    grad_up_sum = lax.psum_scatter(grad_up_whole, "z", scatter_dimension=0, tiled=True)
    pick_half = lax.dynamic_slice_in_dim(pick, lax.axis_index("core") * (CAP // 2), CAP // 2, 1)
    dgate_two = jnp.sum(pick_half.astype(F32) * jnp.sum(dgate_back, -1, keepdims=True), 1).T
    dlogit_mlp = router_back(dgate_two, weights_mlp, onehot_mlp)
    dunit_two = dot(
        pick_half.reshape(-1, tokens), dunit_back.reshape(-1, width), ((0,), (0,))
    ) + dot(dlogit_mlp, router_two, ((1,), (1,)))
    grad_rmlp = dot(unit_two, dlogit_mlp, ((0,), (0,)))
    dmiddle, grad_gain_two, dattention, branch_back = middle_back(
        dunit_two.astype(BF16), middle, out_grad, gain_two, hidden, down_whole
    )

    raw = dot(dattention, out_weights, ((1,), (0,)))
    grad_qkv, dgate_one = attention_back(
        key_rot, val_rows, queries, mixed, raw, prob, cosine, sine, gate_att
    )
    halves = grad_down_sum.reshape(2, mlp_count * share, hidden_local)
    xl = lax.axis_index("xl")
    theirs = lax.ppermute(
        lax.dynamic_index_in_dim(halves, 1 - xl, 0, keepdims=False), "xl", ((0, 1), (1, 0))
    )
    theirs, grad_qkv = lax.optimization_barrier((theirs, grad_qkv))
    grad_down_sum = (
        lax.dynamic_index_in_dim(halves, xl, 0, keepdims=False).astype(F32) + theirs.astype(F32)
    ).astype(BF16)
    dlogit_att = router_back(dgate_one[:, :att_count], weights_att, onehot_att)
    grad_joined = jnp.concatenate([grad_qkv, pad_to(dlogit_att, 128)], 1)
    dunit_one = dot(grad_joined, weights[:, :out_at], ((1,), (1,)))
    grad_gain_one = jnp.sum(dunit_one * normed_one, 0)
    grad_small = jnp.concatenate(
        [
            dot(unit_one, dlogit_att, ((0,), (0,))),
            grad_rmlp,
            grad_gain_one[:, None],
            grad_gain_two[:, None],
        ],
        1,
    )
    gate_slots = jnp.sum(pick_half.astype(F32) * gate_mlp.T[:, None, :], -1, keepdims=True)
    feed = dot(
        pick_half.reshape(-1, tokens),
        (branch_back.astype(F32) * gate_slots).astype(BF16).reshape(-1, width),
        ((0,), (0,)),
    )
    summed_att, ups_sum, downs_sum, output, grad_input, small_sum = finish(
        (
            dot(unit_one, grad_qkv, ((0,), (0,))).astype(BF16),
            pad_to(grad_small, 128).astype(BF16),
            dot(dattention, gmixed, ((0,), (0,))).astype(BF16),
        ),
        grad_up_sum,
        grad_down_sum,
        dunit_one.astype(BF16),
        feed.astype(BF16),
        inputs,
        middle,
        dmiddle,
        gain_one,
    )
    grad_kv = jnp.transpose(
        summed_att[:, :, : 2 * part].reshape(2, share, 2, part), (1, 2, 0, 3)
    ).reshape(share, 2, inner)
    grad_query = jnp.transpose(
        summed_att[:, :, 2 * part : qkv_cols].reshape(2, share, att_count, part), (2, 1, 0, 3)
    ).reshape(att_count, share, inner)
    grad_output = jnp.transpose(
        summed_att[:, :, out_at:].reshape(2, share, att_count, part), (2, 0, 3, 1)
    ).reshape(att_count, inner, share)
    output = reorder(output)
    grad_input = reorder(grad_input)

    grads_up = ups_sum.astype(F32).reshape(mlp_count, share, 2, hidden_local)
    grads_down = jnp.swapaxes(downs_sum.astype(F32), 1, 2)
    return (
        output,
        grad_input,
        grad_kv,
        grad_query,
        grad_output,
        small_sum[:, :3],
        small_sum[:, 7],
        grads_up,
        grads_down,
        small_sum[:, 3:7],
        small_sum[:, 8],
    )


def solution(mesh):
    fine = Mesh(mesh.devices.reshape(4, 2, 4, 2, 2), ALL)
    return jax.shard_map(
        on_device,
        mesh=fine,
        in_specs=(
            P(ALL, None),
            P(DP),
            P(DP, None),
            P(DP, None),
            P(DP, None, TP),
            P(None, DP, TP),
            P(None, TP, DP),
            P(DP, None),
            P(DP),
            P(None, DP, None, TP),
            P(None, TP, DP),
            P(DP, None),
            P(DP),
            P(ALL, None),
        ),
        out_specs=(
            P(ALL, None),
            P(ALL, None),
            P(DP, None, TP),
            P(None, DP, TP),
            P(None, TP, DP),
            P(DP, None),
            P(DP),
            P(None, DP, None, TP),
            P(None, TP, DP),
            P(DP, None),
            P(DP),
        ),
        check_vma=False,
    )
```

```python
import functools
import math

import jax
import jax.numpy as jnp
from jax import lax
from jax.experimental import pallas as pl
from jax.experimental.pallas import tpu as pltpu
from jax.sharding import Mesh, PartitionSpec as P

LANES = 128
WIDE = 256
HD = 128
HEADS = 2
CAP = 320
EPSILON = 1e-06
NEGATIVE = -1e30
ROPE_BASE = 10000.0
MESH_ID = pl.DeviceIdType.MESH
MIB = 1024 * 1024
DP = ("y", "xl", "z")
TP = ("xh", "core")
ALL = DP + TP
F32 = jnp.float32
BF16 = jnp.bfloat16


def mod4(place):
    return lax.rem(place + 4, 4)


def neighbour(axis, step):
    size = 4 if axis in ("y", "z") else 2
    return {axis: lax.rem(lax.axis_index(axis) + step + size, size)}


def chip_along(step):
    at = lax.rem(lax.axis_index("xh") * 2 + lax.axis_index("xl") + step + 4, 4)
    return {"xh": lax.div(at, 2), "xl": lax.rem(at, 2)}


def greet(*devices):
    barrier = pltpu.get_barrier_semaphore()
    for device in devices:
        pl.semaphore_signal(barrier, inc=1, device_id=device, device_id_type=MESH_ID)
    pl.semaphore_wait(barrier, len(devices))


def arrived(ref, sem):
    pltpu.make_async_copy(ref, ref, sem).wait()


class Sends:
    def __init__(self):
        self.copies = []

    def __call__(self, src, dst, send_sem, recv_sem, device):
        copy = pltpu.make_async_remote_copy(
            src_ref=src,
            dst_ref=dst,
            send_sem=send_sem,
            recv_sem=recv_sem,
            device_id=device,
            device_id_type=MESH_ID,
        )
        copy.start()
        self.copies.append(copy)

    def finish(self):
        for copy in self.copies:
            copy.wait_send()


def gather_body(
    x_ref, ups_ref, downs_ref, marks_ref, out_ref, up_ref, down_ref, marks_out,
    loc, xs, xr, s1, r1m, r1p, f1s, f1r, s2, r2m, r2p, f2s, f2r, es, er, ex, ey, ms, mr,
):
    y, xl, z = lax.axis_index("y"), lax.axis_index("xl"), lax.axis_index("z")
    half = x_ref.shape[1] // 2
    quarter = half // 2
    greet(
        neighbour("xl", 1),
        *(neighbour("y", step) for step in (1, 2, 3)),
        *(neighbour("z", step) for step in (1, -1)),
    )
    rings = (("z", "y"), ("y", "z"))
    place = {"y": y, "z": z}
    other = 1 - xl
    both = pl.ds(0, 2)
    sends = Sends()
    send = sends

    def slot(h, first, second, j, start, count):
        yy, zz = (second, first) if h == 0 else (first, second)
        return out_ref.at[zz, j, yy, pl.ds(start, count)]

    own = pltpu.make_async_copy(x_ref.at[xl], out_ref.at[z, xl, y], loc.at[0])
    own.start()
    own_marks = pltpu.make_async_copy(marks_ref, marks_out.at[xl], loc.at[3])
    own_marks.start()
    send(marks_ref, marks_out.at[xl], ms, mr, neighbour("xl", 1))
    experts = ((ups_ref, up_ref), (downs_ref, down_ref))
    kept = []
    for n, (shards, expert) in enumerate(experts):
        place_of = expert.at[xl] if n == 0 else expert
        kept.append(pltpu.make_async_copy(shards.at[y], place_of.at[y], loc.at[1 + n]))
        kept[-1].start()
        if n == 0:
            send(shards.at[y], place_of.at[y], ex.at[0], ey.at[0], neighbour("xl", 1))
        for step in (1, 3, 2):
            send(
                shards.at[mod4(y + step)],
                place_of.at[y],
                es.at[n, step - 1],
                er.at[n, step - 1],
                neighbour("y", step),
            )
    for h in (0, 1):
        first, second = place[rings[h][0]], place[rings[h][1]]
        src = x_ref.at[xl, pl.ds(h * half, half)]
        dst = slot(h, first, second, xl, h * half, half)
        send(x_ref.at[other, pl.ds(h * half, half)], dst, xs.at[h], xr.at[h], neighbour("xl", 1))
        send(src, dst, s1.at[h, 0, 0], r1m.at[h, 0], neighbour(rings[h][0], 1))
        send(src, dst, s1.at[h, 0, 1], r1p.at[h, 0], neighbour(rings[h][0], -1))
    own.wait()

    def send_second(h, k, first):
        block = slot(h, first, place[rings[h][1]], both, h * half, half)
        send(block, block, s2.at[h, k, 0], r2m.at[h, k], neighbour(rings[h][1], 1))
        send(block, block, s2.at[h, k, 1], r2p.at[h, k], neighbour(rings[h][1], -1))

    for h in (0, 1):
        first, second = place[rings[h][0]], place[rings[h][1]]
        block = slot(h, first, second, other, h * half, half)
        arrived(block, xr.at[h])
        send(block, block, s1.at[h, 1, 0], r1m.at[h, 1], neighbour(rings[h][0], 1))
        send(block, block, s1.at[h, 1, 1], r1p.at[h, 1], neighbour(rings[h][0], -1))
        send_second(h, 0, first)
    for j, jx in ((0, xl), (1, other)):
        for h in (0, 1):
            first, second = place[rings[h][0]], place[rings[h][1]]
            arrived(slot(h, mod4(first - 1), second, jx, h * half, half), r1m.at[h, j])
            block = slot(h, mod4(first - 1), second, jx, h * half, quarter)
            send(block, block, f1s.at[h, j, 0], f1r.at[h, j, 0], neighbour(rings[h][0], 1))
            arrived(slot(h, mod4(first + 1), second, jx, h * half, half), r1p.at[h, j])
            block = slot(h, mod4(first + 1), second, jx, h * half + quarter, quarter)
            send(block, block, f1s.at[h, j, 1], f1r.at[h, j, 1], neighbour(rings[h][0], -1))
    for k, step in ((1, -1), (2, 1)):
        for h in (0, 1):
            send_second(h, k, mod4(place[rings[h][0]] + step))
    for h in (0, 1):
        first, second = place[rings[h][0]], place[rings[h][1]]
        for j, jx in ((0, xl), (1, other)):
            for p in (0, 1):
                block = slot(h, mod4(first + 2), second, jx, h * half + p * quarter, quarter)
                arrived(block, f1r.at[h, j, p])
        send_second(h, 3, mod4(first + 2))
    for step in (1, 3, 2):
        landed = up_ref.at[xl, mod4(y - step)]
        arrived(landed, er.at[0, step - 1])
        send(landed, landed, ex.at[step], ey.at[step], neighbour("xl", 1))
    steps = ((0, 0), (1, -1), (2, 1), (3, 2))
    for k, step in steps:
        for h in (0, 1):
            first, second = mod4(place[rings[h][0]] + step), place[rings[h][1]]
            arrived(slot(h, first, mod4(second - 1), both, h * half, half), r2m.at[h, k])
            block = slot(h, first, mod4(second - 1), both, h * half, quarter)
            send(block, block, f2s.at[h, k, 0], f2r.at[h, k, 0], neighbour(rings[h][1], 1))
            arrived(slot(h, first, mod4(second + 1), both, h * half, half), r2p.at[h, k])
            block = slot(h, first, mod4(second + 1), both, h * half + quarter, quarter)
            send(block, block, f2s.at[h, k, 1], f2r.at[h, k, 1], neighbour(rings[h][1], -1))
    for k, step in steps:
        for h in (0, 1):
            first, second = mod4(place[rings[h][0]] + step), place[rings[h][1]]
            for p in (0, 1):
                block = slot(h, first, mod4(second + 2), both, h * half + p * quarter, quarter)
                arrived(block, f2r.at[h, k, p])
    for step in (0, 1, 3, 2):
        arrived(up_ref.at[other, mod4(y - step)], ey.at[step])
    for step in (1, 3, 2):
        arrived(down_ref.at[mod4(y - step)], er.at[1, step - 1])
    for copy in kept:
        copy.wait()
    arrived(marks_out.at[other], mr)
    own_marks.wait()
    sends.finish()


def gather_dp(shard, ups, downs, marks):
    _, rows, cols = shard.shape
    dma = pltpu.SemaphoreType.DMA
    whole, up, down, marks = pl.pallas_call(
        gather_body,
        out_shape=[
            jax.ShapeDtypeStruct((4, 2, 4, rows, cols), shard.dtype),
            jax.ShapeDtypeStruct((2, *ups.shape), ups.dtype),
            jax.ShapeDtypeStruct(downs.shape, downs.dtype),
            jax.ShapeDtypeStruct((2, *marks.shape), marks.dtype),
        ],
        in_specs=[pl.BlockSpec(memory_space=pl.ANY)] * 4,
        out_specs=[pl.BlockSpec(memory_space=pl.ANY)] * 4,
        scratch_shapes=[
            dma((4,)),
            dma((2,)),
            dma((2,)),
            dma((2, 2, 2)),
            dma((2, 2)),
            dma((2, 2)),
            dma((2, 2, 2)),
            dma((2, 2, 2)),
            dma((2, 4, 2)),
            dma((2, 4)),
            dma((2, 4)),
            dma((2, 4, 2)),
            dma((2, 4, 2)),
            dma((2, 3)),
            dma((2, 3)),
            dma((4,)),
            dma((4,)),
            dma,
            dma,
        ],
        compiler_params=pltpu.CompilerParams(collective_id=0, has_side_effects=True),
        name="gather_weights",
    )(shard, ups, downs, marks)
    return whole.reshape(32 * rows, cols), up, down, marks


def reduce_stages(scatter_count, part_refs, core_buf, sum_buf, far_buf, core_s, core_r, far_s, far_r, sends):
    xh, core = lax.axis_index("xh"), lax.axis_index("core")
    rows = part_refs[0].shape[1]
    step = rows // scatter_count
    far, here = 1 - xh, xh
    for n, chunk in enumerate(range(0, rows, step)):
        at = pl.ds(chunk, step)
        for i, part in enumerate(part_refs):
            sends(
                part.at[far * 2 + 1 - core, at],
                core_buf.at[i, 0, at],
                core_s.at[i, n, 0],
                core_r.at[i, n, 0],
                neighbour("core", 1),
            )
    for n, chunk in enumerate(range(0, rows, step)):
        at = pl.ds(chunk, step)
        for i, part in enumerate(part_refs):
            sends(
                part.at[here * 2 + 1 - core, at],
                core_buf.at[i, 1, at],
                core_s.at[i, n, 1],
                core_r.at[i, n, 1],
                neighbour("core", 1),
            )
    yield
    for n, chunk in enumerate(range(0, rows, step)):
        at = pl.ds(chunk, step)
        for i, part in enumerate(part_refs):
            arrived(core_buf.at[i, 0, at], core_r.at[i, n, 0])
            mine = part[far * 2 + core, chunk : chunk + step, :].astype(F32)
            sum_buf[i, chunk : chunk + step, :] = (
                mine + core_buf[i, 0, chunk : chunk + step, :].astype(F32)
            ).astype(BF16)
            sends(
                sum_buf.at[i, at],
                far_buf.at[i, at],
                far_s.at[i, n],
                far_r.at[i, n],
                neighbour("xh", 1),
            )
    yield

    def total(i, n):
        chunk = n * step
        at = pl.ds(chunk, step)
        arrived(core_buf.at[i, 1, at], core_r.at[i, n, 1])
        near = part_refs[i][here * 2 + core, chunk : chunk + step, :].astype(F32)
        near = near + core_buf[i, 1, chunk : chunk + step, :].astype(F32)
        arrived(far_buf.at[i, at], far_r.at[i, n])
        return near + far_buf[i, chunk : chunk + step, :].astype(F32)

    yield total


def ring_reduce_stages(part_ref, core_buf, sum_buf, via_buf, far_buf, core_s, core_r, ring_s, ring_r, sends):
    xl, xh, core = lax.axis_index("xl"), lax.axis_index("xh"), lax.axis_index("core")
    rows = part_ref.shape[3]
    half = rows // 2
    at = xh * 2 + xl
    chips = [lax.rem(at + step, 4) for step in (2, 1, 3, 0)]
    chips = [(lax.rem(chip, 2), lax.div(chip, 2)) for chip in chips]
    for n, (pxl, pxh) in enumerate(chips):
        sends(
            part_ref.at[pxl, pxh, 1 - core],
            core_buf.at[n],
            core_s.at[n],
            core_r.at[n],
            neighbour("core", 1),
        )

    def own(n, start):
        pxl, pxh = chips[n]
        return part_ref[pxl, pxh, core, start : start + half, :].astype(F32)

    def both(n, start):
        return own(n, start) + core_buf[n, start : start + half, :].astype(F32)

    first, second = pl.ds(0, half), pl.ds(half, half)
    ahead, behind = chip_along(1), chip_along(-1)
    yield
    arrived(core_buf.at[0], core_r.at[0])
    sum_buf[0, :half, :] = both(0, 0).astype(BF16)
    sends(sum_buf.at[0, first], via_buf.at[0], ring_s.at[0], ring_r.at[0], ahead)
    sum_buf[0, half:, :] = both(0, half).astype(BF16)
    sends(sum_buf.at[0, second], via_buf.at[1], ring_s.at[1], ring_r.at[1], behind)
    arrived(core_buf.at[1], core_r.at[1])
    sum_buf[1, half:, :] = both(1, half).astype(BF16)
    sends(sum_buf.at[1, second], far_buf.at[0, second], ring_s.at[2], ring_r.at[2], ahead)
    arrived(core_buf.at[2], core_r.at[2])
    sum_buf[2, :half, :] = both(2, 0).astype(BF16)
    sends(sum_buf.at[2, first], far_buf.at[1, first], ring_s.at[3], ring_r.at[3], behind)
    yield
    arrived(via_buf.at[0], ring_r.at[0])
    sum_buf[1, :half, :] = (both(1, 0) + via_buf[0].astype(F32)).astype(BF16)
    sends(sum_buf.at[1, first], far_buf.at[0, first], ring_s.at[4], ring_r.at[4], ahead)
    arrived(via_buf.at[1], ring_r.at[1])
    sum_buf[2, half:, :] = (both(2, half) + via_buf[1].astype(F32)).astype(BF16)
    sends(sum_buf.at[2, second], far_buf.at[1, second], ring_s.at[5], ring_r.at[5], behind)
    arrived(core_buf.at[3], core_r.at[3])

    def total(part):
        rows_at = first if part == 0 else second
        start = part * half
        near = both(3, start)
        arrived(far_buf.at[0, rows_at], ring_r.at[4 if part == 0 else 2])
        near = near + far_buf[0, start : start + half, :].astype(F32)
        arrived(far_buf.at[1, rows_at], ring_r.at[3 if part == 0 else 5])
        return near + far_buf[1, start : start + half, :].astype(F32)

    yield total


def ring_reduce_scratch(rows, width):
    dma = pltpu.SemaphoreType.DMA
    return [
        pltpu.VMEM((4, rows, width), BF16),
        pltpu.VMEM((3, rows, width), BF16),
        pltpu.VMEM((2, rows // 2, width), BF16),
        pltpu.VMEM((2, rows, width), BF16),
        dma((4,)),
        dma((4,)),
        dma((6,)),
        dma((6,)),
    ]


def ring_spread(out_ref, part, ring_s, ring_r, core_s, core_r, sends):
    xl, xh, core = lax.axis_index("xl"), lax.axis_index("xh"), lax.axis_index("core")
    half = out_ref.shape[3] // 2
    mine = out_ref.at[xl, xh, core, pl.ds(part * half, half)]
    sends(mine, mine, ring_s.at[part, 0], ring_r.at[part, 0], chip_along(1))
    sends(mine, mine, ring_s.at[part, 1], ring_r.at[part, 1], chip_along(-1))
    sends(mine, mine, core_s.at[part, 0], core_r.at[part, 0], neighbour("core", 1))


def ring_spread_finish(out_ref, ring_s, ring_r, core_s, core_r, sends):
    xl, xh, core = lax.axis_index("xl"), lax.axis_index("xh"), lax.axis_index("core")
    half = out_ref.shape[3] // 2
    at = xh * 2 + xl

    def block(step, part, which):
        chip = lax.rem(at + step + 4, 4)
        return out_ref.at[lax.rem(chip, 2), lax.div(chip, 2), which, pl.ds(part * half, half)]

    for part in (0, 1):
        for n, (step, on) in enumerate(((-1, 1), (1, -1))):
            landed = block(step, part, core)
            arrived(landed, ring_r.at[part, n])
            if part == n:
                sends(landed, landed, ring_s.at[part, 2], ring_r.at[part, 2], chip_along(on))
            sends(landed, landed, core_s.at[part, 1 + n], core_r.at[part, 1 + n], neighbour("core", 1))
    for part in (0, 1):
        landed = block(2, part, core)
        arrived(landed, ring_r.at[part, 2])
        sends(landed, landed, core_s.at[part, 3], core_r.at[part, 3], neighbour("core", 1))
    for part in (0, 1):
        for n, step in enumerate((0, -1, 1, 2)):
            arrived(block(step, part, 1 - core), core_r.at[part, n])


def ring_spread_scratch():
    dma = pltpu.SemaphoreType.DMA
    return [dma((2, 3)), dma((2, 3)), dma((2, 4)), dma((2, 4))]


def along_x():
    return neighbour("core", 1), neighbour("xh", 1), chip_along(1), chip_along(-1)


CHUNKS = 4


def reduce_scratch(count, rows, width):
    dma = pltpu.SemaphoreType.DMA
    return [
        pltpu.VMEM((count, 2, rows, width), BF16),
        pltpu.VMEM((count, rows, width), BF16),
        pltpu.VMEM((count, rows, width), BF16),
        dma((count, CHUNKS, 2)),
        dma((count, CHUNKS, 2)),
        dma((count, CHUNKS)),
        dma((count, CHUNKS)),
    ]


def spread_chunk(out_ref, n, step, sems, sends):
    xh, core = lax.axis_index("xh"), lax.axis_index("core")
    at = pl.ds(n * step, step)
    mine = out_ref.at[xh * 2 + core, at]
    far_s, far_r, core_s, core_r = sems
    sends(mine, mine, far_s.at[n], far_r.at[n], neighbour("xh", 1))
    sends(mine, mine, core_s.at[n, 0], core_r.at[n, 0], neighbour("core", 1))


def spread_finish(out_ref, step, sems, sends):
    xh, core = lax.axis_index("xh"), lax.axis_index("core")
    far_s, far_r, core_s, core_r = sems
    for n in range(CHUNKS):
        at = pl.ds(n * step, step)
        theirs = out_ref.at[(1 - xh) * 2 + core, at]
        arrived(theirs, far_r.at[n])
        sends(theirs, theirs, core_s.at[n, 1], core_r.at[n, 1], neighbour("core", 1))
    for n in range(CHUNKS):
        at = pl.ds(n * step, step)
        arrived(out_ref.at[xh * 2 + 1 - core, at], core_r.at[n, 0])
        arrived(out_ref.at[(1 - xh) * 2 + 1 - core, at], core_r.at[n, 1])


def spread_scratch():
    dma = pltpu.SemaphoreType.DMA
    return [dma((CHUNKS,)), dma((CHUNKS,)), dma((CHUNKS, 2)), dma((CHUNKS, 2))]


def middle_body(part_ref, x_ref, gain_ref, middle_ref, unit_ref, *scratch):
    sends = Sends()
    greet(*along_x())
    *_, total = ring_reduce_stages(part_ref, *scratch[:8], sends)
    me = lax.axis_index("xh") * 2 + lax.axis_index("core")
    step = x_ref.shape[0] // CHUNKS
    half = x_ref.shape[0] // 2
    for part in (0, 1):
        rows = slice(part * half, (part + 1) * half)
        middle = x_ref[rows, :].astype(F32) + total(part)
        middle_ref[rows, :] = middle
        inverse = lax.rsqrt(jnp.mean(middle * middle, 1, keepdims=True) + EPSILON)
        unit_ref[me, rows, :] = (middle * inverse * gain_ref[...]).astype(BF16)
        for n in range(part * CHUNKS // 2, (part + 1) * CHUNKS // 2):
            spread_chunk(unit_ref, n, step, scratch[8:], sends)
    spread_finish(unit_ref, step, scratch[8:], sends)
    sends.finish()


def vmem(count):
    return [pl.BlockSpec(memory_space=pltpu.VMEM)] * count


def middle_and_unit(part, x, gain):
    rows, width = x.shape
    middle, unit = pl.pallas_call(
        middle_body,
        out_shape=[
            jax.ShapeDtypeStruct((rows, width), F32),
            jax.ShapeDtypeStruct((4, rows, width), BF16),
        ],
        in_specs=vmem(3),
        out_specs=vmem(2),
        scratch_shapes=ring_reduce_scratch(rows, width) + spread_scratch(),
        compiler_params=pltpu.CompilerParams(
            collective_id=1, has_side_effects=True, vmem_limit_bytes=32 * MIB
        ),
        name="middle_and_unit",
    )(part.reshape(2, 2, 2, rows, width), x, gain[None])
    return middle, unit.reshape(4 * rows, width)


def back_body(
    part_ref, middle_ref, grad_ref, gain_ref, hidden_ref, down_ref, dmiddle_ref, dgain_ref, spread_ref, branch_out,
    hidden, down, branch, branch_buf, branch_sum, loc, cs, cr, ys, yr, *scratch,
):
    sends = Sends()
    y, core = lax.axis_index("y"), lax.axis_index("core")
    loads = []
    for n, (src, dst) in enumerate(((hidden_ref, hidden), (down_ref, down))):
        loads.append(pltpu.make_async_copy(src, dst, loc.at[n]))
        loads[-1].start()
    greet(*along_x(), *(neighbour("y", step) for step in (1, 2, 3)))
    stages = reduce_stages(CHUNKS, [part_ref], *scratch[:7], sends)
    next(stages)
    slots = branch_out.shape[1]
    mine = pl.ds(pl.multiple_of(core * slots, slots), slots)
    theirs = pl.ds(pl.multiple_of((1 - core) * slots, slots), slots)

    def output(step):
        target = mod4(y + step)
        branch[step] = dot(hidden[target], down[...], ((1,), (1,))).astype(BF16)
        sends(
            branch.at[step, theirs], branch_buf.at[step], cs.at[step], cr.at[step], neighbour("core", 1)
        )

    def pass_on(step):
        arrived(branch_buf.at[step], cr.at[step])
        value = (branch[step, mine, :].astype(F32) + branch_buf[step].astype(F32)).astype(BF16)
        if step == 0:
            branch_out[y] = value
        else:
            branch_sum[step - 1] = value
            sends(
                branch_sum.at[step - 1],
                branch_out.at[y],
                ys.at[step - 1],
                yr.at[step - 1],
                neighbour("y", step),
            )

    next(stages)
    for load in loads:
        load.wait()
    output(2)
    output(1)
    pass_on(2)
    output(3)
    pass_on(1)
    output(0)
    pass_on(3)
    total = next(stages)
    xl, xh = lax.axis_index("xl"), lax.axis_index("xh")
    step = middle_ref.shape[0] // CHUNKS
    for n in range(CHUNKS):
        rows = slice(n * step, (n + 1) * step)
        middle = middle_ref[rows, :]
        inverse = lax.rsqrt(jnp.mean(middle * middle, 1, keepdims=True) + EPSILON)
        normed = middle * inverse
        dunit = total(0, n)
        product = dunit * normed
        dgain = jnp.sum(product, 0, keepdims=True)
        if n == 0:
            dgain_ref[...] = dgain
        else:
            dgain_ref[...] += dgain
        mean = jnp.mean(product * gain_ref[...], 1, keepdims=True)
        dmiddle = grad_ref[rows, :].astype(F32) + inverse * (dunit * gain_ref[...] - normed * mean)
        dmiddle_ref[rows, :] = dmiddle
        spread_ref[xl, xh, core, rows, :] = dmiddle.astype(BF16)
        if n % 2 == 1:
            ring_spread(spread_ref, n // 2, *scratch[7:], sends)
    pass_on(0)
    ring_spread_finish(spread_ref, *scratch[7:], sends)
    for step in (1, 3, 2):
        arrived(branch_out.at[mod4(y - step)], yr.at[step - 1])
    sends.finish()


def middle_back(part, middle, grad, gain, hidden, down):
    rows, width = middle.shape
    count, inner = hidden.shape
    slots = count // 4
    dma = pltpu.SemaphoreType.DMA
    anywhere = pl.BlockSpec(memory_space=pl.ANY)
    dmiddle, dgain, spread, branch = pl.pallas_call(
        back_body,
        out_shape=[
            jax.ShapeDtypeStruct((rows, width), F32),
            jax.ShapeDtypeStruct((1, width), F32),
            jax.ShapeDtypeStruct((2, 2, 2, rows, width), BF16),
            jax.ShapeDtypeStruct((4, slots // 2, width), BF16),
        ],
        in_specs=vmem(4) + [anywhere] * 2,
        out_specs=vmem(4),
        scratch_shapes=[
            pltpu.VMEM((4, slots, inner), BF16),
            pltpu.VMEM(down.shape, BF16),
            pltpu.VMEM((4, slots, width), BF16),
            pltpu.VMEM((4, slots // 2, width), BF16),
            pltpu.VMEM((3, slots // 2, width), BF16),
            dma((2,)),
            dma((4,)),
            dma((4,)),
            dma((3,)),
            dma((3,)),
        ]
        + reduce_scratch(1, rows, width)
        + ring_spread_scratch(),
        compiler_params=pltpu.CompilerParams(
            collective_id=2, has_side_effects=True, vmem_limit_bytes=56 * MIB
        ),
        name="middle_back",
    )(part.reshape(4, rows, width), middle, grad, gain[None], hidden.reshape(4, slots, inner), down)
    return dmiddle, dgain[0], spread.reshape(8 * rows, width), branch


def rows_body(rows_ref, out_ref, loc, far_s, far_r, core_s, core_r):
    y, core = lax.axis_index("y"), lax.axis_index("core")
    half = rows_ref.shape[1] // 2
    sends = Sends()
    greet(neighbour("core", 1), *(neighbour("y", step) for step in (1, 2, 3)))
    at = pl.ds(pl.multiple_of(core * half, half), half)
    own = pltpu.make_async_copy(rows_ref.at[y], out_ref.at[y], loc)
    own.start()
    for step in (2, 1, 3):
        target = mod4(y + step)
        sends(
            rows_ref.at[target, at],
            out_ref.at[y, at],
            far_s.at[step - 1],
            far_r.at[step - 1],
            neighbour("y", step),
        )
    for step in (1, 3, 2):
        source = mod4(y - step)
        block = out_ref.at[source, at]
        arrived(block, far_r.at[step - 1])
        sends(block, block, core_s.at[step - 1], core_r.at[step - 1], neighbour("core", 1))
    own.wait()
    other = pl.ds(pl.multiple_of((1 - core) * half, half), half)
    for step in (1, 3, 2):
        arrived(out_ref.at[mod4(y - step), other], core_r.at[step - 1])
    sends.finish()


def rows_to_experts(rows):
    dma = pltpu.SemaphoreType.DMA
    return pl.pallas_call(
        rows_body,
        out_shape=jax.ShapeDtypeStruct(rows.shape, rows.dtype),
        in_specs=[pl.BlockSpec(memory_space=pl.ANY)],
        out_specs=pl.BlockSpec(memory_space=pl.ANY),
        scratch_shapes=[dma, dma((3,)), dma((3,)), dma((3,)), dma((3,))],
        compiler_params=pltpu.CompilerParams(
            collective_id=4, has_side_effects=True, vmem_limit_bytes=40 * MIB
        ),
        name="rows_to_experts",
    )(rows)


STEPS = (2, 1, -1, 0)


def finish_body(
    qkv_ref, small_ref, o_ref, ups_ref, downs_ref, part_ref, feed_ref, x_ref, middle_ref, dmiddle_ref, gain_ref,
    out_ref, up_out, down_out, output_ref, dinput_ref, small_out,
    g_ref, loc, t_buf, r_buf, tb_buf, rb_buf, c_buf,
    t_s, t_r, r_s, r_r, tb_s, tb_r, rb_s, rb_r, c_s, c_r,
    up_own, up_buf, up_sum, ex, ey, es, er,
    small_own, small_buf, small_s, small_r, *scratch,
):
    xl, xh, core = lax.axis_index("xl"), lax.axis_index("xh"), lax.axis_index("core")
    place = {"y": lax.axis_index("y"), "z": lax.axis_index("z")}
    my_y = place["y"]
    half = g_ref.shape[3] // 2
    quarter = half // 2
    rings = (("z", "y"), ("y", "z"))
    sends = Sends()
    column = 0
    parts = []
    for n, ref in enumerate((qkv_ref, small_ref, o_ref)):
        cols = ref.shape[-1]
        parts.append(pltpu.make_async_copy(ref, g_ref.at[..., pl.ds(column, cols)], loc.at[n]))
        parts[-1].start()
        column += cols
    for n, (src, dst) in enumerate(((ups_ref.at[xl], up_own), (downs_ref.at[my_y], down_out.at[my_y]))):
        parts.append(pltpu.make_async_copy(src, dst, loc.at[3 + n]))
        parts[-1].start()
    peers = ({"xh": xh, "core": 1 - core}, {"xh": 1 - xh, "core": core}, {"xh": 1 - xh, "core": 1 - core})
    greet(
        *peers,
        chip_along(1),
        chip_along(-1),
        *(neighbour("y", step) for step in (1, 2, 3)),
        *(neighbour("z", step) for step in (1, -1)),
    )
    both = slice(0, 2)
    ring_stages = ring_reduce_stages(part_ref, *scratch[7:15], sends)
    feed_stages = reduce_stages(CHUNKS, [feed_ref], *scratch[:7], sends)
    for step in (2, 1, 3, 0):
        sends(
            ups_ref.at[1 - xl, mod4(my_y + step)],
            up_buf.at[step],
            ex.at[step],
            ey.at[step],
            neighbour("xl", 1),
        )
    next(ring_stages)
    next(feed_stages)
    for part in parts[:3]:
        part.wait()

    def grad_ref(h, first, second, start):
        zz, yy = (first, second) if h == 0 else (second, first)
        return g_ref.at[zz, both, yy, pl.ds(h * half + start, quarter)]

    def grad(h, first, second, j, start, count):
        zz, yy = (first, second) if h == 0 else (second, first)
        return g_ref[zz, j, yy, h * half + start : h * half + start + count, :].astype(F32)

    def firsts(h, k):
        return mod4(place[rings[h][0]] + STEPS[k])

    for k in range(4):
        for h in (0, 1):
            second = place[rings[h][1]]
            for d, way in ((0, 1), (1, -1)):
                sends(
                    grad_ref(h, firsts(h, k), mod4(second + 2), d * quarter),
                    t_buf.at[h, d, k],
                    t_s.at[h, d, k],
                    t_r.at[h, d, k],
                    neighbour(rings[h][1], way),
                )
    for k in range(4):
        for h in (0, 1):
            second = place[rings[h][1]]
            for d, way in ((0, 1), (1, -1)):
                sends(
                    grad_ref(h, firsts(h, k), mod4(second + way), (1 - d) * quarter),
                    r_buf.at[h, d, k, both, pl.ds((1 - d) * quarter, quarter)],
                    r_s.at[h, d, k, 0],
                    r_r.at[h, d, k, 0],
                    neighbour(rings[h][1], way),
                )
    next(ring_stages)
    next(feed_stages)
    for k in range(4):
        for h in (0, 1):
            second = place[rings[h][1]]
            for d, way in ((0, 1), (1, -1)):
                arrived(t_buf.at[h, d, k], t_r.at[h, d, k])
                for j in (0, 1):
                    t_buf[h, d, k, j] = (
                        t_buf[h, d, k, j].astype(F32)
                        + grad(h, firsts(h, k), mod4(second + way), j, d * quarter, quarter)
                    ).astype(BF16)
                sends(
                    t_buf.at[h, d, k],
                    r_buf.at[h, d, k, both, pl.ds(d * quarter, quarter)],
                    r_s.at[h, d, k, 1],
                    r_r.at[h, d, k, 1],
                    neighbour(rings[h][1], way),
                )
    total = next(ring_stages)
    for step in (2, 1, 3):
        sends(
            downs_ref.at[mod4(my_y + step)],
            down_out.at[my_y],
            es.at[1, step - 1],
            er.at[1, step - 1],
            neighbour("y", step),
        )
    for part in parts[3:]:
        part.wait()
    for step in (2, 1, 3, 0):
        target = mod4(my_y + step)
        arrived(up_buf.at[step], ey.at[step])
        value = (up_own[target].astype(F32) + up_buf[step].astype(F32)).astype(BF16)
        if step == 0:
            up_out[my_y] = value
        else:
            up_sum[step - 1] = value
            sends(
                up_sum.at[step - 1],
                up_out.at[my_y],
                es.at[0, step - 1],
                er.at[0, step - 1],
                neighbour("y", step),
            )
    for k in range(4):
        for h in (0, 1):
            second = place[rings[h][1]]
            for d in (0, 1):
                arrived(r_buf.at[h, d, k, both, pl.ds((1 - d) * quarter, quarter)], r_r.at[h, d, k, 0])
                arrived(r_buf.at[h, d, k, both, pl.ds(d * quarter, quarter)], r_r.at[h, d, k, 1])
            for j in (0, 1):
                r_buf[h, 0, k, j] = (
                    r_buf[h, 0, k, j].astype(F32)
                    + r_buf[h, 1, k, j].astype(F32)
                    + grad(h, firsts(h, k), second, j, 0, half)
                ).astype(BF16)
            for d, way in ((0, 1), (1, -1)):
                device = neighbour(rings[h][0], way)
                if k == 0:
                    sends(
                        r_buf.at[h, 0, 0, both, pl.ds(d * quarter, quarter)],
                        tb_buf.at[h, d],
                        tb_s.at[h, d],
                        tb_r.at[h, d],
                        device,
                    )
                if k == 1 + d:
                    sends(
                        r_buf.at[h, 0, k, both, pl.ds((1 - d) * quarter, quarter)],
                        rb_buf.at[h, d, both, pl.ds((1 - d) * quarter, quarter)],
                        rb_s.at[h, d, 0],
                        rb_r.at[h, d, 0],
                        device,
                    )
                    arrived(tb_buf.at[h, d], tb_r.at[h, d])
                    for j in (0, 1):
                        tb_buf[h, d, j] = (
                            tb_buf[h, d, j].astype(F32)
                            + r_buf[h, 0, k, j, d * quarter : (d + 1) * quarter, :].astype(F32)
                        ).astype(BF16)
                    sends(
                        tb_buf.at[h, d],
                        rb_buf.at[h, d, both, pl.ds(d * quarter, quarter)],
                        rb_s.at[h, d, 1],
                        rb_r.at[h, d, 1],
                        device,
                    )
    rows_half = x_ref.shape[0] // 2
    for part in (0, 1):
        rows = slice(part * rows_half, (part + 1) * rows_half)
        x = x_ref[rows, :].astype(F32)
        inverse = lax.rsqrt(jnp.mean(x * x, 1, keepdims=True) + EPSILON)
        normed = x * inverse
        dscaled = total(part) * gain_ref[...]
        mean = jnp.mean(dscaled * normed, 1, keepdims=True)
        dinput_ref[rows, :] = dmiddle_ref[rows, :] + inverse * (dscaled - normed * mean)
    for h in (0, 1):
        for d in (0, 1):
            arrived(rb_buf.at[h, d, both, pl.ds((1 - d) * quarter, quarter)], rb_r.at[h, d, 0])
            arrived(rb_buf.at[h, d, both, pl.ds(d * quarter, quarter)], rb_r.at[h, d, 1])
        for j in (0, 1):
            rb_buf[h, 0, j] = (
                rb_buf[h, 0, j].astype(F32)
                + rb_buf[h, 1, j].astype(F32)
                + r_buf[h, 0, 3, j].astype(F32)
            ).astype(BF16)
        sends(rb_buf.at[h, 0, 1 - xl], c_buf.at[h], c_s.at[h], c_r.at[h], neighbour("xl", 1))
        out_ref[xl, h * half : (h + 1) * half, :] = rb_buf[h, 0, xl].astype(F32)
    for h in (0, 1):
        arrived(c_buf.at[h], c_r.at[h])
        out_ref[1 - xl, h * half : (h + 1) * half, :] = c_buf[h].astype(F32)
    first, last = qkv_ref.shape[-1], qkv_ref.shape[-1] + small_ref.shape[-1]
    small_own[...] = out_ref[0, :, first:last] + out_ref[1, :, first:last]
    for n, peer in enumerate(peers):
        sends(small_own, small_buf.at[n], small_s.at[n], small_r.at[n], peer)
    feed = next(feed_stages)
    step = x_ref.shape[0] // CHUNKS
    for n in range(CHUNKS):
        rows = slice(n * step, (n + 1) * step)
        output_ref[rows, :] = (middle_ref[rows, :] + feed(0, n)).astype(BF16)
    for n, result in enumerate((up_out, down_out)):
        for step in (1, 3, 2):
            arrived(result.at[mod4(my_y - step)], er.at[n, step - 1])
    for n in range(3):
        arrived(small_buf.at[n], small_r.at[n])
    small_out[...] = (small_own[...] + small_buf[1]) + (small_buf[0] + small_buf[2])
    sends.finish()


def finish(grads, ups, downs, part, feed, x, middle, dmiddle, gain):
    rows, cols = grads[0].shape[0], sum(grad.shape[1] for grad in grads)
    share = rows // 32
    half, quarter = share // 2, share // 4
    dma = pltpu.SemaphoreType.DMA
    up_cols, down_cols = ups.shape[1], downs.shape[1]
    small = (share, grads[1].shape[1])
    own_rows, width = x.shape
    anywhere = pl.BlockSpec(memory_space=pl.ANY)
    return pl.pallas_call(
        finish_body,
        out_shape=[
            jax.ShapeDtypeStruct((2, share, cols), F32),
            jax.ShapeDtypeStruct((4, share, up_cols), BF16),
            jax.ShapeDtypeStruct((4, share, down_cols), BF16),
            jax.ShapeDtypeStruct((own_rows, width), BF16),
            jax.ShapeDtypeStruct((own_rows, width), F32),
            jax.ShapeDtypeStruct(small, F32),
        ],
        in_specs=[anywhere] * 5 + vmem(6),
        out_specs=vmem(6),
        scratch_shapes=[
            pltpu.VMEM((4, 2, 4, share, cols), BF16),
            dma((5,)),
            pltpu.VMEM((2, 2, 4, 2, quarter, cols), BF16),
            pltpu.VMEM((2, 2, 4, 2, half, cols), BF16),
            pltpu.VMEM((2, 2, 2, quarter, cols), BF16),
            pltpu.VMEM((2, 2, 2, half, cols), BF16),
            pltpu.VMEM((2, half, cols), BF16),
            dma((2, 2, 4)),
            dma((2, 2, 4)),
            dma((2, 2, 4, 2)),
            dma((2, 2, 4, 2)),
            dma((2, 2)),
            dma((2, 2)),
            dma((2, 2, 2)),
            dma((2, 2, 2)),
            dma((2,)),
            dma((2,)),
            pltpu.VMEM((4, share, up_cols), BF16),
            pltpu.VMEM((4, share, up_cols), BF16),
            pltpu.VMEM((3, share, up_cols), BF16),
            dma((4,)),
            dma((4,)),
            dma((2, 3)),
            dma((2, 3)),
            pltpu.VMEM(small, F32),
            pltpu.VMEM((3, *small), F32),
            dma((3,)),
            dma((3,)),
        ]
        + reduce_scratch(1, own_rows, width)
        + ring_reduce_scratch(own_rows, width),
        compiler_params=pltpu.CompilerParams(
            collective_id=5, has_side_effects=True, vmem_limit_bytes=60 * MIB
        ),
        name="finish",
    )(
        *(grad.reshape(4, 2, 4, share, grad.shape[1]) for grad in grads),
        ups.reshape(2, 4, share, up_cols),
        downs.reshape(4, share, down_cols),
        part.reshape(2, 2, 2, own_rows, width),
        feed.reshape(4, own_rows, width),
        x,
        middle,
        dmiddle,
        gain[None],
    )


def dot(a, b, dims):
    return lax.dot_general(a, b, (dims, ((), ())), preferred_element_type=F32)


def joined_body(rows_ref, gate_up_ref, linear_up_ref, gate_out, linear_out):
    up = jnp.concatenate([gate_up_ref[...], linear_up_ref[...]], 1)
    joined = dot(rows_ref[...], up, ((1,), (0,)))
    gate_out[...] = joined[:, :LANES]
    linear_out[...] = joined[:, LANES:]


def joined_rows(rows, up):
    count, width, hidden = rows.shape[0], up.shape[0], up.shape[1] // 2
    chunks = hidden // LANES
    chunk = pl.BlockSpec((count, LANES), lambda j: (0, j))
    return pl.pallas_call(
        joined_body,
        grid=(chunks,),
        in_specs=[
            pl.BlockSpec((count, width), lambda j: (0, 0)),
            pl.BlockSpec((width, LANES), lambda j: (0, j)),
            pl.BlockSpec((width, LANES), lambda j: (0, chunks + j)),
        ],
        out_specs=[chunk] * 2,
        out_shape=[jax.ShapeDtypeStruct((count, hidden), F32)] * 2,
        compiler_params=pltpu.CompilerParams(vmem_limit_bytes=48 * MIB),
        name="joined_rows",
    )(rows, up, up)


def experts_body(
    grad_ref, down_ref, gate_pre_ref, linear_ref, gate_ref,
    dgate_pre_out, dlinear_out, hidden_out, gated_out, dgate_out, *, units,
):
    j = pl.program_id(0)

    @pl.when(j == 0)
    def _():
        dgate_out[...] = jnp.zeros_like(dgate_out)

    dhidden = dot(grad_ref[...], down_ref[...], ((1,), (0,)))
    gate_pre, linear = gate_pre_ref[...], linear_ref[...]
    sigmoid = jax.nn.sigmoid(gate_pre)
    silu = gate_pre * sigmoid
    hidden = silu * linear
    gate = gate_ref[...]
    product = hidden * dhidden
    dgate_out[...] += product[:, :LANES] + jnp.where(j * WIDE + LANES < units, product[:, LANES:], 0.0)
    dhidden = dhidden * gate
    hidden_out[...] = hidden.astype(BF16)
    gated_out[...] = (hidden * gate).astype(BF16)
    dgate_pre_out[...] = (dhidden * linear * (sigmoid + silu * (1.0 - sigmoid))).astype(BF16)
    dlinear_out[...] = (dhidden * silu).astype(BF16)


def experts(grads, down, gate_pre, linear, gates):
    count, hidden = gate_pre.shape
    width = down.shape[0]
    chunk = pl.BlockSpec((count, WIDE), lambda j: (0, j))
    some = jax.ShapeDtypeStruct((count, hidden), BF16)
    return pl.pallas_call(
        functools.partial(experts_body, units=hidden),
        grid=(pl.cdiv(hidden, WIDE),),
        in_specs=[
            pl.BlockSpec((count, width), lambda j: (0, 0)),
            pl.BlockSpec((width, WIDE), lambda j: (0, j)),
            chunk,
            chunk,
            pl.BlockSpec((count, 1), lambda j: (0, 0)),
        ],
        out_specs=[chunk] * 4 + [pl.BlockSpec((count, LANES), lambda j: (0, 0))],
        out_shape=[some] * 4 + [jax.ShapeDtypeStruct((count, LANES), F32)],
        compiler_params=pltpu.CompilerParams(vmem_limit_bytes=56 * MIB),
        name="experts",
    )(grads, down, gate_pre, linear, gates)


def return_body(
    dgate_pre_ref, dlinear_ref, up_ref, dgate_ref, rows_ref,
    dunit_out, dgate_out, up_out,
    djoined, up, rows, dunit, dgate_own, dunit_buf, dgate_buf, dunit_sum, dgate_sum, block,
    loc, core_s, core_r, far_s, far_r, out_sem,
):
    y, core = lax.axis_index("y"), lax.axis_index("core")
    slots = dgate_ref.shape[1]
    half = slots // 2
    hidden = dgate_pre_ref.shape[1]
    sends = Sends()
    loads = []
    for n, (src, dst) in enumerate(
        (
            (up_ref, up),
            (dgate_pre_ref, djoined.at[:, pl.ds(0, hidden)]),
            (dlinear_ref, djoined.at[:, pl.ds(hidden, hidden)]),
            (rows_ref.at[:, pl.ds(0, rows.shape[1])], rows),
        )
    ):
        loads.append(pltpu.make_async_copy(src, dst, loc.at[1, n]))
        loads[-1].start()
    greet(neighbour("core", 1), *(neighbour("y", step) for step in (1, 2, 3)))
    mine = pl.ds(pl.multiple_of(core * half, half), half)
    theirs = pl.ds(pl.multiple_of((1 - core) * half, half), half)
    order = (2, 1, 3, 0)
    own = []
    for step in order:
        target = mod4(y + step)
        sends(
            dgate_ref.at[target, theirs],
            dgate_buf.at[step],
            core_s.at[1, step],
            core_r.at[1, step],
            neighbour("core", 1),
        )
        own.append(pltpu.make_async_copy(dgate_ref.at[target, mine], dgate_own.at[step], loc.at[0, step]))
        own[-1].start()
    for load in loads[:3]:
        load.wait()
    for copy in own:
        copy.wait()

    def compute(step):
        at = pl.ds(pl.multiple_of(mod4(y + step) * slots, slots), slots)
        dunit[step] = dot(djoined[at, :], up[...], ((1,), (1,))).astype(BF16)
        sends(
            dunit.at[step, theirs],
            dunit_buf.at[step],
            core_s.at[0, step],
            core_r.at[0, step],
            neighbour("core", 1),
        )

    def pass_on(step):
        arrived(dunit_buf.at[step], core_r.at[0, step])
        arrived(dgate_buf.at[step], core_r.at[1, step])
        dunit_value = (dunit[step, mine, :].astype(F32) + dunit_buf[step].astype(F32)).astype(BF16)
        dgate_value = dgate_own[step] + dgate_buf[step]
        if step == 0:
            dunit_out[y] = dunit_value
            dgate_out[y] = dgate_value
            return
        dunit_sum[step - 1] = dunit_value
        dgate_sum[step - 1] = dgate_value
        for n, (summed, result) in enumerate(((dunit_sum, dunit_out), (dgate_sum, dgate_out))):
            sends(
                summed.at[step - 1],
                result.at[y],
                far_s.at[n, step - 1],
                far_r.at[n, step - 1],
                neighbour("y", step),
            )

    compute(2)
    compute(1)
    pass_on(2)
    compute(3)
    pass_on(1)
    compute(0)
    pass_on(3)
    loads[3].wait()
    blocks = up_out.shape[0] // WIDE

    @pl.loop(0, blocks)
    def _(j):
        at = pl.ds(pl.multiple_of(j * WIDE, WIDE), WIDE)
        slot = lax.rem(j, 2)

        @pl.when(j >= 2)
        def _():
            pltpu.make_async_copy(block.at[slot], up_out.at[at], out_sem.at[slot]).wait()

        block[slot] = dot(rows[:, at], djoined[...], ((0,), (0,))).astype(BF16)
        pltpu.make_async_copy(block.at[slot], up_out.at[at], out_sem.at[slot]).start()

    pass_on(0)
    for slot in (0, 1):
        pltpu.make_async_copy(block.at[slot], up_out.at[pl.ds(0, WIDE)], out_sem.at[slot]).wait()
    for n, result in enumerate((dunit_out, dgate_out)):
        for step in (1, 3, 2):
            arrived(result.at[mod4(y - step)], far_r.at[n, step - 1])
    sends.finish()


def return_rows(dgate_pre, dlinear, up, dgate, rows):
    _, slots, lanes = dgate.shape
    half = slots // 2
    width, wide = up.shape
    count = dlinear.shape[0]
    dma = pltpu.SemaphoreType.DMA
    anywhere = pl.BlockSpec(memory_space=pl.ANY)
    return pl.pallas_call(
        return_body,
        out_shape=[
            jax.ShapeDtypeStruct((4, half, width), BF16),
            jax.ShapeDtypeStruct((4, half, lanes), F32),
            jax.ShapeDtypeStruct((width, wide), BF16),
        ],
        in_specs=[anywhere] * 5,
        out_specs=vmem(2) + [anywhere],
        scratch_shapes=[
            pltpu.VMEM((count, wide), BF16),
            pltpu.VMEM((width, wide), BF16),
            pltpu.VMEM((count, width), BF16),
            pltpu.VMEM((4, slots, width), BF16),
            pltpu.VMEM((4, half, lanes), F32),
            pltpu.VMEM((4, half, width), BF16),
            pltpu.VMEM((4, half, lanes), F32),
            pltpu.VMEM((3, half, width), BF16),
            pltpu.VMEM((3, half, lanes), F32),
            pltpu.VMEM((2, WIDE, wide), BF16),
            dma((2, 4)),
            dma((2, 4)),
            dma((2, 4)),
            dma((2, 3)),
            dma((2, 3)),
            dma((2,)),
        ],
        compiler_params=pltpu.CompilerParams(
            collective_id=3, has_side_effects=True, vmem_limit_bytes=62 * MIB
        ),
        name="return_rows",
    )(dgate_pre, dlinear, up, dgate, rows)


def attention_body(
    k_ref, v_ref, q0, q1, q2, cos_ref, sin_ref, col_ref, row_ref, gate_ref,
    key_out, val_out, que_out, mix_out, gmix_out, prob_out,
):
    h = pl.program_id(1)
    cosine, sine = cos_ref[...], sin_ref[...]
    scale = 1.0 / math.sqrt(HD)

    def rotated(v):
        return v * cosine + pltpu.roll(v, HD // 2, 1) * sine

    key = rotated(k_ref[...]).astype(BF16)
    val = v_ref[...].astype(BF16)
    key_out[...] = key
    val_out[...] = val
    tokens = key.shape[0]
    half = tokens // 2
    allowed = []
    for start in (0, half):
        seen = start + half
        at_row = start + lax.broadcasted_iota(jnp.int32, (half, seen), 0)
        at_col = lax.broadcasted_iota(jnp.int32, (half, seen), 1)
        seg_row, seg_col = row_ref[0, :, :seen], col_ref[start : start + half, :]
        allowed.append((at_col <= at_row) & ((seg_row == 0) | (seg_row == seg_col)))
    for e, q_ref in enumerate((q0, q1, q2)):
        query = (rotated(q_ref[...]) * scale).astype(BF16)
        at = pl.ds(pl.multiple_of((e * HEADS + h) * HD, HD), HD)
        que_out[:, at] = query
        for n, start in enumerate((0, half)):
            rows, seen = slice(start, start + half), start + half
            scores = jnp.where(allowed[n], dot(query[rows], key[:seen], ((1,), (1,))), NEGATIVE)
            largest = jnp.max(scores, 1, keepdims=True)
            expsum = jnp.exp(scores - largest)
            prob = (expsum * (1.0 / jnp.sum(expsum, 1, keepdims=True))).astype(BF16)
            prob_out[0, 0, e, rows, :seen] = prob
            mixed = dot(prob, val[:seen], ((1,), (0,))).astype(BF16)
            mix_out[rows, at] = mixed
            gmix_out[rows, at] = (mixed.astype(F32) * gate_ref[rows, e : e + 1]).astype(BF16)


def block_specs(tokens):
    def column(n):
        return pl.BlockSpec((tokens, HD), lambda g, h: (g, n * HEADS + h))

    def rows(width):
        return pl.BlockSpec((tokens, width), lambda g, h: (g, 0))

    return column, rows


def prob_spec(tokens):
    return pl.BlockSpec((1, 1, 3, tokens, tokens), lambda g, h: (g, h, 0, 0, 0))


def attention_forward(joined, cosine, sine, segments, gates):
    groups, tokens = segments.shape
    column, rows = block_specs(tokens)
    wide = jax.ShapeDtypeStruct((groups * tokens, 3 * HEADS * HD), BF16)
    narrow = jax.ShapeDtypeStruct((groups * tokens, HEADS * HD), BF16)
    return pl.pallas_call(
        attention_body,
        grid=(groups, HEADS),
        in_specs=[column(n) for n in range(5)]
        + [rows(HD)] * 2
        + [rows(1), pl.BlockSpec((1, 1, tokens), lambda g, h: (g, 0, 0)), rows(gates.shape[1])],
        out_specs=[column(0), column(0)] + [rows(wide.shape[1])] * 3 + [prob_spec(tokens)],
        out_shape=[narrow, narrow, wide, wide, wide]
        + [jax.ShapeDtypeStruct((groups, HEADS, 3, tokens, tokens), BF16)],
        compiler_params=pltpu.CompilerParams(vmem_limit_bytes=48 * MIB),
        name="attention_forward",
    )(
        *[joined] * 5, cosine, sine, segments.reshape(-1, 1), segments[:, None], gates
    )


def attention_back_body(
    key_ref, val_ref, q0, q1, q2, m0, m1, m2, h0, h1, h2, prob_ref, cos_ref, sin_ref, gate_ref,
    grad_out, dgate_out,
):
    h = pl.program_id(1)
    cosine, sine = cos_ref[...], sin_ref[...]
    scale = 1.0 / math.sqrt(HD)

    def rotated_back(v):
        return v * cosine - pltpu.roll(v, HD // 2, 1) * sine

    key, val = key_ref[...], val_ref[...]
    tokens = key.shape[0]
    half = tokens // 2
    dkeys = [jnp.zeros((half, HD), F32)] * 2
    dvals = [jnp.zeros((half, HD), F32)] * 2
    lane = lax.broadcasted_iota(jnp.int32, (tokens, HD), 1)
    dgates = jnp.zeros((tokens, HD), F32)
    for e, (q_ref, m_ref, h_ref) in enumerate(((q0, m0, h0), (q1, m1, h1), (q2, m2, h2))):
        query, mixed, raw = q_ref[...], m_ref[...].astype(F32), h_ref[...]
        inner = jnp.sum(mixed * raw, 1, keepdims=True)
        dgates = dgates + jnp.where(lane == e, inner, 0.0)
        gate = gate_ref[:, e : e + 1]
        dmixed = (raw * gate).astype(BF16)
        delta = jnp.sum(dmixed.astype(F32) * mixed, 1, keepdims=True)
        dqueries = []
        for start in (0, half):
            rows, seen = slice(start, start + half), start + half
            prob = prob_ref[0, 0, e, rows, :seen]
            dprob = dot(dmixed[rows], val[:seen], ((1,), (1,)))
            dscores = (prob.astype(F32) * (dprob - delta[rows])).astype(BF16)
            dqueries.append(dot(dscores, key[:seen], ((1,), (0,))))
            dval = dot(prob, dmixed[rows], ((0,), (0,)))
            dkey = dot(dscores, query[rows], ((0,), (0,)))
            dvals[0] = dvals[0] + dval[:half]
            dkeys[0] = dkeys[0] + dkey[:half]
            if start:
                dvals[1] = dvals[1] + dval[half:]
                dkeys[1] = dkeys[1] + dkey[half:]
        dquery = jnp.concatenate(dqueries, 0)
        at = pl.ds(pl.multiple_of(((2 + e) * HEADS + h) * HD, HD), HD)
        grad_out[:, at] = rotated_back(dquery * scale).astype(BF16)
    dkey, dval = jnp.concatenate(dkeys, 0), jnp.concatenate(dvals, 0)
    grad_out[:, pl.ds(pl.multiple_of(h * HD, HD), HD)] = rotated_back(dkey).astype(BF16)
    grad_out[:, pl.ds(pl.multiple_of((HEADS + h) * HD, HD), HD)] = dval.astype(BF16)

    @pl.when(h == 0)
    def _():
        dgate_out[...] = dgates

    @pl.when(h > 0)
    def _():
        dgate_out[...] += dgates


def attention_back(key, val, que, mix, raw, prob, cosine, sine, gates):
    groups, tokens = prob.shape[0], prob.shape[-1]
    column, rows = block_specs(tokens)
    thirds = [column(n) for n in range(3)]
    grads = jax.ShapeDtypeStruct((groups * tokens, 5 * HEADS * HD), BF16)
    return pl.pallas_call(
        attention_back_body,
        grid=(groups, HEADS),
        in_specs=[column(0), column(0)]
        + thirds * 3
        + [prob_spec(tokens)]
        + [rows(HD)] * 2
        + [rows(gates.shape[1])],
        out_specs=[rows(grads.shape[1]), rows(HD)],
        out_shape=[grads, jax.ShapeDtypeStruct((groups * tokens, HD), F32)],
        compiler_params=pltpu.CompilerParams(vmem_limit_bytes=48 * MIB),
        name="attention_back",
    )(key, val, que, que, que, mix, mix, mix, raw, raw, raw, prob, cosine, sine, gates)


def positions(segments):
    index = jnp.arange(segments.shape[0], dtype=jnp.int32)
    prompt = jnp.sum((segments == 0).astype(jnp.int32))
    first = jnp.sum((segments == 1).astype(jnp.int32))
    before = jnp.where(segments == 0, 0, jnp.where(segments == 1, prompt, prompt + first))
    return jnp.where(segments == 0, index, prompt + index - before)


def route_gates(logits, routes, count):
    onehot = (routes[:, :, None] == jnp.arange(count, dtype=jnp.int32)).astype(F32)
    chosen = jnp.sum(onehot * logits[:, None, :], -1)
    expsum = jnp.exp(chosen - jnp.max(chosen, -1, keepdims=True))
    weights = expsum / jnp.sum(expsum, -1, keepdims=True)
    return weights, onehot, jnp.sum(weights[:, :, None] * onehot, 1)


def router_back(dgate, weights, onehot):
    dchosen = jnp.sum(dgate[:, None, :] * onehot, -1)
    dselect = weights * (dchosen - jnp.sum(weights * dchosen, -1, keepdims=True))
    return jnp.sum(dselect[:, :, None] * onehot, 1).astype(BF16)


def normalize(activations):
    inverse = lax.rsqrt(jnp.mean(activations * activations, -1, keepdims=True) + EPSILON)
    return activations * inverse, inverse


def reorder(rows):
    count, width = rows.shape
    return jnp.transpose(rows.reshape(count, 4, 2, 4, width // 32), (0, 3, 2, 1, 4)).reshape(count, width)


def pad_to(array, width):
    return jnp.pad(array, ((0, 0), (0, width - array.shape[1])))


def on_device(
    inputs,
    segments,
    att_routes,
    mlp_routes,
    key_value,
    query_proj,
    output_proj,
    router_att,
    gain_att,
    gate_up,
    down_proj,
    router_mlp,
    gain_mlp,
    out_grad,
):
    width = inputs.shape[1]
    inner = query_proj.shape[2]
    hidden_local = down_proj.shape[1]
    att_count = query_proj.shape[0]
    mlp_count = gate_up.shape[0]
    share = gate_up.shape[1]
    part = inner // 2
    qkv_cols = (2 + att_count) * part
    small_at = qkv_cols
    out_at = qkv_cols + 128
    small = jnp.concatenate([router_att, router_mlp, gain_att[:, None], gain_mlp[:, None]], 1)
    own_att = jnp.concatenate(
        [
            jnp.transpose(key_value.reshape(share, 2, 2, part), (2, 0, 1, 3)).reshape(2, share, -1),
            jnp.transpose(query_proj.reshape(att_count, share, 2, part), (2, 1, 0, 3)).reshape(
                2, share, -1
            ),
            jnp.broadcast_to(pad_to(small, 128), (2, share, 128)),
            jnp.transpose(output_proj.reshape(att_count, 2, part, share), (1, 3, 0, 2)).reshape(
                2, share, -1
            ),
        ],
        2,
    )
    inputs = reorder(inputs)
    out_grad = reorder(out_grad)
    x_all = lax.all_gather(inputs, ("xl", *TP), axis=0, tiled=True)
    grad_all = lax.all_gather(out_grad, TP, axis=0, tiled=True)
    marks = pad_to(jnp.concatenate([segments[:, None], att_routes], 1), LANES).astype(BF16)
    weights, up_parts, down_parts, marks = gather_dp(
        own_att,
        gate_up.reshape(mlp_count, share, -1),
        jnp.swapaxes(down_proj, 1, 2),
        marks,
    )
    marks = marks[:, :, :3].astype(jnp.int32)
    up_whole = lax.all_gather(
        up_parts.reshape(2 * mlp_count * share, -1), "z", axis=0, tiled=True
    )
    xl = lax.axis_index("xl")
    down_theirs = lax.ppermute(down_parts, "xl", ((0, 1), (1, 0)))

    tokens = segments.shape[0]
    match = jnp.sum((mlp_routes[:, :, None] == jnp.arange(mlp_count, dtype=jnp.int32)).astype(BF16), 1)
    index = jnp.arange(tokens, dtype=jnp.int32)
    lower = (index[None, :] < index[:, None]).astype(BF16)
    rank = dot(lower, match, ((1,), (0,)))
    slot = jnp.where(match > 0, rank.astype(jnp.int32), -1)
    pick = (slot.T[:, None, :] == jnp.arange(CAP, dtype=jnp.int32)[None, :, None]).astype(BF16)
    pick_rows = pick.reshape(mlp_count * CAP, tokens)
    grad_rows = dot(pick_rows, grad_all, ((1,), (0,))).astype(BF16)
    grad_in = lax.all_to_all(grad_rows.reshape(mlp_count, CAP, width), "y", 0, 0, tiled=True)
    grad_in = grad_in.reshape(mlp_count * CAP, width)

    small_all = weights[:, small_at : small_at + 128].astype(F32)
    gain_one, gain_two = small_all[:, 7], small_all[:, 8]
    segments = marks[:, :, 0]
    att_routes = marks[:, :, 1:].reshape(2 * tokens, 2)
    places = jax.vmap(positions)(segments).reshape(-1).astype(F32)
    frequency = ROPE_BASE ** (-2.0 * jnp.arange(HD // 2, dtype=F32) / HD)
    angles = places[:, None] * frequency[None, :]
    cosine = jnp.concatenate([jnp.cos(angles)] * 2, 1)
    sine = jnp.concatenate([-jnp.sin(angles), jnp.sin(angles)], 1)
    normed_one, _ = normalize(x_all.astype(F32))
    unit_one = (normed_one * gain_one).astype(BF16)
    joined_att = dot(unit_one, weights[:, :out_at], ((1,), (0,)))
    weights_att, onehot_att, gate_att = route_gates(
        joined_att[:, small_at : small_at + att_count], att_routes, att_count
    )
    key_rot, val_rows, queries, mixed, gmixed, prob = attention_forward(
        joined_att, cosine, sine, segments, gate_att
    )
    down_theirs, gmixed = lax.optimization_barrier((down_theirs, gmixed))
    down_pair = jnp.where(
        xl == 0, jnp.stack([down_parts, down_theirs]), jnp.stack([down_theirs, down_parts])
    )
    down_whole = lax.all_gather(
        down_pair.reshape(2 * mlp_count * share, -1), "z", axis=0, tiled=True
    )
    out_weights = weights[:, out_at:]
    attention = dot(gmixed, out_weights, ((1,), (1,))).astype(BF16)
    middle, unit_two = middle_and_unit(attention, inputs, gain_two)

    router_two = weights[:, small_at + att_count : small_at + att_count + mlp_count]
    logit_mlp = dot(unit_two, router_two, ((1,), (0,)))
    weights_mlp, onehot_mlp, gate_mlp = route_gates(logit_mlp, mlp_routes, mlp_count)
    gate_high = gate_mlp.astype(BF16)
    gate_low = (gate_mlp - gate_high.astype(F32)).astype(BF16)
    extended = jnp.concatenate([unit_two, pad_to(jnp.concatenate([gate_high, gate_low], 1), 128)], 1)
    rows_out = dot(pick_rows, extended, ((1,), (0,))).astype(BF16)
    rows_ext = rows_to_experts(rows_out.reshape(mlp_count, CAP, width + 128))
    rows_ext = rows_ext.reshape(mlp_count * CAP, width + 128)
    gates_ext = rows_ext[:, width : width + 2 * mlp_count].astype(F32)
    mine = (jnp.arange(2 * mlp_count) % mlp_count == lax.axis_index("y")).astype(F32)
    gates_in = jnp.sum(gates_ext * mine, 1, keepdims=True)
    gate_pre, linear = joined_rows(rows_ext, up_whole)
    dgate_pre, dlinear, hidden, gated, dgate_part = experts(
        grad_in, down_whole, gate_pre, linear, gates_in
    )
    grad_down_whole = dot(grad_in, gated, ((0,), (0,))).astype(BF16)
    dgate_part, grad_down_whole = lax.optimization_barrier((dgate_part, grad_down_whole))
    grad_down_sum = lax.psum_scatter(grad_down_whole, "z", scatter_dimension=0, tiled=True)
    dunit_back, dgate_back, grad_up_whole = return_rows(
        dgate_pre, dlinear, up_whole, dgate_part.reshape(mlp_count, CAP, LANES), rows_ext
    )
    grad_up_sum = lax.psum_scatter(grad_up_whole, "z", scatter_dimension=0, tiled=True)
    pick_half = lax.dynamic_slice_in_dim(pick, lax.axis_index("core") * (CAP // 2), CAP // 2, 1)
    dgate_two = jnp.sum(pick_half.astype(F32) * jnp.sum(dgate_back, -1, keepdims=True), 1).T
    dlogit_mlp = router_back(dgate_two, weights_mlp, onehot_mlp)
    dunit_two = dot(
        pick_half.reshape(-1, tokens), dunit_back.reshape(-1, width), ((0,), (0,))
    ) + dot(dlogit_mlp, router_two, ((1,), (1,)))
    dmiddle, grad_gain_two, dattention, branch_back = middle_back(
        dunit_two.astype(BF16), middle, out_grad, gain_two, hidden, down_whole
    )

    grad_down_sum, dattention = lax.optimization_barrier((grad_down_sum, dattention))
    raw = dot(dattention, out_weights, ((1,), (0,)))
    grad_qkv, dgate_one = attention_back(
        key_rot, val_rows, queries, mixed, raw, prob, cosine, sine, gate_att
    )
    halves = grad_down_sum.reshape(2, mlp_count * share, hidden_local)
    theirs = lax.ppermute(
        lax.dynamic_index_in_dim(halves, 1 - xl, 0, keepdims=False), "xl", ((0, 1), (1, 0))
    )
    theirs, grad_qkv, gmixed, dattention, branch_back, dlogit_mlp = lax.optimization_barrier(
        (theirs, grad_qkv, gmixed, dattention, branch_back, dlogit_mlp)
    )
    grad_rmlp = dot(unit_two, dlogit_mlp, ((0,), (0,)))
    grad_down_sum = (
        lax.dynamic_index_in_dim(halves, xl, 0, keepdims=False).astype(F32) + theirs.astype(F32)
    ).astype(BF16)
    dlogit_att = router_back(dgate_one[:, :att_count], weights_att, onehot_att)
    grad_joined = jnp.concatenate([grad_qkv, pad_to(dlogit_att, 128)], 1)
    dunit_one = dot(grad_joined, weights[:, :out_at], ((1,), (1,)))
    grad_gain_one = jnp.sum(dunit_one * normed_one, 0)
    grad_small = jnp.concatenate(
        [
            dot(unit_one, dlogit_att, ((0,), (0,))),
            grad_rmlp,
            grad_gain_one[:, None],
            grad_gain_two[:, None],
        ],
        1,
    )
    gate_slots = jnp.sum(pick_half.astype(F32) * gate_mlp.T[:, None, :], -1, keepdims=True)
    feed = dot(
        pick_half.reshape(-1, tokens),
        (branch_back.astype(F32) * gate_slots).astype(BF16).reshape(-1, width),
        ((0,), (0,)),
    )
    summed_att, ups_sum, downs_sum, output, grad_input, small_sum = finish(
        (
            dot(unit_one, grad_qkv, ((0,), (0,))).astype(BF16),
            pad_to(grad_small, 128).astype(BF16),
            dot(dattention, gmixed, ((0,), (0,))).astype(BF16),
        ),
        grad_up_sum,
        grad_down_sum,
        dunit_one.astype(BF16),
        feed.astype(BF16),
        inputs,
        middle,
        dmiddle,
        gain_one,
    )
    grad_kv = jnp.transpose(
        summed_att[:, :, : 2 * part].reshape(2, share, 2, part), (1, 2, 0, 3)
    ).reshape(share, 2, inner)
    grad_query = jnp.transpose(
        summed_att[:, :, 2 * part : qkv_cols].reshape(2, share, att_count, part), (2, 1, 0, 3)
    ).reshape(att_count, share, inner)
    grad_output = jnp.transpose(
        summed_att[:, :, out_at:].reshape(2, share, att_count, part), (2, 0, 3, 1)
    ).reshape(att_count, inner, share)
    output = reorder(output)
    grad_input = reorder(grad_input)

    grads_up = ups_sum.astype(F32).reshape(mlp_count, share, 2, hidden_local)
    grads_down = jnp.swapaxes(downs_sum.astype(F32), 1, 2)
    return (
        output,
        grad_input,
        grad_kv,
        grad_query,
        grad_output,
        small_sum[:, :3],
        small_sum[:, 7],
        grads_up,
        grads_down,
        small_sum[:, 3:7],
        small_sum[:, 8],
    )


def solution(mesh):
    fine = Mesh(mesh.devices.reshape(4, 2, 4, 2, 2), ALL)
    return jax.shard_map(
        on_device,
        mesh=fine,
        in_specs=(
            P(ALL, None),
            P(DP),
            P(DP, None),
            P(DP, None),
            P(DP, None, TP),
            P(None, DP, TP),
            P(None, TP, DP),
            P(DP, None),
            P(DP),
            P(None, DP, None, TP),
            P(None, TP, DP),
            P(DP, None),
            P(DP),
            P(ALL, None),
        ),
        out_specs=(
            P(ALL, None),
            P(ALL, None),
            P(DP, None, TP),
            P(None, DP, TP),
            P(None, TP, DP),
            P(DP, None),
            P(DP),
            P(None, DP, None, TP),
            P(None, TP, DP),
            P(DP, None),
            P(DP),
        ),
        check_vma=False,
    )
```

```python
import functools
import math

import jax
import jax.numpy as jnp
from jax import lax
from jax.experimental import pallas as pl
from jax.experimental.pallas import tpu as pltpu
from jax.sharding import Mesh, PartitionSpec as P

LANES = 128
WIDE = 256
HD = 128
HEADS = 2
CAP = 320
EPSILON = 1e-06
NEGATIVE = -1e30
ROPE_BASE = 10000.0
MESH_ID = pl.DeviceIdType.MESH
MIB = 1024 * 1024
DP = ("y", "xl", "z")
TP = ("xh", "core")
ALL = DP + TP
F32 = jnp.float32
BF16 = jnp.bfloat16


def mod4(place):
    return lax.rem(place + 4, 4)


def neighbour(axis, step):
    size = 4 if axis in ("y", "z") else 2
    return {axis: lax.rem(lax.axis_index(axis) + step + size, size)}


def chip_along(step):
    at = lax.rem(lax.axis_index("xh") * 2 + lax.axis_index("xl") + step + 4, 4)
    return {"xh": lax.div(at, 2), "xl": lax.rem(at, 2)}


def greet(*devices):
    barrier = pltpu.get_barrier_semaphore()
    for device in devices:
        pl.semaphore_signal(barrier, inc=1, device_id=device, device_id_type=MESH_ID)
    pl.semaphore_wait(barrier, len(devices))


def arrived(ref, sem):
    pltpu.make_async_copy(ref, ref, sem).wait()


class Sends:
    def __init__(self):
        self.copies = []

    def __call__(self, src, dst, send_sem, recv_sem, device):
        copy = pltpu.make_async_remote_copy(
            src_ref=src,
            dst_ref=dst,
            send_sem=send_sem,
            recv_sem=recv_sem,
            device_id=device,
            device_id_type=MESH_ID,
        )
        copy.start()
        self.copies.append(copy)

    def finish(self):
        for copy in self.copies:
            copy.wait_send()


def gather_body(
    x_ref, ups_ref, downs_ref, marks_ref, out_ref, up_ref, down_ref, marks_out,
    loc, xs, xr, s1, r1m, r1p, f1s, f1r, s2, r2m, r2p, f2s, f2r, es, er, ex, ey, ms, mr,
):
    y, xl, z = lax.axis_index("y"), lax.axis_index("xl"), lax.axis_index("z")
    half = x_ref.shape[1] // 2
    quarter = half // 2
    greet(
        neighbour("xl", 1),
        *(neighbour("y", step) for step in (1, 2, 3)),
        *(neighbour("z", step) for step in (1, -1)),
    )
    rings = (("z", "y"), ("y", "z"))
    place = {"y": y, "z": z}
    other = 1 - xl
    both = pl.ds(0, 2)
    sends = Sends()
    send = sends

    def slot(h, first, second, j, start, count):
        yy, zz = (second, first) if h == 0 else (first, second)
        return out_ref.at[zz, j, yy, pl.ds(start, count)]

    own = pltpu.make_async_copy(x_ref.at[xl], out_ref.at[z, xl, y], loc.at[0])
    own.start()
    own_marks = pltpu.make_async_copy(marks_ref, marks_out.at[xl], loc.at[3])
    own_marks.start()
    send(marks_ref, marks_out.at[xl], ms, mr, neighbour("xl", 1))
    experts = ((ups_ref, up_ref), (downs_ref, down_ref))
    kept = []
    for n, (shards, expert) in enumerate(experts):
        place_of = expert.at[xl] if n == 0 else expert
        kept.append(pltpu.make_async_copy(shards.at[y], place_of.at[y], loc.at[1 + n]))
        kept[-1].start()
        if n == 0:
            send(shards.at[y], place_of.at[y], ex.at[0], ey.at[0], neighbour("xl", 1))
        for step in (1, 3, 2):
            send(
                shards.at[mod4(y + step)],
                place_of.at[y],
                es.at[n, step - 1],
                er.at[n, step - 1],
                neighbour("y", step),
            )
    for h in (0, 1):
        first, second = place[rings[h][0]], place[rings[h][1]]
        src = x_ref.at[xl, pl.ds(h * half, half)]
        dst = slot(h, first, second, xl, h * half, half)
        send(x_ref.at[other, pl.ds(h * half, half)], dst, xs.at[h], xr.at[h], neighbour("xl", 1))
        send(src, dst, s1.at[h, 0, 0], r1m.at[h, 0], neighbour(rings[h][0], 1))
        send(src, dst, s1.at[h, 0, 1], r1p.at[h, 0], neighbour(rings[h][0], -1))
    own.wait()

    def send_second(h, k, first):
        block = slot(h, first, place[rings[h][1]], both, h * half, half)
        send(block, block, s2.at[h, k, 0], r2m.at[h, k], neighbour(rings[h][1], 1))
        send(block, block, s2.at[h, k, 1], r2p.at[h, k], neighbour(rings[h][1], -1))

    for h in (0, 1):
        first, second = place[rings[h][0]], place[rings[h][1]]
        block = slot(h, first, second, other, h * half, half)
        arrived(block, xr.at[h])
        send(block, block, s1.at[h, 1, 0], r1m.at[h, 1], neighbour(rings[h][0], 1))
        send(block, block, s1.at[h, 1, 1], r1p.at[h, 1], neighbour(rings[h][0], -1))
        send_second(h, 0, first)
    for j, jx in ((0, xl), (1, other)):
        for h in (0, 1):
            first, second = place[rings[h][0]], place[rings[h][1]]
            arrived(slot(h, mod4(first - 1), second, jx, h * half, half), r1m.at[h, j])
            block = slot(h, mod4(first - 1), second, jx, h * half, quarter)
            send(block, block, f1s.at[h, j, 0], f1r.at[h, j, 0], neighbour(rings[h][0], 1))
            arrived(slot(h, mod4(first + 1), second, jx, h * half, half), r1p.at[h, j])
            block = slot(h, mod4(first + 1), second, jx, h * half + quarter, quarter)
            send(block, block, f1s.at[h, j, 1], f1r.at[h, j, 1], neighbour(rings[h][0], -1))
    for k, step in ((1, -1), (2, 1)):
        for h in (0, 1):
            send_second(h, k, mod4(place[rings[h][0]] + step))
    for h in (0, 1):
        first, second = place[rings[h][0]], place[rings[h][1]]
        for j, jx in ((0, xl), (1, other)):
            for p in (0, 1):
                block = slot(h, mod4(first + 2), second, jx, h * half + p * quarter, quarter)
                arrived(block, f1r.at[h, j, p])
        send_second(h, 3, mod4(first + 2))
    for step in (1, 3, 2):
        landed = up_ref.at[xl, mod4(y - step)]
        arrived(landed, er.at[0, step - 1])
        send(landed, landed, ex.at[step], ey.at[step], neighbour("xl", 1))
    steps = ((0, 0), (1, -1), (2, 1), (3, 2))
    for k, step in steps:
        for h in (0, 1):
            first, second = mod4(place[rings[h][0]] + step), place[rings[h][1]]
            arrived(slot(h, first, mod4(second - 1), both, h * half, half), r2m.at[h, k])
            block = slot(h, first, mod4(second - 1), both, h * half, quarter)
            send(block, block, f2s.at[h, k, 0], f2r.at[h, k, 0], neighbour(rings[h][1], 1))
            arrived(slot(h, first, mod4(second + 1), both, h * half, half), r2p.at[h, k])
            block = slot(h, first, mod4(second + 1), both, h * half + quarter, quarter)
            send(block, block, f2s.at[h, k, 1], f2r.at[h, k, 1], neighbour(rings[h][1], -1))
    for k, step in steps:
        for h in (0, 1):
            first, second = mod4(place[rings[h][0]] + step), place[rings[h][1]]
            for p in (0, 1):
                block = slot(h, first, mod4(second + 2), both, h * half + p * quarter, quarter)
                arrived(block, f2r.at[h, k, p])
    for step in (0, 1, 3, 2):
        arrived(up_ref.at[other, mod4(y - step)], ey.at[step])
    for step in (1, 3, 2):
        arrived(down_ref.at[mod4(y - step)], er.at[1, step - 1])
    for copy in kept:
        copy.wait()
    arrived(marks_out.at[other], mr)
    own_marks.wait()
    sends.finish()


def gather_dp(shard, ups, downs, marks):
    _, rows, cols = shard.shape
    dma = pltpu.SemaphoreType.DMA
    whole, up, down, marks = pl.pallas_call(
        gather_body,
        out_shape=[
            jax.ShapeDtypeStruct((4, 2, 4, rows, cols), shard.dtype),
            jax.ShapeDtypeStruct((2, *ups.shape), ups.dtype),
            jax.ShapeDtypeStruct(downs.shape, downs.dtype),
            jax.ShapeDtypeStruct((2, *marks.shape), marks.dtype),
        ],
        in_specs=[pl.BlockSpec(memory_space=pl.ANY)] * 4,
        out_specs=[pl.BlockSpec(memory_space=pl.ANY)] * 4,
        scratch_shapes=[
            dma((4,)),
            dma((2,)),
            dma((2,)),
            dma((2, 2, 2)),
            dma((2, 2)),
            dma((2, 2)),
            dma((2, 2, 2)),
            dma((2, 2, 2)),
            dma((2, 4, 2)),
            dma((2, 4)),
            dma((2, 4)),
            dma((2, 4, 2)),
            dma((2, 4, 2)),
            dma((2, 3)),
            dma((2, 3)),
            dma((4,)),
            dma((4,)),
            dma,
            dma,
        ],
        compiler_params=pltpu.CompilerParams(collective_id=0, has_side_effects=True),
        name="gather_weights",
    )(shard, ups, downs, marks)
    return whole.reshape(32 * rows, cols), up, down, marks


def reduce_stages(scatter_count, part_refs, core_buf, sum_buf, far_buf, core_s, core_r, far_s, far_r, sends):
    xh, core = lax.axis_index("xh"), lax.axis_index("core")
    rows = part_refs[0].shape[1]
    step = rows // scatter_count
    far, here = 1 - xh, xh
    for n, chunk in enumerate(range(0, rows, step)):
        at = pl.ds(chunk, step)
        for i, part in enumerate(part_refs):
            sends(
                part.at[far * 2 + 1 - core, at],
                core_buf.at[i, 0, at],
                core_s.at[i, n, 0],
                core_r.at[i, n, 0],
                neighbour("core", 1),
            )
    for n, chunk in enumerate(range(0, rows, step)):
        at = pl.ds(chunk, step)
        for i, part in enumerate(part_refs):
            sends(
                part.at[here * 2 + 1 - core, at],
                core_buf.at[i, 1, at],
                core_s.at[i, n, 1],
                core_r.at[i, n, 1],
                neighbour("core", 1),
            )
    yield
    for n, chunk in enumerate(range(0, rows, step)):
        at = pl.ds(chunk, step)
        for i, part in enumerate(part_refs):
            arrived(core_buf.at[i, 0, at], core_r.at[i, n, 0])
            mine = part[far * 2 + core, chunk : chunk + step, :].astype(F32)
            sum_buf[i, chunk : chunk + step, :] = (
                mine + core_buf[i, 0, chunk : chunk + step, :].astype(F32)
            ).astype(BF16)
            sends(
                sum_buf.at[i, at],
                far_buf.at[i, at],
                far_s.at[i, n],
                far_r.at[i, n],
                neighbour("xh", 1),
            )
    yield

    def total(i, n):
        chunk = n * step
        at = pl.ds(chunk, step)
        arrived(core_buf.at[i, 1, at], core_r.at[i, n, 1])
        near = part_refs[i][here * 2 + core, chunk : chunk + step, :].astype(F32)
        near = near + core_buf[i, 1, chunk : chunk + step, :].astype(F32)
        arrived(far_buf.at[i, at], far_r.at[i, n])
        return near + far_buf[i, chunk : chunk + step, :].astype(F32)

    yield total


def ring_reduce_stages(part_ref, core_buf, sum_buf, via_buf, far_buf, core_s, core_r, ring_s, ring_r, sends):
    xl, xh, core = lax.axis_index("xl"), lax.axis_index("xh"), lax.axis_index("core")
    rows = part_ref.shape[3]
    half = rows // 2
    at = xh * 2 + xl
    chips = [lax.rem(at + step, 4) for step in (2, 1, 3, 0)]
    chips = [(lax.rem(chip, 2), lax.div(chip, 2)) for chip in chips]
    for n, (pxl, pxh) in enumerate(chips):
        sends(
            part_ref.at[pxl, pxh, 1 - core],
            core_buf.at[n],
            core_s.at[n],
            core_r.at[n],
            neighbour("core", 1),
        )

    def own(n, start):
        pxl, pxh = chips[n]
        return part_ref[pxl, pxh, core, start : start + half, :].astype(F32)

    def both(n, start):
        return own(n, start) + core_buf[n, start : start + half, :].astype(F32)

    first, second = pl.ds(0, half), pl.ds(half, half)
    ahead, behind = chip_along(1), chip_along(-1)
    yield
    arrived(core_buf.at[0], core_r.at[0])
    sum_buf[0, :half, :] = both(0, 0).astype(BF16)
    sends(sum_buf.at[0, first], via_buf.at[0], ring_s.at[0], ring_r.at[0], ahead)
    sum_buf[0, half:, :] = both(0, half).astype(BF16)
    sends(sum_buf.at[0, second], via_buf.at[1], ring_s.at[1], ring_r.at[1], behind)
    arrived(core_buf.at[1], core_r.at[1])
    sum_buf[1, half:, :] = both(1, half).astype(BF16)
    sends(sum_buf.at[1, second], far_buf.at[0, second], ring_s.at[2], ring_r.at[2], ahead)
    arrived(core_buf.at[2], core_r.at[2])
    sum_buf[2, :half, :] = both(2, 0).astype(BF16)
    sends(sum_buf.at[2, first], far_buf.at[1, first], ring_s.at[3], ring_r.at[3], behind)
    yield
    arrived(via_buf.at[0], ring_r.at[0])
    sum_buf[1, :half, :] = (both(1, 0) + via_buf[0].astype(F32)).astype(BF16)
    sends(sum_buf.at[1, first], far_buf.at[0, first], ring_s.at[4], ring_r.at[4], ahead)
    arrived(via_buf.at[1], ring_r.at[1])
    sum_buf[2, half:, :] = (both(2, half) + via_buf[1].astype(F32)).astype(BF16)
    sends(sum_buf.at[2, second], far_buf.at[1, second], ring_s.at[5], ring_r.at[5], behind)
    arrived(core_buf.at[3], core_r.at[3])

    def total(part):
        rows_at = first if part == 0 else second
        start = part * half
        near = both(3, start)
        arrived(far_buf.at[0, rows_at], ring_r.at[4 if part == 0 else 2])
        near = near + far_buf[0, start : start + half, :].astype(F32)
        arrived(far_buf.at[1, rows_at], ring_r.at[3 if part == 0 else 5])
        return near + far_buf[1, start : start + half, :].astype(F32)

    yield total


def ring_reduce_scratch(rows, width):
    dma = pltpu.SemaphoreType.DMA
    return [
        pltpu.VMEM((4, rows, width), BF16),
        pltpu.VMEM((3, rows, width), BF16),
        pltpu.VMEM((2, rows // 2, width), BF16),
        pltpu.VMEM((2, rows, width), BF16),
        dma((4,)),
        dma((4,)),
        dma((6,)),
        dma((6,)),
    ]


def ring_spread(out_ref, part, ring_s, ring_r, core_s, core_r, sends):
    xl, xh, core = lax.axis_index("xl"), lax.axis_index("xh"), lax.axis_index("core")
    half = out_ref.shape[3] // 2
    mine = out_ref.at[xl, xh, core, pl.ds(part * half, half)]
    sends(mine, mine, ring_s.at[part, 0], ring_r.at[part, 0], chip_along(1))
    sends(mine, mine, ring_s.at[part, 1], ring_r.at[part, 1], chip_along(-1))
    sends(mine, mine, core_s.at[part, 0], core_r.at[part, 0], neighbour("core", 1))


def ring_spread_finish(out_ref, ring_s, ring_r, core_s, core_r, sends):
    xl, xh, core = lax.axis_index("xl"), lax.axis_index("xh"), lax.axis_index("core")
    half = out_ref.shape[3] // 2
    at = xh * 2 + xl

    def block(step, part, which):
        chip = lax.rem(at + step + 4, 4)
        return out_ref.at[lax.rem(chip, 2), lax.div(chip, 2), which, pl.ds(part * half, half)]

    for part in (0, 1):
        for n, (step, on) in enumerate(((-1, 1), (1, -1))):
            landed = block(step, part, core)
            arrived(landed, ring_r.at[part, n])
            if part == n:
                sends(landed, landed, ring_s.at[part, 2], ring_r.at[part, 2], chip_along(on))
            sends(landed, landed, core_s.at[part, 1 + n], core_r.at[part, 1 + n], neighbour("core", 1))
    for part in (0, 1):
        landed = block(2, part, core)
        arrived(landed, ring_r.at[part, 2])
        sends(landed, landed, core_s.at[part, 3], core_r.at[part, 3], neighbour("core", 1))
    for part in (0, 1):
        for n, step in enumerate((0, -1, 1, 2)):
            arrived(block(step, part, 1 - core), core_r.at[part, n])


def ring_spread_scratch():
    dma = pltpu.SemaphoreType.DMA
    return [dma((2, 3)), dma((2, 3)), dma((2, 4)), dma((2, 4))]


def along_x():
    return neighbour("core", 1), neighbour("xh", 1), chip_along(1), chip_along(-1)


CHUNKS = 4


def reduce_scratch(count, rows, width):
    dma = pltpu.SemaphoreType.DMA
    return [
        pltpu.VMEM((count, 2, rows, width), BF16),
        pltpu.VMEM((count, rows, width), BF16),
        pltpu.VMEM((count, rows, width), BF16),
        dma((count, CHUNKS, 2)),
        dma((count, CHUNKS, 2)),
        dma((count, CHUNKS)),
        dma((count, CHUNKS)),
    ]


def spread_chunk(out_ref, n, step, sems, sends):
    xh, core = lax.axis_index("xh"), lax.axis_index("core")
    at = pl.ds(n * step, step)
    mine = out_ref.at[xh * 2 + core, at]
    far_s, far_r, core_s, core_r = sems
    sends(mine, mine, far_s.at[n], far_r.at[n], neighbour("xh", 1))
    sends(mine, mine, core_s.at[n, 0], core_r.at[n, 0], neighbour("core", 1))


def spread_finish(out_ref, step, sems, sends):
    xh, core = lax.axis_index("xh"), lax.axis_index("core")
    far_s, far_r, core_s, core_r = sems
    for n in range(CHUNKS):
        at = pl.ds(n * step, step)
        theirs = out_ref.at[(1 - xh) * 2 + core, at]
        arrived(theirs, far_r.at[n])
        sends(theirs, theirs, core_s.at[n, 1], core_r.at[n, 1], neighbour("core", 1))
    for n in range(CHUNKS):
        at = pl.ds(n * step, step)
        arrived(out_ref.at[xh * 2 + 1 - core, at], core_r.at[n, 0])
        arrived(out_ref.at[(1 - xh) * 2 + 1 - core, at], core_r.at[n, 1])


def spread_scratch():
    dma = pltpu.SemaphoreType.DMA
    return [dma((CHUNKS,)), dma((CHUNKS,)), dma((CHUNKS, 2)), dma((CHUNKS, 2))]


def middle_body(part_ref, x_ref, gain_ref, middle_ref, unit_ref, *scratch):
    sends = Sends()
    greet(*along_x())
    *_, total = ring_reduce_stages(part_ref, *scratch[:8], sends)
    me = lax.axis_index("xh") * 2 + lax.axis_index("core")
    step = x_ref.shape[0] // CHUNKS
    half = x_ref.shape[0] // 2
    for part in (0, 1):
        rows = slice(part * half, (part + 1) * half)
        middle = x_ref[rows, :].astype(F32) + total(part)
        middle_ref[rows, :] = middle
        inverse = lax.rsqrt(jnp.mean(middle * middle, 1, keepdims=True) + EPSILON)
        unit_ref[me, rows, :] = (middle * inverse * gain_ref[...]).astype(BF16)
        for n in range(part * CHUNKS // 2, (part + 1) * CHUNKS // 2):
            spread_chunk(unit_ref, n, step, scratch[8:], sends)
    spread_finish(unit_ref, step, scratch[8:], sends)
    sends.finish()


def vmem(count):
    return [pl.BlockSpec(memory_space=pltpu.VMEM)] * count


def middle_and_unit(part, x, gain):
    rows, width = x.shape
    middle, unit = pl.pallas_call(
        middle_body,
        out_shape=[
            jax.ShapeDtypeStruct((rows, width), F32),
            jax.ShapeDtypeStruct((4, rows, width), BF16),
        ],
        in_specs=vmem(3),
        out_specs=vmem(2),
        scratch_shapes=ring_reduce_scratch(rows, width) + spread_scratch(),
        compiler_params=pltpu.CompilerParams(
            collective_id=1, has_side_effects=True, vmem_limit_bytes=32 * MIB
        ),
        name="middle_and_unit",
    )(part.reshape(2, 2, 2, rows, width), x, gain[None])
    return middle, unit.reshape(4 * rows, width)


def back_body(
    part_ref, middle_ref, grad_ref, gain_ref, hidden_ref, down_ref, dmiddle_ref, dgain_ref, spread_ref, branch_out,
    hidden, down, branch, branch_buf, branch_sum, loc, cs, cr, ys, yr, *scratch,
):
    sends = Sends()
    y, core = lax.axis_index("y"), lax.axis_index("core")
    loads = []
    for n, (src, dst) in enumerate(((hidden_ref, hidden), (down_ref, down))):
        loads.append(pltpu.make_async_copy(src, dst, loc.at[n]))
        loads[-1].start()
    greet(*along_x(), *(neighbour("y", step) for step in (1, 2, 3)))
    stages = reduce_stages(CHUNKS, [part_ref], *scratch[:7], sends)
    next(stages)
    slots = branch_out.shape[1]
    mine = pl.ds(pl.multiple_of(core * slots, slots), slots)
    theirs = pl.ds(pl.multiple_of((1 - core) * slots, slots), slots)

    def output(step):
        target = mod4(y + step)
        branch[step] = dot(hidden[target], down[...], ((1,), (1,))).astype(BF16)
        sends(
            branch.at[step, theirs], branch_buf.at[step], cs.at[step], cr.at[step], neighbour("core", 1)
        )

    def pass_on(step):
        arrived(branch_buf.at[step], cr.at[step])
        value = (branch[step, mine, :].astype(F32) + branch_buf[step].astype(F32)).astype(BF16)
        if step == 0:
            branch_out[y] = value
        else:
            branch_sum[step - 1] = value
            sends(
                branch_sum.at[step - 1],
                branch_out.at[y],
                ys.at[step - 1],
                yr.at[step - 1],
                neighbour("y", step),
            )

    next(stages)
    for load in loads:
        load.wait()
    output(2)
    output(1)
    pass_on(2)
    output(3)
    pass_on(1)
    output(0)
    pass_on(3)
    total = next(stages)
    xl, xh = lax.axis_index("xl"), lax.axis_index("xh")
    step = middle_ref.shape[0] // CHUNKS
    for n in range(CHUNKS):
        rows = slice(n * step, (n + 1) * step)
        middle = middle_ref[rows, :]
        inverse = lax.rsqrt(jnp.mean(middle * middle, 1, keepdims=True) + EPSILON)
        normed = middle * inverse
        dunit = total(0, n)
        product = dunit * normed
        dgain = jnp.sum(product, 0, keepdims=True)
        if n == 0:
            dgain_ref[...] = dgain
        else:
            dgain_ref[...] += dgain
        mean = jnp.mean(product * gain_ref[...], 1, keepdims=True)
        dmiddle = grad_ref[rows, :].astype(F32) + inverse * (dunit * gain_ref[...] - normed * mean)
        dmiddle_ref[rows, :] = dmiddle
        spread_ref[xl, xh, core, rows, :] = dmiddle.astype(BF16)
        if n % 2 == 1:
            ring_spread(spread_ref, n // 2, *scratch[7:], sends)
    pass_on(0)
    ring_spread_finish(spread_ref, *scratch[7:], sends)
    for step in (1, 3, 2):
        arrived(branch_out.at[mod4(y - step)], yr.at[step - 1])
    sends.finish()


def middle_back(part, middle, grad, gain, hidden, down):
    rows, width = middle.shape
    count, inner = hidden.shape
    slots = count // 4
    dma = pltpu.SemaphoreType.DMA
    anywhere = pl.BlockSpec(memory_space=pl.ANY)
    dmiddle, dgain, spread, branch = pl.pallas_call(
        back_body,
        out_shape=[
            jax.ShapeDtypeStruct((rows, width), F32),
            jax.ShapeDtypeStruct((1, width), F32),
            jax.ShapeDtypeStruct((2, 2, 2, rows, width), BF16),
            jax.ShapeDtypeStruct((4, slots // 2, width), BF16),
        ],
        in_specs=vmem(4) + [anywhere] * 2,
        out_specs=vmem(4),
        scratch_shapes=[
            pltpu.VMEM((4, slots, inner), BF16),
            pltpu.VMEM(down.shape, BF16),
            pltpu.VMEM((4, slots, width), BF16),
            pltpu.VMEM((4, slots // 2, width), BF16),
            pltpu.VMEM((3, slots // 2, width), BF16),
            dma((2,)),
            dma((4,)),
            dma((4,)),
            dma((3,)),
            dma((3,)),
        ]
        + reduce_scratch(1, rows, width)
        + ring_spread_scratch(),
        compiler_params=pltpu.CompilerParams(
            collective_id=2, has_side_effects=True, vmem_limit_bytes=56 * MIB
        ),
        name="middle_back",
    )(part.reshape(4, rows, width), middle, grad, gain[None], hidden.reshape(4, slots, inner), down)
    return dmiddle, dgain[0], spread.reshape(8 * rows, width), branch


def rows_body(rows_ref, out_ref, loc, far_s, far_r, core_s, core_r):
    y, core = lax.axis_index("y"), lax.axis_index("core")
    half = rows_ref.shape[1] // 2
    sends = Sends()
    greet(neighbour("core", 1), *(neighbour("y", step) for step in (1, 2, 3)))
    at = pl.ds(pl.multiple_of(core * half, half), half)
    own = pltpu.make_async_copy(rows_ref.at[y], out_ref.at[y], loc)
    own.start()
    for step in (2, 1, 3):
        target = mod4(y + step)
        sends(
            rows_ref.at[target, at],
            out_ref.at[y, at],
            far_s.at[step - 1],
            far_r.at[step - 1],
            neighbour("y", step),
        )
    for step in (1, 3, 2):
        source = mod4(y - step)
        block = out_ref.at[source, at]
        arrived(block, far_r.at[step - 1])
        sends(block, block, core_s.at[step - 1], core_r.at[step - 1], neighbour("core", 1))
    own.wait()
    other = pl.ds(pl.multiple_of((1 - core) * half, half), half)
    for step in (1, 3, 2):
        arrived(out_ref.at[mod4(y - step), other], core_r.at[step - 1])
    sends.finish()


def rows_to_experts(rows):
    dma = pltpu.SemaphoreType.DMA
    return pl.pallas_call(
        rows_body,
        out_shape=jax.ShapeDtypeStruct(rows.shape, rows.dtype),
        in_specs=[pl.BlockSpec(memory_space=pl.ANY)],
        out_specs=pl.BlockSpec(memory_space=pl.ANY),
        scratch_shapes=[dma, dma((3,)), dma((3,)), dma((3,)), dma((3,))],
        compiler_params=pltpu.CompilerParams(
            collective_id=4, has_side_effects=True, vmem_limit_bytes=40 * MIB
        ),
        name="rows_to_experts",
    )(rows)


STEPS = (2, 1, -1, 0)


def finish_body(
    qkv_ref, small_ref, o_ref, ups_ref, downs_ref, part_ref, feed_ref, x_ref, middle_ref, dmiddle_ref, gain_ref,
    out_ref, up_out, down_out, output_ref, dinput_ref, small_out,
    g_ref, loc, t_buf, r_buf, tb_buf, rb_buf, c_buf,
    t_s, t_r, r_s, r_r, tb_s, tb_r, rb_s, rb_r, c_s, c_r,
    up_own, up_buf, up_sum, ex, ey, es, er,
    small_own, small_buf, small_s, small_r, *scratch,
):
    xl, xh, core = lax.axis_index("xl"), lax.axis_index("xh"), lax.axis_index("core")
    place = {"y": lax.axis_index("y"), "z": lax.axis_index("z")}
    my_y = place["y"]
    half = g_ref.shape[3] // 2
    quarter = half // 2
    rings = (("z", "y"), ("y", "z"))
    sends = Sends()
    column = 0
    parts = []
    for n, ref in enumerate((qkv_ref, small_ref, o_ref)):
        cols = ref.shape[-1]
        parts.append(pltpu.make_async_copy(ref, g_ref.at[..., pl.ds(column, cols)], loc.at[n]))
        parts[-1].start()
        column += cols
    for n, (src, dst) in enumerate(((ups_ref.at[xl], up_own), (downs_ref.at[my_y], down_out.at[my_y]))):
        parts.append(pltpu.make_async_copy(src, dst, loc.at[3 + n]))
        parts[-1].start()
    peers = ({"xh": xh, "core": 1 - core}, {"xh": 1 - xh, "core": core}, {"xh": 1 - xh, "core": 1 - core})
    greet(
        *peers,
        chip_along(1),
        chip_along(-1),
        *(neighbour("y", step) for step in (1, 2, 3)),
        *(neighbour("z", step) for step in (1, -1)),
    )
    both = slice(0, 2)
    ring_stages = ring_reduce_stages(part_ref, *scratch[7:15], sends)
    feed_stages = reduce_stages(CHUNKS, [feed_ref], *scratch[:7], sends)
    for step in (2, 1, 3, 0):
        sends(
            ups_ref.at[1 - xl, mod4(my_y + step)],
            up_buf.at[step],
            ex.at[step],
            ey.at[step],
            neighbour("xl", 1),
        )
    next(ring_stages)
    next(feed_stages)
    for part in parts[:3]:
        part.wait()

    def grad_ref(h, first, second, start):
        zz, yy = (first, second) if h == 0 else (second, first)
        return g_ref.at[zz, both, yy, pl.ds(h * half + start, quarter)]

    def grad(h, first, second, j, start, count):
        zz, yy = (first, second) if h == 0 else (second, first)
        return g_ref[zz, j, yy, h * half + start : h * half + start + count, :].astype(F32)

    def firsts(h, k):
        return mod4(place[rings[h][0]] + STEPS[k])

    for k in range(4):
        for h in (0, 1):
            second = place[rings[h][1]]
            for d, way in ((0, 1), (1, -1)):
                sends(
                    grad_ref(h, firsts(h, k), mod4(second + 2), d * quarter),
                    t_buf.at[h, d, k],
                    t_s.at[h, d, k],
                    t_r.at[h, d, k],
                    neighbour(rings[h][1], way),
                )
    for k in range(4):
        for h in (0, 1):
            second = place[rings[h][1]]
            for d, way in ((0, 1), (1, -1)):
                sends(
                    grad_ref(h, firsts(h, k), mod4(second + way), (1 - d) * quarter),
                    r_buf.at[h, d, k, both, pl.ds((1 - d) * quarter, quarter)],
                    r_s.at[h, d, k, 0],
                    r_r.at[h, d, k, 0],
                    neighbour(rings[h][1], way),
                )
    next(ring_stages)
    next(feed_stages)
    for part in parts[3:]:
        part.wait()
    for step in (2, 1, 3):
        sends(
            downs_ref.at[mod4(my_y + step)],
            down_out.at[my_y],
            es.at[1, step - 1],
            er.at[1, step - 1],
            neighbour("y", step),
        )
    for k, step in enumerate((2, 1, 3, 0)):
        arrived(up_buf.at[step], ey.at[step])
        value = (up_own[mod4(my_y + step)].astype(F32) + up_buf[step].astype(F32)).astype(BF16)
        if step == 0:
            up_out[my_y] = value
        else:
            up_sum[step - 1] = value
            sends(
                up_sum.at[step - 1],
                up_out.at[my_y],
                es.at[0, step - 1],
                er.at[0, step - 1],
                neighbour("y", step),
            )
        for h in (0, 1):
            second = place[rings[h][1]]
            for d, way in ((0, 1), (1, -1)):
                arrived(t_buf.at[h, d, k], t_r.at[h, d, k])
                for j in (0, 1):
                    t_buf[h, d, k, j] = (
                        t_buf[h, d, k, j].astype(F32)
                        + grad(h, firsts(h, k), mod4(second + way), j, d * quarter, quarter)
                    ).astype(BF16)
                sends(
                    t_buf.at[h, d, k],
                    r_buf.at[h, d, k, both, pl.ds(d * quarter, quarter)],
                    r_s.at[h, d, k, 1],
                    r_r.at[h, d, k, 1],
                    neighbour(rings[h][1], way),
                )
    total = next(ring_stages)
    for k in range(4):
        for h in (0, 1):
            second = place[rings[h][1]]
            for d in (0, 1):
                arrived(r_buf.at[h, d, k, both, pl.ds((1 - d) * quarter, quarter)], r_r.at[h, d, k, 0])
                arrived(r_buf.at[h, d, k, both, pl.ds(d * quarter, quarter)], r_r.at[h, d, k, 1])
            for j in (0, 1):
                r_buf[h, 0, k, j] = (
                    r_buf[h, 0, k, j].astype(F32)
                    + r_buf[h, 1, k, j].astype(F32)
                    + grad(h, firsts(h, k), second, j, 0, half)
                ).astype(BF16)
            for d, way in ((0, 1), (1, -1)):
                device = neighbour(rings[h][0], way)
                if k == 0:
                    sends(
                        r_buf.at[h, 0, 0, both, pl.ds(d * quarter, quarter)],
                        tb_buf.at[h, d],
                        tb_s.at[h, d],
                        tb_r.at[h, d],
                        device,
                    )
                if k == 1 + d:
                    sends(
                        r_buf.at[h, 0, k, both, pl.ds((1 - d) * quarter, quarter)],
                        rb_buf.at[h, d, both, pl.ds((1 - d) * quarter, quarter)],
                        rb_s.at[h, d, 0],
                        rb_r.at[h, d, 0],
                        device,
                    )
                    arrived(tb_buf.at[h, d], tb_r.at[h, d])
                    for j in (0, 1):
                        tb_buf[h, d, j] = (
                            tb_buf[h, d, j].astype(F32)
                            + r_buf[h, 0, k, j, d * quarter : (d + 1) * quarter, :].astype(F32)
                        ).astype(BF16)
                    sends(
                        tb_buf.at[h, d],
                        rb_buf.at[h, d, both, pl.ds(d * quarter, quarter)],
                        rb_s.at[h, d, 1],
                        rb_r.at[h, d, 1],
                        device,
                    )
    rows_half = x_ref.shape[0] // 2
    for part in (0, 1):
        rows = slice(part * rows_half, (part + 1) * rows_half)
        x = x_ref[rows, :].astype(F32)
        inverse = lax.rsqrt(jnp.mean(x * x, 1, keepdims=True) + EPSILON)
        normed = x * inverse
        dscaled = total(part) * gain_ref[...]
        mean = jnp.mean(dscaled * normed, 1, keepdims=True)
        dinput_ref[rows, :] = dmiddle_ref[rows, :] + inverse * (dscaled - normed * mean)
    for h in (0, 1):
        for d in (0, 1):
            arrived(rb_buf.at[h, d, both, pl.ds((1 - d) * quarter, quarter)], rb_r.at[h, d, 0])
            arrived(rb_buf.at[h, d, both, pl.ds(d * quarter, quarter)], rb_r.at[h, d, 1])
        for j in (0, 1):
            rb_buf[h, 0, j] = (
                rb_buf[h, 0, j].astype(F32)
                + rb_buf[h, 1, j].astype(F32)
                + r_buf[h, 0, 3, j].astype(F32)
            ).astype(BF16)
        sends(rb_buf.at[h, 0, 1 - xl], c_buf.at[h], c_s.at[h], c_r.at[h], neighbour("xl", 1))
        out_ref[xl, h * half : (h + 1) * half, :] = rb_buf[h, 0, xl].astype(F32)
    for h in (0, 1):
        arrived(c_buf.at[h], c_r.at[h])
        out_ref[1 - xl, h * half : (h + 1) * half, :] = c_buf[h].astype(F32)
    first, last = qkv_ref.shape[-1], qkv_ref.shape[-1] + small_ref.shape[-1]
    small_own[...] = out_ref[0, :, first:last] + out_ref[1, :, first:last]
    for n, peer in enumerate(peers):
        sends(small_own, small_buf.at[n], small_s.at[n], small_r.at[n], peer)
    feed = next(feed_stages)
    step = x_ref.shape[0] // CHUNKS
    for n in range(CHUNKS):
        rows = slice(n * step, (n + 1) * step)
        output_ref[rows, :] = (middle_ref[rows, :] + feed(0, n)).astype(BF16)
    for n, result in enumerate((up_out, down_out)):
        for step in (1, 3, 2):
            arrived(result.at[mod4(my_y - step)], er.at[n, step - 1])
    for n in range(3):
        arrived(small_buf.at[n], small_r.at[n])
    small_out[...] = (small_own[...] + small_buf[1]) + (small_buf[0] + small_buf[2])
    sends.finish()


def finish(grads, ups, downs, part, feed, x, middle, dmiddle, gain):
    rows, cols = grads[0].shape[0], sum(grad.shape[1] for grad in grads)
    share = rows // 32
    half, quarter = share // 2, share // 4
    dma = pltpu.SemaphoreType.DMA
    up_cols, down_cols = ups.shape[1], downs.shape[1]
    small = (share, grads[1].shape[1])
    own_rows, width = x.shape
    anywhere = pl.BlockSpec(memory_space=pl.ANY)
    return pl.pallas_call(
        finish_body,
        out_shape=[
            jax.ShapeDtypeStruct((2, share, cols), F32),
            jax.ShapeDtypeStruct((4, share, up_cols), BF16),
            jax.ShapeDtypeStruct((4, share, down_cols), BF16),
            jax.ShapeDtypeStruct((own_rows, width), BF16),
            jax.ShapeDtypeStruct((own_rows, width), F32),
            jax.ShapeDtypeStruct(small, F32),
        ],
        in_specs=[anywhere] * 5 + vmem(6),
        out_specs=vmem(6),
        scratch_shapes=[
            pltpu.VMEM((4, 2, 4, share, cols), BF16),
            dma((5,)),
            pltpu.VMEM((2, 2, 4, 2, quarter, cols), BF16),
            pltpu.VMEM((2, 2, 4, 2, half, cols), BF16),
            pltpu.VMEM((2, 2, 2, quarter, cols), BF16),
            pltpu.VMEM((2, 2, 2, half, cols), BF16),
            pltpu.VMEM((2, half, cols), BF16),
            dma((2, 2, 4)),
            dma((2, 2, 4)),
            dma((2, 2, 4, 2)),
            dma((2, 2, 4, 2)),
            dma((2, 2)),
            dma((2, 2)),
            dma((2, 2, 2)),
            dma((2, 2, 2)),
            dma((2,)),
            dma((2,)),
            pltpu.VMEM((4, share, up_cols), BF16),
            pltpu.VMEM((4, share, up_cols), BF16),
            pltpu.VMEM((3, share, up_cols), BF16),
            dma((4,)),
            dma((4,)),
            dma((2, 3)),
            dma((2, 3)),
            pltpu.VMEM(small, F32),
            pltpu.VMEM((3, *small), F32),
            dma((3,)),
            dma((3,)),
        ]
        + reduce_scratch(1, own_rows, width)
        + ring_reduce_scratch(own_rows, width),
        compiler_params=pltpu.CompilerParams(
            collective_id=5, has_side_effects=True, vmem_limit_bytes=60 * MIB
        ),
        name="finish",
    )(
        *(grad.reshape(4, 2, 4, share, grad.shape[1]) for grad in grads),
        ups.reshape(2, 4, share, up_cols),
        downs.reshape(4, share, down_cols),
        part.reshape(2, 2, 2, own_rows, width),
        feed.reshape(4, own_rows, width),
        x,
        middle,
        dmiddle,
        gain[None],
    )


def dot(a, b, dims):
    return lax.dot_general(a, b, (dims, ((), ())), preferred_element_type=F32)


def joined_body(rows_ref, gate_up_ref, linear_up_ref, gate_out, linear_out):
    up = jnp.concatenate([gate_up_ref[...], linear_up_ref[...]], 1)
    joined = dot(rows_ref[...], up, ((1,), (0,)))
    gate_out[...] = joined[:, :LANES]
    linear_out[...] = joined[:, LANES:]


def joined_rows(rows, up):
    count, width, hidden = rows.shape[0], up.shape[0], up.shape[1] // 2
    chunks = hidden // LANES
    chunk = pl.BlockSpec((count, LANES), lambda j: (0, j))
    return pl.pallas_call(
        joined_body,
        grid=(chunks,),
        in_specs=[
            pl.BlockSpec((count, width), lambda j: (0, 0)),
            pl.BlockSpec((width, LANES), lambda j: (0, j)),
            pl.BlockSpec((width, LANES), lambda j: (0, chunks + j)),
        ],
        out_specs=[chunk] * 2,
        out_shape=[jax.ShapeDtypeStruct((count, hidden), F32)] * 2,
        compiler_params=pltpu.CompilerParams(vmem_limit_bytes=48 * MIB),
        name="joined_rows",
    )(rows, up, up)


def experts_body(
    grad_ref, down_ref, gate_pre_ref, linear_ref, gate_ref,
    dgate_pre_out, dlinear_out, hidden_out, gated_out, dgate_out, *, units,
):
    j = pl.program_id(0)

    @pl.when(j == 0)
    def _():
        dgate_out[...] = jnp.zeros_like(dgate_out)

    dhidden = dot(grad_ref[...], down_ref[...], ((1,), (0,)))
    gate_pre, linear = gate_pre_ref[...], linear_ref[...]
    sigmoid = jax.nn.sigmoid(gate_pre)
    silu = gate_pre * sigmoid
    hidden = silu * linear
    gate = gate_ref[...]
    product = hidden * dhidden
    dgate_out[...] += product[:, :LANES] + jnp.where(j * WIDE + LANES < units, product[:, LANES:], 0.0)
    dhidden = dhidden * gate
    hidden_out[...] = hidden.astype(BF16)
    gated_out[...] = (hidden * gate).astype(BF16)
    dgate_pre_out[...] = (dhidden * linear * (sigmoid + silu * (1.0 - sigmoid))).astype(BF16)
    dlinear_out[...] = (dhidden * silu).astype(BF16)


def experts(grads, down, gate_pre, linear, gates):
    count, hidden = gate_pre.shape
    width = down.shape[0]
    chunk = pl.BlockSpec((count, WIDE), lambda j: (0, j))
    some = jax.ShapeDtypeStruct((count, hidden), BF16)
    return pl.pallas_call(
        functools.partial(experts_body, units=hidden),
        grid=(pl.cdiv(hidden, WIDE),),
        in_specs=[
            pl.BlockSpec((count, width), lambda j: (0, 0)),
            pl.BlockSpec((width, WIDE), lambda j: (0, j)),
            chunk,
            chunk,
            pl.BlockSpec((count, 1), lambda j: (0, 0)),
        ],
        out_specs=[chunk] * 4 + [pl.BlockSpec((count, LANES), lambda j: (0, 0))],
        out_shape=[some] * 4 + [jax.ShapeDtypeStruct((count, LANES), F32)],
        compiler_params=pltpu.CompilerParams(vmem_limit_bytes=56 * MIB),
        name="experts",
    )(grads, down, gate_pre, linear, gates)


def return_body(
    dgate_pre_ref, dlinear_ref, up_ref, dgate_ref, rows_ref,
    dunit_out, dgate_out, up_out,
    djoined, up, rows, dunit, dgate_own, dunit_buf, dgate_buf, dunit_sum, dgate_sum, block,
    loc, core_s, core_r, far_s, far_r, out_sem,
):
    y, core = lax.axis_index("y"), lax.axis_index("core")
    slots = dgate_ref.shape[1]
    half = slots // 2
    hidden = dgate_pre_ref.shape[1]
    sends = Sends()
    loads = []
    for n, (src, dst) in enumerate(
        (
            (up_ref, up),
            (dgate_pre_ref, djoined.at[:, pl.ds(0, hidden)]),
            (dlinear_ref, djoined.at[:, pl.ds(hidden, hidden)]),
            (rows_ref.at[:, pl.ds(0, rows.shape[1])], rows),
        )
    ):
        loads.append(pltpu.make_async_copy(src, dst, loc.at[1, n]))
        loads[-1].start()
    greet(neighbour("core", 1), *(neighbour("y", step) for step in (1, 2, 3)))
    mine = pl.ds(pl.multiple_of(core * half, half), half)
    theirs = pl.ds(pl.multiple_of((1 - core) * half, half), half)
    order = (2, 1, 3, 0)
    own = []
    for step in order:
        target = mod4(y + step)
        sends(
            dgate_ref.at[target, theirs],
            dgate_buf.at[step],
            core_s.at[1, step],
            core_r.at[1, step],
            neighbour("core", 1),
        )
        own.append(pltpu.make_async_copy(dgate_ref.at[target, mine], dgate_own.at[step], loc.at[0, step]))
        own[-1].start()
    for load in loads[:3]:
        load.wait()
    for copy in own:
        copy.wait()

    def compute(step):
        at = pl.ds(pl.multiple_of(mod4(y + step) * slots, slots), slots)
        dunit[step] = dot(djoined[at, :], up[...], ((1,), (1,))).astype(BF16)
        sends(
            dunit.at[step, theirs],
            dunit_buf.at[step],
            core_s.at[0, step],
            core_r.at[0, step],
            neighbour("core", 1),
        )

    def pass_on(step):
        arrived(dunit_buf.at[step], core_r.at[0, step])
        arrived(dgate_buf.at[step], core_r.at[1, step])
        dunit_value = (dunit[step, mine, :].astype(F32) + dunit_buf[step].astype(F32)).astype(BF16)
        dgate_value = dgate_own[step] + dgate_buf[step]
        if step == 0:
            dunit_out[y] = dunit_value
            dgate_out[y] = dgate_value
            return
        dunit_sum[step - 1] = dunit_value
        dgate_sum[step - 1] = dgate_value
        for n, (summed, result) in enumerate(((dunit_sum, dunit_out), (dgate_sum, dgate_out))):
            sends(
                summed.at[step - 1],
                result.at[y],
                far_s.at[n, step - 1],
                far_r.at[n, step - 1],
                neighbour("y", step),
            )

    compute(2)
    compute(1)
    pass_on(2)
    compute(3)
    pass_on(1)
    compute(0)
    pass_on(3)
    loads[3].wait()
    blocks = up_out.shape[0] // WIDE

    @pl.loop(0, blocks)
    def _(j):
        at = pl.ds(pl.multiple_of(j * WIDE, WIDE), WIDE)
        slot = lax.rem(j, 2)

        @pl.when(j >= 2)
        def _():
            pltpu.make_async_copy(block.at[slot], up_out.at[at], out_sem.at[slot]).wait()

        block[slot] = dot(rows[:, at], djoined[...], ((0,), (0,))).astype(BF16)
        pltpu.make_async_copy(block.at[slot], up_out.at[at], out_sem.at[slot]).start()

    pass_on(0)
    for slot in (0, 1):
        pltpu.make_async_copy(block.at[slot], up_out.at[pl.ds(0, WIDE)], out_sem.at[slot]).wait()
    for n, result in enumerate((dunit_out, dgate_out)):
        for step in (1, 3, 2):
            arrived(result.at[mod4(y - step)], far_r.at[n, step - 1])
    sends.finish()


def return_rows(dgate_pre, dlinear, up, dgate, rows):
    _, slots, lanes = dgate.shape
    half = slots // 2
    width, wide = up.shape
    count = dlinear.shape[0]
    dma = pltpu.SemaphoreType.DMA
    anywhere = pl.BlockSpec(memory_space=pl.ANY)
    return pl.pallas_call(
        return_body,
        out_shape=[
            jax.ShapeDtypeStruct((4, half, width), BF16),
            jax.ShapeDtypeStruct((4, half, lanes), F32),
            jax.ShapeDtypeStruct((width, wide), BF16),
        ],
        in_specs=[anywhere] * 5,
        out_specs=vmem(2) + [anywhere],
        scratch_shapes=[
            pltpu.VMEM((count, wide), BF16),
            pltpu.VMEM((width, wide), BF16),
            pltpu.VMEM((count, width), BF16),
            pltpu.VMEM((4, slots, width), BF16),
            pltpu.VMEM((4, half, lanes), F32),
            pltpu.VMEM((4, half, width), BF16),
            pltpu.VMEM((4, half, lanes), F32),
            pltpu.VMEM((3, half, width), BF16),
            pltpu.VMEM((3, half, lanes), F32),
            pltpu.VMEM((2, WIDE, wide), BF16),
            dma((2, 4)),
            dma((2, 4)),
            dma((2, 4)),
            dma((2, 3)),
            dma((2, 3)),
            dma((2,)),
        ],
        compiler_params=pltpu.CompilerParams(
            collective_id=3, has_side_effects=True, vmem_limit_bytes=62 * MIB
        ),
        name="return_rows",
    )(dgate_pre, dlinear, up, dgate, rows)


def attention_body(
    k_ref, v_ref, q0, q1, q2, cos_ref, sin_ref, col_ref, row_ref, gate_ref,
    key_out, val_out, que_out, mix_out, gmix_out, prob_out,
):
    h = pl.program_id(1)
    cosine, sine = cos_ref[...], sin_ref[...]
    scale = 1.0 / math.sqrt(HD)

    def rotated(v):
        return v * cosine + pltpu.roll(v, HD // 2, 1) * sine

    key = rotated(k_ref[...]).astype(BF16)
    val = v_ref[...].astype(BF16)
    key_out[...] = key
    val_out[...] = val
    tokens = key.shape[0]
    half = tokens // 2
    allowed = []
    for start in (0, half):
        seen = start + half
        at_row = start + lax.broadcasted_iota(jnp.int32, (half, seen), 0)
        at_col = lax.broadcasted_iota(jnp.int32, (half, seen), 1)
        seg_row, seg_col = row_ref[0, :, :seen], col_ref[start : start + half, :]
        allowed.append((at_col <= at_row) & ((seg_row == 0) | (seg_row == seg_col)))
    for e, q_ref in enumerate((q0, q1, q2)):
        query = (rotated(q_ref[...]) * scale).astype(BF16)
        at = pl.ds(pl.multiple_of((e * HEADS + h) * HD, HD), HD)
        que_out[:, at] = query
        for n, start in enumerate((0, half)):
            rows, seen = slice(start, start + half), start + half
            scores = jnp.where(allowed[n], dot(query[rows], key[:seen], ((1,), (1,))), NEGATIVE)
            largest = jnp.max(scores, 1, keepdims=True)
            expsum = jnp.exp(scores - largest)
            prob = (expsum * (1.0 / jnp.sum(expsum, 1, keepdims=True))).astype(BF16)
            prob_out[0, 0, e, rows, :seen] = prob
            mixed = dot(prob, val[:seen], ((1,), (0,))).astype(BF16)
            mix_out[rows, at] = mixed
            gmix_out[rows, at] = (mixed.astype(F32) * gate_ref[rows, e : e + 1]).astype(BF16)


def block_specs(tokens):
    def column(n):
        return pl.BlockSpec((tokens, HD), lambda g, h: (g, n * HEADS + h))

    def rows(width):
        return pl.BlockSpec((tokens, width), lambda g, h: (g, 0))

    return column, rows


def prob_spec(tokens):
    return pl.BlockSpec((1, 1, 3, tokens, tokens), lambda g, h: (g, h, 0, 0, 0))


def attention_forward(joined, cosine, sine, segments, gates):
    groups, tokens = segments.shape
    column, rows = block_specs(tokens)
    wide = jax.ShapeDtypeStruct((groups * tokens, 3 * HEADS * HD), BF16)
    narrow = jax.ShapeDtypeStruct((groups * tokens, HEADS * HD), BF16)
    return pl.pallas_call(
        attention_body,
        grid=(groups, HEADS),
        in_specs=[column(n) for n in range(5)]
        + [rows(HD)] * 2
        + [rows(1), pl.BlockSpec((1, 1, tokens), lambda g, h: (g, 0, 0)), rows(gates.shape[1])],
        out_specs=[column(0), column(0)] + [rows(wide.shape[1])] * 3 + [prob_spec(tokens)],
        out_shape=[narrow, narrow, wide, wide, wide]
        + [jax.ShapeDtypeStruct((groups, HEADS, 3, tokens, tokens), BF16)],
        compiler_params=pltpu.CompilerParams(vmem_limit_bytes=48 * MIB),
        name="attention_forward",
    )(
        *[joined] * 5, cosine, sine, segments.reshape(-1, 1), segments[:, None], gates
    )


def attention_back_body(
    key_ref, val_ref, q0, q1, q2, m0, m1, m2, h0, h1, h2, prob_ref, cos_ref, sin_ref, gate_ref,
    grad_out, dgate_out,
):
    h = pl.program_id(1)
    cosine, sine = cos_ref[...], sin_ref[...]
    scale = 1.0 / math.sqrt(HD)

    def rotated_back(v):
        return v * cosine - pltpu.roll(v, HD // 2, 1) * sine

    key, val = key_ref[...], val_ref[...]
    tokens = key.shape[0]
    half = tokens // 2
    dkeys = [jnp.zeros((half, HD), F32)] * 2
    dvals = [jnp.zeros((half, HD), F32)] * 2
    lane = lax.broadcasted_iota(jnp.int32, (tokens, HD), 1)
    dgates = jnp.zeros((tokens, HD), F32)
    for e, (q_ref, m_ref, h_ref) in enumerate(((q0, m0, h0), (q1, m1, h1), (q2, m2, h2))):
        query, mixed, raw = q_ref[...], m_ref[...].astype(F32), h_ref[...]
        inner = jnp.sum(mixed * raw, 1, keepdims=True)
        dgates = dgates + jnp.where(lane == e, inner, 0.0)
        gate = gate_ref[:, e : e + 1]
        dmixed = (raw * gate).astype(BF16)
        delta = jnp.sum(dmixed.astype(F32) * mixed, 1, keepdims=True)
        dqueries = []
        for start in (0, half):
            rows, seen = slice(start, start + half), start + half
            prob = prob_ref[0, 0, e, rows, :seen]
            dprob = dot(dmixed[rows], val[:seen], ((1,), (1,)))
            dscores = (prob.astype(F32) * (dprob - delta[rows])).astype(BF16)
            dqueries.append(dot(dscores, key[:seen], ((1,), (0,))))
            dval = dot(prob, dmixed[rows], ((0,), (0,)))
            dkey = dot(dscores, query[rows], ((0,), (0,)))
            dvals[0] = dvals[0] + dval[:half]
            dkeys[0] = dkeys[0] + dkey[:half]
            if start:
                dvals[1] = dvals[1] + dval[half:]
                dkeys[1] = dkeys[1] + dkey[half:]
        dquery = jnp.concatenate(dqueries, 0)
        at = pl.ds(pl.multiple_of(((2 + e) * HEADS + h) * HD, HD), HD)
        grad_out[:, at] = rotated_back(dquery * scale).astype(BF16)
    dkey, dval = jnp.concatenate(dkeys, 0), jnp.concatenate(dvals, 0)
    grad_out[:, pl.ds(pl.multiple_of(h * HD, HD), HD)] = rotated_back(dkey).astype(BF16)
    grad_out[:, pl.ds(pl.multiple_of((HEADS + h) * HD, HD), HD)] = dval.astype(BF16)

    @pl.when(h == 0)
    def _():
        dgate_out[...] = dgates

    @pl.when(h > 0)
    def _():
        dgate_out[...] += dgates


def attention_back(key, val, que, mix, raw, prob, cosine, sine, gates):
    groups, tokens = prob.shape[0], prob.shape[-1]
    column, rows = block_specs(tokens)
    thirds = [column(n) for n in range(3)]
    grads = jax.ShapeDtypeStruct((groups * tokens, 5 * HEADS * HD), BF16)
    return pl.pallas_call(
        attention_back_body,
        grid=(groups, HEADS),
        in_specs=[column(0), column(0)]
        + thirds * 3
        + [prob_spec(tokens)]
        + [rows(HD)] * 2
        + [rows(gates.shape[1])],
        out_specs=[rows(grads.shape[1]), rows(HD)],
        out_shape=[grads, jax.ShapeDtypeStruct((groups * tokens, HD), F32)],
        compiler_params=pltpu.CompilerParams(vmem_limit_bytes=48 * MIB),
        name="attention_back",
    )(key, val, que, que, que, mix, mix, mix, raw, raw, raw, prob, cosine, sine, gates)


def positions(segments):
    index = jnp.arange(segments.shape[0], dtype=jnp.int32)
    prompt = jnp.sum((segments == 0).astype(jnp.int32))
    first = jnp.sum((segments == 1).astype(jnp.int32))
    before = jnp.where(segments == 0, 0, jnp.where(segments == 1, prompt, prompt + first))
    return jnp.where(segments == 0, index, prompt + index - before)


def route_gates(logits, routes, count):
    onehot = (routes[:, :, None] == jnp.arange(count, dtype=jnp.int32)).astype(F32)
    chosen = jnp.sum(onehot * logits[:, None, :], -1)
    expsum = jnp.exp(chosen - jnp.max(chosen, -1, keepdims=True))
    weights = expsum / jnp.sum(expsum, -1, keepdims=True)
    return weights, onehot, jnp.sum(weights[:, :, None] * onehot, 1)


def router_back(dgate, weights, onehot):
    dchosen = jnp.sum(dgate[:, None, :] * onehot, -1)
    dselect = weights * (dchosen - jnp.sum(weights * dchosen, -1, keepdims=True))
    return jnp.sum(dselect[:, :, None] * onehot, 1).astype(BF16)


def normalize(activations):
    inverse = lax.rsqrt(jnp.mean(activations * activations, -1, keepdims=True) + EPSILON)
    return activations * inverse, inverse


def reorder(rows):
    count, width = rows.shape
    return jnp.transpose(rows.reshape(count, 4, 2, 4, width // 32), (0, 3, 2, 1, 4)).reshape(count, width)


def pad_to(array, width):
    return jnp.pad(array, ((0, 0), (0, width - array.shape[1])))


def on_device(
    inputs,
    segments,
    att_routes,
    mlp_routes,
    key_value,
    query_proj,
    output_proj,
    router_att,
    gain_att,
    gate_up,
    down_proj,
    router_mlp,
    gain_mlp,
    out_grad,
):
    width = inputs.shape[1]
    inner = query_proj.shape[2]
    hidden_local = down_proj.shape[1]
    att_count = query_proj.shape[0]
    mlp_count = gate_up.shape[0]
    share = gate_up.shape[1]
    part = inner // 2
    qkv_cols = (2 + att_count) * part
    small_at = qkv_cols
    out_at = qkv_cols + 128
    small = jnp.concatenate([router_att, router_mlp, gain_att[:, None], gain_mlp[:, None]], 1)
    own_att = jnp.concatenate(
        [
            jnp.transpose(key_value.reshape(share, 2, 2, part), (2, 0, 1, 3)).reshape(2, share, -1),
            jnp.transpose(query_proj.reshape(att_count, share, 2, part), (2, 1, 0, 3)).reshape(
                2, share, -1
            ),
            jnp.broadcast_to(pad_to(small, 128), (2, share, 128)),
            jnp.transpose(output_proj.reshape(att_count, 2, part, share), (1, 3, 0, 2)).reshape(
                2, share, -1
            ),
        ],
        2,
    )
    inputs = reorder(inputs)
    out_grad = reorder(out_grad)
    x_all = lax.all_gather(inputs, ("xl", *TP), axis=0, tiled=True)
    grad_all = lax.all_gather(out_grad, TP, axis=0, tiled=True)
    marks = pad_to(jnp.concatenate([segments[:, None], att_routes], 1), LANES).astype(BF16)
    weights, up_parts, down_parts, marks = gather_dp(
        own_att,
        gate_up.reshape(mlp_count, share, -1),
        jnp.swapaxes(down_proj, 1, 2),
        marks,
    )
    marks = marks[:, :, :3].astype(jnp.int32)
    up_whole = lax.all_gather(
        up_parts.reshape(2 * mlp_count * share, -1), "z", axis=0, tiled=True
    )
    xl = lax.axis_index("xl")
    down_theirs = lax.ppermute(down_parts, "xl", ((0, 1), (1, 0)))

    tokens = segments.shape[0]
    match = jnp.sum((mlp_routes[:, :, None] == jnp.arange(mlp_count, dtype=jnp.int32)).astype(BF16), 1)
    index = jnp.arange(tokens, dtype=jnp.int32)
    lower = (index[None, :] < index[:, None]).astype(BF16)
    rank = dot(lower, match, ((1,), (0,)))
    slot = jnp.where(match > 0, rank.astype(jnp.int32), -1)
    pick = (slot.T[:, None, :] == jnp.arange(CAP, dtype=jnp.int32)[None, :, None]).astype(BF16)
    pick_rows = pick.reshape(mlp_count * CAP, tokens)
    grad_rows = dot(pick_rows, grad_all, ((1,), (0,))).astype(BF16)
    grad_in = lax.all_to_all(grad_rows.reshape(mlp_count, CAP, width), "y", 0, 0, tiled=True)
    grad_in = grad_in.reshape(mlp_count * CAP, width)

    small_all = weights[:, small_at : small_at + 128].astype(F32)
    gain_one, gain_two = small_all[:, 7], small_all[:, 8]
    segments = marks[:, :, 0]
    att_routes = marks[:, :, 1:].reshape(2 * tokens, 2)
    places = jax.vmap(positions)(segments).reshape(-1).astype(F32)
    frequency = ROPE_BASE ** (-2.0 * jnp.arange(HD // 2, dtype=F32) / HD)
    angles = places[:, None] * frequency[None, :]
    cosine = jnp.concatenate([jnp.cos(angles)] * 2, 1)
    sine = jnp.concatenate([-jnp.sin(angles), jnp.sin(angles)], 1)
    normed_one, _ = normalize(x_all.astype(F32))
    unit_one = (normed_one * gain_one).astype(BF16)
    joined_att = dot(unit_one, weights[:, :out_at], ((1,), (0,)))
    weights_att, onehot_att, gate_att = route_gates(
        joined_att[:, small_at : small_at + att_count], att_routes, att_count
    )
    key_rot, val_rows, queries, mixed, gmixed, prob = attention_forward(
        joined_att, cosine, sine, segments, gate_att
    )
    down_theirs, gmixed = lax.optimization_barrier((down_theirs, gmixed))
    down_pair = jnp.where(
        xl == 0, jnp.stack([down_parts, down_theirs]), jnp.stack([down_theirs, down_parts])
    )
    down_whole = lax.all_gather(
        down_pair.reshape(2 * mlp_count * share, -1), "z", axis=0, tiled=True
    )
    out_weights = weights[:, out_at:]
    attention = dot(gmixed, out_weights, ((1,), (1,))).astype(BF16)
    middle, unit_two = middle_and_unit(attention, inputs, gain_two)

    router_two = weights[:, small_at + att_count : small_at + att_count + mlp_count]
    logit_mlp = dot(unit_two, router_two, ((1,), (0,)))
    weights_mlp, onehot_mlp, gate_mlp = route_gates(logit_mlp, mlp_routes, mlp_count)
    gate_high = gate_mlp.astype(BF16)
    gate_low = (gate_mlp - gate_high.astype(F32)).astype(BF16)
    extended = jnp.concatenate([unit_two, pad_to(jnp.concatenate([gate_high, gate_low], 1), 128)], 1)
    rows_out = dot(pick_rows, extended, ((1,), (0,))).astype(BF16)
    rows_ext = rows_to_experts(rows_out.reshape(mlp_count, CAP, width + 128))
    rows_ext = rows_ext.reshape(mlp_count * CAP, width + 128)
    gates_ext = rows_ext[:, width : width + 2 * mlp_count].astype(F32)
    mine = (jnp.arange(2 * mlp_count) % mlp_count == lax.axis_index("y")).astype(F32)
    gates_in = jnp.sum(gates_ext * mine, 1, keepdims=True)
    gate_pre, linear = joined_rows(rows_ext, up_whole)
    dgate_pre, dlinear, hidden, gated, dgate_part = experts(
        grad_in, down_whole, gate_pre, linear, gates_in
    )
    grad_down_whole = dot(grad_in, gated, ((0,), (0,))).astype(BF16)
    dgate_part, grad_down_whole = lax.optimization_barrier((dgate_part, grad_down_whole))
    grad_down_sum = lax.psum_scatter(grad_down_whole, "z", scatter_dimension=0, tiled=True)
    dunit_back, dgate_back, grad_up_whole = return_rows(
        dgate_pre, dlinear, up_whole, dgate_part.reshape(mlp_count, CAP, LANES), rows_ext
    )
    grad_up_sum = lax.psum_scatter(grad_up_whole, "z", scatter_dimension=0, tiled=True)
    pick_half = lax.dynamic_slice_in_dim(pick, lax.axis_index("core") * (CAP // 2), CAP // 2, 1)
    dgate_two = jnp.sum(pick_half.astype(F32) * jnp.sum(dgate_back, -1, keepdims=True), 1).T
    dlogit_mlp = router_back(dgate_two, weights_mlp, onehot_mlp)
    dunit_two = dot(
        pick_half.reshape(-1, tokens), dunit_back.reshape(-1, width), ((0,), (0,))
    ) + dot(dlogit_mlp, router_two, ((1,), (1,)))
    dmiddle, grad_gain_two, dattention, branch_back = middle_back(
        dunit_two.astype(BF16), middle, out_grad, gain_two, hidden, down_whole
    )

    grad_down_sum, dattention = lax.optimization_barrier((grad_down_sum, dattention))
    raw = dot(dattention, out_weights, ((1,), (0,)))
    grad_qkv, dgate_one = attention_back(
        key_rot, val_rows, queries, mixed, raw, prob, cosine, sine, gate_att
    )
    halves = grad_down_sum.reshape(2, mlp_count * share, hidden_local)
    theirs = lax.ppermute(
        lax.dynamic_index_in_dim(halves, 1 - xl, 0, keepdims=False), "xl", ((0, 1), (1, 0))
    )
    theirs, grad_qkv, gmixed, dattention, branch_back, dlogit_mlp = lax.optimization_barrier(
        (theirs, grad_qkv, gmixed, dattention, branch_back, dlogit_mlp)
    )
    grad_rmlp = dot(unit_two, dlogit_mlp, ((0,), (0,)))
    grad_down_sum = (
        lax.dynamic_index_in_dim(halves, xl, 0, keepdims=False).astype(F32) + theirs.astype(F32)
    ).astype(BF16)
    dlogit_att = router_back(dgate_one[:, :att_count], weights_att, onehot_att)
    grad_joined = jnp.concatenate([grad_qkv, pad_to(dlogit_att, 128)], 1)
    dunit_one = dot(grad_joined, weights[:, :out_at], ((1,), (1,)))
    grad_gain_one = jnp.sum(dunit_one * normed_one, 0)
    grad_small = jnp.concatenate(
        [
            dot(unit_one, dlogit_att, ((0,), (0,))),
            grad_rmlp,
            grad_gain_one[:, None],
            grad_gain_two[:, None],
        ],
        1,
    )
    gate_slots = jnp.sum(pick_half.astype(F32) * gate_mlp.T[:, None, :], -1, keepdims=True)
    feed = dot(
        pick_half.reshape(-1, tokens),
        (branch_back.astype(F32) * gate_slots).astype(BF16).reshape(-1, width),
        ((0,), (0,)),
    )
    summed_att, ups_sum, downs_sum, output, grad_input, small_sum = finish(
        (
            dot(unit_one, grad_qkv, ((0,), (0,))).astype(BF16),
            pad_to(grad_small, 128).astype(BF16),
            dot(dattention, gmixed, ((0,), (0,))).astype(BF16),
        ),
        grad_up_sum,
        grad_down_sum,
        dunit_one.astype(BF16),
        feed.astype(BF16),
        inputs,
        middle,
        dmiddle,
        gain_one,
    )
    grad_kv = jnp.transpose(
        summed_att[:, :, : 2 * part].reshape(2, share, 2, part), (1, 2, 0, 3)
    ).reshape(share, 2, inner)
    grad_query = jnp.transpose(
        summed_att[:, :, 2 * part : qkv_cols].reshape(2, share, att_count, part), (2, 1, 0, 3)
    ).reshape(att_count, share, inner)
    grad_output = jnp.transpose(
        summed_att[:, :, out_at:].reshape(2, share, att_count, part), (2, 0, 3, 1)
    ).reshape(att_count, inner, share)
    output = reorder(output)
    grad_input = reorder(grad_input)

    grads_up = ups_sum.astype(F32).reshape(mlp_count, share, 2, hidden_local)
    grads_down = jnp.swapaxes(downs_sum.astype(F32), 1, 2)
    return (
        output,
        grad_input,
        grad_kv,
        grad_query,
        grad_output,
        small_sum[:, :3],
        small_sum[:, 7],
        grads_up,
        grads_down,
        small_sum[:, 3:7],
        small_sum[:, 8],
    )


def solution(mesh):
    fine = Mesh(mesh.devices.reshape(4, 2, 4, 2, 2), ALL)
    return jax.shard_map(
        on_device,
        mesh=fine,
        in_specs=(
            P(ALL, None),
            P(DP),
            P(DP, None),
            P(DP, None),
            P(DP, None, TP),
            P(None, DP, TP),
            P(None, TP, DP),
            P(DP, None),
            P(DP),
            P(None, DP, None, TP),
            P(None, TP, DP),
            P(DP, None),
            P(DP),
            P(ALL, None),
        ),
        out_specs=(
            P(ALL, None),
            P(ALL, None),
            P(DP, None, TP),
            P(None, DP, TP),
            P(None, TP, DP),
            P(DP, None),
            P(DP),
            P(None, DP, None, TP),
            P(None, TP, DP),
            P(DP, None),
            P(DP),
        ),
        check_vma=False,
    )
```
